32 devices in a mesh: dp: 8 (over z, y), mp: 4 (over x, core).
Axes of the slice: x: 2, y: 2, z: 4, core: 2. Of those that a mesh axis runs over, the one named last changes fastest.
Arguments:
- states: bfloat16 [8, 1024, 1024], P(None, 'dp', 'mp'), may hold values from -6 to 6
- memory: bfloat16 [8, 1024, 1024], P(None, 'dp', 'mp'), may hold values from -6 to 6
- cotangent: bfloat16 [8, 1024, 1024], P('dp', 'mp'), may hold values from -6 to 6
- lengths: int32 [8], replicated, may hold values from 512 to 1024, as said below
- memory_lengths: int32 [8], replicated, may hold values from 64 to 1024, as said below
- regroup_order: int32 [8], replicated, may hold values from 0 to 7, as said below
- attn_weights: float32 [8, 1024, 1024], P(None, 'dp', 'mp')
- ffn_weights: float32 [2, 1024, 4096], P(None, 'dp', 'mp')
- norm_params: float32 [8, 1024], P(None, 'dp')
- attn_mean: float32 [8, 1024, 1024], P(None, 'dp', 'mp'), may hold values from -0.00015258789 to 0.00015258789
- ffn_mean: float32 [2, 1024, 4096], P(None, 'dp', 'mp'), may hold values from -0.00015258789 to 0.00015258789
- norm_mean: float32 [8, 1024], P(None, 'dp'), may hold values from -0.00048828125 to 0.00048828125
- attn_square: float32 [8, 1024, 1024], P(None, 'dp', 'mp'), may hold values from 5.960465e-11 to 2.384186e-10
- ffn_square: float32 [2, 1024, 4096], P(None, 'dp', 'mp'), may hold values from 5.960465e-11 to 2.384186e-10
- norm_square: float32 [8, 1024], P(None, 'dp'), may hold values from 5.364418e-10 to 2.1457671e-09
- attn_average: float32 [8, 1024, 1024], P(None, 'dp', 'mp'), may hold values from -0.1875 to 0.1875
- ffn_average: float32 [2, 1024, 4096], P(None, 'dp', 'mp'), may hold values from -0.1875 to 0.1875
- norm_average: float32 [8, 1024], P(None, 'dp'), may hold values from -0.5 to 1.5
Outputs:
- layer_output: bfloat16 [8, 1024, 1024], P('dp', 'mp')
- states_grad: float32 [8, 1024, 1024], P(None, 'dp', 'mp')
- memory_grad: float32 [8, 1024, 1024], P(None, 'dp', 'mp')
- attn_updated: float32 [8, 1024, 1024], P(None, 'dp', 'mp')
- ffn_updated: float32 [2, 1024, 4096], P(None, 'dp', 'mp')
- norm_updated: float32 [8, 1024], P(None, 'dp')
- mean_attn: float32 [8, 1024, 1024], P(None, 'dp', 'mp')
- mean_ffn: float32 [2, 1024, 4096], P(None, 'dp', 'mp')
- mean_norm: float32 [8, 1024], P(None, 'dp')
- square_attn: float32 [8, 1024, 1024], P(None, 'dp', 'mp')
- square_ffn: float32 [2, 1024, 4096], P(None, 'dp', 'mp')
- square_norm: float32 [8, 1024], P(None, 'dp')
- average_attn: float32 [8, 1024, 1024], P(None, 'dp', 'mp')
- average_ffn: float32 [2, 1024, 4096], P(None, 'dp', 'mp')
- average_norm: float32 [8, 1024], P(None, 'dp')
- grad_norm: float32 [], replicated
The draws below stay inside these ranges and needn't reach their ends.
Inputs may be any that keep to these rules, and one draw needn't show every extreme that they name: `lengths`: some utterance has exactly 1024 units. `memory_lengths`: some memory has exactly 1024 frames. `regroup_order`: every number from 0 to 7 appears once.
All inputs are finite; a program needn't handle non-finite values.
Results may differ from the reference program's by a relative error of at most 0.03.
The reference program's roundings to bfloat16 on the way count: a program that leaves them out, or rounds other values in their place, can miss the bound.
Values may be sent and summed in bfloat16 or wider, within the bound.
A program may use at most 192 MiB of HBM per device.

```python
import math
import jax
import jax.numpy as jnp
from jax import lax

D = 1024
HEADS = 16
HD = 64
FF = 4096
UTT_DEV = 1
SLOT = 1024
MSLOT = 1024
LMIN = 512
MMIN = 64
STEP = 10
UTTS = 8


def rising(width, lowest, highest):
    return lowest + (highest - lowest) * jnp.arange(width, dtype=jnp.float32) / max(width - 1, 1)


def length_base(key):
    values = jax.random.randint(jax.random.fold_in(key, 5), (UTTS,), LMIN, SLOT + 1)
    longest_at = jax.random.randint(jax.random.fold_in(key, 6), (), 0, UTTS)
    return values.at[longest_at].set(SLOT)


def draw_lengths(key, part):
    shared = length_base(key)
    return shared.astype(jnp.int32)


def draw_regroup_order(key, part):
    shared = length_base(key)
    key = jax.random.fold_in(key, 2)
    tiebreak = jax.random.permutation(key, UTTS)
    scores = shared * UTTS + tiebreak
    ranking = jnp.argsort(-scores)
    devices = UTTS // UTT_DEV
    device_index = jnp.arange(devices)[:, None]
    slot_index = jnp.arange(UTT_DEV)[None, :]
    choose = slot_index * devices + jnp.where(slot_index % 2 == 0, device_index, devices - 1 - device_index)
    return ranking[choose.reshape(-1)].astype(jnp.int32)


def draw_memory_lengths(key, part):
    key = jax.random.fold_in(key, 3)
    values = jax.random.randint(jax.random.fold_in(key, 1), (UTTS,), MMIN, MSLOT + 1)
    longest_at = jax.random.randint(jax.random.fold_in(key, 2), (), 0, UTTS)
    return values.at[longest_at].set(MSLOT).astype(jnp.int32)


def draw_attn_weights(key, part):
    key = jax.random.fold_in(key, 11)
    random_part = jnp.clip(jax.random.normal(key, (8, D, D), jnp.float32), -4.0, 4.0)
    inner = D ** (-0.5)
    outer = (D // 8) ** (-0.5)
    scales = jnp.array([inner, inner, inner, outer, inner, inner, inner, outer], jnp.float32)
    columns = rising(D, 0.7, 1.4)
    return random_part * scales[:, None, None] * columns[None, None, :]


def draw_ffn_weights(key, part):
    key = jax.random.fold_in(key, 12)
    random_part = jnp.clip(jax.random.normal(key, (2, D, FF), jnp.float32), -4.0, 4.0)
    scales = jnp.array([D ** (-0.5), FF ** (-0.5)], jnp.float32)
    columns = rising(FF, 0.7, 1.4)
    return random_part * scales[:, None, None] * columns[None, None, :]


def draw_norm_params(key, part):
    key = jax.random.fold_in(key, 13)
    factors = jnp.exp(jax.random.uniform(jax.random.fold_in(key, 1), (4, D), jnp.float32, -0.35, 0.35))
    gains = rising(D, 0.7, 1.6)[None, :] * factors
    biases = 0.3 * jnp.clip(jax.random.normal(jax.random.fold_in(key, 2), (4, D), jnp.float32), -4.0, 4.0)
    return jnp.concatenate([gains, biases], axis=0)


def steps_of(key, shape, cuts, low, high):
    loudness = 1.0
    for axis_at, blocks in cuts:
        heights = jax.random.uniform(jax.random.fold_in(jax.random.fold_in(key, 6), axis_at), (blocks,), jnp.float32, low / len(cuts), high / len(cuts))
        loudness = loudness * jnp.repeat(jnp.exp(heights), shape[axis_at] // blocks).reshape((-1,) + (1,) * (len(shape) - 1 - axis_at))
    return loudness


def bell_draw(rng, extent, scale, bound, pieces=(), kind=jnp.bfloat16):
    loudness = steps_of(rng, extent, pieces, -0.22, 0.18) if pieces else 1.0
    drawn = jax.random.normal(rng, extent, jnp.float32) * scale * loudness
    return jnp.minimum(jnp.maximum(drawn, -bound), bound).astype(kind)


def setup_inputs(seed: int = 0) -> dict:
    splits = jax.random.split(jax.random.key(seed), 19)
    states = bell_draw(splits[0], (UTTS, SLOT, D), 1.0, 6.0, ((1, 8), (2, 4)))
    memory = bell_draw(splits[1], (UTTS, MSLOT, D), 1.0, 6.0, ((1, 8), (2, 4)))
    cotangent = bell_draw(splits[2], (UTTS, SLOT, D), 1.0, 6.0, ((0, 8), (1, 4)))
    lengths = draw_lengths(jax.random.fold_in(splits[18], 71), 0)
    memory_lengths = draw_memory_lengths(jax.random.fold_in(splits[18], 71), 0)
    regroup_order = draw_regroup_order(jax.random.fold_in(splits[18], 71), 0)
    attn_weights = draw_attn_weights(jax.random.fold_in(splits[18], 71), 0)
    ffn_weights = draw_ffn_weights(jax.random.fold_in(splits[18], 71), 0)
    norm_params = draw_norm_params(jax.random.fold_in(splits[18], 71), 0)
    attn_mean = bell_draw(splits[9], (8, D, D), (0.111 / (8 * D * D + 2 * D * FF) ** 0.5), 0.00015258789, ((1, 8), (2, 4)), jnp.float32)
    ffn_mean = bell_draw(splits[10], (2, D, FF), (0.111 / (8 * D * D + 2 * D * FF) ** 0.5), 0.00015258789, ((1, 8), (2, 4)), jnp.float32)
    norm_mean = bell_draw(splits[11], (8, D), (0.333 / (8 * D * D + 2 * D * FF) ** 0.5), 0.00048828125, ((1, 8),), jnp.float32)
    attn_square = jnp.clip(jnp.exp(math.log(2.3841859042583735e-10) - 1.3862944 * jax.random.uniform(splits[12], (8, D, D), jnp.float32) ** steps_of(splits[12], (8, D, D), ((1, 8), (2, 4)), -0.2, 0.2)), 5.960464760645934e-11, 2.3841859042583735e-10)
    ffn_square = jnp.clip(jnp.exp(math.log(2.3841859042583735e-10) - 1.3862944 * jax.random.uniform(splits[13], (2, D, FF), jnp.float32) ** steps_of(splits[13], (2, D, FF), ((1, 8), (2, 4)), -0.2, 0.2)), 5.960464760645934e-11, 2.3841859042583735e-10)
    norm_square = jnp.clip(jnp.exp(math.log(2.145767119543507e-09) - 1.3862944 * jax.random.uniform(splits[14], (8, D), jnp.float32) ** steps_of(splits[14], (8, D), ((1, 8),), -0.2, 0.2)), 5.364417798858767e-10, 2.145767119543507e-09)
    attn_average = bell_draw(splits[15], (8, D, D), (1 / D ** 0.5), 0.1875, ((1, 8), (2, 4)), jnp.float32)
    ffn_average = bell_draw(splits[16], (2, D, FF), (1 / D ** 0.5), 0.1875, ((1, 8), (2, 4)), jnp.float32)
    norm_average = jnp.clip(-0.5 + 2.0 * jax.random.uniform(splits[17], (8, D), jnp.float32) ** steps_of(splits[17], (8, D), ((1, 8),), -0.2, 0.2), -0.5, 1.5)
    return {"states": states, "memory": memory, "cotangent": cotangent, "lengths": lengths, "memory_lengths": memory_lengths, "regroup_order": regroup_order, "attn_weights": attn_weights, "ffn_weights": ffn_weights, "norm_params": norm_params, "attn_mean": attn_mean, "ffn_mean": ffn_mean, "norm_mean": norm_mean, "attn_square": attn_square, "ffn_square": ffn_square, "norm_square": norm_square, "attn_average": attn_average, "ffn_average": ffn_average, "norm_average": norm_average}


EPSILON = 1e-05
NEGATIVE = -1000000000.0
BETA_FIRST = 0.9
BETA_SECOND = 0.999
ADAM_EPSILON = 1e-08
MATRIX_RATE = 0.05
NORM_RATE = 1.0
MATRIX_DECAY = 0.1
AVERAGING = 0.7
THRESHOLD = 1.0
HIGHEST = lax.Precision.HIGHEST

@jax.custom_vjp
def low(v):
    return lax.optimization_barrier(v.astype(jnp.bfloat16)).astype(jnp.float32)

@jax.custom_vjp
def low_back(v):
    return v

def low_keep(v):
    return (low(v), None)

def low_pass(kept, grad):
    return (grad,)

def back_keep(v):
    return (v, None)

def back_low(kept, grad):
    return (low(grad),)
low.defvjp(low_keep, low_pass)
low_back.defvjp(back_keep, back_low)

def layer_norm(values, gains, biases):
    centered = values - lax.optimization_barrier(jnp.mean(values, axis=-1, keepdims=True))
    variance = lax.optimization_barrier(jnp.mean(centered * centered, axis=-1, keepdims=True))
    return centered * lax.rsqrt(variance + EPSILON) * gains + biases

def project(inputs, weight):
    return jnp.dot(inputs, weight, precision=HIGHEST)

def attend(queries, key_set, value_set, allowed):
    query_len = queries.shape[0]
    key_len = key_set.shape[0]
    query_heads = queries.reshape(query_len, HEADS, HD)
    key_heads = key_set.reshape(key_len, HEADS, HD)
    value_heads = value_set.reshape(key_len, HEADS, HD)
    scores = low_back(jnp.einsum('qhd,khd->hqk', query_heads, key_heads, precision=HIGHEST) * HD ** (-0.5))
    scores = jnp.where(allowed[None], scores, NEGATIVE)
    weights = low(jax.nn.softmax(scores, axis=-1))
    mixed_rows = jnp.einsum('hqk,khd->qhd', weights, value_heads, precision=HIGHEST).reshape(query_len, HEADS * HD)
    return low(low_back(mixed_rows))

def layer_step(state_rows, memory_rows, length, memory_length, attn_set, ffn_set, norm_set):
    positions = jnp.arange(SLOT, dtype=jnp.int32)
    frames = jnp.arange(MSLOT, dtype=jnp.int32)
    causal = (positions[None, :] <= positions[:, None]) & (positions[None, :] < length)
    reach = jnp.broadcast_to(frames[None, :] < memory_length, (SLOT, MSLOT))
    normed = low(layer_norm(state_rows, norm_set[0], norm_set[4]))
    queries = low(low_back(project(normed, attn_set[0])))
    key_set = low(low_back(project(normed, attn_set[1])))
    value_set = low(low_back(project(normed, attn_set[2])))
    mixed_self = attend(queries, key_set, value_set, causal)
    after_self = state_rows + low_back(project(mixed_self, attn_set[3].T))
    normed = low(layer_norm(after_self, norm_set[1], norm_set[5]))
    queries = low(low_back(project(normed, attn_set[4])))
    key_set = low(low_back(project(memory_rows, attn_set[5])))
    value_set = low(low_back(project(memory_rows, attn_set[6])))
    mixed_cross = attend(queries, key_set, value_set, reach)
    after_cross = after_self + low_back(project(mixed_cross, attn_set[7].T))
    normed = low(layer_norm(after_cross, norm_set[2], norm_set[6]))
    hidden = low_back(project(normed, ffn_set[0]))
    active = low(jax.nn.gelu(hidden))
    after_ffn = after_cross + low_back(project(active, ffn_set[1].T))
    return layer_norm(after_ffn, norm_set[3], norm_set[7])

def adam_step(weight, moment, square, gradient, step_rate, weight_decay):
    moment_new = BETA_FIRST * moment + (1.0 - BETA_FIRST) * gradient
    square_new = BETA_SECOND * square + (1.0 - BETA_SECOND) * gradient * gradient
    moment_hat = moment_new / (1.0 - BETA_FIRST ** STEP)
    square_hat = square_new / (1.0 - BETA_SECOND ** STEP)
    updated = weight - step_rate * (moment_hat / (jnp.sqrt(square_hat) + ADAM_EPSILON) + weight_decay * weight)
    return (updated, moment_new, square_new)

def reference(states, memory, cotangent, lengths, memory_lengths, regroup_order, attn_weights, ffn_weights, norm_params, attn_mean, ffn_mean, norm_mean, attn_square, ffn_square, norm_square, attn_average, ffn_average, norm_average):
    length_order = jnp.take(lengths, regroup_order, axis=0)
    reach_order = jnp.take(memory_lengths, regroup_order, axis=0)
    attn_copy = low(attn_weights)
    ffn_copy = low(ffn_weights)
    norm_copy = low(norm_params)

    def forward(state_in, memory_in, attn_set, ffn_set, norm_set):
        ordered_states = jnp.take(state_in, regroup_order, axis=0)
        ordered_memory = jnp.take(memory_in, regroup_order, axis=0)

        def single(inputs):
            return layer_step(inputs[0], inputs[1], inputs[2], inputs[3], attn_set, ffn_set, norm_set)
        return lax.map(jax.checkpoint(single), (ordered_states, ordered_memory, length_order, reach_order))
    output, pullback = jax.vjp(forward, states.astype(jnp.float32), memory.astype(jnp.float32), attn_copy, ffn_copy, norm_copy)
    positions = jnp.arange(SLOT, dtype=jnp.int32)
    live = positions[None, :] < length_order[:, None]
    seed_grad = jnp.where(live[:, :, None], cotangent.astype(jnp.float32), 0.0)
    states_grad, memory_grad, attn_grad, ffn_grad, norm_grad = pullback(seed_grad)
    square_sum = jnp.sum(attn_grad * attn_grad) + jnp.sum(ffn_grad * ffn_grad) + jnp.sum(norm_grad * norm_grad)
    grad_norm = jnp.sqrt(square_sum)
    clip_scale = jnp.minimum(1.0, THRESHOLD / (grad_norm + 1e-06))
    attn_updated, mean_attn, square_attn = adam_step(attn_weights, attn_mean, attn_square, clip_scale * attn_grad, MATRIX_RATE, MATRIX_DECAY)
    ffn_updated, mean_ffn, square_ffn = adam_step(ffn_weights, ffn_mean, ffn_square, clip_scale * ffn_grad, MATRIX_RATE, MATRIX_DECAY)
    norm_updated, mean_norm, square_norm = adam_step(norm_params, norm_mean, norm_square, clip_scale * norm_grad, NORM_RATE, 0.0)
    average_attn = AVERAGING * attn_average + (1.0 - AVERAGING) * attn_updated
    average_ffn = AVERAGING * ffn_average + (1.0 - AVERAGING) * ffn_updated
    average_norm = AVERAGING * norm_average + (1.0 - AVERAGING) * norm_updated
    return (output.astype(jnp.bfloat16), states_grad, memory_grad, attn_updated, ffn_updated, norm_updated, mean_attn, mean_ffn, mean_norm, square_attn, square_ffn, square_norm, average_attn, average_ffn, average_norm, grad_norm)
```

```python
import functools

import jax
import jax.numpy as jnp
from jax import lax
from jax.experimental import pallas as pl
from jax.experimental.pallas import tpu as pltpu
from jax.sharding import PartitionSpec as P

HD = 64
STEP = 10


EPSILON = 1e-05
NEGATIVE = -1000000000.0
BETA_FIRST = 0.9
BETA_SECOND = 0.999
ADAM_EPSILON = 1e-08
MATRIX_RATE = 0.05
NORM_RATE = 1.0
MATRIX_DECAY = 0.1
AVERAGING = 0.7
THRESHOLD = 1.0
BF = jnp.bfloat16
F32 = jnp.float32


def grid_sizes():
    dp = lax.axis_size("dp")
    mp = lax.axis_size("mp")
    ny = 1 << ((dp.bit_length() - 1) // 2)
    return {"z": dp // ny, "y": ny, "x": mp // 2, "c": 2}


def grid_place():
    n = grid_sizes()
    dp = lax.axis_index("dp")
    mp = lax.axis_index("mp")
    return {"z": dp // n["y"], "y": dp % n["y"], "x": mp // 2, "c": mp % 2}


def hop(value, axis, step=1):
    n = grid_sizes()
    pairs = []
    for z in range(n["z"]):
        for y in range(n["y"]):
            for x in range(n["x"]):
                for c in range(2):
                    at = {"z": z, "y": y, "x": x, "c": c}
                    to = dict(at)
                    to[axis] = (at[axis] + step) % n[axis]
                    number = lambda p: ((p["z"] * n["y"] + p["y"]) * n["x"] + p["x"]) * 2 + p["c"]
                    pairs.append((number(at), number(to)))
    return lax.ppermute(value, ("dp", "mp"), pairs)


def pick(value, index, dim):
    return lax.dynamic_index_in_dim(value, index, dim, keepdims=False)


def gather_along(value, axis, dim):
    n = grid_sizes()[axis]
    me = grid_place()[axis]
    pieces = [value] + [hop(value, axis, s) for s in range(1, n)]
    if n == 2:
        low = jnp.where(me == 0, pieces[0], pieces[1])
        high = jnp.where(me == 0, pieces[1], pieces[0])
        return jnp.stack([low, high], dim)
    shape = value.shape[:dim] + (n,) + value.shape[dim:]
    out = jnp.zeros(shape, value.dtype)
    for s, piece in enumerate(pieces):
        out = lax.dynamic_update_index_in_dim(out, piece, (me - s) % n, dim)
    return out


def reduce_along(value, axis, dim):
    n = grid_sizes()[axis]
    me = grid_place()[axis]
    total = pick(value, me, dim).astype(F32)
    for s in range(1, n):
        total = total + hop(pick(value, (me + s) % n, dim).astype(BF), axis, s).astype(F32)
    return total


def dot(left, right, left_dim, right_dim):
    return lax.dot_general(
        left, right, (((left_dim,), (right_dim,)), ((), ())), preferred_element_type=F32
    )


def layer_norm(values, gains, biases):
    centered = values - jnp.mean(values, axis=-1, keepdims=True)
    variance = jnp.mean(centered * centered, axis=-1, keepdims=True)
    return centered * lax.rsqrt(variance + EPSILON) * gains + biases


def norm_back(values, gains, biases, upstream):
    result, pullback = jax.vjp(layer_norm, values, gains, biases)
    return pullback(upstream)


PAIR = 2 * HD


def key_bound(scalars, width, causal):
    limit = scalars[0]
    if not causal:
        return jnp.full((1, width), limit, jnp.int32)
    reach = lax.broadcasted_iota(jnp.int32, (1, width), 1) + scalars[1] + 1
    return jnp.minimum(reach, limit)


def only_head(value, head):
    lane = lax.broadcasted_iota(jnp.int32, value.shape, 1)
    keep = (lane < HD) if head == 0 else (lane >= HD)
    return jnp.where(keep, value, jnp.zeros_like(value))


def attend_forward_kernel(
    causal, chunk, scalars, q_ref, k_ref, v_ref, o_ref, sum_ref, score_ref, weight_ref
):
    rows, keys = q_ref.shape[0], k_ref.shape[0]
    bound = key_bound(scalars, rows, causal)
    queries = q_ref[...] * BF(HD**-0.5)
    values = v_ref[...]
    mixed = []
    for head in range(2):
        masked = only_head(queries, head)
        top = None
        for start in range(0, keys, chunk):
            block = slice(start, start + chunk)
            scores = dot(k_ref[block, :], masked, 1, 1)
            position = lax.broadcasted_iota(jnp.int32, scores.shape, 0) + start
            scores = jnp.where(position < bound, scores, NEGATIVE)
            score_ref[head, block, :] = scores
            highest = jnp.max(scores, axis=0, keepdims=True)
            top = highest if top is None else jnp.maximum(top, highest)
        total = None
        for start in range(0, keys, chunk):
            block = slice(start, start + chunk)
            raised = jnp.exp(score_ref[head, block, :] - top)
            part = jnp.sum(raised, axis=0, keepdims=True)
            total = part if total is None else total + part
            score_ref[head, block, :] = raised
        inverse = 1.0 / total
        for start in range(0, keys, chunk):
            block = slice(start, start + chunk)
            weight_ref[head, block, :] = (score_ref[head, block, :] * inverse).astype(BF)
        mixed.append(dot(values, weight_ref[head], 0, 0)[head * HD : (head + 1) * HD])
        sum_ref[head : head + 1, :] = top + jnp.log(total)
    o_ref[...] = jnp.concatenate(mixed, axis=0).T.astype(BF)


def attend_forward(scalars, queries, keys, values, causal):
    rows, width = queries.shape
    count = keys.shape[0]
    pairs = width // PAIR
    q_spec = pl.BlockSpec((rows, PAIR), lambda p: (0, p))
    k_spec = pl.BlockSpec((count, PAIR), lambda p: (0, p))
    return pl.pallas_call(
        functools.partial(attend_forward_kernel, causal, 256),
        grid=(pairs,),
        in_specs=[pl.BlockSpec(memory_space=pltpu.SMEM), q_spec, k_spec, k_spec],
        out_specs=[q_spec, pl.BlockSpec((None, 2, rows), lambda p: (p, 0, 0))],
        out_shape=[
            jax.ShapeDtypeStruct((rows, width), BF),
            jax.ShapeDtypeStruct((pairs, 2, rows), F32),
        ],
        scratch_shapes=[pltpu.VMEM((2, count, rows), F32), pltpu.VMEM((2, count, rows), BF)],
        compiler_params=pltpu.CompilerParams(vmem_limit_bytes=24 * 2**20),
        name="attend_forward",
        cost_estimate=pl.CostEstimate(
            flops=4 * rows * count * width,
            bytes_accessed=4 * width * (rows + count),
            transcendentals=rows * count * width // HD,
        ),
    )(scalars, queries, keys, values)


def attend_backward_kernel(
    causal, chunk, scalars, q_ref, k_ref, v_ref, o_ref, sum_ref, g_ref, dq_ref, dk_ref, dv_ref, ds_ref
):
    rows, keys = q_ref.shape[0], k_ref.shape[0]
    bound = key_bound(scalars, rows, causal)
    queries = q_ref[...] * BF(HD**-0.5)
    grads = g_ref[...]
    product = (grads.astype(F32) * o_ref[...].astype(F32)).T
    head_q = [only_head(queries, head) for head in range(2)]
    head_g = [only_head(grads, head) for head in range(2)]
    shift = [
        jnp.sum(product[head * HD : (head + 1) * HD], axis=0, keepdims=True) for head in range(2)
    ]
    for start in range(0, keys, chunk):
        block = slice(start, start + chunk)
        key_block, value_block = k_ref[block, :], v_ref[block, :]
        grad_value, grad_key = 0.0, 0.0
        for head in range(2):
            scores = dot(key_block, head_q[head], 1, 1)
            position = lax.broadcasted_iota(jnp.int32, scores.shape, 0) + start
            scores = jnp.where(position < bound, scores, NEGATIVE)
            weights = jnp.exp(scores - sum_ref[head : head + 1, :])
            grad_weights = dot(value_block, head_g[head], 1, 1)
            grad_scores = (weights * (grad_weights - shift[head])).astype(BF)
            ds_ref[head, block, :] = grad_scores
            grad_value = grad_value + dot(weights.astype(BF), head_g[head], 1, 0)
            grad_key = grad_key + dot(grad_scores, head_q[head], 1, 0)
        dv_ref[block, :] = grad_value.astype(BF)
        dk_ref[block, :] = grad_key.astype(BF)
    key_all = k_ref[...]
    parts = [dot(key_all, ds_ref[h], 0, 0)[h * HD : (h + 1) * HD] for h in range(2)]
    dq_ref[...] = (jnp.concatenate(parts, axis=0).T * HD**-0.5).astype(BF)


def attend_backward(scalars, queries, keys, values, mixed, logsum, grads, causal):
    rows, width = queries.shape
    count = keys.shape[0]
    pairs = width // PAIR
    q_spec = pl.BlockSpec((rows, PAIR), lambda p: (0, p))
    k_spec = pl.BlockSpec((count, PAIR), lambda p: (0, p))
    sum_spec = pl.BlockSpec((None, 2, rows), lambda p: (p, 0, 0))
    return pl.pallas_call(
        functools.partial(attend_backward_kernel, causal, 256),
        grid=(pairs,),
        in_specs=[
            pl.BlockSpec(memory_space=pltpu.SMEM), q_spec, k_spec, k_spec, q_spec, sum_spec, q_spec
        ],
        out_specs=[q_spec, k_spec, k_spec],
        out_shape=[jax.ShapeDtypeStruct((rows, width), BF)]
        + [jax.ShapeDtypeStruct((count, width), BF)] * 2,
        scratch_shapes=[pltpu.VMEM((2, count, rows), BF)],
        compiler_params=pltpu.CompilerParams(vmem_limit_bytes=24 * 2**20),
        name="attend_backward",
        cost_estimate=pl.CostEstimate(
            flops=10 * rows * count * width,
            bytes_accessed=8 * width * (rows + count),
            transcendentals=rows * count * width // HD,
        ),
    )(scalars, queries, keys, values, mixed, logsum, grads)


class Wires:
    def __init__(self, sizes, place, send_sem, recv_sem):
        self.sizes, self.place = sizes, place
        self.send_sem, self.recv_sem = send_sem, recv_sem
        self.count = 0
        self.started = []

    def peer(self, z=0, y=0, x=0, c=0):
        n, at = self.sizes, self.place
        pz, py = (at["z"] + z) % n["z"], (at["y"] + y) % n["y"]
        px, pc = (at["x"] + x) % n["x"], (at["c"] + c) % 2
        return (pz * n["y"] + py, px * 2 + pc)

    def send(self, src, dst, **shift):
        copy = pltpu.make_async_remote_copy(
            src_ref=src,
            dst_ref=dst,
            send_sem=self.send_sem.at[self.count],
            recv_sem=self.recv_sem.at[self.count],
            device_id=self.peer(**shift),
            device_id_type=pl.DeviceIdType.MESH,
        )
        self.count += 1
        copy.start()
        self.started.append(copy)
        return copy

    def greet(self, shifts):
        barrier = pltpu.get_barrier_semaphore()
        for shift in shifts:
            pl.semaphore_signal(
                barrier, inc=1, device_id=self.peer(**shift), device_id_type=pl.DeviceIdType.MESH
            )
        pl.semaphore_wait(barrier, len(shifts))

    def close(self):
        for copy in self.started:
            copy.wait_send()


def dp_shifts(n):
    return [{"z": z, "y": y} for z in range(n["z"]) for y in range(n["y"]) if z or y]


def mp_shifts(n):
    return [{"x": x, "c": c} for x in range(n["x"]) for c in range(2) if x or c]


def entry_kernel(
    n, w_ref, p_ref, s_ref, m_ref, ow_ref, op_ref, os_ref, om_ref, send_sem, recv_sem, local_sem
):
    at = grid_place()
    z, y, x, c = at["z"], at["y"], at["x"], at["c"]
    data = z * n["y"] + y
    wires = Wires(n, at, send_sem, recv_sem)
    wires.greet(
        dp_shifts(n) + [{"x": s} for s in range(1, n["x"])] + [{"c": 1}]
    )
    rows, wide = w_ref.shape[1], w_ref.shape[2]
    lines, deep = s_ref.shape[1], s_ref.shape[2]

    def spot(sz, sy, sx, mats=slice(None)):
        block = ((z - sz) % n["z"]) * n["y"] + (y - sy) % n["y"]
        column = (x - sx) % n["x"]
        return ow_ref.at[
            mats,
            pl.ds(pl.multiple_of(block * rows, rows), rows),
            pl.ds(pl.multiple_of(column * wide, wide), wide),
        ]

    def column(ref, sx, sc):
        index = ((x - sx) % n["x"]) * 2 + (c - sc) % 2
        return ref.at[:, pl.ds(pl.multiple_of(index * deep, deep), deep)]

    def patch(ref):
        index = x * 2 + c
        return ref.at[
            pl.ds(pl.multiple_of(data * lines, lines), lines),
            pl.ds(pl.multiple_of(index * deep, deep), deep),
        ]

    def stripe(ref):
        return ref.at[data]

    own = [
        pltpu.make_async_copy(w_ref, spot(0, 0, 0), local_sem.at[0]),
        pltpu.make_async_copy(p_ref, stripe(op_ref), local_sem.at[1]),
        pltpu.make_async_copy(s_ref.at[data], patch(os_ref), local_sem.at[2]),
        pltpu.make_async_copy(m_ref.at[data], patch(om_ref), local_sem.at[3]),
    ]
    for copy in own:
        copy.start()

    def spread(ref, out):
        copies = []
        for shift in dp_shifts(n):
            target = wires.peer(**shift)[0]
            copies.append(wires.send(ref.at[target], patch(out), **shift))
        return copies

    def forward_columns(out, copies):
        for copy in copies:
            copy.wait_recv()
        near = [wires.send(column(out, 0, 0), column(out, 0, 0), x=s) for s in range(1, n["x"])]
        pair = [wires.send(column(out, 0, 0), column(out, 0, 0), c=1)]
        return near, pair

    def finish_columns(out, near, pair):
        for s in range(1, n["x"]):
            near[s - 1].wait_recv()
            pair.append(wires.send(column(out, s, 0), column(out, s, 0), c=1))
        for copy in pair:
            copy.wait_recv()

    to_z = {s: wires.send(w_ref, spot(0, 0, 0), z=s) for s in range(1, n["z"])}
    to_y = {(0, s): wires.send(w_ref, spot(0, 0, 0), y=s) for s in range(1, n["y"])}
    to_x = {(0, s): wires.send(w_ref, spot(0, 0, 0), x=s) for s in range(1, n["x"])}
    params = [wires.send(p_ref, stripe(op_ref), **shift) for shift in dp_shifts(n)]
    states = spread(s_ref, os_ref)
    memory = spread(m_ref, om_ref)

    for sz in range(1, n["z"]):
        to_z[sz].wait_recv()
        for s in range(1, n["y"]):
            to_y[sz, s] = wires.send(spot(sz, 0, 0), spot(sz, 0, 0), y=s)
        for s in range(1, n["x"]):
            to_x[sz, s] = wires.send(spot(sz, 0, 0), spot(sz, 0, 0), x=s)
    for copy in own:
        copy.wait()
    states = forward_columns(os_ref, states)
    last = []
    cut = max(1, w_ref.shape[0] // 4)
    for sz in range(n["z"]):
        for sy in range(1, n["y"]):
            to_y[sz, sy].wait_recv()
            part = spot(sz, sy, 0, slice(0, cut))
            for s in range(1, n["x"]):
                last.append(wires.send(part, part, x=s))
        for sx in range(1, n["x"]):
            to_x[sz, sx].wait_recv()
            part = spot(sz, 0, sx, slice(cut, w_ref.shape[0]))
            for s in range(1, n["y"]):
                last.append(wires.send(part, part, y=s))
    memory = forward_columns(om_ref, memory)
    finish_columns(os_ref, *states)
    finish_columns(om_ref, *memory)
    for copy in params + last:
        copy.wait_recv()
    wires.close()


def entry(weights, params, states, memory):
    n = grid_sizes()
    count, rows, wide = weights.shape
    utterances, lines, deep = states.shape
    nz, ny, nx = n["z"], n["y"], n["x"]
    data = nz * ny
    copies = (
        (nz - 1)
        + nz * (ny - 1 + nx - 1)
        + 2 * nz * (ny - 1) * (nx - 1)
        + 3 * (data - 1)
        + 2 * (2 * (nx - 1) + 1)
    )
    hbm = pl.BlockSpec(memory_space=pl.ANY)
    return pl.pallas_call(
        functools.partial(entry_kernel, n),
        out_shape=[
            jax.ShapeDtypeStruct((count, data * rows, nx * wide), BF),
            jax.ShapeDtypeStruct((data,) + params.shape, F32),
            jax.ShapeDtypeStruct((data * lines, 2 * nx * deep), BF),
            jax.ShapeDtypeStruct((data * lines, 2 * nx * deep), BF),
        ],
        in_specs=[pl.BlockSpec(memory_space=pltpu.VMEM)] * 4,
        out_specs=[hbm] * 4,
        scratch_shapes=[
            pltpu.SemaphoreType.DMA((copies,)),
            pltpu.SemaphoreType.DMA((copies,)),
            pltpu.SemaphoreType.DMA((4,)),
        ],
        compiler_params=pltpu.CompilerParams(
            collective_id=0, has_side_effects=True, vmem_limit_bytes=16 * 2**20
        ),
        name="entry",
    )(weights, params, states, memory)


def closing_kernel(
    n,
    g0_ref,
    g1_ref,
    g2_ref,
    g3_ref,
    h_ref,
    x_ref,
    d_ref,
    gain_ref,
    m_ref,
    p_ref,
    og_ref,
    os_ref,
    om_ref,
    op_ref,
    ra1_ref,
    rb1_ref,
    sa2_ref,
    sb2_ref,
    ra2_ref,
    rb2_ref,
    acc_ref,
    s3_ref,
    r3_ref,
    rc_ref,
    sx_ref,
    rx_ref,
    dx_ref,
    np_ref,
    nn_ref,
    nf_ref,
    send_sem,
    recv_sem,
    move_send_sem,
    move_recv_sem,
    local_sem,
):
    at = grid_place()
    z, y, x, c = at["z"], at["y"], at["x"], at["c"]
    nz, ny, nx = n["z"], n["y"], n["x"]
    data, model = z * ny + y, x * 2 + c
    wires = Wires(n, at, send_sem, recv_sem)
    everyone = [
        dict(z=sz, y=sy, x=sx, c=sc)
        for sz in range(nz)
        for sy in range(ny)
        for sx in range(nx)
        for sc in range(2)
        if sz or sy or sx or sc
    ]
    wires.greet(everyone)
    first, second = (g0_ref, g1_ref), (g2_ref, g3_ref)
    rows, wide = og_ref.shape[1], og_ref.shape[2]

    def bands(ref, band, count, col):
        return ref.at[
            pl.ds(pl.multiple_of(band * rows, rows), count * rows),
            pl.ds(pl.multiple_of(col * wide, wide), wide),
        ]

    def full_band(ref, band):
        return ref.at[pl.ds(pl.multiple_of(band * rows, rows), rows)]

    order = list(range(1, nz)) + [0]
    to_c = wires.send(h_ref.at[:, 1 - c], rc_ref, c=1)
    by_x, by_y = {}, {}
    for s in order:
        zone = ((z + s) % nz) * ny
        for t in range(1, nx):
            col = (x + t) % nx
            by_x[s, t] = [
                wires.send(bands(ref, zone, ny, col), ra1_ref.at[t - 1, s, i], x=t)
                for i, ref in enumerate(first)
            ]
        for t in range(1, ny):
            band = zone + (y + t) % ny
            by_y[s, t] = [
                wires.send(full_band(ref, band), rb1_ref.at[t - 1, s, i], y=t)
                for i, ref in enumerate(second)
            ]
    spread = []
    for i, shift in enumerate(dp_shifts(n)):
        target = wires.peer(**shift)[0]
        spread.append(wires.send(m_ref.at[target], om_ref.at[data], **shift))
    keep = pltpu.make_async_copy(m_ref.at[data], om_ref.at[data], local_sem)
    keep.start()

    to_c.wait_recv()
    near = []
    for t in range(1, nx):
        index = (x + t) % nx
        sx_ref[t - 1] = (h_ref[index, c].astype(F32) + rc_ref[index].astype(F32)).astype(BF)
        near.append(wires.send(sx_ref.at[t - 1], rx_ref.at[t - 1], x=t))

    next_y, next_x = {}, {}
    for s in order:
        zone = ((z + s) % nz) * ny
        for t in range(1, nx):
            for copy in by_x[s, t]:
                copy.wait_recv()
        for i, ref in enumerate(first):
            for b in range(ny):
                band = (y + b) % ny
                total = bands(ref, zone + band, 1, x)[...].astype(F32)
                for t in range(1, nx):
                    part = ra1_ref.at[
                        t - 1, s, i, pl.ds(pl.multiple_of(band * rows, rows), rows)
                    ]
                    total = total + part[...].astype(F32)
                if b == 0:
                    acc_ref[s, i] = total
                else:
                    sa2_ref[b - 1, s, i] = total.astype(BF)
        for t in range(1, ny):
            next_y[s, t] = wires.send(sa2_ref.at[t - 1, s], ra2_ref.at[t - 1, s], y=t)
        for t in range(1, ny):
            for copy in by_y[s, t]:
                copy.wait_recv()
        for i, ref in enumerate(second):
            for b in range(nx):
                col = pl.ds(pl.multiple_of(((x + b) % nx) * wide, wide), wide)
                total = bands(ref, zone + y, 1, (x + b) % nx)[...].astype(F32)
                for t in range(1, ny):
                    total = total + rb1_ref[t - 1, s, i, :, col].astype(F32)
                if b == 0:
                    acc_ref[s, 2 + i] = total
                else:
                    sb2_ref[b - 1, s, i] = total.astype(BF)
        for t in range(1, nx):
            next_x[s, t] = wires.send(sb2_ref.at[t - 1, s], rb2_ref.at[t - 1, s], x=t)

    grad = h_ref[x, c].astype(F32) + rc_ref[x].astype(F32)
    for t in range(1, nx):
        near[t - 1].wait_recv()
        grad = grad + rx_ref[t - 1].astype(F32)
    values = x_ref[...].astype(F32)
    centered = values - jnp.mean(values, axis=-1, keepdims=True)
    scale = lax.rsqrt(jnp.mean(centered * centered, axis=-1, keepdims=True) + EPSILON)
    normed = centered * scale
    up = grad * gain_ref[...]
    back = scale * (
        up
        - jnp.mean(up, axis=-1, keepdims=True)
        - normed * jnp.mean(up * normed, axis=-1, keepdims=True)
    )
    dx_ref[...] = (d_ref[...] + back).astype(BF)
    lines, deep = os_ref.shape[1], os_ref.shape[2]
    blocks = dx_ref.shape[0] // lines

    def moves():
        for b in range(blocks):
            for m in range(2 * nx):
                target = (model * blocks + b, m)
                src = dx_ref.at[b * lines : (b + 1) * lines, m * deep : (m + 1) * deep]
                mine = jnp.logical_and(target[0] == data, model == m)
                remote = pltpu.make_async_remote_copy(
                    src_ref=src,
                    dst_ref=os_ref.at[data],
                    send_sem=move_send_sem.at[b * 2 * nx + m],
                    recv_sem=move_recv_sem.at[data],
                    device_id=target,
                    device_id_type=pl.DeviceIdType.MESH,
                )
                yield mine, remote, pltpu.make_async_copy(src, os_ref.at[data], move_recv_sem.at[data])

    for mine, remote, here in moves():
        pl.when(mine)(lambda: here.start())
        pl.when(jnp.logical_not(mine))(lambda: remote.start())

    line = lax.broadcasted_iota(jnp.int32, p_ref.shape, 0)
    gain_grad = jnp.sum(grad * normed, axis=0, keepdims=True)
    bias_grad = jnp.sum(grad, axis=0, keepdims=True)
    params = p_ref[...] + jnp.where(line == 0, gain_grad, 0.0) + jnp.where(line == 4, bias_grad, 0.0)
    columns = op_ref.shape[1]
    for k in range(nz * ny):
        np_ref[0, k] = params[:, k * columns : (k + 1) * columns]
    norm_near = [wires.send(np_ref.at[0], nn_ref.at[i], **s) for i, s in enumerate(mp_shifts(n))]

    to_z = {}
    for s in order:
        for t in range(1, ny):
            next_y[s, t].wait_recv()
        for t in range(1, nx):
            next_x[s, t].wait_recv()
        for i in range(4):
            total = acc_ref[s, i]
            if i < 2:
                for t in range(1, ny):
                    total = total + ra2_ref[t - 1, s, i].astype(F32)
            else:
                for t in range(1, nx):
                    total = total + rb2_ref[t - 1, s, i - 2].astype(F32)
            if s == 0:
                acc_ref[s, i] = total
            else:
                s3_ref[s - 1, i] = total.astype(BF)
        if s:
            to_z[s] = wires.send(s3_ref.at[s - 1], r3_ref.at[s - 1], z=s)

    total = np_ref[0]
    for i, copy in enumerate(norm_near):
        copy.wait_recv()
        total = total + nn_ref[i]
    np_ref[1] = total
    norm_far = []
    for i, shift in enumerate(dp_shifts(n)):
        target = wires.peer(**shift)[0]
        norm_far.append(wires.send(np_ref.at[1, target], nf_ref.at[i], **shift))
    for s in range(1, nz):
        to_z[s].wait_recv()
    for i in range(4):
        total = acc_ref[0, i]
        for s in range(1, nz):
            total = total + r3_ref[s - 1, i].astype(F32)
        og_ref[i] = total
    total = np_ref[1, data]
    for i, copy in enumerate(norm_far):
        copy.wait_recv()
        total = total + nf_ref[i]
    op_ref[...] = total
    for copy in spread:
        copy.wait_recv()
    keep.wait()
    for mine, remote, here in moves():
        pl.when(jnp.logical_not(mine))(lambda: remote.wait_send())
    for r in range(nz * ny):
        pltpu.make_async_copy(os_ref.at[r], os_ref.at[r], move_recv_sem.at[r]).wait()
    wires.close()


def closing(grads, partial, inputs, upstream, gain, memory, params):
    n = grid_sizes()
    nz, ny, nx = n["z"], n["y"], n["x"]
    data, model = nz * ny, 2 * nx
    width, local = grads[0].shape
    rows, wide = width // data, local // nx
    own = inputs.shape[0]
    utterances, lines, deep = memory.shape
    columns = width // data
    copies = (
        1
        + nz * 2 * (nx - 1 + ny - 1)
        + (data - 1)
        + (nx - 1)
        + nz * (ny - 1 + nx - 1)
        + (model - 1)
        + (nz - 1)
        + (data - 1)
    )
    vmem = pl.BlockSpec(memory_space=pltpu.VMEM)
    hbm = pl.BlockSpec(memory_space=pl.ANY)
    return pl.pallas_call(
        functools.partial(closing_kernel, n),
        out_shape=[
            jax.ShapeDtypeStruct((4, rows, wide), F32),
            jax.ShapeDtypeStruct((data, lines, deep), BF),
            jax.ShapeDtypeStruct((data, lines, deep), BF),
            jax.ShapeDtypeStruct((params.shape[0], columns), F32),
        ],
        in_specs=[vmem] * 8 + [hbm, vmem],
        out_specs=[vmem, hbm, hbm, vmem],
        scratch_shapes=[
            pltpu.VMEM((nx - 1, nz, 2, ny * rows, wide), BF),
            pltpu.VMEM((ny - 1, nz, 2, rows, nx * wide), BF),
            pltpu.VMEM((ny - 1, nz, 2, rows, wide), BF),
            pltpu.VMEM((nx - 1, nz, 2, rows, wide), BF),
            pltpu.VMEM((ny - 1, nz, 2, rows, wide), BF),
            pltpu.VMEM((nx - 1, nz, 2, rows, wide), BF),
            pltpu.VMEM((nz, 4, rows, wide), F32),
            pltpu.VMEM((nz - 1, 4, rows, wide), BF),
            pltpu.VMEM((nz - 1, 4, rows, wide), BF),
            pltpu.VMEM((nx, own, width), BF),
            pltpu.VMEM((nx - 1, own, width), BF),
            pltpu.VMEM((nx - 1, own, width), BF),
            pltpu.VMEM((own, width), BF),
            pltpu.VMEM((2, data, params.shape[0], columns), F32),
            pltpu.VMEM((model - 1, data, params.shape[0], columns), F32),
            pltpu.VMEM((data - 1, params.shape[0], columns), F32),
            pltpu.SemaphoreType.DMA((copies,)),
            pltpu.SemaphoreType.DMA((copies,)),
            pltpu.SemaphoreType.DMA((data,)),
            pltpu.SemaphoreType.DMA((data,)),
            pltpu.SemaphoreType.DMA,
        ],
        compiler_params=pltpu.CompilerParams(
            collective_id=1, has_side_effects=True, vmem_limit_bytes=48 * 2**20
        ),
        name="closing",
    )(*grads, partial, inputs, upstream, gain, memory, params)


def place_kernel(n, plan, by_x, *refs):
    at = grid_place()
    out, sem = refs[-2], refs[-1]
    rows, wide = refs[0].shape[2], refs[0].shape[3]
    copies = []
    for ref, (sy, sx) in zip(refs[:-2], plan):
        for sz in range(n["z"]):
            block = ((at["z"] - sz) % n["z"]) * n["y"] + (at["y"] - sy) % n["y"]
            column = (at["x"] - sx) % n["x"] if by_x else 0
            target = out.at[
                :,
                pl.ds(pl.multiple_of(block * rows, rows), rows),
                pl.ds(pl.multiple_of(column * wide, wide), wide),
            ]
            copy = pltpu.make_async_copy(ref.at[sz], target, sem.at[len(copies)])
            copy.start()
            copies.append(copy)
    for copy in copies:
        copy.wait()


def gather_weights(group, by_x):
    n = grid_sizes()
    zone = jnp.stack([group] + [hop(group, "z", s) for s in range(1, n["z"])])
    blocks, plan = [zone], [(0, 0)]
    for s in range(1, n["y"]):
        blocks.append(hop(zone, "y", s))
        plan.append((s, 0))
    if by_x:
        for s in range(1, n["x"]):
            for block, (sy, _) in list(zip(blocks, plan))[: n["y"]]:
                blocks.append(hop(block, "x", s))
                plan.append((sy, s))
    count, rows, wide = group.shape
    hbm = pl.BlockSpec(memory_space=pl.ANY)
    columns = wide * (n["x"] if by_x else 1)
    return pl.pallas_call(
        functools.partial(place_kernel, n, tuple(plan), by_x),
        out_shape=jax.ShapeDtypeStruct((count, n["z"] * n["y"] * rows, columns), BF),
        in_specs=[hbm] * len(blocks),
        out_specs=pl.BlockSpec(memory_space=pltpu.VMEM),
        scratch_shapes=[pltpu.SemaphoreType.DMA((len(blocks) * n["z"],))],
        compiler_params=pltpu.CompilerParams(vmem_limit_bytes=16 * 2**20),
        name="place",
    )(*blocks)


def after(value, *others):
    return lax.optimization_barrier((value,) + others)[0]


def square_sum_kernel(n, g_ref, o_ref, near_ref, sum_ref, far_ref, send_sem, recv_sem):
    wires = Wires(n, grid_place(), send_sem, recv_sem)
    wires.greet(dp_shifts(n) + mp_shifts(n))
    copies = [wires.send(g_ref, near_ref.at[i], **shift) for i, shift in enumerate(mp_shifts(n))]
    total = g_ref[...]
    for i, copy in enumerate(copies):
        copy.wait_recv()
        total = total + near_ref[i]
    sum_ref[...] = total
    copies = [wires.send(sum_ref, far_ref.at[i], **shift) for i, shift in enumerate(dp_shifts(n))]
    for i, copy in enumerate(copies):
        copy.wait_recv()
        total = total + far_ref[i]
    o_ref[...] = total
    wires.close()


def square_sum(partial):
    n = grid_sizes()
    data = n["z"] * n["y"]
    model = 2 * n["x"]
    vmem = pl.BlockSpec(memory_space=pltpu.VMEM)
    copies = data - 1 + model - 1
    return pl.pallas_call(
        functools.partial(square_sum_kernel, n),
        out_shape=jax.ShapeDtypeStruct(partial.shape, F32),
        in_specs=[vmem],
        out_specs=vmem,
        scratch_shapes=[
            pltpu.VMEM((model - 1,) + partial.shape, F32),
            pltpu.VMEM(partial.shape, F32),
            pltpu.VMEM((data - 1,) + partial.shape, F32),
            pltpu.SemaphoreType.DMA((copies,)),
            pltpu.SemaphoreType.DMA((copies,)),
        ],
        compiler_params=pltpu.CompilerParams(collective_id=2, has_side_effects=True),
        name="square_sum",
    )(partial)


def adam_step(weight, moment, square, gradient, step_rate, weight_decay):
    moment_new = BETA_FIRST * moment + (1.0 - BETA_FIRST) * gradient
    square_new = BETA_SECOND * square + (1.0 - BETA_SECOND) * gradient * gradient
    moment_hat = moment_new / (1.0 - BETA_FIRST**STEP)
    square_hat = square_new / (1.0 - BETA_SECOND**STEP)
    updated = weight - step_rate * (
        moment_hat / (jnp.sqrt(square_hat) + ADAM_EPSILON) + weight_decay * weight
    )
    return (updated, moment_new, square_new)


def per_device(
    states,
    memory,
    cotangent,
    lengths,
    memory_lengths,
    regroup_order,
    attn_weights,
    ffn_weights,
    norm_params,
    attn_mean,
    ffn_mean,
    norm_mean,
    attn_square,
    ffn_square,
    norm_square,
    attn_average,
    ffn_average,
    norm_average,
):
    n = grid_sizes()
    at = grid_place()
    nz, ny, nx = n["z"], n["y"], n["x"]
    data_index = lax.axis_index("dp")
    model_index = lax.axis_index("mp")
    data_size = lax.axis_size("dp")
    width = states.shape[2] * lax.axis_size("mp")
    slot = states.shape[1] * data_size
    own_rows = cotangent.shape[1]
    chip_rows = 2 * own_rows
    chip_start = at["x"] * chip_rows

    def own_of(value):
        return lax.dynamic_slice_in_dim(value, at["c"] * own_rows, own_rows, 0)

    def other_of(value):
        return lax.dynamic_slice_in_dim(value, (1 - at["c"]) * own_rows, own_rows, 0)

    def pair_rows(value):
        other = hop(value, "c")
        first = at["c"] == 0
        return jnp.concatenate(
            [jnp.where(first, value, other), jnp.where(first, other, value)], axis=0
        )

    def chip_of(value):
        return lax.dynamic_slice_in_dim(value, chip_start, chip_rows, 0)

    attn_low = attn_weights.astype(BF)
    ffn_low = ffn_weights.astype(BF)

    weights_self, norm_values, inputs, frames = entry(
        attn_low[0:4],
        norm_params.astype(BF).astype(F32),
        jnp.take(states, regroup_order, axis=0),
        jnp.take(memory, regroup_order, axis=0),
    )
    norm_values = jnp.swapaxes(norm_values, 0, 1).reshape(norm_params.shape[0], width)
    length = lengths[regroup_order[data_index]]
    reach = memory_lengths[regroup_order[data_index]]

    self_scalars = jnp.stack([length, chip_start]).astype(jnp.int32)
    cross_scalars = jnp.stack([reach, chip_start]).astype(jnp.int32)

    weights_cross = gather_weights(after(attn_low[4:8], weights_self), True)
    ffn_maps = gather_weights(after(ffn_low, weights_self), False)
    up_map, down_map = ffn_maps[0], ffn_maps[1]

    resid_zero_full = inputs.astype(F32)
    normed_first = layer_norm(resid_zero_full, norm_values[0], norm_values[4]).astype(BF)
    normed_first_chip = chip_of(normed_first)
    resid_zero = chip_of(resid_zero_full)
    query_self = dot(normed_first_chip, weights_self[0], 1, 0).astype(BF)
    key_self = dot(normed_first, weights_self[1], 1, 0).astype(BF)
    value_self = dot(normed_first, weights_self[2], 1, 0).astype(BF)
    mixed_self, logsum_self = attend_forward(
        self_scalars, query_self, key_self, value_self, True
    )

    def core_sum(partial):
        partial = partial.astype(BF)
        return partial.astype(F32) + hop(partial, "c").astype(F32)

    resid_one = resid_zero + core_sum(dot(mixed_self, weights_self[3], 1, 1))
    normed_second = layer_norm(resid_one, norm_values[1], norm_values[5]).astype(BF)

    query_cross = dot(normed_second, weights_cross[0], 1, 0).astype(BF)
    key_cross = dot(frames, weights_cross[1], 1, 0).astype(BF)
    value_cross = dot(frames, weights_cross[2], 1, 0).astype(BF)
    mixed_cross, logsum_cross = attend_forward(
        cross_scalars, query_cross, key_cross, value_cross, False
    )
    resid_two = resid_one + core_sum(dot(mixed_cross, weights_cross[3], 1, 1))
    normed_third = layer_norm(resid_two, norm_values[2], norm_values[6]).astype(BF)

    def far_rows(own):
        near = [hop(own, "x", s) for s in range(1, nx)]
        cross = hop(jnp.stack(near), "c")
        return jnp.concatenate([v for s in range(nx - 1) for v in (near[s], cross[s])], axis=0)

    def scatter_rows(partial_chip, partial_far):
        total = own_of(partial_chip) + hop(other_of(partial_chip).astype(BF), "c").astype(F32)
        far = partial_far.reshape(nx - 1, 2, own_rows, width)
        far = far[:, 0] + hop(far[:, 1].astype(BF), "c").astype(F32)
        for s in range(1, nx):
            total = total + hop(far[s - 1].astype(BF), "x", nx - s).astype(F32)
        return total

    normed_far = far_rows(own_of(normed_third))
    hidden_chip = dot(normed_third, up_map, 1, 0)
    hidden_far = dot(normed_far, up_map, 1, 0)
    active_chip = jax.nn.gelu(hidden_chip).astype(BF)
    active_far = jax.nn.gelu(hidden_far).astype(BF)
    resid_two_own = own_of(resid_two)
    resid_three = resid_two_own + scatter_rows(
        dot(active_chip, down_map, 1, 1), dot(active_far, down_map, 1, 1)
    )
    layer_output = layer_norm(resid_three, norm_values[3], norm_values[7]).astype(BF)

    positions = model_index * own_rows + jnp.arange(own_rows, dtype=jnp.int32)
    seed_grad = jnp.where((positions < length)[:, None], cotangent[0].astype(F32), 0.0)
    grad_three, gain_final, bias_final = norm_back(
        resid_three, norm_values[3], norm_values[7], seed_grad
    )
    down_own = grad_three.astype(BF)
    down_far = far_rows(down_own)
    down_chip = pair_rows(down_own)

    def hidden_back(rows, hidden):
        grad_active = dot(rows, down_map, 1, 0)
        result, pull = jax.vjp(jax.nn.gelu, hidden)
        return pull(grad_active)[0].astype(BF)

    grad_hidden_chip = hidden_back(down_chip, hidden_chip)
    grad_hidden_far = hidden_back(down_far, hidden_far)
    grad_normed = scatter_rows(
        dot(grad_hidden_chip, up_map, 1, 1), dot(grad_hidden_far, up_map, 1, 1)
    )

    def band_of(value, band):
        return pick(value.reshape(value.shape[0], nz, ny, -1), band, 2).reshape(value.shape[0], -1)

    def scatter_ffn(lefts, rights):
        def part(step):
            band = (at["y"] + step) % ny
            total = sum(dot(band_of(l, band), r, 0, 0) for l, r in zip(lefts, rights))
            return total.reshape(nz, -1, rights[0].shape[1])

        others = [hop(part(s).astype(BF), "y", s) for s in range(1, ny)]
        total = part(0)

        def finish(*ready):
            value = total
            for piece in others:
                value = value + after(piece, *ready).astype(F32)
            return reduce_along(value, "z", 0)

        return finish

    finish_down = scatter_ffn((down_chip, down_far), (active_chip, active_far))
    finish_up = scatter_ffn((normed_third, normed_far), (grad_hidden_chip, grad_hidden_far))

    def columns_of(value, index):
        return pick(value.reshape(value.shape[0], nx, -1), index, 1)

    def scatter_attn(lefts, rights):
        def part(step):
            return [dot(l, columns_of(r, (at["x"] + step) % nx), 0, 0) for l, r in zip(lefts, rights)]

        others = [
            hop(jnp.stack([v.astype(BF) for v in part(s)]), "x", s) for s in range(1, nx)
        ]
        own = part(0)

        def finish(*ready):
            total = jnp.stack(own)
            for piece in others:
                total = total + after(piece, *ready).astype(F32)
            total = total.reshape(len(own), nz, ny, -1, total.shape[2])
            return reduce_along(reduce_along(total, "y", 2), "z", 1)

        return finish

    step_back, gain_third, bias_third = norm_back(
        resid_two_own, norm_values[2], norm_values[6], grad_normed
    )
    grad_two = grad_three + step_back

    cross_rows = pair_rows(grad_two.astype(BF))
    grad_mixed_cross = dot(cross_rows, weights_cross[3], 1, 0).astype(BF)
    query_grad_cross, key_grad_cross, value_grad_cross = attend_backward(
        cross_scalars,
        query_cross,
        key_cross,
        value_cross,
        mixed_cross,
        logsum_cross,
        grad_mixed_cross,
        False,
    )

    def core_scatter(partial):
        return own_of(partial) + hop(other_of(partial).astype(BF), "c").astype(F32)

    grad_normed_cross = core_scatter(dot(query_grad_cross, weights_cross[0], 1, 1))
    step_back, gain_second, bias_second = norm_back(
        own_of(resid_one), norm_values[1], norm_values[5], grad_normed_cross
    )
    grad_one = grad_two + step_back
    finish_cross = scatter_attn(
        (normed_second, frames, frames, cross_rows),
        (query_grad_cross, key_grad_cross, value_grad_cross, mixed_cross),
    )
    shard_down = finish_down(query_grad_cross)
    shard_up = finish_up(query_grad_cross)
    memory_part = dot(key_grad_cross, weights_cross[1], 1, 1) + dot(
        value_grad_cross, weights_cross[2], 1, 1
    )
    memory_part = memory_part.reshape(slot, nx, 2, -1)
    memory_part = reduce_along(reduce_along(memory_part, "c", 2), "x", 1)
    self_rows = pair_rows(grad_one.astype(BF))
    grad_mixed_self = dot(self_rows, weights_self[3], 1, 0).astype(BF)
    query_grad, key_grad, value_grad = attend_backward(
        self_scalars,
        query_self,
        key_self,
        value_self,
        mixed_self,
        logsum_self,
        grad_mixed_self,
        True,
    )
    shard_cross = finish_cross(query_grad)
    self_grads = [
        dot(normed_first_chip, query_grad, 0, 0).astype(BF),
        dot(normed_first, key_grad, 0, 0).astype(BF),
        dot(normed_first, value_grad, 0, 0).astype(BF),
        dot(self_rows, mixed_self, 0, 0).astype(BF),
    ]
    part = dot(key_grad, weights_self[1], 1, 1) + dot(value_grad, weights_self[2], 1, 1)
    query_part = dot(query_grad, weights_self[0], 1, 1)
    part = lax.dynamic_update_slice_in_dim(part, chip_of(part) + query_part, chip_start, 0)
    empty = jnp.zeros_like(gain_third)
    norm_grad = jnp.stack(
        [empty, gain_second, gain_third, gain_final, empty, bias_second, bias_third, bias_final]
    )
    shard_self, back_states, back_memory, norm_shard = closing(
        self_grads,
        part.astype(BF).reshape(nx, 2, own_rows, width),
        own_of(chip_of(inputs)),
        grad_one,
        norm_values[0:1],
        memory_part.astype(BF).reshape(data_size, -1, memory_part.shape[1]),
        norm_grad,
    )
    attn_shard = jnp.concatenate([shard_self, shard_cross], axis=0)
    ffn_shard = jnp.stack([shard_up, shard_down])

    inverse = jnp.argsort(regroup_order)
    states_grad = jnp.take(back_states, inverse, axis=0).astype(F32)
    memory_grad = jnp.take(back_memory, inverse, axis=0).astype(F32)
    def squares(value):
        return jnp.sum((value * value).reshape(-1, 8, 128), axis=0)

    norm_squares = jnp.sum(norm_shard * norm_shard) / lax.axis_size("mp")
    local_squares = squares(attn_shard) + squares(ffn_shard) + norm_squares / 1024.0
    grad_norm = jnp.sqrt(jnp.sum(square_sum(local_squares)))
    clip_scale = jnp.minimum(1.0, THRESHOLD / (grad_norm + 1e-06))
    attn_updated, mean_attn, square_attn = adam_step(
        attn_weights, attn_mean, attn_square, clip_scale * attn_shard, MATRIX_RATE, MATRIX_DECAY
    )
    ffn_updated, mean_ffn, square_ffn = adam_step(
        ffn_weights, ffn_mean, ffn_square, clip_scale * ffn_shard, MATRIX_RATE, MATRIX_DECAY
    )
    norm_updated, mean_norm, square_norm = adam_step(
        norm_params, norm_mean, norm_square, clip_scale * norm_shard, NORM_RATE, 0.0
    )
    average_attn = AVERAGING * attn_average + (1.0 - AVERAGING) * attn_updated
    average_ffn = AVERAGING * ffn_average + (1.0 - AVERAGING) * ffn_updated
    average_norm = AVERAGING * norm_average + (1.0 - AVERAGING) * norm_updated
    return (
        layer_output[None],
        states_grad,
        memory_grad,
        attn_updated,
        ffn_updated,
        norm_updated,
        mean_attn,
        mean_ffn,
        mean_norm,
        square_attn,
        square_ffn,
        square_norm,
        average_attn,
        average_ffn,
        average_norm,
        grad_norm,
    )


def solution(mesh):
    rows = P(None, "dp", "mp")
    line = P(None, "dp")
    return jax.shard_map(
        per_device,
        mesh=mesh,
        in_specs=(rows, rows, P("dp", "mp", None), P(), P(), P())
        + (rows, rows, line) * 4,
        out_specs=(P("dp", "mp", None), rows, rows) + (rows, rows, line) * 4 + (P(),),
        check_vma=False,
    )
```

```python
import functools

import jax
import jax.numpy as jnp
from jax import lax
from jax.experimental import pallas as pl
from jax.experimental.pallas import tpu as pltpu
from jax.sharding import PartitionSpec as P

HD = 64
STEP = 10


EPSILON = 1e-05
NEGATIVE = -1000000000.0
BETA_FIRST = 0.9
BETA_SECOND = 0.999
ADAM_EPSILON = 1e-08
MATRIX_RATE = 0.05
NORM_RATE = 1.0
MATRIX_DECAY = 0.1
AVERAGING = 0.7
THRESHOLD = 1.0
BF = jnp.bfloat16
F32 = jnp.float32


def grid_sizes():
    dp = lax.axis_size("dp")
    mp = lax.axis_size("mp")
    ny = 1 << ((dp.bit_length() - 1) // 2)
    return {"z": dp // ny, "y": ny, "x": mp // 2, "c": 2}


def grid_place():
    n = grid_sizes()
    dp = lax.axis_index("dp")
    mp = lax.axis_index("mp")
    return {"z": dp // n["y"], "y": dp % n["y"], "x": mp // 2, "c": mp % 2}


def dot(left, right, left_dim, right_dim):
    return lax.dot_general(
        left, right, (((left_dim,), (right_dim,)), ((), ())), preferred_element_type=F32
    )


PAIR = 2 * HD


def only_head(value, head):
    lane = lax.broadcasted_iota(jnp.int32, value.shape, 1)
    keep = (lane < HD) if head == 0 else (lane >= HD)
    return jnp.where(keep, value, jnp.zeros_like(value))


def attend_pair(p, chunk, bound, q_ref, k_ref, v_ref, o_ref, sum_ref, score_ref, weight_ref):
    lanes = pl.ds(pl.multiple_of(p * PAIR, PAIR), PAIR)
    keys = k_ref.shape[0]
    queries = q_ref[:, lanes] * BF(HD**-0.5)
    values = v_ref[:, lanes]
    mixed = []
    for head in range(2):
        masked = only_head(queries, head)
        top = None
        for start in range(0, keys, chunk):
            block = slice(start, start + chunk)
            scores = dot(k_ref[block, lanes], masked, 1, 1)
            position = lax.broadcasted_iota(jnp.int32, scores.shape, 0) + start
            scores = jnp.where(position < bound, scores, NEGATIVE)
            score_ref[head, block, :] = scores
            highest = jnp.max(scores, axis=0, keepdims=True)
            top = highest if top is None else jnp.maximum(top, highest)
        total = None
        for start in range(0, keys, chunk):
            block = slice(start, start + chunk)
            raised = jnp.exp(score_ref[head, block, :] - top)
            part = jnp.sum(raised, axis=0, keepdims=True)
            total = part if total is None else total + part
            weight_ref[head, block, :] = raised.astype(BF)
        out = dot(values, weight_ref[head], 0, 0)[head * HD : (head + 1) * HD]
        mixed.append(out * (1.0 / total))
        sum_ref[p, head : head + 1, :] = top + jnp.log(total)
    o_ref[:, lanes] = jnp.concatenate(mixed, axis=0).T.astype(BF)


def attend_pair_back(
    p, chunk, bound, q_ref, k_ref, v_ref, o_ref, sum_ref, g_ref, dq_ref, dk_ref, dv_ref, ds_ref
):
    lanes = pl.ds(pl.multiple_of(p * PAIR, PAIR), PAIR)
    keys = k_ref.shape[0]
    queries = q_ref[:, lanes] * BF(HD**-0.5)
    grads = g_ref[:, lanes]
    product = (grads.astype(F32) * o_ref[:, lanes].astype(F32)).T
    head_q = [only_head(queries, head) for head in range(2)]
    head_g = [only_head(grads, head) for head in range(2)]
    shift = [
        jnp.sum(product[head * HD : (head + 1) * HD], axis=0, keepdims=True) for head in range(2)
    ]
    for start in range(0, keys, chunk):
        block = slice(start, start + chunk)
        key_block, value_block = k_ref[block, lanes], v_ref[block, lanes]
        grad_value, grad_key = 0.0, 0.0
        for head in range(2):
            scores = dot(key_block, head_q[head], 1, 1)
            position = lax.broadcasted_iota(jnp.int32, scores.shape, 0) + start
            scores = jnp.where(position < bound, scores, NEGATIVE)
            weights = jnp.exp(scores - sum_ref[p, head : head + 1, :])
            grad_weights = dot(value_block, head_g[head], 1, 1)
            grad_scores = (weights * (grad_weights - shift[head])).astype(BF)
            ds_ref[head, block, :] = grad_scores
            grad_value = grad_value + dot(weights.astype(BF), head_g[head], 1, 0)
            grad_key = grad_key + dot(grad_scores, head_q[head], 1, 0)
        dv_ref[block, lanes] = grad_value.astype(BF)
        dk_ref[block, lanes] = grad_key.astype(BF)
    key_all = k_ref[:, lanes]
    parts = [dot(key_all, ds_ref[h], 0, 0)[h * HD : (h + 1) * HD] for h in range(2)]
    dq_ref[:, lanes] = (jnp.concatenate(parts, axis=0).T * HD**-0.5).astype(BF)


class Wires:
    def __init__(self, sizes, place, send_sem, recv_sem):
        self.sizes, self.place = sizes, place
        self.send_sem, self.recv_sem = send_sem, recv_sem
        self.count = 0
        self.started = []

    def peer(self, z=0, y=0, x=0, c=0):
        n, at = self.sizes, self.place
        pz, py = (at["z"] + z) % n["z"], (at["y"] + y) % n["y"]
        px, pc = (at["x"] + x) % n["x"], (at["c"] + c) % 2
        return (pz * n["y"] + py, px * 2 + pc)

    def send(self, src, dst, **shift):
        copy = pltpu.make_async_remote_copy(
            src_ref=src,
            dst_ref=dst,
            send_sem=self.send_sem.at[self.count],
            recv_sem=self.recv_sem.at[self.count],
            device_id=self.peer(**shift),
            device_id_type=pl.DeviceIdType.MESH,
        )
        self.count += 1
        copy.start()
        self.started.append(copy)
        return copy

    def greet(self, shifts):
        barrier = pltpu.get_barrier_semaphore()
        for shift in shifts:
            pl.semaphore_signal(
                barrier, inc=1, device_id=self.peer(**shift), device_id_type=pl.DeviceIdType.MESH
            )
        pl.semaphore_wait(barrier, len(shifts))

    def close(self):
        for copy in self.started:
            copy.wait_send()


def dp_shifts(n):
    return [{"z": z, "y": y} for z in range(n["z"]) for y in range(n["y"]) if z or y]


def mp_shifts(n):
    return [{"x": x, "c": c} for x in range(n["x"]) for c in range(2) if x or c]


def entry_kernel(
    n, w_ref, p_ref, s_ref, m_ref, ow_ref, op_ref, os_ref, om_ref, send_sem, recv_sem, local_sem
):
    at = grid_place()
    z, y, x, c = at["z"], at["y"], at["x"], at["c"]
    data = z * n["y"] + y
    wires = Wires(n, at, send_sem, recv_sem)
    wires.greet(
        dp_shifts(n) + [{"x": s} for s in range(1, n["x"])] + [{"c": 1}]
    )
    rows, wide = w_ref.shape[1], w_ref.shape[2]
    lines, deep = s_ref.shape[1], s_ref.shape[2]

    def spot(sz, sy, sx, mats=slice(None)):
        block = ((z - sz) % n["z"]) * n["y"] + (y - sy) % n["y"]
        column = (x - sx) % n["x"]
        return ow_ref.at[
            mats,
            pl.ds(pl.multiple_of(block * rows, rows), rows),
            pl.ds(pl.multiple_of(column * wide, wide), wide),
        ]

    def column(ref, sx, sc):
        index = ((x - sx) % n["x"]) * 2 + (c - sc) % 2
        return ref.at[:, pl.ds(pl.multiple_of(index * deep, deep), deep)]

    def patch(ref):
        index = x * 2 + c
        return ref.at[
            pl.ds(pl.multiple_of(data * lines, lines), lines),
            pl.ds(pl.multiple_of(index * deep, deep), deep),
        ]

    def stripe(ref):
        return ref.at[data]

    own = [
        pltpu.make_async_copy(w_ref, spot(0, 0, 0), local_sem.at[0]),
        pltpu.make_async_copy(p_ref, stripe(op_ref), local_sem.at[1]),
        pltpu.make_async_copy(s_ref.at[data], patch(os_ref), local_sem.at[2]),
        pltpu.make_async_copy(m_ref.at[data], patch(om_ref), local_sem.at[3]),
    ]
    for copy in own:
        copy.start()

    def spread(ref, out):
        copies = []
        for shift in dp_shifts(n):
            target = wires.peer(**shift)[0]
            copies.append(wires.send(ref.at[target], patch(out), **shift))
        return copies

    def forward_columns(out, copies):
        for copy in copies:
            copy.wait_recv()
        near = [wires.send(column(out, 0, 0), column(out, 0, 0), x=s) for s in range(1, n["x"])]
        pair = [wires.send(column(out, 0, 0), column(out, 0, 0), c=1)]
        return near, pair

    def finish_columns(out, near, pair):
        for s in range(1, n["x"]):
            near[s - 1].wait_recv()
            pair.append(wires.send(column(out, s, 0), column(out, s, 0), c=1))
        for copy in pair:
            copy.wait_recv()

    to_z = {s: wires.send(w_ref, spot(0, 0, 0), z=s) for s in range(1, n["z"])}
    to_y = {(0, s): wires.send(w_ref, spot(0, 0, 0), y=s) for s in range(1, n["y"])}
    to_x = {(0, s): wires.send(w_ref, spot(0, 0, 0), x=s) for s in range(1, n["x"])}
    params = [wires.send(p_ref, stripe(op_ref), **shift) for shift in dp_shifts(n)]
    states = spread(s_ref, os_ref)
    memory = spread(m_ref, om_ref)

    for sz in range(1, n["z"]):
        to_z[sz].wait_recv()
        for s in range(1, n["y"]):
            to_y[sz, s] = wires.send(spot(sz, 0, 0), spot(sz, 0, 0), y=s)
        for s in range(1, n["x"]):
            to_x[sz, s] = wires.send(spot(sz, 0, 0), spot(sz, 0, 0), x=s)
    for copy in own:
        copy.wait()
    states = forward_columns(os_ref, states)
    last = []
    cut = max(1, w_ref.shape[0] // 4)
    for sz in range(n["z"]):
        for sy in range(1, n["y"]):
            to_y[sz, sy].wait_recv()
            part = spot(sz, sy, 0, slice(0, cut))
            for s in range(1, n["x"]):
                last.append(wires.send(part, part, x=s))
        for sx in range(1, n["x"]):
            to_x[sz, sx].wait_recv()
            part = spot(sz, 0, sx, slice(cut, w_ref.shape[0]))
            for s in range(1, n["y"]):
                last.append(wires.send(part, part, y=s))
    memory = forward_columns(om_ref, memory)
    finish_columns(os_ref, *states)
    finish_columns(om_ref, *memory)
    for copy in params + last:
        copy.wait_recv()
    wires.close()


def entry(weights, params, states, memory):
    n = grid_sizes()
    count, rows, wide = weights.shape
    utterances, lines, deep = states.shape
    nz, ny, nx = n["z"], n["y"], n["x"]
    data = nz * ny
    copies = (
        (nz - 1)
        + nz * (ny - 1 + nx - 1)
        + 2 * nz * (ny - 1) * (nx - 1)
        + 3 * (data - 1)
        + 2 * (2 * (nx - 1) + 1)
    )
    hbm = pl.BlockSpec(memory_space=pl.ANY)
    return pl.pallas_call(
        functools.partial(entry_kernel, n),
        out_shape=[
            jax.ShapeDtypeStruct((count, data * rows, nx * wide), BF),
            jax.ShapeDtypeStruct((data,) + params.shape, F32),
            jax.ShapeDtypeStruct((data * lines, 2 * nx * deep), BF),
            jax.ShapeDtypeStruct((data * lines, 2 * nx * deep), BF),
        ],
        in_specs=[pl.BlockSpec(memory_space=pltpu.VMEM)] * 4,
        out_specs=[hbm] * 4,
        scratch_shapes=[
            pltpu.SemaphoreType.DMA((copies,)),
            pltpu.SemaphoreType.DMA((copies,)),
            pltpu.SemaphoreType.DMA((4,)),
        ],
        compiler_params=pltpu.CompilerParams(
            collective_id=0, has_side_effects=True, vmem_limit_bytes=16 * 2**20
        ),
        name="entry",
    )(weights, params, states, memory)


def loop_rows(total, step, body):
    def one(i, carry):
        body(pl.ds(pl.multiple_of(i * step, step), step))
        return carry

    lax.fori_loop(0, total // step, one, 0)


def shifted(rows, offset):
    return pl.ds(pl.multiple_of(rows.start + offset, rows.size), rows.size)


def mat_rows(out_ref, left_ref, right_ref, total, step, offset=0):
    def body(rows):
        left = left_ref[shifted(rows, offset), :]
        out_ref[rows, :] = dot(left, right_ref[...], 1, 0).astype(BF)

    loop_rows(total, step, body)


class Moves:
    def __init__(self, sem):
        self.sem = sem
        self.count = 0
        self.open = []

    def start(self, src, dst):
        copy = pltpu.make_async_copy(src, dst, self.sem.at[self.count])
        self.count += 1
        copy.start()
        return copy

    def store(self, src, dst):
        self.open.append(self.start(src, dst))

    def close(self):
        for copy in self.open:
            copy.wait()


class Gather:
    def __init__(self, wires, src, out, by_x, cut):
        self.wires, self.src, self.out = wires, src, out
        self.n, self.at = wires.sizes, wires.place
        self.by_x, self.cut = by_x, cut
        self.to_z, self.to_y, self.to_x = {}, {}, {}
        self.last = []
        nz = self.n["z"]
        self.order = [0] + sorted(range(1, nz), key=lambda s: min(s, nz - s))

    def spot(self, sz, sy, sx, mats=slice(None)):
        rows, wide = self.src.shape[1], self.src.shape[2]
        n, at = self.n, self.at
        block = ((at["z"] - sz) % n["z"]) * n["y"] + (at["y"] - sy) % n["y"]
        column = (at["x"] - sx) % n["x"] if self.by_x else 0
        return self.out.at[
            mats,
            pl.ds(pl.multiple_of(block * rows, rows), rows),
            pl.ds(pl.multiple_of(column * wide, wide), wide),
        ]

    def fan(self, sz):
        src = self.src if sz == 0 else self.spot(sz, 0, 0)
        spot = self.spot(sz, 0, 0)
        for s in range(1, self.n["y"]):
            self.to_y[sz, s] = self.wires.send(src, spot, y=s)
        if self.by_x:
            for s in range(1, self.n["x"]):
                self.to_x[sz, s] = self.wires.send(src, spot, x=s)

    def start_z(self, place):
        if place < len(self.order):
            s = self.order[place]
            self.to_z[s] = self.wires.send(self.src, self.spot(0, 0, 0), z=s)

    def corner(self, sz):
        for sy in range(1, self.n["y"]):
            self.to_y[sz, sy].wait_recv()
            if self.by_x and self.cut:
                part = self.spot(sz, sy, 0, slice(0, self.cut))
                for s in range(1, self.n["x"]):
                    self.last.append(self.wires.send(part, part, x=s))
        if self.by_x:
            for sx in range(1, self.n["x"]):
                self.to_x[sz, sx].wait_recv()
                if self.cut < self.src.shape[0]:
                    part = self.spot(sz, 0, sx, slice(self.cut, self.src.shape[0]))
                    for s in range(1, self.n["y"]):
                        self.last.append(self.wires.send(part, part, y=s))

    def arrive(self, place):
        sz = self.order[place]
        self.to_z[sz].wait_recv()
        self.start_z(place + 1)
        self.fan(sz)

    def begin(self):
        self.start_z(1)
        self.fan(0)

    def steps(self):
        count = len(self.order)
        for place in range(1, count):
            yield functools.partial(self.arrive, place)
            yield functools.partial(self.corner, self.order[place - 1])
        yield functools.partial(self.corner, self.order[count - 1])
        yield self.finish

    def finish(self):
        for copy in self.last:
            copy.wait_recv()

    @staticmethod
    def copies(n, by_x, cut, count):
        nz, ny, nx = n["z"], n["y"], n["x"]
        total = nz - 1 + nz * (ny - 1)
        if by_x:
            total += nz * (nx - 1) + 2 * nz * (ny - 1) * (nx - 1)
        return total


def norm_rows(values, p_ref, index):
    centered = values - jnp.mean(values, axis=-1, keepdims=True)
    variance = jnp.mean(centered * centered, axis=-1, keepdims=True)
    normed = centered * lax.rsqrt(variance + EPSILON)
    return (normed * p_ref[index : index + 1, :] + p_ref[index + 4 : index + 5, :]).astype(BF)


STRIP = 256


def forward_kernel(
    n, own_rows, length, reach, x_hbm, m_hbm, w_hbm, p_ref, wc_ref, wf_ref,
    owc, owf, oh1, oq, ok, ov, oo, ol, ox1, oh2, oq2, ok2, ov2, oo2, ol2, ox2, oh3,
    x_s, m_s, w_s, c_s, h1_s, q_s, k_s, v_s, o_s, l_s, x1_s, h2_s, q2_s, k2_s, v2_s, o2_s, l2_s,
    x2_s, h3_s, give_s, got_s, score_s, weight_s, send_sem, recv_sem, move_sem,
):
    at = grid_place()
    wires = Wires(n, at, send_sem, recv_sem)
    moves = Moves(move_sem)
    get_x = moves.start(x_hbm, x_s)
    get_w = moves.start(w_hbm, w_s)
    get_m = moves.start(m_hbm, m_s)
    wires.greet(
        [{"z": s} for s in range(1, n["z"])]
        + [{"y": s} for s in range(1, n["y"])]
        + [{"x": s} for s in range(1, n["x"])]
        + [{"c": 1}]
    )
    cross = Gather(wires, wc_ref, c_s, True, 3)
    cross.begin()
    own_cross = moves.start(wc_ref, cross.spot(0, 0, 0))
    up_down = Gather(wires, wf_ref, owf, False, 0)
    own_ffn = moves.start(wf_ref, up_down.spot(0, 0, 0))
    first, second = list(cross.steps()), list(up_down.steps())
    zone = 2 * (n["z"] - 1)
    queue = first[:zone] + [up_down.begin] + first[zone:]
    for i, step in enumerate(second):
        queue.insert(min(len(queue), zone + 2 + 2 * i), step)
    needed = queue.index(first[-1]) + 1
    done = [0]

    def advance(limit):
        while done[0] < min(limit, len(queue)):
            queue[done[0]]()
            done[0] += 1

    slot, width = x_s.shape
    chip_rows = 2 * own_rows
    chip_start = at["x"] * chip_rows
    strip = min(STRIP, own_rows)
    pairs = q_s.shape[1] // PAIR
    own = pl.ds(pl.multiple_of(at["c"] * own_rows, own_rows), own_rows)

    get_x.wait()

    def first_norm(rows):
        h1_s[rows, :] = norm_rows(x_s[rows, :].astype(F32), p_ref, 0)

    loop_rows(slot, strip, first_norm)
    get_w.wait()
    advance(1)
    moves.store(h1_s, oh1)
    mat_rows(q_s, h1_s, w_s.at[0], chip_rows, strip, chip_start)
    mat_rows(k_s, h1_s, w_s.at[1], slot, strip)
    advance(2)
    mat_rows(v_s, h1_s, w_s.at[2], slot, strip)
    advance(3)
    for ref, out in ((q_s, oq), (k_s, ok), (v_s, ov)):
        moves.store(ref, out)
    reach_self = lax.broadcasted_iota(jnp.int32, (1, chip_rows), 1) + chip_start + 1
    reach_self = jnp.minimum(reach_self, length[0])
    for p in range(pairs):
        attend_pair(p, 256, reach_self, q_s, k_s, v_s, o_s, l_s, score_s, weight_s)
        advance(4 + p)
    moves.store(o_s, oo)
    moves.store(l_s, ol)

    def give(index, mixed, out_map):
        def body(rows):
            give_s[index, rows, :] = dot(mixed[rows, :], out_map[...], 1, 1).astype(BF)

        loop_rows(chip_rows, strip, body)
        return wires.send(give_s.at[index], got_s.at[index], c=1)

    def total(index, rows):
        return give_s[index, rows, :].astype(F32) + got_s[index, rows, :].astype(F32)

    swap = give(0, o_s, w_s.at[3])
    get_m.wait()
    swap.wait_recv()

    def second_norm(rows):
        values = x_s[shifted(rows, chip_start), :].astype(F32) + total(0, rows)
        x1_s[rows, :] = values
        h2_s[rows, :] = norm_rows(values, p_ref, 1)

    loop_rows(chip_rows, strip, second_norm)
    moves.store(x1_s.at[own], ox1)
    moves.store(h2_s, oh2)
    advance(needed)
    own_cross.wait()
    moves.store(c_s, owc)
    mat_rows(q2_s, h2_s, c_s.at[0], chip_rows, strip)
    mat_rows(k2_s, m_s, c_s.at[1], slot, strip)
    mat_rows(v2_s, m_s, c_s.at[2], slot, strip)
    advance(needed + 1)
    for ref, out in ((q2_s, oq2), (k2_s, ok2), (v2_s, ov2)):
        moves.store(ref, out)
    reach_cross = jnp.full((1, chip_rows), reach[0], jnp.int32)
    for p in range(pairs):
        attend_pair(p, 256, reach_cross, q2_s, k2_s, v2_s, o2_s, l2_s, score_s, weight_s)
        advance(needed + 2 + p)
    moves.store(o2_s, oo2)
    moves.store(l2_s, ol2)
    swap = give(1, o2_s, c_s.at[3])
    advance(needed + 7)
    swap.wait_recv()

    def third_norm(rows):
        values = x1_s[rows, :] + total(1, rows)
        x2_s[rows, :] = values
        h3_s[rows, :] = norm_rows(values, p_ref, 2)

    loop_rows(chip_rows, strip, third_norm)
    moves.store(x2_s.at[own], ox2)
    moves.store(h3_s, oh3)
    advance(len(queue))
    own_ffn.wait()
    moves.close()
    wires.close()


def forward(length, reach, inputs, frames, weights_self, params, cross_shard, ffn_shard, own_rows):
    n = grid_sizes()
    slot, width = inputs.shape
    mats, _, local = weights_self.shape
    hidden = ffn_shard.shape[2]
    chip_rows = 2 * own_rows
    pairs = local // PAIR
    copies = Gather.copies(n, True, 3, 4) + Gather.copies(n, False, 0, 2) + 2
    vmem = pl.BlockSpec(memory_space=pltpu.VMEM)
    smem = pl.BlockSpec(memory_space=pltpu.SMEM)
    hbm = pl.BlockSpec(memory_space=pl.ANY)
    half = lambda *shape: (shape, BF)
    full = lambda *shape: (shape, F32)
    outs = [
        half(mats, width, local),
        half(2, width, hidden),
        half(slot, width),
        half(chip_rows, local),
        half(slot, local),
        half(slot, local),
        half(chip_rows, local),
        full(pairs, 2, chip_rows),
        full(own_rows, width),
        half(chip_rows, width),
        half(chip_rows, local),
        half(slot, local),
        half(slot, local),
        half(chip_rows, local),
        full(pairs, 2, chip_rows),
        full(own_rows, width),
        half(chip_rows, width),
    ]
    scratch = [
        half(slot, width),
        half(slot, width),
        half(mats, width, local),
        half(mats, width, local),
        half(slot, width),
        half(chip_rows, local),
        half(slot, local),
        half(slot, local),
        half(chip_rows, local),
        full(pairs, 2, chip_rows),
        full(chip_rows, width),
        half(chip_rows, width),
        half(chip_rows, local),
        half(slot, local),
        half(slot, local),
        half(chip_rows, local),
        full(pairs, 2, chip_rows),
        full(chip_rows, width),
        half(chip_rows, width),
        half(2, chip_rows, width),
        half(2, chip_rows, width),
        full(2, slot, chip_rows),
        half(2, slot, chip_rows),
    ]
    return pl.pallas_call(
        functools.partial(forward_kernel, n, own_rows),
        out_shape=[jax.ShapeDtypeStruct(s, t) for s, t in outs],
        in_specs=[smem, smem, hbm, hbm, hbm, vmem, vmem, vmem],
        out_specs=[hbm] * len(outs),
        scratch_shapes=[pltpu.VMEM(s, t) for s, t in scratch]
        + [
            pltpu.SemaphoreType.DMA((copies,)),
            pltpu.SemaphoreType.DMA((copies,)),
            pltpu.SemaphoreType.DMA((24,)),
        ],
        compiler_params=pltpu.CompilerParams(
            collective_id=3, has_side_effects=True, vmem_limit_bytes=56 * 2**20
        ),
        name="forward",
    )(length, reach, inputs, frames, weights_self, params, cross_shard, ffn_shard)


def norm_back_rows(values, grad, gain):
    centered = values - jnp.mean(values, axis=-1, keepdims=True)
    scale = lax.rsqrt(jnp.mean(centered * centered, axis=-1, keepdims=True) + EPSILON)
    normed = centered * scale
    up = grad * gain
    back = scale * (
        up
        - jnp.mean(up, axis=-1, keepdims=True)
        - normed * jnp.mean(up * normed, axis=-1, keepdims=True)
    )
    return back, normed


def row_sum(values):
    return jnp.sum(values, axis=0, keepdims=True)


SPLIT = 2


def ffn_kernel(
    n, length, h_hbm, x_ref, w_hbm, ct_ref, p_ref,
    oy_ref, odx_ref, odc, odw, on_ref,
    h_s, f_s, a_s, d_s, u_s, w_s, keep_s, far_s, give_s, got_s, cross_s, crossed_s, back_s, come_s,
    x3_s, dx3_s, dc_s, dw_s, send_sem, recv_sem, move_sem,
):
    at = grid_place()
    wires = Wires(n, at, send_sem, recv_sem)
    moves = Moves(move_sem)
    nx, c = n["x"], at["c"]
    own, width = x_ref.shape
    part = own // SPLIT
    start_own = pl.multiple_of(c * own, own)
    start_other = pl.multiple_of((1 - c) * own, own)
    get_w = moves.start(w_hbm, w_s)
    get_own = moves.start(h_hbm.at[pl.ds(start_own, own)], h_s.at[pl.ds(0, own)])
    get_other = moves.start(h_hbm.at[pl.ds(start_other, own)], h_s.at[pl.ds(own, own)])
    wires.greet([{"x": s} for s in range(1, nx)] + [{"c": 1}])

    def far_at(t, k, j):
        return 2 * own + (((t - 1) * SPLIT + k) * 2 + j) * part

    def spread(src, dst, k):
        return [
            wires.send(src.at[pl.ds(k * part, part)], dst.at[pl.ds(far_at(t, k, 0), part)], x=t)
            for t in range(1, nx)
        ]

    def onward(dst, t, k):
        return wires.send(
            dst.at[pl.ds(far_at(t, k, 0), part)], dst.at[pl.ds(far_at(t, k, 1), part)], c=1
        )

    def up(rows):
        hidden = dot(h_s[rows, :], w_s[0], 1, 0)
        inner = 0.7978845608028654 * (hidden + 0.044715 * (hidden * hidden * hidden))
        bend = jnp.tanh(inner)
        a_s[rows, :] = (0.5 * hidden * (1.0 + bend)).astype(BF)
        slope = 0.7978845608028654 * (1.0 + 0.134145 * (hidden * hidden))
        d_s[rows, :] = 0.5 * (1.0 + bend) + 0.5 * hidden * (1.0 - bend * bend) * slope
        return dot(a_s[rows, :], w_s[1], 1, 1)

    def down(rows):
        grad = dot(f_s[rows, :], w_s[1], 1, 0)
        u_s[rows, :] = (grad * d_s[rows, :]).astype(BF)
        return dot(u_s[rows, :], w_s[0], 1, 1)

    def other_core(phase, work):
        give_s[phase] = work(slice(own, 2 * own)).astype(BF)
        return wires.send(give_s.at[phase], got_s.at[phase], c=1)

    def far_part(phase, work, t, k):
        sums = work(slice(far_at(t, k, 0), far_at(t, k, 0) + 2 * part))
        far_s[t - 1, k] = sums[:part]
        cross_s[phase, t - 1, k] = sums[part:].astype(BF)
        return wires.send(cross_s.at[phase, t - 1, k], crossed_s.at[phase, t - 1, k], c=1)

    def return_part(phase, t, k, crossing):
        crossing.wait_recv()
        back_s[phase, t - 1, k] = (far_s[t - 1, k] + crossed_s[phase, t - 1, k].astype(F32)).astype(
            BF
        )
        return wires.send(back_s.at[phase, t - 1, k], come_s.at[phase, t - 1, k], x=nx - t)

    def far_phase(phase, work, buffer, arriving):
        homing = {}
        for k in range(SPLIT):
            crossed = []
            for t in range(1, nx):
                arriving[k][t - 1].wait_recv()
                crossed.append(onward(buffer, t, k))
            crossing = []
            for t in range(1, nx):
                crossed[t - 1].wait_recv()
                crossing.append(far_part(phase, work, t, k))
            for t in range(1, nx):
                homing[k, t] = return_part(phase, t, k, crossing[t - 1])
        return homing

    def own_part(phase, k, homing):
        rows = slice(k * part, (k + 1) * part)
        total = keep_s[rows, :] + got_s[phase, rows, :].astype(F32)
        for t in range(1, nx):
            homing[k, t].wait_recv()
            total = total + come_s[phase, t - 1, k].astype(F32)
        return total

    get_own.wait()
    arriving = [spread(h_s, h_s, k) for k in range(SPLIT)]
    get_w.wait()
    get_other.wait()
    swap = other_core(0, up)
    keep_s[...] = up(slice(0, own))
    homing = far_phase(0, up, h_s, arriving)
    swap.wait_recv()
    gain_final, bias_final = 0.0, 0.0
    arriving, near = [], []
    first_row = (at["x"] * 2 + c) * own
    for k in range(SPLIT):
        rows = slice(k * part, (k + 1) * part)
        values = x_ref[rows, :] + own_part(0, k, homing)
        x3 = values
        centered = x3 - jnp.mean(x3, axis=-1, keepdims=True)
        variance = jnp.mean(centered * centered, axis=-1, keepdims=True)
        normed = centered * lax.rsqrt(variance + EPSILON)
        oy_ref[rows, :] = (normed * p_ref[3:4, :] + p_ref[7:8, :]).astype(BF)
        position = lax.broadcasted_iota(jnp.int32, (part, 1), 0) + (first_row + k * part)
        seed = jnp.where(position < length[0], ct_ref[rows, :].astype(F32), 0.0)
        grad, normed = norm_back_rows(x3, seed, p_ref[3:4, :])
        gain_final = gain_final + row_sum(seed * normed)
        bias_final = bias_final + row_sum(seed)
        dx3_s[rows, :] = grad
        f_s[rows, :] = grad.astype(BF)
        arriving.append(spread(f_s, f_s, k))
        near.append(
            wires.send(f_s.at[pl.ds(k * part, part)], f_s.at[pl.ds(own + k * part, part)], c=1)
        )
    keep_s[...] = down(slice(0, own))
    for copy in near:
        copy.wait_recv()
    swap = other_core(1, down)
    homing = far_phase(1, down, f_s, arriving)
    step = min(256, width)
    for i, (left, right) in ((1, (f_s, a_s)), (0, (h_s, u_s))):
        for col in range(0, width, step):
            cols = slice(col, col + step)
            dw_s[i, cols, :] = dot(left[:, cols], right[...], 0, 0).astype(BF)
        moves.store(dw_s.at[i], odw.at[i])
    swap.wait_recv()
    gain_third, bias_third = 0.0, 0.0
    near = []
    for k in range(SPLIT):
        rows = slice(k * part, (k + 1) * part)
        upstream = own_part(1, k, homing)
        grad, normed = norm_back_rows(x_ref[rows, :], upstream, p_ref[2:3, :])
        gain_third = gain_third + row_sum(upstream * normed)
        bias_third = bias_third + row_sum(upstream)
        total = dx3_s[rows, :] + grad
        odx_ref[rows, :] = total
        here = pl.ds(start_own + k * part, part)
        dc_s[here, :] = total.astype(BF)
        near.append(wires.send(dc_s.at[here], dc_s.at[here], c=1))
    line = lax.broadcasted_iota(jnp.int32, on_ref.shape, 0)
    sums = jnp.zeros(on_ref.shape, F32)
    for index, value in ((2, gain_third), (3, gain_final), (6, bias_third), (7, bias_final)):
        sums = sums + jnp.where(line == index, value, 0.0)
    on_ref[...] = sums
    for copy in near:
        copy.wait_recv()
    moves.store(dc_s, odc)
    moves.close()
    wires.close()


def feed_forward(length, normed, resid, maps, cotangent, params):
    n = grid_sizes()
    chip_rows, width = normed.shape
    own = chip_rows // 2
    hidden = maps.shape[2]
    nx = n["x"]
    rows = chip_rows * nx
    part = own // SPLIT
    copies = 2 * (SPLIT * (nx - 1) * 4 + 1) + 2 * SPLIT
    vmem = pl.BlockSpec(memory_space=pltpu.VMEM)
    smem = pl.BlockSpec(memory_space=pltpu.SMEM)
    hbm = pl.BlockSpec(memory_space=pl.ANY)
    far = (2, nx - 1, SPLIT, part, width)
    return pl.pallas_call(
        functools.partial(ffn_kernel, n),
        out_shape=[
            jax.ShapeDtypeStruct((own, width), BF),
            jax.ShapeDtypeStruct((own, width), F32),
            jax.ShapeDtypeStruct((chip_rows, width), BF),
            jax.ShapeDtypeStruct((2, width, hidden), BF),
            jax.ShapeDtypeStruct(params.shape, F32),
        ],
        in_specs=[smem, hbm, vmem, hbm, vmem, vmem],
        out_specs=[vmem, vmem, hbm, hbm, vmem],
        scratch_shapes=[
            pltpu.VMEM((rows, width), BF),
            pltpu.VMEM((rows, width), BF),
            pltpu.VMEM((rows, hidden), BF),
            pltpu.VMEM((rows, hidden), F32),
            pltpu.VMEM((rows, hidden), BF),
            pltpu.VMEM((2, width, hidden), BF),
            pltpu.VMEM((own, width), F32),
            pltpu.VMEM((nx - 1, SPLIT, part, width), F32),
            pltpu.VMEM((2, own, width), BF),
            pltpu.VMEM((2, own, width), BF),
            pltpu.VMEM(far, BF),
            pltpu.VMEM(far, BF),
            pltpu.VMEM(far, BF),
            pltpu.VMEM(far, BF),
            pltpu.VMEM((own, width), F32),
            pltpu.VMEM((own, width), F32),
            pltpu.VMEM((chip_rows, width), BF),
            pltpu.VMEM((2, width, hidden), BF),
            pltpu.SemaphoreType.DMA((copies,)),
            pltpu.SemaphoreType.DMA((copies,)),
            pltpu.SemaphoreType.DMA((8,)),
        ],
        compiler_params=pltpu.CompilerParams(
            collective_id=4, has_side_effects=True, vmem_limit_bytes=56 * 2**20
        ),
        name="feed_forward",
    )(length, normed, resid, maps, cotangent, params)


def zone_order(n):
    return list(range(1, n["z"])) + [0]


def cross_back_kernel(
    n, reach, dc_hbm, dx_ref, w_hbm, q_hbm, k_hbm, v_hbm, o_hbm, l_ref, h_hbm, m_hbm, x_ref, p_ref,
    dw_hbm, of_ref, og, odx_ref, odb, om, on_ref,
    dc_s, w_s, q_s, k_s, v_s, o_s, h_s, m_s, g_s, dq_s, dk_s, dv_s, ds_s, gr_s, give_s, got_s,
    db_s, pm_s, rm_s, sm_s, cm_s, om_s, fown_s, fy_s, fkeep_s, fz_s, fr_s,
    send_sem, recv_sem, move_sem,
):
    at = grid_place()
    z, y, x, c = at["z"], at["y"], at["x"], at["c"]
    nz, ny, nx = n["z"], n["y"], n["x"]
    wires = Wires(n, at, send_sem, recv_sem)
    moves = Moves(move_sem)
    loads = [
        moves.start(a, b)
        for a, b in (
            (dc_hbm, dc_s), (w_hbm, w_s), (q_hbm, q_s), (k_hbm, k_s), (v_hbm, v_s), (o_hbm, o_s)
        )
    ]
    later = [moves.start(h_hbm, h_s), moves.start(m_hbm, m_s)]
    rows = of_ref.shape[1]
    order = zone_order(n)

    def band(s, t):
        index = ((z + s) % nz) * ny + (y + t) % ny
        return pl.ds(pl.multiple_of(index * rows, rows), rows)

    owned = [moves.start(dw_hbm.at[:, band(s, 0)], fown_s.at[s]) for s in range(nz)]
    wires.greet(
        [{"z": s} for s in range(1, nz)]
        + [{"y": s} for s in range(1, ny)]
        + [{"x": s} for s in range(1, nx)]
        + [{"c": 1}]
    )
    by_y = {
        (s, t): wires.send(dw_hbm.at[:, band(s, t)], fy_s.at[t - 1, s], y=t)
        for s in order
        for t in range(1, ny)
    }
    by_z = {}

    def ffn_zone(s):
        owned[s].wait()
        for t in range(1, ny):
            by_y[s, t].wait_recv()
        for i in range(2):
            total = fown_s[s, i].astype(F32)
            for t in range(1, ny):
                total = total + fy_s[t - 1, s, i].astype(F32)
            if s:
                fz_s[s - 1, i] = total.astype(BF)
            else:
                fkeep_s[i] = total
        if s:
            by_z[s] = wires.send(fz_s.at[s - 1], fr_s.at[s - 1], z=s)

    def ffn_finish():
        for s in range(1, nz):
            by_z[s].wait_recv()
        for i in range(2):
            total = fkeep_s[i]
            for s in range(1, nz):
                total = total + fr_s[s - 1, i].astype(F32)
            of_ref[i] = total

    queue = [functools.partial(ffn_zone, s) for s in order] + [ffn_finish]
    done = [0]

    def advance(limit):
        while done[0] < min(limit, len(queue)):
            queue[done[0]]()
            done[0] += 1

    chip_rows, width = dc_s.shape
    slot = m_s.shape[0]
    own = chip_rows // 2
    strip = min(STRIP, own)
    pairs = q_s.shape[1] // PAIR
    mine = pl.ds(pl.multiple_of(c * own, own), own)
    other = pl.ds(pl.multiple_of((1 - c) * own, own), own)
    for copy in loads:
        copy.wait()
    mat_rows(g_s, dc_s, w_s.at[3], chip_rows, strip)
    bound = jnp.full((1, chip_rows), reach[0], jnp.int32)
    for p in range(pairs):
        attend_pair_back(
            p, 256, bound, q_s, k_s, v_s, o_s, l_ref, g_s, dq_s, dk_s, dv_s, ds_s
        )
        advance(p)

    def input_part(rows_):
        give_s[rows_, :] = dot(dq_s[rows_, :], w_s[0], 1, 1).astype(BF)

    loop_rows(chip_rows, strip, input_part)
    swap = wires.send(give_s.at[other], got_s, c=1)
    deep = om_s.shape[1]
    piece = min(512, width)

    def memory_part(rows_):
        for col in range(0, width, piece):
            some = slice(col, col + piece)
            sums = dot(dk_s[rows_, :], w_s[1, some, :], 1, 1)
            sums = (sums + dot(dv_s[rows_, :], w_s[2, some, :], 1, 1)).astype(BF)
            for b in range(piece // deep):
                index = col // deep + b
                pm_s[index // 2, index % 2, rows_, :] = sums[:, b * deep : (b + 1) * deep]

    loop_rows(slot, strip, memory_part)
    to_c = wires.send(pm_s.at[:, 1 - c], rm_s, c=1)
    swap.wait_recv()
    upstream = give_s[mine, :].astype(F32) + got_s[...].astype(F32)
    grad, normed = norm_back_rows(x_ref[...], upstream, p_ref[1:2, :])
    total = dx_ref[...] + grad
    odx_ref[...] = total
    db_s[mine, :] = total.astype(BF)
    near = wires.send(db_s.at[mine], db_s.at[mine], c=1)
    line = lax.broadcasted_iota(jnp.int32, on_ref.shape, 0)
    on_ref[...] = jnp.where(line == 1, row_sum(upstream * normed), 0.0) + jnp.where(
        line == 5, row_sum(upstream), 0.0
    )
    to_c.wait_recv()
    to_x = []
    for t in range(1, nx):
        index = (x + t) % nx
        sm_s[t - 1] = (pm_s[index, c].astype(F32) + rm_s[index].astype(F32)).astype(BF)
        to_x.append(wires.send(sm_s.at[t - 1], cm_s.at[t - 1], x=t))
    advance(pairs)
    for copy in later:
        copy.wait()
    step = min(256, width)
    for i, (left, right) in enumerate(((h_s, dq_s), (m_s, dk_s), (m_s, dv_s), (dc_s, o_s))):
        for col in range(0, width, step):
            cols = slice(col, col + step)
            gr_s[i, cols, :] = dot(left[:, cols], right[...], 0, 0).astype(BF)
        moves.store(gr_s.at[i], og.at[i])
    total = pm_s[x, c].astype(F32) + rm_s[x].astype(F32)
    for t in range(1, nx):
        to_x[t - 1].wait_recv()
        total = total + cm_s[t - 1].astype(F32)
    om_s[...] = total.astype(BF)
    moves.store(om_s, om)
    near.wait_recv()
    moves.store(db_s, odb)
    advance(len(queue))
    moves.close()
    wires.close()


def cross_back(reach, rows_grad, resid_grad, maps, saved, normed, frames, resid, params, ffn_grads):
    n = grid_sizes()
    nz, ny, nx = n["z"], n["y"], n["x"]
    queries, keys, values, mixed, logsum = saved
    chip_rows, width = rows_grad.shape
    own = chip_rows // 2
    slot, local = keys.shape
    hidden = ffn_grads.shape[2]
    rows = width // (nz * ny)
    deep = width // (2 * nx)
    copies = nz * (ny - 1) + (nz - 1) + 3 + (nx - 1)
    vmem = pl.BlockSpec(memory_space=pltpu.VMEM)
    smem = pl.BlockSpec(memory_space=pltpu.SMEM)
    hbm = pl.BlockSpec(memory_space=pl.ANY)
    half = lambda *shape: pltpu.VMEM(shape, BF)
    return pl.pallas_call(
        functools.partial(cross_back_kernel, n),
        out_shape=[
            jax.ShapeDtypeStruct((2, rows, hidden), F32),
            jax.ShapeDtypeStruct((4, width, local), BF),
            jax.ShapeDtypeStruct((own, width), F32),
            jax.ShapeDtypeStruct((chip_rows, width), BF),
            jax.ShapeDtypeStruct((slot, deep), BF),
            jax.ShapeDtypeStruct(params.shape, F32),
        ],
        in_specs=[smem, hbm, vmem, hbm, hbm, hbm, hbm, hbm, vmem, hbm, hbm, vmem, vmem, hbm],
        out_specs=[vmem, hbm, vmem, hbm, hbm, vmem],
        scratch_shapes=[
            half(chip_rows, width),
            half(4, width, local),
            half(chip_rows, local),
            half(slot, local),
            half(slot, local),
            half(chip_rows, local),
            half(chip_rows, width),
            half(slot, width),
            half(chip_rows, local),
            half(chip_rows, local),
            half(slot, local),
            half(slot, local),
            half(2, slot, chip_rows),
            half(4, width, local),
            half(chip_rows, width),
            half(own, width),
            half(chip_rows, width),
            half(nx, 2, slot, deep),
            half(nx, slot, deep),
            half(nx - 1, slot, deep),
            half(nx - 1, slot, deep),
            half(slot, deep),
            half(nz, 2, rows, hidden),
            half(ny - 1, nz, 2, rows, hidden),
            pltpu.VMEM((2, rows, hidden), F32),
            half(nz - 1, 2, rows, hidden),
            half(nz - 1, 2, rows, hidden),
            pltpu.SemaphoreType.DMA((copies,)),
            pltpu.SemaphoreType.DMA((copies,)),
            pltpu.SemaphoreType.DMA((16 + nz,)),
        ],
        compiler_params=pltpu.CompilerParams(
            collective_id=5, has_side_effects=True, vmem_limit_bytes=56 * 2**20
        ),
        name="cross_back",
    )(
        reach, rows_grad, resid_grad, maps, queries, keys, values, mixed, logsum, normed, frames,
        resid, params, ffn_grads,
    )


class Scatter:
    def __init__(self, wires, grads, ra1, rb1, sa2, sb2, ra2, rb2, acc, s3, r3):
        self.wires, self.grads = wires, grads
        self.n, self.at = wires.sizes, wires.place
        self.ra1, self.rb1, self.sa2, self.sb2 = ra1, rb1, sa2, sb2
        self.ra2, self.rb2, self.acc, self.s3, self.r3 = ra2, rb2, acc, s3, r3
        self.rows, self.wide = acc.shape[2], acc.shape[3]
        self.by_x, self.by_y, self.next_x, self.next_y, self.to_z = {}, {}, {}, {}, {}

    @staticmethod
    def copies(n):
        nz, ny, nx = n["z"], n["y"], n["x"]
        return nz * 2 * (nx - 1 + ny - 1) + nz * (ny - 1 + nx - 1) + nz - 1

    @staticmethod
    def scratch(n, rows, wide):
        nz, ny, nx = n["z"], n["y"], n["x"]
        return [
            pltpu.VMEM((nx - 1, nz, 2, ny * rows, wide), BF),
            pltpu.VMEM((ny - 1, nz, 2, rows, nx * wide), BF),
            pltpu.VMEM((ny - 1, nz, 2, rows, wide), BF),
            pltpu.VMEM((nx - 1, nz, 2, rows, wide), BF),
            pltpu.VMEM((ny - 1, nz, 2, rows, wide), BF),
            pltpu.VMEM((nx - 1, nz, 2, rows, wide), BF),
            pltpu.VMEM((nz, 4, rows, wide), F32),
            pltpu.VMEM((nz - 1, 4, rows, wide), BF),
            pltpu.VMEM((nz - 1, 4, rows, wide), BF),
        ]

    def bands(self, i, band, count, col):
        rows, wide = self.rows, self.wide
        return self.grads.at[
            i,
            pl.ds(pl.multiple_of(band * rows, rows), count * rows),
            pl.ds(pl.multiple_of(col * wide, wide), wide),
        ]

    def zone(self, s):
        return ((self.at["z"] + s) % self.n["z"]) * self.n["y"]

    def begin(self, mats=(0, 1, 2, 3)):
        nx, ny, rows = self.n["x"], self.n["y"], self.rows
        for s in zone_order(self.n):
            zone = self.zone(s)
            for i in mats:
                if i < 2:
                    for t in range(1, nx):
                        src = self.bands(i, zone, ny, (self.at["x"] + t) % nx)
                        self.by_x[s, t, i] = self.wires.send(src, self.ra1.at[t - 1, s, i], x=t)
                else:
                    for t in range(1, ny):
                        band = zone + (self.at["y"] + t) % ny
                        src = self.grads.at[i, pl.ds(pl.multiple_of(band * rows, rows), rows)]
                        self.by_y[s, t, i] = self.wires.send(src, self.rb1.at[t - 1, s, i - 2], y=t)

    def middle(self, s):
        nx, ny, rows, wide = self.n["x"], self.n["y"], self.rows, self.wide
        x, y = self.at["x"], self.at["y"]
        zone = self.zone(s)
        for i in range(2):
            for t in range(1, nx):
                self.by_x[s, t, i].wait_recv()
            for b in range(ny):
                band = (y + b) % ny
                total = self.bands(i, zone + band, 1, x)[...].astype(F32)
                for t in range(1, nx):
                    lines = pl.ds(pl.multiple_of(band * rows, rows), rows)
                    total = total + self.ra1[t - 1, s, i, lines, :].astype(F32)
                if b == 0:
                    self.acc[s, i] = total
                else:
                    self.sa2[b - 1, s, i] = total.astype(BF)
        for t in range(1, ny):
            self.next_y[s, t] = self.wires.send(self.sa2.at[t - 1, s], self.ra2.at[t - 1, s], y=t)
        for i in range(2, 4):
            for t in range(1, ny):
                self.by_y[s, t, i].wait_recv()
            for b in range(nx):
                column = (x + b) % nx
                total = self.bands(i, zone + y, 1, column)[...].astype(F32)
                for t in range(1, ny):
                    lanes = pl.ds(pl.multiple_of(column * wide, wide), wide)
                    total = total + self.rb1[t - 1, s, i - 2, :, lanes].astype(F32)
                if b == 0:
                    self.acc[s, i] = total
                else:
                    self.sb2[b - 1, s, i - 2] = total.astype(BF)
        for t in range(1, nx):
            self.next_x[s, t] = self.wires.send(self.sb2.at[t - 1, s], self.rb2.at[t - 1, s], x=t)

    def along_z(self, s):
        nx, ny = self.n["x"], self.n["y"]
        for t in range(1, ny):
            self.next_y[s, t].wait_recv()
        for t in range(1, nx):
            self.next_x[s, t].wait_recv()
        for i in range(4):
            total = self.acc[s, i]
            if i < 2:
                for t in range(1, ny):
                    total = total + self.ra2[t - 1, s, i].astype(F32)
            else:
                for t in range(1, nx):
                    total = total + self.rb2[t - 1, s, i - 2].astype(F32)
            if s:
                self.s3[s - 1, i] = total.astype(BF)
            else:
                self.acc[s, i] = total
        if s:
            self.to_z[s] = self.wires.send(self.s3.at[s - 1], self.r3.at[s - 1], z=s)

    def finish(self, out):
        nz = self.n["z"]
        for s in range(1, nz):
            self.to_z[s].wait_recv()
        for i in range(4):
            total = self.acc[0, i]
            for s in range(1, nz):
                total = total + self.r3[s - 1, i].astype(F32)
            out[i] = total


def self_back_kernel(
    n, length, db_hbm, dx_ref, w_hbm, q_hbm, k_hbm, v_hbm, o_hbm, l_ref, h_hbm, x_ref, p_ref,
    cg_hbm, m_hbm, np_ref, oc_ref, og_ref, os_ref, om_ref, on_ref, *scratch,
):
    (
        db_s, w_s, q_s, k_s, v_s, o_s, h_s, g_s, dq_s, dk_s, dv_s, ds_s, cg_s, gr_s, part_s, rc_s,
        sx_s, rx_s, out_s, np_s, nn_s, nf_s,
    ) = scratch[:22]
    send_sem, recv_sem, go_sem, come_sem, move_sem = scratch[-5:]
    at = grid_place()
    z, y, x, c = at["z"], at["y"], at["x"], at["c"]
    nz, ny, nx = n["z"], n["y"], n["x"]
    data, model = z * ny + y, x * 2 + c
    wires = Wires(n, at, send_sem, recv_sem)
    moves = Moves(move_sem)
    get_cross = moves.start(cg_hbm, cg_s)
    loads = [
        moves.start(a, b)
        for a, b in (
            (db_hbm, db_s), (w_hbm, w_s), (q_hbm, q_s), (k_hbm, k_s), (v_hbm, v_s), (o_hbm, o_s),
            (h_hbm, h_s),
        )
    ]
    wires.greet(
        [
            dict(z=sz, y=sy, x=sx, c=sc)
            for sz in range(nz)
            for sy in range(ny)
            for sx in range(nx)
            for sc in range(2)
            if sz or sy or sx or sc
        ]
    )
    cross = Scatter(wires, cg_s, *scratch[22:31])
    own_sum = Scatter(wires, gr_s, *scratch[31:40])
    get_cross.wait()
    cross.begin()
    order = zone_order(n)
    queue = [functools.partial(cross.middle, s) for s in order]
    queue += [functools.partial(cross.along_z, s) for s in order]
    done = [0]

    def advance(limit):
        while done[0] < min(limit, len(queue)):
            queue[done[0]]()
            done[0] += 1

    spread = []
    for i, shift in enumerate(dp_shifts(n)):
        target = wires.peer(**shift)[0]
        spread.append(wires.send(m_hbm.at[target], om_ref.at[data], **shift))
    keep = moves.start(m_hbm.at[data], om_ref.at[data])

    chip_rows, width = db_s.shape
    slot = h_s.shape[0]
    own = chip_rows // 2
    strip = min(STRIP, own)
    pairs = q_s.shape[1] // PAIR
    chip_start = x * chip_rows
    for copy in loads:
        copy.wait()
    mat_rows(g_s, db_s, w_s.at[3], chip_rows, strip)
    bound = lax.broadcasted_iota(jnp.int32, (1, chip_rows), 1) + chip_start + 1
    bound = jnp.minimum(bound, length[0])
    for p in range(pairs):
        attend_pair_back(
            p, 256, bound, q_s, k_s, v_s, o_s, l_ref, g_s, dq_s, dk_s, dv_s, ds_s
        )
        advance(p + 1)

    def input_part(rows_):
        sums = dot(dk_s[rows_, :], w_s[1], 1, 1) + dot(dv_s[rows_, :], w_s[2], 1, 1)
        part_s[rows_, :] = sums.astype(BF)

    loop_rows(slot, strip, input_part)

    def query_part(rows_):
        here = shifted(rows_, chip_start)
        sums = part_s[here, :].astype(F32) + dot(dq_s[rows_, :], w_s[0], 1, 1)
        part_s[here, :] = sums.astype(BF)

    loop_rows(chip_rows, strip, query_part)

    def block(chip, core):
        return pl.ds(pl.multiple_of((chip * 2 + core) * own, own), own)

    to_c = [
        wires.send(part_s.at[block(b, 1 - c)], rc_s.at[b], c=1) for b in range(nx)
    ]
    step = min(256, width)

    def weight_grad(i, left, right):
        for col in range(0, width, step):
            cols = slice(col, col + step)
            gr_s[i, cols, :] = dot(left[:, cols], right[...], 0, 0).astype(BF)
        own_sum.begin((i,))

    chip_lines = pl.ds(pl.multiple_of(chip_start, chip_rows), chip_rows)
    weight_grad(1, h_s, dk_s)
    for copy in to_c:
        copy.wait_recv()
    to_x = []
    for t in range(1, nx):
        index = (x + t) % nx
        sums = part_s[block(index, c), :].astype(F32) + rc_s[index].astype(F32)
        sx_s[t - 1] = sums.astype(BF)
        to_x.append(wires.send(sx_s.at[t - 1], rx_s.at[t - 1], x=t))
    weight_grad(2, h_s, dv_s)
    weight_grad(3, db_s, o_s)
    weight_grad(0, h_s.at[chip_lines], dq_s)
    advance(2 * nz)

    upstream = part_s[block(x, c), :].astype(F32) + rc_s[x].astype(F32)
    for t in range(1, nx):
        to_x[t - 1].wait_recv()
        upstream = upstream + rx_s[t - 1].astype(F32)
    grad, normed = norm_back_rows(x_ref[...].astype(F32), upstream, p_ref[0:1, :])
    out_s[...] = (dx_ref[...] + grad).astype(BF)
    lines, deep = os_ref.shape[1], os_ref.shape[2]
    blocks = own // lines

    def homeward():
        for b in range(blocks):
            for m in range(2 * nx):
                target = (model * blocks + b, m)
                src = out_s.at[b * lines : (b + 1) * lines, m * deep : (m + 1) * deep]
                mine = jnp.logical_and(target[0] == data, model == m)
                remote = pltpu.make_async_remote_copy(
                    src_ref=src,
                    dst_ref=os_ref.at[data],
                    send_sem=go_sem.at[b * 2 * nx + m],
                    recv_sem=come_sem.at[data],
                    device_id=target,
                    device_id_type=pl.DeviceIdType.MESH,
                )
                yield mine, remote, pltpu.make_async_copy(src, os_ref.at[data], come_sem.at[data])

    for mine, remote, here in homeward():
        pl.when(mine)(lambda: here.start())
        pl.when(jnp.logical_not(mine))(lambda: remote.start())

    line = lax.broadcasted_iota(jnp.int32, np_ref.shape, 0)
    params = (
        np_ref[...]
        + jnp.where(line == 0, row_sum(upstream * normed), 0.0)
        + jnp.where(line == 4, row_sum(upstream), 0.0)
    )
    columns = on_ref.shape[1]
    for k in range(nz * ny):
        np_s[0, k] = params[:, k * columns : (k + 1) * columns]
    norm_near = [wires.send(np_s.at[0], nn_s.at[i], **s) for i, s in enumerate(mp_shifts(n))]

    for s in order:
        own_sum.middle(s)
    total = np_s[0]
    for i, copy in enumerate(norm_near):
        copy.wait_recv()
        total = total + nn_s[i]
    np_s[1] = total
    norm_far = []
    for i, shift in enumerate(dp_shifts(n)):
        target = wires.peer(**shift)[0]
        norm_far.append(wires.send(np_s.at[1, target], nf_s.at[i], **shift))
    for s in order:
        own_sum.along_z(s)
    cross.finish(oc_ref)
    total = np_s[1, data]
    for i, copy in enumerate(norm_far):
        copy.wait_recv()
        total = total + nf_s[i]
    on_ref[...] = total
    own_sum.finish(og_ref)
    for copy in spread:
        copy.wait_recv()
    keep.wait()
    for mine, remote, here in homeward():
        pl.when(jnp.logical_not(mine))(lambda: remote.wait_send())
    for r in range(nz * ny):
        pltpu.make_async_copy(os_ref.at[r], os_ref.at[r], come_sem.at[r]).wait()
    wires.close()


def self_back(
    length, rows_grad, resid_grad, maps, saved, normed, inputs, params, cross_grads, memory, norm_part
):
    n = grid_sizes()
    nz, ny, nx = n["z"], n["y"], n["x"]
    data, model = nz * ny, 2 * nx
    queries, keys, values, mixed, logsum = saved
    chip_rows, width = rows_grad.shape
    own = chip_rows // 2
    slot, local = keys.shape
    rows, wide = width // data, local // nx
    utterances, lines, deep = memory.shape
    columns = width // data
    copies = 2 * Scatter.copies(n) + 2 * (data - 1) + nx + (nx - 1) + (model - 1)
    vmem = pl.BlockSpec(memory_space=pltpu.VMEM)
    smem = pl.BlockSpec(memory_space=pltpu.SMEM)
    hbm = pl.BlockSpec(memory_space=pl.ANY)
    half = lambda *shape: pltpu.VMEM(shape, BF)
    return pl.pallas_call(
        functools.partial(self_back_kernel, n),
        out_shape=[
            jax.ShapeDtypeStruct((4, rows, wide), F32),
            jax.ShapeDtypeStruct((4, rows, wide), F32),
            jax.ShapeDtypeStruct((data, lines, deep), BF),
            jax.ShapeDtypeStruct((data, lines, deep), BF),
            jax.ShapeDtypeStruct((params.shape[0], columns), F32),
        ],
        in_specs=[smem, hbm, vmem] + [hbm] * 5 + [vmem, hbm, vmem, vmem, hbm, hbm, vmem],
        out_specs=[vmem, vmem, hbm, hbm, vmem],
        scratch_shapes=[
            half(chip_rows, width),
            half(4, width, local),
            half(chip_rows, local),
            half(slot, local),
            half(slot, local),
            half(chip_rows, local),
            half(slot, width),
            half(chip_rows, local),
            half(chip_rows, local),
            half(slot, local),
            half(slot, local),
            half(2, slot, chip_rows),
            half(4, width, local),
            half(4, width, local),
            half(slot, width),
            half(nx, own, width),
            half(nx - 1, own, width),
            half(nx - 1, own, width),
            half(own, width),
            pltpu.VMEM((2, data, params.shape[0], columns), F32),
            pltpu.VMEM((model - 1, data, params.shape[0], columns), F32),
            pltpu.VMEM((data - 1, params.shape[0], columns), F32),
        ]
        + Scatter.scratch(n, rows, wide)
        + Scatter.scratch(n, rows, wide)
        + [
            pltpu.SemaphoreType.DMA((copies,)),
            pltpu.SemaphoreType.DMA((copies,)),
            pltpu.SemaphoreType.DMA((data,)),
            pltpu.SemaphoreType.DMA((data,)),
            pltpu.SemaphoreType.DMA((12,)),
        ],
        compiler_params=pltpu.CompilerParams(
            collective_id=1, has_side_effects=True, vmem_limit_bytes=58 * 2**20
        ),
        name="self_back",
    )(
        length, rows_grad, resid_grad, maps, queries, keys, values, mixed, logsum, normed, inputs,
        params, cross_grads, memory, norm_part,
    )


def square_sum_kernel(n, g_ref, o_ref, near_ref, sum_ref, far_ref, send_sem, recv_sem):
    wires = Wires(n, grid_place(), send_sem, recv_sem)
    wires.greet(dp_shifts(n) + mp_shifts(n))
    copies = [wires.send(g_ref, near_ref.at[i], **shift) for i, shift in enumerate(mp_shifts(n))]
    total = g_ref[...]
    for i, copy in enumerate(copies):
        copy.wait_recv()
        total = total + near_ref[i]
    sum_ref[...] = total
    copies = [wires.send(sum_ref, far_ref.at[i], **shift) for i, shift in enumerate(dp_shifts(n))]
    for i, copy in enumerate(copies):
        copy.wait_recv()
        total = total + far_ref[i]
    o_ref[...] = total
    wires.close()


def square_sum(partial):
    n = grid_sizes()
    data = n["z"] * n["y"]
    model = 2 * n["x"]
    vmem = pl.BlockSpec(memory_space=pltpu.VMEM)
    copies = data - 1 + model - 1
    return pl.pallas_call(
        functools.partial(square_sum_kernel, n),
        out_shape=jax.ShapeDtypeStruct(partial.shape, F32),
        in_specs=[vmem],
        out_specs=vmem,
        scratch_shapes=[
            pltpu.VMEM((model - 1,) + partial.shape, F32),
            pltpu.VMEM(partial.shape, F32),
            pltpu.VMEM((data - 1,) + partial.shape, F32),
            pltpu.SemaphoreType.DMA((copies,)),
            pltpu.SemaphoreType.DMA((copies,)),
        ],
        compiler_params=pltpu.CompilerParams(collective_id=2, has_side_effects=True),
        name="square_sum",
    )(partial)


def adam_step(weight, moment, square, gradient, step_rate, weight_decay):
    moment_new = BETA_FIRST * moment + (1.0 - BETA_FIRST) * gradient
    square_new = BETA_SECOND * square + (1.0 - BETA_SECOND) * gradient * gradient
    moment_hat = moment_new / (1.0 - BETA_FIRST**STEP)
    square_hat = square_new / (1.0 - BETA_SECOND**STEP)
    updated = weight - step_rate * (
        moment_hat / (jnp.sqrt(square_hat) + ADAM_EPSILON) + weight_decay * weight
    )
    return (updated, moment_new, square_new)


def per_device(
    states,
    memory,
    cotangent,
    lengths,
    memory_lengths,
    regroup_order,
    attn_weights,
    ffn_weights,
    norm_params,
    attn_mean,
    ffn_mean,
    norm_mean,
    attn_square,
    ffn_square,
    norm_square,
    attn_average,
    ffn_average,
    norm_average,
):
    n = grid_sizes()
    at = grid_place()
    nz, ny, nx = n["z"], n["y"], n["x"]
    data_index = lax.axis_index("dp")
    model_index = lax.axis_index("mp")
    data_size = lax.axis_size("dp")
    width = states.shape[2] * lax.axis_size("mp")
    slot = states.shape[1] * data_size
    own_rows = cotangent.shape[1]
    chip_rows = 2 * own_rows
    chip_start = at["x"] * chip_rows

    attn_low = attn_weights.astype(BF)
    ffn_low = ffn_weights.astype(BF)

    weights_self, norm_values, inputs, frames = entry(
        attn_low[0:4],
        norm_params.astype(BF).astype(F32),
        jnp.take(states, regroup_order, axis=0),
        jnp.take(memory, regroup_order, axis=0),
    )
    norm_values = jnp.swapaxes(norm_values, 0, 1).reshape(norm_params.shape[0], width)
    length = lengths[regroup_order[data_index]]
    reach = memory_lengths[regroup_order[data_index]]

    (
        weights_cross,
        ffn_maps,
        normed_first,
        query_self,
        key_self,
        value_self,
        mixed_self,
        logsum_self,
        resid_one_own,
        normed_second,
        query_cross,
        key_cross,
        value_cross,
        mixed_cross,
        logsum_cross,
        resid_two_own,
        normed_third,
    ) = forward(
        length[None],
        reach[None],
        inputs,
        frames,
        weights_self,
        norm_values,
        attn_low[4:8],
        ffn_low,
        own_rows,
    )
    layer_output, grad_two, cross_rows, ffn_grads, norm_ffn = feed_forward(
        length[None], normed_third, resid_two_own, ffn_maps, cotangent[0], norm_values
    )
    ffn_shard, cross_grads, grad_one, self_rows, memory_part, norm_cross = cross_back(
        reach[None],
        cross_rows,
        grad_two,
        weights_cross,
        (query_cross, key_cross, value_cross, mixed_cross, logsum_cross),
        normed_second,
        frames,
        resid_one_own,
        norm_values,
        ffn_grads,
    )
    shard_cross, shard_self, back_states, back_memory, norm_shard = self_back(
        length[None],
        self_rows,
        grad_one,
        weights_self,
        (query_self, key_self, value_self, mixed_self, logsum_self),
        normed_first,
        lax.dynamic_slice_in_dim(inputs, model_index * own_rows, own_rows, 0),
        norm_values,
        cross_grads,
        memory_part.reshape(data_size, -1, memory_part.shape[1]),
        norm_ffn + norm_cross,
    )
    attn_shard = jnp.concatenate([shard_self, shard_cross], axis=0)

    inverse = jnp.argsort(regroup_order)
    states_grad = jnp.take(back_states, inverse, axis=0).astype(F32)
    memory_grad = jnp.take(back_memory, inverse, axis=0).astype(F32)
    def squares(value):
        return jnp.sum((value * value).reshape(-1, 8, 128), axis=0)

    norm_squares = jnp.sum(norm_shard * norm_shard) / lax.axis_size("mp")
    local_squares = squares(attn_shard) + squares(ffn_shard) + norm_squares / 1024.0
    grad_norm = jnp.sqrt(jnp.sum(square_sum(local_squares)))
    clip_scale = jnp.minimum(1.0, THRESHOLD / (grad_norm + 1e-06))
    attn_updated, mean_attn, square_attn = adam_step(
        attn_weights, attn_mean, attn_square, clip_scale * attn_shard, MATRIX_RATE, MATRIX_DECAY
    )
    ffn_updated, mean_ffn, square_ffn = adam_step(
        ffn_weights, ffn_mean, ffn_square, clip_scale * ffn_shard, MATRIX_RATE, MATRIX_DECAY
    )
    norm_updated, mean_norm, square_norm = adam_step(
        norm_params, norm_mean, norm_square, clip_scale * norm_shard, NORM_RATE, 0.0
    )
    average_attn = AVERAGING * attn_average + (1.0 - AVERAGING) * attn_updated
    average_ffn = AVERAGING * ffn_average + (1.0 - AVERAGING) * ffn_updated
    average_norm = AVERAGING * norm_average + (1.0 - AVERAGING) * norm_updated
    return (
        layer_output[None],
        states_grad,
        memory_grad,
        attn_updated,
        ffn_updated,
        norm_updated,
        mean_attn,
        mean_ffn,
        mean_norm,
        square_attn,
        square_ffn,
        square_norm,
        average_attn,
        average_ffn,
        average_norm,
        grad_norm,
    )


def solution(mesh):
    rows = P(None, "dp", "mp")
    line = P(None, "dp")
    return jax.shard_map(
        per_device,
        mesh=mesh,
        in_specs=(rows, rows, P("dp", "mp", None), P(), P(), P())
        + (rows, rows, line) * 4,
        out_specs=(P("dp", "mp", None), rows, rows) + (rows, rows, line) * 4 + (P(),),
        check_vma=False,
    )
```

```python
import functools

import jax
import jax.numpy as jnp
from jax import lax
from jax.experimental import pallas as pl
from jax.experimental.pallas import tpu as pltpu
from jax.sharding import PartitionSpec as P

HD = 64
STEP = 10


EPSILON = 1e-05
NEGATIVE = -1000000000.0
BETA_FIRST = 0.9
BETA_SECOND = 0.999
ADAM_EPSILON = 1e-08
MATRIX_RATE = 0.05
NORM_RATE = 1.0
MATRIX_DECAY = 0.1
AVERAGING = 0.7
THRESHOLD = 1.0
BF = jnp.bfloat16
F32 = jnp.float32


(
    CROSS, DOWN, FIRST, GRAD, HOME, INPUT, KEYS, LOAD, MEMORY, OUT, QUERY, ROWS, SECOND, SELF, STATES, THIRD, UP,
) = range(1000, 18000, 1000)
(
    ALONG, BEGIN, END, FAN, GO, HEADS, LINE, MIDDLE, NORM, ON, OTHER, OUTPUT, PART, PASS, QUERIES, TURN, TWIN,
) = range(10, 180, 10)


def grid_sizes():
    dp = lax.axis_size("dp")
    mp = lax.axis_size("mp")
    ny = 1 << ((dp.bit_length() - 1) // 2)
    return {"z": dp // ny, "y": ny, "x": mp // 2, "c": 2}


def grid_place():
    n = grid_sizes()
    dp = lax.axis_index("dp")
    mp = lax.axis_index("mp")
    return {"z": dp // n["y"], "y": dp % n["y"], "x": mp // 2, "c": mp % 2}


def dot(left, right, left_dim, right_dim):
    return lax.dot_general(
        left, right, (((left_dim,), (right_dim,)), ((), ())), preferred_element_type=F32
    )


PAIR = 2 * HD


def only_head(value, head):
    lane = lax.broadcasted_iota(jnp.int32, value.shape, 1)
    keep = (lane < HD) if head == 0 else (lane >= HD)
    return jnp.where(keep, value, jnp.zeros_like(value))


def attend_pair(p, chunk, bound, q_ref, k_ref, v_ref, o_ref, sum_ref, score_ref, weight_ref):
    lanes = pl.ds(pl.multiple_of(p * PAIR, PAIR), PAIR)
    keys = k_ref.shape[0]
    queries = q_ref[:, lanes] * BF(HD**-0.5)
    values = v_ref[:, lanes]
    mixed = []
    for head in range(2):
        masked = only_head(queries, head)
        top = None
        for start in range(0, keys, chunk):
            block = slice(start, start + chunk)
            scores = dot(k_ref[block, lanes], masked, 1, 1)
            position = lax.broadcasted_iota(jnp.int32, scores.shape, 0) + start
            scores = jnp.where(position < bound, scores, NEGATIVE)
            score_ref[head, block, :] = scores
            highest = jnp.max(scores, axis=0, keepdims=True)
            top = highest if top is None else jnp.maximum(top, highest)
        total = None
        for start in range(0, keys, chunk):
            block = slice(start, start + chunk)
            raised = jnp.exp(score_ref[head, block, :] - top)
            part = jnp.sum(raised, axis=0, keepdims=True)
            total = part if total is None else total + part
            weight_ref[head, block, :] = raised.astype(BF)
        out = dot(values, weight_ref[head], 0, 0)[head * HD : (head + 1) * HD]
        mixed.append(out * (1.0 / total))
        sum_ref[p, head : head + 1, :] = top + jnp.log(total)
    o_ref[:, lanes] = jnp.concatenate(mixed, axis=0).T.astype(BF)


def attend_pair_back(
    p, chunk, bound, q_ref, k_ref, v_ref, o_ref, sum_ref, g_ref, dq_ref, dk_ref, dv_ref, ds_ref
):
    lanes = pl.ds(pl.multiple_of(p * PAIR, PAIR), PAIR)
    keys = k_ref.shape[0]
    queries = q_ref[:, lanes] * BF(HD**-0.5)
    grads = g_ref[:, lanes]
    product = (grads.astype(F32) * o_ref[:, lanes].astype(F32)).T
    head_q = [only_head(queries, head) for head in range(2)]
    head_g = [only_head(grads, head) for head in range(2)]
    shift = [
        jnp.sum(product[head * HD : (head + 1) * HD], axis=0, keepdims=True) for head in range(2)
    ]
    for start in range(0, keys, chunk):
        block = slice(start, start + chunk)
        key_block, value_block = k_ref[block, lanes], v_ref[block, lanes]
        grad_value, grad_key = 0.0, 0.0
        for head in range(2):
            scores = dot(key_block, head_q[head], 1, 1)
            position = lax.broadcasted_iota(jnp.int32, scores.shape, 0) + start
            scores = jnp.where(position < bound, scores, NEGATIVE)
            weights = jnp.exp(scores - sum_ref[p, head : head + 1, :])
            grad_weights = dot(value_block, head_g[head], 1, 1)
            grad_scores = (weights * (grad_weights - shift[head])).astype(BF)
            ds_ref[head, block, :] = grad_scores
            grad_value = grad_value + dot(weights.astype(BF), head_g[head], 1, 0)
            grad_key = grad_key + dot(grad_scores, head_q[head], 1, 0)
        dv_ref[block, lanes] = grad_value.astype(BF)
        dk_ref[block, lanes] = grad_key.astype(BF)
    key_all = k_ref[:, lanes]
    parts = [dot(key_all, ds_ref[h], 0, 0)[h * HD : (h + 1) * HD] for h in range(2)]
    dq_ref[:, lanes] = (jnp.concatenate(parts, axis=0).T * HD**-0.5).astype(BF)


def flipped(index, mask):
    bit = 1
    result = index
    while bit <= mask:
        if mask & bit:
            result = result + bit * (1 - 2 * ((index // bit) % 2))
        bit *= 2
    return result


class Wires:
    def __init__(self, sizes, place, send_sem, recv_sem):
        self.sizes, self.place = sizes, place
        self.send_sem, self.recv_sem = send_sem, recv_sem
        self.count = 0
        self.started = []
        self.maybe = []

    def peer(self, z=0, y=0, x=0, c=0, flip=0):
        n, at = self.sizes, self.place
        pz, py = (at["z"] + z) % n["z"], (at["y"] + y) % n["y"]
        if flip:
            pz = flipped(at["z"], flip)
        px, pc = (at["x"] + x) % n["x"], (at["c"] + c) % 2
        return (pz * n["y"] + py, px * 2 + pc)

    def send(self, src, dst, **shift):
        copy = pltpu.make_async_remote_copy(
            src_ref=src,
            dst_ref=dst,
            send_sem=self.send_sem.at[self.count],
            recv_sem=self.recv_sem.at[self.count],
            device_id=self.peer(**shift),
            device_id_type=pl.DeviceIdType.MESH,
        )
        self.count += 1
        copy.start()
        self.started.append(copy)
        return copy

    def send_if(self, condition, src, dst, recv_sem, **shift):
        copy = pltpu.make_async_remote_copy(
            src_ref=src,
            dst_ref=dst,
            send_sem=self.send_sem.at[self.count],
            recv_sem=recv_sem,
            device_id=self.peer(**shift),
            device_id_type=pl.DeviceIdType.MESH,
        )
        self.count += 1
        pl.when(condition)(copy.start)
        self.maybe.append((condition, copy))

    def greet(self, shifts):
        barrier = pltpu.get_barrier_semaphore()
        for shift in shifts:
            pl.semaphore_signal(
                barrier, inc=1, device_id=self.peer(**shift), device_id_type=pl.DeviceIdType.MESH
            )
        pl.semaphore_wait(barrier, len(shifts))

    def close(self):
        for copy in self.started:
            copy.wait_send()
        for condition, copy in self.maybe:
            pl.when(condition)(copy.wait_send)


def dp_shifts(n):
    return [{"z": z, "y": y} for z in range(n["z"]) for y in range(n["y"]) if z or y]


def mp_shifts(n):
    return [{"x": x, "c": c} for x in range(n["x"]) for c in range(2) if x or c]


def loop_rows(total, step, body):
    def one(i, carry):
        body(pl.ds(pl.multiple_of(i * step, step), step))
        return carry

    lax.fori_loop(0, total // step, one, 0)


def shifted(rows, offset):
    return pl.ds(pl.multiple_of(rows.start + offset, rows.size), rows.size)


def mat_rows(out_ref, left_ref, right_ref, total, step, offset=0):
    def body(rows):
        left = left_ref[shifted(rows, offset), :]
        out_ref[rows, :] = dot(left, right_ref[...], 1, 0).astype(BF)

    loop_rows(total, step, body)


class Moves:
    def __init__(self, sem):
        self.sem = sem
        self.count = 0
        self.open = []

    def start(self, src, dst):
        copy = pltpu.make_async_copy(src, dst, self.sem.at[self.count])
        self.count += 1
        copy.start()
        return copy

    def store(self, src, dst):
        self.open.append(self.start(src, dst))

    def close(self):
        for copy in self.open:
            copy.wait()


class Line:
    def __init__(self, wires, spot, sem):
        self.wires, self.spot, self.sem = wires, spot, sem
        self.nz, self.z = wires.sizes["z"], wires.place["z"]

    def start(self, src):
        z, nz = self.z, self.nz
        if nz > 1:
            self.wires.send_if(z < nz - 1, src, self.spot(z), self.sem.at[1], z=1)
            self.wires.send_if(z > 0, src, self.spot(z), self.sem.at[nz - 1], z=nz - 1)

    def step_back(self, k):
        total = 0
        for i in range(self.nz):
            order = sorted(range(1, self.nz), key=lambda s: s if s <= i else self.nz - s)
            total = total + jnp.where(self.z == i, order[k - 1], 0)
        return total

    def arrive(self, k):
        z, nz = self.z, self.nz
        s = self.step_back(k)
        source = (z + nz - s) % nz
        spot = self.spot(source)
        pltpu.make_async_copy(spot, spot, self.sem.at[s]).wait()
        below = s <= z
        above = s > z
        self.wires.send_if(
            jnp.logical_and(below, z < nz - 1), spot, spot, self.sem.at[(s + 1) % nz], z=1
        )
        self.wires.send_if(
            jnp.logical_and(above, z > 0), spot, spot, self.sem.at[s - 1], z=nz - 1
        )
        return source

    @staticmethod
    def copies(nz):
        return 2 + 2 * (nz - 1)


class Gather:
    def __init__(self, wires, src, out, cut, sem):
        self.wires, self.src, self.out, self.cut = wires, src, out, cut
        self.n, self.at = wires.sizes, wires.place
        self.line = Line(wires, lambda i: self.spot(i, 0, 0), sem)
        self.source, self.to_y, self.to_x = {0: self.at["z"]}, {}, {}
        self.last = []

    def spot(self, chip_z, sy, sx, mats=slice(None)):
        rows, wide = self.src.shape[1], self.src.shape[2]
        n, at = self.n, self.at
        block = chip_z * n["y"] + (at["y"] + n["y"] - sy) % n["y"]
        column = (at["x"] + n["x"] - sx) % n["x"]
        return self.out.at[
            mats,
            pl.ds(pl.multiple_of(block * rows, rows), rows),
            pl.ds(pl.multiple_of(column * wide, wide), wide),
        ]

    def fan(self, k, src=None):
        spot = self.spot(self.source[k], 0, 0)
        src = spot if src is None else src
        for s in range(1, self.n["y"]):
            self.to_y[k, s] = self.wires.send(src, spot, y=s)
        for s in range(1, self.n["x"]):
            self.to_x[k, s] = self.wires.send(src, spot, x=s)

    def begin(self):
        self.line.start(self.src)
        self.fan(0, self.src)

    def arrive(self, k):
        self.source[k] = self.line.arrive(k)
        self.fan(k)

    def corner(self, k):
        count = self.src.shape[0]
        for sy in range(1, self.n["y"]):
            self.to_y[k, sy].wait_recv()
            part = self.spot(self.source[k], sy, 0, slice(0, self.cut))
            for s in range(1, self.n["x"]):
                self.last.append(self.wires.send(part, part, x=s))
        for sx in range(1, self.n["x"]):
            self.to_x[k, sx].wait_recv()
            if self.cut < count:
                part = self.spot(self.source[k], 0, sx, slice(self.cut, count))
                for s in range(1, self.n["y"]):
                    self.last.append(self.wires.send(part, part, y=s))

    def finish(self):
        for copy in self.last:
            copy.wait_recv()

    @staticmethod
    def copies(n):
        nz, ny, nx = n["z"], n["y"], n["x"]
        return Line.copies(nz) + nz * (ny - 1 + nx - 1) + 2 * nz * (ny - 1) * (nx - 1)


class RowGather:
    def __init__(self, wires, src, out, z_first, sem):
        self.wires, self.src, self.out, self.z_first = wires, src, out, z_first
        self.n, self.at = wires.sizes, wires.place
        spot = (lambda i: self.spot(i, 0)) if z_first else self.band
        self.line = Line(wires, spot, sem)
        self.to_y = []

    def spot(self, chip_z, sy):
        rows, ny = self.src.shape[0], self.n["y"]
        block = chip_z * ny + (self.at["y"] + ny - sy) % ny
        return self.out.at[pl.ds(pl.multiple_of(block * rows, rows), rows)]

    def band(self, chip_z):
        rows = self.src.shape[0] * self.n["y"]
        return self.out.at[pl.ds(pl.multiple_of(chip_z * rows, rows), rows)]

    def across(self, source, src=None):
        spot = self.spot(source, 0)
        src = spot if src is None else src
        for s in range(1, self.n["y"]):
            self.to_y.append(self.wires.send(src, spot, y=s))

    def begin(self):
        if self.z_first:
            self.line.start(self.src)
        self.across(self.at["z"], self.src)

    def turn(self):
        for copy in self.to_y:
            copy.wait_recv()
        self.line.start(self.band(self.at["z"]))

    def arrive(self, k):
        source = self.line.arrive(k)
        if self.z_first:
            self.across(source)

    def finish(self):
        if self.z_first:
            for copy in self.to_y:
                copy.wait_recv()

    @staticmethod
    def copies(n):
        return Line.copies(n["z"]) + n["z"] * (n["y"] - 1)


def norm_rows(values, p_ref, index):
    centered = values - jnp.mean(values, axis=-1, keepdims=True)
    variance = jnp.mean(centered * centered, axis=-1, keepdims=True)
    normed = centered * lax.rsqrt(variance + EPSILON)
    return (normed * p_ref[index : index + 1, :] + p_ref[index + 4 : index + 5, :]).astype(BF)


STRIP = 256


FORWARD_PLAN = (
    CROSS + FAN, SELF + FAN, SELF + LINE, SELF + PASS + 1, SELF + PASS + 2, CROSS + TURN + 0,
    STATES + GO, CROSS + LINE, SELF + PASS + 3, DOWN + BEGIN, MEMORY + GO, SELF + TURN + 0,
    CROSS + PASS + 1, SELF + TURN + 1, SELF + TURN + 3, STATES + ON, SELF + TURN + 2, UP + BEGIN,
    DOWN + LINE, STATES + TWIN, MEMORY + ON, STATES + END, CROSS + PASS + 2, DOWN + PASS + 1,
    FIRST + NORM, SELF + END, SELF + HEADS, CROSS + PASS + 3, SELF + TWIN + 0, CROSS + TURN + 1,
    SELF + TWIN + 1, MEMORY + TWIN, SELF + TWIN + 2, CROSS + TURN + 2, DOWN + PASS + 2,
    SELF + TWIN + 3, MEMORY + END, CROSS + TURN + 3, SELF + OUTPUT, UP + PASS + 1, UP + PASS + 2,
    SECOND + NORM, CROSS + END, MEMORY + HEADS, CROSS + QUERIES, CROSS + TWIN + 0,
    CROSS + TWIN + 1, UP + PASS + 3, CROSS + TWIN + 2, CROSS + TWIN + 3, CROSS + OUTPUT,
    DOWN + PASS + 3, UP + END, DOWN + END, THIRD + NORM,
)


def forward_plan(nz, pairs):
    if nz == 4 and pairs == 4:
        return FORWARD_PLAN
    passes = lambda group: [group + PASS + k for k in range(1, nz)]
    turns = lambda group: [group + TURN + k for k in range(nz)]
    plan = [STATES + GO, SELF + LINE, SELF + FAN, CROSS + LINE, CROSS + FAN, MEMORY + GO]
    plan += [STATES + ON, STATES + TWIN, STATES + END, FIRST + NORM]
    plan += passes(SELF) + turns(SELF) + [MEMORY + ON, MEMORY + TWIN, SELF + END]
    plan += [SELF + HEADS] + [SELF + TWIN + p for p in range(pairs)] + [SELF + OUTPUT]
    plan += [UP + BEGIN, DOWN + BEGIN] + passes(CROSS) + turns(CROSS) + passes(UP)
    plan += [SECOND + NORM, MEMORY + END, CROSS + END, DOWN + LINE, MEMORY + HEADS]
    plan += [CROSS + QUERIES] + [CROSS + TWIN + p for p in range(pairs)] + [CROSS + OUTPUT]
    return tuple(plan + passes(DOWN) + [THIRD + NORM, UP + END, DOWN + END])


def forward_kernel(
    n, own_rows, order, lengths, reaches, st_ref, me_ref, pr_ref, wa_ref, wf_ref,
    ows, owc, owf, op_ref, ofr, oin, oh1, oq, ok, ov, oo, ol, ox1, oh2, oq2, ok2, ov2, oo2, ol2,
    ox2, oh3,
    stage_s, pin_s, pall_s, p_s, wl_s, fl_s,
    x_s, m_s, w_s, c_s, h1_s, q_s, k_s, v_s, o_s, l_s, x1_s, h2_s, q2_s, k2_s, v2_s, o2_s, l2_s,
    x2_s, h3_s, give_s, got_s, score_s, weight_s,
    send_sem, recv_sem, self_sem, cross_sem, up_sem, down_sem, move_sem,
):
    at = grid_place()
    z, y, x, c = at["z"], at["y"], at["x"], at["c"]
    nz, ny, nx = n["z"], n["y"], n["x"]
    data, model = z * ny + y, x * 2 + c
    wires = Wires(n, at, send_sem, recv_sem)
    moves = Moves(move_sem)
    utterances, lines, deep = st_ref.shape
    mats = w_s.shape[0]
    for r in range(utterances):
        stage_s[0, r] = st_ref[order[r]]
        stage_s[1, r] = me_ref[order[r]]
    wl_s[...] = wa_ref[...].astype(BF)
    fl_s[...] = wf_ref[...].astype(BF)
    pin_s[...] = pr_ref[...].astype(BF).astype(F32)
    wires.greet(dp_shifts(n) + [{"x": s} for s in range(1, nx)] + [{"c": 1}])

    def patch(ref):
        return ref.at[
            pl.ds(pl.multiple_of(data * lines, lines), lines),
            pl.ds(pl.multiple_of(model * deep, deep), deep),
        ]

    def column(ref, sx, sc):
        index = ((x + nx - sx) % nx) * 2 + (c + 2 - sc) % 2
        return ref.at[:, pl.ds(pl.multiple_of(index * deep, deep), deep)]

    def spread(i, out):
        copies = []
        for shift in dp_shifts(n):
            target = wires.peer(**shift)[0]
            copies.append(wires.send(stage_s.at[i, target], patch(out), **shift))
        return copies, moves.start(stage_s.at[i, data], patch(out))

    def forward_columns(out, spreading):
        copies, own = spreading
        own.wait()
        for copy in copies:
            copy.wait_recv()
        near = [wires.send(column(out, 0, 0), column(out, 0, 0), x=s) for s in range(1, nx)]
        return near, [wires.send(column(out, 0, 0), column(out, 0, 0), c=1)]

    def pair_columns(out, near, pair):
        for s in range(1, nx):
            near[s - 1].wait_recv()
            pair.append(wires.send(column(out, s, 0), column(out, s, 0), c=1))

    own_self = wl_s.at[0:mats]
    own_cross = wl_s.at[mats : 2 * mats]
    near_self = Gather(wires, own_self, w_s, mats // 2, self_sem)
    near_cross = Gather(wires, own_cross, c_s, mats // 2, cross_sem)
    up_gather = RowGather(wires, fl_s.at[0], owf.at[0], True, up_sem)
    down_gather = RowGather(wires, fl_s.at[1], owf.at[1], False, down_sem)
    here = [
        moves.start(own_self, near_self.spot(z, 0, 0)),
        moves.start(own_cross, near_cross.spot(z, 0, 0)),
        moves.start(pin_s, pall_s.at[data]),
    ]
    down_here = moves.start(fl_s.at[1], down_gather.spot(z, 0))
    up_here = moves.start(fl_s.at[0], up_gather.spot(z, 0))
    params = [wires.send(pin_s, pall_s.at[data], **shift) for shift in dp_shifts(n)]
    slot, width = x_s.shape
    chip_rows = 2 * own_rows
    chip_start = x * chip_rows
    strip = min(STRIP, own_rows)
    pairs = q_s.shape[1] // PAIR
    own = pl.ds(pl.multiple_of(c * own_rows, own_rows), own_rows)
    held = {}
    steps = {}

    def step(name):
        def keep(function):
            steps[name] = function
            return function

        return keep

    for name, i, ref in ((STATES, 0, x_s), (MEMORY, 1, m_s)):

        def go(name=name, i=i, ref=ref):
            held[name] = spread(i, ref)

        def on(name=name, ref=ref):
            held[name] = forward_columns(ref, held[name])

        def pair(name=name, ref=ref):
            pair_columns(ref, *held[name])

        def end(name=name):
            for copy in held[name][1]:
                copy.wait_recv()

        steps.update(
            {name + GO: go, name + ON: on, name + TWIN: pair, name + END: end}
        )
    for name, gather in ((SELF, near_self), (CROSS, near_cross)):
        steps[name + LINE] = functools.partial(gather.line.start, gather.src)
        steps[name + FAN] = functools.partial(gather.fan, 0, gather.src)
        for k in range(nz):
            steps[name + PASS + k] = functools.partial(gather.arrive, k)
            steps[name + TURN + k] = functools.partial(gather.corner, k)
    for name, gather in ((UP, up_gather), (DOWN, down_gather)):
        steps[name + BEGIN] = gather.begin
        steps[name + END] = gather.finish
        for k in range(1, nz):
            steps[name + PASS + k] = functools.partial(gather.arrive, k)

    @step(DOWN + LINE)
    def _():
        down_here.wait()
        down_gather.turn()

    @step(SELF + END)
    def _():
        for copy in here[:1]:
            copy.wait()
        near_self.finish()
        moves.store(w_s, ows)

    @step(CROSS + END)
    def _():
        here[1].wait()
        near_cross.finish()
        moves.store(c_s, owc)

    @step(FIRST + NORM)
    def _():
        for copy in params:
            copy.wait_recv()
        here[2].wait()
        for i in range(nz * ny):
            columns = pall_s.shape[2]
            p_s[:, i * columns : (i + 1) * columns] = pall_s[i]
        op_ref[...] = p_s[...]

        def first_norm(rows):
            h1_s[rows, :] = norm_rows(x_s[rows, :].astype(F32), p_s, 0)

        loop_rows(slot, strip, first_norm)
        moves.store(h1_s, oh1)
        moves.store(x_s.at[pl.ds(pl.multiple_of(model * own_rows, own_rows), own_rows)], oin)

    @step(SELF + HEADS)
    def _():
        mat_rows(q_s, h1_s, w_s.at[0], chip_rows, strip, chip_start)
        mat_rows(k_s, h1_s, w_s.at[1], slot, strip)
        mat_rows(v_s, h1_s, w_s.at[2], slot, strip)
        for ref, out in ((q_s, oq), (k_s, ok), (v_s, ov)):
            moves.store(ref, out)

    @step(MEMORY + HEADS)
    def _():
        mat_rows(k2_s, m_s, c_s.at[1], slot, strip)
        mat_rows(v2_s, m_s, c_s.at[2], slot, strip)
        for ref, out in ((k2_s, ok2), (v2_s, ov2), (m_s, ofr)):
            moves.store(ref, out)

    @step(CROSS + QUERIES)
    def _():
        mat_rows(q2_s, h2_s, c_s.at[0], chip_rows, strip)
        moves.store(q2_s, oq2)

    reach_self = lax.broadcasted_iota(jnp.int32, (1, chip_rows), 1) + chip_start + 1
    reach_self = jnp.minimum(reach_self, lengths[order[data]])
    reach_cross = jnp.full((1, chip_rows), reaches[order[data]], jnp.int32)
    for p in range(pairs):

        def self_pair(p=p):
            attend_pair(p, 256, reach_self, q_s, k_s, v_s, o_s, l_s, score_s, weight_s)

        def cross_pair(p=p):
            attend_pair(p, 256, reach_cross, q2_s, k2_s, v2_s, o2_s, l2_s, score_s, weight_s)

        steps[SELF + TWIN + p] = self_pair
        steps[CROSS + TWIN + p] = cross_pair

    def give(index, mixed, out_map):
        def body(rows):
            give_s[index, rows, :] = dot(mixed[rows, :], out_map[...], 1, 1).astype(BF)

        loop_rows(chip_rows, strip, body)
        held[index] = wires.send(give_s.at[index], got_s.at[index], c=1)

    def total(index, rows):
        return give_s[index, rows, :].astype(F32) + got_s[index, rows, :].astype(F32)

    @step(SELF + OUTPUT)
    def _():
        moves.store(o_s, oo)
        moves.store(l_s, ol)
        give(0, o_s, w_s.at[3])

    @step(CROSS + OUTPUT)
    def _():
        moves.store(o2_s, oo2)
        moves.store(l2_s, ol2)
        give(1, o2_s, c_s.at[3])

    @step(SECOND + NORM)
    def _():
        held[0].wait_recv()

        def second_norm(rows):
            values = x_s[shifted(rows, chip_start), :].astype(F32) + total(0, rows)
            x1_s[rows, :] = values
            h2_s[rows, :] = norm_rows(values, p_s, 1)

        loop_rows(chip_rows, strip, second_norm)
        moves.store(x1_s.at[own], ox1)
        moves.store(h2_s, oh2)

    @step(THIRD + NORM)
    def _():
        held[1].wait_recv()

        def third_norm(rows):
            values = x1_s[rows, :] + total(1, rows)
            x2_s[rows, :] = values
            h3_s[rows, :] = norm_rows(values, p_s, 2)

        loop_rows(chip_rows, strip, third_norm)
        moves.store(x2_s.at[own], ox2)
        moves.store(h3_s, oh3)

    for name in forward_plan(nz, pairs):
        steps[name]()
    up_here.wait()
    moves.close()
    wires.close()


def forward(order, lengths, reaches, states, memory, params, attn, ffn, own_rows):
    n = grid_sizes()
    nz, ny, nx = n["z"], n["y"], n["x"]
    data = nz * ny
    utterances, lines, deep = states.shape
    slot, width = lines * data, deep * 2 * nx
    mats = attn.shape[0] // 2
    local = attn.shape[2] * nx
    hidden = ffn.shape[2]
    chip_rows = 2 * own_rows
    pairs = local // PAIR
    copies = (
        2 * Gather.copies(n) + 2 * RowGather.copies(n) + 3 * (data - 1) + 2 * (2 * (nx - 1) + 1) + 2
    )
    vmem = pl.BlockSpec(memory_space=pltpu.VMEM)
    smem = pl.BlockSpec(memory_space=pltpu.SMEM)
    hbm = pl.BlockSpec(memory_space=pl.ANY)
    half = lambda *shape: (shape, BF)
    full = lambda *shape: (shape, F32)
    saved = [
        half(slot, width),
        half(chip_rows, local),
        half(slot, local),
        half(slot, local),
        half(chip_rows, local),
        full(pairs, 2, chip_rows),
        full(own_rows, width),
        half(chip_rows, width),
        half(chip_rows, local),
        half(slot, local),
        half(slot, local),
        half(chip_rows, local),
        full(pairs, 2, chip_rows),
        full(own_rows, width),
        half(chip_rows, width),
    ]
    outs = [
        half(mats, width, local),
        half(mats, width, local),
        half(2, width, hidden),
        full(params.shape[0], width),
        half(slot, width),
        half(own_rows, width),
    ] + saved
    scratch = [
        half(2, utterances, lines, deep),
        full(*params.shape),
        full(data, *params.shape),
        full(params.shape[0], width),
        half(*attn.shape),
        half(*ffn.shape),
        half(slot, width),
        half(slot, width),
        half(mats, width, local),
        half(mats, width, local),
        half(slot, width),
        half(chip_rows, local),
        half(slot, local),
        half(slot, local),
        half(chip_rows, local),
        full(pairs, 2, chip_rows),
        full(chip_rows, width),
        half(chip_rows, width),
        half(chip_rows, local),
        half(slot, local),
        half(slot, local),
        half(chip_rows, local),
        full(pairs, 2, chip_rows),
        full(chip_rows, width),
        half(chip_rows, width),
        half(2, chip_rows, width),
        half(2, chip_rows, width),
        full(2, slot, chip_rows),
        half(2, slot, chip_rows),
    ]
    return pl.pallas_call(
        functools.partial(forward_kernel, n, own_rows),
        out_shape=[jax.ShapeDtypeStruct(s, t) for s, t in outs],
        in_specs=[smem, smem, smem, vmem, vmem, vmem, vmem, vmem],
        out_specs=[hbm] * 3 + [vmem] + [hbm] * (len(outs) - 4),
        scratch_shapes=[pltpu.VMEM(s, t) for s, t in scratch]
        + [
            pltpu.SemaphoreType.DMA((copies,)),
            pltpu.SemaphoreType.DMA((copies,)),
        ]
        + [pltpu.SemaphoreType.DMA((nz,))] * 4
        + [pltpu.SemaphoreType.DMA((32,))],
        compiler_params=pltpu.CompilerParams(
            collective_id=3, has_side_effects=True, vmem_limit_bytes=56 * 2**20
        ),
        name="forward",
    )(order, lengths, reaches, states, memory, params, attn, ffn)


def norm_back_rows(values, grad, gain):
    centered = values - jnp.mean(values, axis=-1, keepdims=True)
    scale = lax.rsqrt(jnp.mean(centered * centered, axis=-1, keepdims=True) + EPSILON)
    normed = centered * scale
    up = grad * gain
    back = scale * (
        up
        - jnp.mean(up, axis=-1, keepdims=True)
        - normed * jnp.mean(up * normed, axis=-1, keepdims=True)
    )
    return back, normed


def row_sum(values):
    return jnp.sum(values, axis=0, keepdims=True)


SPLIT = 2


def ffn_kernel(
    n, order, lengths, h_hbm, x_ref, w_hbm, ct_ref, p_ref,
    oy_ref, odx_ref, odc, odw, on_ref,
    h_s, f_s, a_s, d_s, u_s, w_s, keep_s, far_s, give_s, got_s, cross_s, crossed_s, back_s, come_s,
    x3_s, dx3_s, dc_s, dw_s, send_sem, recv_sem, move_sem,
):
    at = grid_place()
    wires = Wires(n, at, send_sem, recv_sem)
    moves = Moves(move_sem)
    nx, c = n["x"], at["c"]
    length = lengths[order[at["z"] * n["y"] + at["y"]]]
    own, width = x_ref.shape
    part = own // SPLIT
    start_own = pl.multiple_of(c * own, own)
    start_other = pl.multiple_of((1 - c) * own, own)
    get_w = moves.start(w_hbm, w_s)
    get_own = moves.start(h_hbm.at[pl.ds(start_own, own)], h_s.at[pl.ds(0, own)])
    get_other = moves.start(h_hbm.at[pl.ds(start_other, own)], h_s.at[pl.ds(own, own)])
    wires.greet([{"x": s} for s in range(1, nx)] + [{"c": 1}])

    def far_at(t, k, j):
        return 2 * own + (((t - 1) * SPLIT + k) * 2 + j) * part

    def spread(src, dst, k):
        return [
            wires.send(src.at[pl.ds(k * part, part)], dst.at[pl.ds(far_at(t, k, 0), part)], x=t)
            for t in range(1, nx)
        ]

    def onward(dst, t, k):
        return wires.send(
            dst.at[pl.ds(far_at(t, k, 0), part)], dst.at[pl.ds(far_at(t, k, 1), part)], c=1
        )

    def up(rows):
        hidden = dot(h_s[rows, :], w_s[0], 1, 0)
        inner = 0.7978845608028654 * (hidden + 0.044715 * (hidden * hidden * hidden))
        bend = jnp.tanh(inner)
        a_s[rows, :] = (0.5 * hidden * (1.0 + bend)).astype(BF)
        slope = 0.7978845608028654 * (1.0 + 0.134145 * (hidden * hidden))
        d_s[rows, :] = 0.5 * (1.0 + bend) + 0.5 * hidden * (1.0 - bend * bend) * slope
        return dot(a_s[rows, :], w_s[1], 1, 1)

    def down(rows):
        grad = dot(f_s[rows, :], w_s[1], 1, 0)
        u_s[rows, :] = (grad * d_s[rows, :]).astype(BF)
        return dot(u_s[rows, :], w_s[0], 1, 1)

    def other_core(phase, work):
        give_s[phase] = work(slice(own, 2 * own)).astype(BF)
        return wires.send(give_s.at[phase], got_s.at[phase], c=1)

    def far_part(phase, work, t, k):
        sums = work(slice(far_at(t, k, 0), far_at(t, k, 0) + 2 * part))
        far_s[t - 1, k] = sums[:part]
        cross_s[phase, t - 1, k] = sums[part:].astype(BF)
        return wires.send(cross_s.at[phase, t - 1, k], crossed_s.at[phase, t - 1, k], c=1)

    def return_part(phase, t, k, crossing):
        crossing.wait_recv()
        back_s[phase, t - 1, k] = (far_s[t - 1, k] + crossed_s[phase, t - 1, k].astype(F32)).astype(
            BF
        )
        return wires.send(back_s.at[phase, t - 1, k], come_s.at[phase, t - 1, k], x=nx - t)

    def far_phase(phase, work, buffer, arriving):
        homing = {}
        for k in range(SPLIT):
            crossed = []
            for t in range(1, nx):
                arriving[k][t - 1].wait_recv()
                crossed.append(onward(buffer, t, k))
            crossing = []
            for t in range(1, nx):
                crossed[t - 1].wait_recv()
                crossing.append(far_part(phase, work, t, k))
            for t in range(1, nx):
                homing[k, t] = return_part(phase, t, k, crossing[t - 1])
        return homing

    def own_part(phase, k, homing):
        rows = slice(k * part, (k + 1) * part)
        total = keep_s[rows, :] + got_s[phase, rows, :].astype(F32)
        for t in range(1, nx):
            homing[k, t].wait_recv()
            total = total + come_s[phase, t - 1, k].astype(F32)
        return total

    get_own.wait()
    arriving = [spread(h_s, h_s, k) for k in range(SPLIT)]
    get_w.wait()
    get_other.wait()
    swap = other_core(0, up)
    keep_s[...] = up(slice(0, own))
    homing = far_phase(0, up, h_s, arriving)
    swap.wait_recv()
    gain_final, bias_final = 0.0, 0.0
    arriving, near = [], []
    first_row = (at["x"] * 2 + c) * own
    for k in range(SPLIT):
        rows = slice(k * part, (k + 1) * part)
        values = x_ref[rows, :] + own_part(0, k, homing)
        x3 = values
        centered = x3 - jnp.mean(x3, axis=-1, keepdims=True)
        variance = jnp.mean(centered * centered, axis=-1, keepdims=True)
        normed = centered * lax.rsqrt(variance + EPSILON)
        oy_ref[rows, :] = (normed * p_ref[3:4, :] + p_ref[7:8, :]).astype(BF)
        position = lax.broadcasted_iota(jnp.int32, (part, 1), 0) + (first_row + k * part)
        seed = jnp.where(position < length, ct_ref[rows, :].astype(F32), 0.0)
        grad, normed = norm_back_rows(x3, seed, p_ref[3:4, :])
        gain_final = gain_final + row_sum(seed * normed)
        bias_final = bias_final + row_sum(seed)
        dx3_s[rows, :] = grad
        f_s[rows, :] = grad.astype(BF)
        arriving.append(spread(f_s, f_s, k))
        near.append(
            wires.send(f_s.at[pl.ds(k * part, part)], f_s.at[pl.ds(own + k * part, part)], c=1)
        )
    keep_s[...] = down(slice(0, own))
    for copy in near:
        copy.wait_recv()
    swap = other_core(1, down)
    homing = far_phase(1, down, f_s, arriving)
    step = min(256, width)
    for i, (left, right) in ((1, (f_s, a_s)), (0, (h_s, u_s))):
        for col in range(0, width, step):
            cols = slice(col, col + step)
            dw_s[i, cols, :] = dot(left[:, cols], right[...], 0, 0).astype(BF)
        moves.store(dw_s.at[i], odw.at[i])
    swap.wait_recv()
    gain_third, bias_third = 0.0, 0.0
    near = []
    for k in range(SPLIT):
        rows = slice(k * part, (k + 1) * part)
        upstream = own_part(1, k, homing)
        grad, normed = norm_back_rows(x_ref[rows, :], upstream, p_ref[2:3, :])
        gain_third = gain_third + row_sum(upstream * normed)
        bias_third = bias_third + row_sum(upstream)
        total = dx3_s[rows, :] + grad
        odx_ref[rows, :] = total
        here = pl.ds(start_own + k * part, part)
        dc_s[here, :] = total.astype(BF)
        near.append(wires.send(dc_s.at[here], dc_s.at[here], c=1))
    line = lax.broadcasted_iota(jnp.int32, on_ref.shape, 0)
    sums = jnp.zeros(on_ref.shape, F32)
    for index, value in ((2, gain_third), (3, gain_final), (6, bias_third), (7, bias_final)):
        sums = sums + jnp.where(line == index, value, 0.0)
    on_ref[...] = sums
    for copy in near:
        copy.wait_recv()
    moves.store(dc_s, odc)
    moves.close()
    wires.close()


def feed_forward(order, lengths, normed, resid, maps, cotangent, params):
    n = grid_sizes()
    chip_rows, width = normed.shape
    own = chip_rows // 2
    hidden = maps.shape[2]
    nx = n["x"]
    rows = chip_rows * nx
    part = own // SPLIT
    copies = 2 * (SPLIT * (nx - 1) * 4 + 1) + 2 * SPLIT
    vmem = pl.BlockSpec(memory_space=pltpu.VMEM)
    smem = pl.BlockSpec(memory_space=pltpu.SMEM)
    hbm = pl.BlockSpec(memory_space=pl.ANY)
    far = (2, nx - 1, SPLIT, part, width)
    return pl.pallas_call(
        functools.partial(ffn_kernel, n),
        out_shape=[
            jax.ShapeDtypeStruct((own, width), BF),
            jax.ShapeDtypeStruct((own, width), F32),
            jax.ShapeDtypeStruct((chip_rows, width), BF),
            jax.ShapeDtypeStruct((2, width, hidden), BF),
            jax.ShapeDtypeStruct(params.shape, F32),
        ],
        in_specs=[smem, smem, hbm, vmem, hbm, vmem, vmem],
        out_specs=[vmem, vmem, hbm, hbm, vmem],
        scratch_shapes=[
            pltpu.VMEM((rows, width), BF),
            pltpu.VMEM((rows, width), BF),
            pltpu.VMEM((rows, hidden), BF),
            pltpu.VMEM((rows, hidden), F32),
            pltpu.VMEM((rows, hidden), BF),
            pltpu.VMEM((2, width, hidden), BF),
            pltpu.VMEM((own, width), F32),
            pltpu.VMEM((nx - 1, SPLIT, part, width), F32),
            pltpu.VMEM((2, own, width), BF),
            pltpu.VMEM((2, own, width), BF),
            pltpu.VMEM(far, BF),
            pltpu.VMEM(far, BF),
            pltpu.VMEM(far, BF),
            pltpu.VMEM(far, BF),
            pltpu.VMEM((own, width), F32),
            pltpu.VMEM((own, width), F32),
            pltpu.VMEM((chip_rows, width), BF),
            pltpu.VMEM((2, width, hidden), BF),
            pltpu.SemaphoreType.DMA((copies,)),
            pltpu.SemaphoreType.DMA((copies,)),
            pltpu.SemaphoreType.DMA((8,)),
        ],
        compiler_params=pltpu.CompilerParams(
            collective_id=4, has_side_effects=True, vmem_limit_bytes=56 * 2**20
        ),
        name="feed_forward",
    )(order, lengths, normed, resid, maps, cotangent, params)


CROSS_PLAN = (
    DOWN + BEGIN + 3, UP + BEGIN + 3, LOAD, DOWN + BEGIN + 2, GRAD + OUTPUT, DOWN + ALONG + 3,
    UP + BEGIN + 1, UP + BEGIN + 2, HEADS, TWIN + 0, OUT + BEGIN + 2, OUT + BEGIN + 3,
    OUT + BEGIN + 0, UP + ALONG + 3, TWIN + 1, TWIN + 2, DOWN + ALONG + 2, TWIN + 3,
    GRAD + QUERIES, QUERY + BEGIN + 3, UP + ALONG + 1, OUT + MIDDLE + 3, QUERY + BEGIN + 2,
    QUERY + BEGIN + 1, DOWN + BEGIN + 1, GRAD + TWIN, QUERY + MIDDLE + 2, QUERY + BEGIN + 0,
    INPUT + PART, QUERY + MIDDLE + 1, UP + BEGIN + 0, OUT + BEGIN + 1, UP + ALONG + 2,
    DOWN + ALONG + 1, MEMORY + PART, QUERY + MIDDLE + 3, OUT + MIDDLE + 1, OUT + ALONG + 3,
    MEMORY + ON, OUT + MIDDLE + 2, QUERY + ALONG + 3, QUERY + MIDDLE + 0, NORM, DOWN + BEGIN + 0,
    QUERY + ALONG + 1, OUT + ALONG + 1, UP + ALONG + 0, OUT + ALONG + 2, OUT + MIDDLE + 0,
    QUERY + ALONG + 2, MEMORY + END, DOWN + ALONG + 0, QUERY + ALONG + 0, ROWS + END,
    OUT + ALONG + 0,
)

SELF_PLAN = (
    MEMORY + GO, LOAD + OTHER, LOAD, CROSS + BEGIN + 3, CROSS + BEGIN + 2, GRAD + OUTPUT,
    OUT + BEGIN + 1, CROSS + BEGIN + 1, OUT + BEGIN + 0, HEADS, OUT + BEGIN + 3, OUT + BEGIN + 2,
    TWIN + 0, TWIN + 1, CROSS + MIDDLE + 3, TWIN + 2, TWIN + 3, GRAD + QUERIES, OUT + MIDDLE + 3,
    QUERY + BEGIN + 3, QUERY + BEGIN + 1, GRAD + TWIN, KEYS + BEGIN + 3, INPUT + PART,
    OUT + MIDDLE + 2, CROSS + ALONG + 3, OUT + ALONG + 3, CROSS + MIDDLE + 2, INPUT + ON,
    KEYS + BEGIN + 2, QUERY + MIDDLE + 3, OUT + MIDDLE + 1, KEYS + MIDDLE + 3, KEYS + MIDDLE + 2,
    OUT + ALONG + 2, CROSS + ALONG + 2, KEYS + BEGIN + 1, QUERY + BEGIN + 2, MEMORY + END,
    QUERY + MIDDLE + 1, OUT + ALONG + 1, QUERY + ALONG + 3, NORM, KEYS + ALONG + 3,
    QUERY + ALONG + 1, CROSS + BEGIN + 0, CROSS + MIDDLE + 1, QUERY + MIDDLE + 2,
    KEYS + ALONG + 2, QUERY + BEGIN + 0, HOME + END, KEYS + BEGIN + 0, KEYS + MIDDLE + 1,
    CROSS + MIDDLE + 0, OUT + MIDDLE + 0, CROSS + ALONG + 1, QUERY + ALONG + 2,
    KEYS + MIDDLE + 0, KEYS + ALONG + 1, QUERY + MIDDLE + 0, QUERY + ALONG + 0,
    CROSS + ALONG + 0, OUT + ALONG + 0, KEYS + ALONG + 0,
)

def backward_plan(tuned, nz, pairs, head, parts, tail):
    if nz == 4 and pairs == 4:
        return tuned
    plan = list(head) + [TWIN + p for p in range(pairs)] + list(parts)
    return tuple(plan) + tuple(tail)


class Halving:
    def zones(self):
        return range(self.n["z"] - 1, -1, -1)

    def zone(self, m):
        return flipped(self.at["z"], m)

    def sources(self, m):
        top = (m & -m) if m else self.n["z"]
        found, bit = [], 1
        while bit < top:
            found.append(m + bit)
            bit *= 2
        return found

    def settle(self, m, total, out):
        for k in self.sources(m):
            self.by_z[k].wait_recv()
            total = total + self.r3[k - 1].astype(F32)
        if m:
            self.s3[m - 1] = total.astype(BF)
            self.by_z[m] = self.wires.send(self.s3.at[m - 1], self.r3.at[m - 1], flip=m & -m)
        else:
            out[...] = total


def flips(n):
    found, bit = [], 1
    while bit < n["z"]:
        found.append({"flip": bit})
        bit *= 2
    return found


class RowScatter(Halving):
    def __init__(self, wires, moves, src, own, r1, s3, r3, out):
        self.wires, self.moves, self.src, self.own = wires, moves, src, own
        self.r1, self.s3, self.r3, self.out = r1, s3, r3, out
        self.n, self.at = wires.sizes, wires.place
        self.by_y, self.by_z = {}, {}
        self.loads = {m: moves.start(self.band(m, 0), own.at[m]) for m in self.zones()}

    def band(self, m, t):
        rows = self.own.shape[1]
        index = self.zone(m) * self.n["y"] + (self.at["y"] + t) % self.n["y"]
        return self.src.at[pl.ds(pl.multiple_of(index * rows, rows), rows)]

    def begin(self, m):
        for t in range(1, self.n["y"]):
            self.by_y[m, t] = self.wires.send(self.band(m, t), self.r1.at[t - 1, m], y=t)

    def along(self, m):
        self.loads[m].wait()
        total = self.own[m].astype(F32)
        for t in range(1, self.n["y"]):
            self.by_y[m, t].wait_recv()
            total = total + self.r1[t - 1, m].astype(F32)
        self.settle(m, total, self.out)

    @staticmethod
    def copies(n):
        return n["z"] * (n["y"] - 1) + n["z"] - 1

    @staticmethod
    def scratch(n, rows, wide):
        nz, ny = n["z"], n["y"]
        return [
            pltpu.VMEM((nz, rows, wide), BF),
            pltpu.VMEM((ny - 1, nz, rows, wide), BF),
            pltpu.VMEM((nz - 1, rows, wide), BF),
            pltpu.VMEM((nz - 1, rows, wide), BF),
        ]


class Scatter(Halving):
    def __init__(self, wires, grads, first, count, x_first, r1, s2, r2, acc, s3, r3, out):
        self.wires, self.grads = wires, grads
        self.first, self.count, self.x_first = first, count, x_first
        self.r1, self.s2, self.r2, self.acc, self.s3, self.r3 = r1, s2, r2, acc, s3, r3
        self.out = out
        self.n, self.at = wires.sizes, wires.place
        self.rows, self.wide = acc.shape[2], acc.shape[3]
        self.stage1, self.stage2, self.by_z = {}, {}, {}

    def part(self, m, band, bands, column, columns):
        rows, wide = self.rows, self.wide
        start = self.zone(m) * self.n["y"] + band
        return self.grads.at[
            pl.ds(self.first, self.count),
            pl.ds(pl.multiple_of(start * rows, rows), bands * rows),
            pl.ds(pl.multiple_of(column * wide, wide), columns * wide),
        ]

    def begin(self, m):
        nx, ny = self.n["x"], self.n["y"]
        if self.x_first:
            for t in range(1, nx):
                src = self.part(m, 0, ny, (self.at["x"] + t) % nx, 1)
                self.stage1[m, t] = self.wires.send(src, self.r1.at[t - 1, m], x=t)
        else:
            for t in range(1, ny):
                src = self.part(m, (self.at["y"] + t) % ny, 1, 0, nx)
                self.stage1[m, t] = self.wires.send(src, self.r1.at[t - 1, m], y=t)

    def middle(self, m):
        nx, ny, rows, wide = self.n["x"], self.n["y"], self.rows, self.wide
        x, y = self.at["x"], self.at["y"]
        inner, outer = (ny, nx) if self.x_first else (nx, ny)
        for t in range(1, outer):
            self.stage1[m, t].wait_recv()
        for b in range(inner):
            if self.x_first:
                band = (y + b) % ny
                total = self.part(m, band, 1, x, 1)[...].astype(F32)
                here = (slice(None), pl.ds(pl.multiple_of(band * rows, rows), rows), slice(None))
            else:
                column = (x + b) % nx
                total = self.part(m, y, 1, column, 1)[...].astype(F32)
                here = (slice(None), slice(None), pl.ds(pl.multiple_of(column * wide, wide), wide))
            for t in range(1, outer):
                total = total + self.r1.at[t - 1, m][here].astype(F32)
            if b == 0:
                self.acc[m] = total
            else:
                self.s2[b - 1, m] = total.astype(BF)
        for t in range(1, inner):
            way = {"y": t} if self.x_first else {"x": t}
            self.stage2[m, t] = self.wires.send(self.s2.at[t - 1, m], self.r2.at[t - 1, m], **way)

    def along(self, m):
        inner = self.n["y"] if self.x_first else self.n["x"]
        total = self.acc[m]
        for t in range(1, inner):
            self.stage2[m, t].wait_recv()
            total = total + self.r2[t - 1, m].astype(F32)
        self.settle(m, total, self.out)

    @staticmethod
    def copies(n):
        nz, ny, nx = n["z"], n["y"], n["x"]
        return nz * (nx - 1 + ny - 1) + nz - 1

    @staticmethod
    def scratch(n, count, x_first, rows, wide):
        nz, ny, nx = n["z"], n["y"], n["x"]
        inner = ny if x_first else nx
        if x_first:
            first = (nx - 1, nz, count, ny * rows, wide)
        else:
            first = (ny - 1, nz, count, rows, nx * wide)
        return [
            pltpu.VMEM(first, BF),
            pltpu.VMEM((inner - 1, nz, count, rows, wide), BF),
            pltpu.VMEM((inner - 1, nz, count, rows, wide), BF),
            pltpu.VMEM((nz, count, rows, wide), F32),
            pltpu.VMEM((nz - 1, count, rows, wide), BF),
            pltpu.VMEM((nz - 1, count, rows, wide), BF),
        ]


ONE = (8, 128)


def squares(refs):
    total = jnp.zeros(ONE, F32)
    for ref in refs:
        value = ref[...]
        total = total + jnp.sum((value * value).reshape((-1,) + ONE), axis=0)
    return total


def register(steps, name, group):
    for m in group.zones():
        steps[name + BEGIN + m] = functools.partial(group.begin, m)
        steps[name + ALONG + m] = functools.partial(group.along, m)
        if hasattr(group, "middle"):
            steps[name + MIDDLE + m] = functools.partial(group.middle, m)


def spelled(n, names):
    plan = []
    for name, kinds in names:
        for kind in kinds:
            plan += [name + kind + m for m in range(n["z"] - 1, -1, -1)]
    return plan


WHOLE = (BEGIN, MIDDLE, ALONG)


def cross_back_kernel(
    n, order, reaches, dc_hbm, dx_ref, w_hbm, q_hbm, k_hbm, v_hbm, o_hbm, l_ref, h_hbm, m_hbm, x_ref, p_ref,
    dw_hbm, oup_ref, odown_ref, oq_ref, oo_ref, og, odx_ref, odb, om, on_ref, osq_ref, *scratch,
):
    (
        dc_s, w_s, q_s, k_s, v_s, o_s, h_s, m_s, g_s, dq_s, dk_s, dv_s, ds_s, gr_s, give_s, got_s,
        db_s, pm_s, rm_s, sm_s, cm_s, om_s,
    ) = scratch[:22]
    send_sem, recv_sem, move_sem = scratch[-3:]
    at = grid_place()
    x, c = at["x"], at["c"]
    nz, ny, nx = n["z"], n["y"], n["x"]
    wires = Wires(n, at, send_sem, recv_sem)
    moves = Moves(move_sem)
    loads = [
        moves.start(a, b)
        for a, b in (
            (dc_hbm, dc_s), (w_hbm.at[3], w_s.at[3]), (o_hbm, o_s), (q_hbm, q_s), (k_hbm, k_s),
            (v_hbm, v_s),
        )
    ]
    down = RowScatter(wires, moves, dw_hbm.at[1], *scratch[22:26], odown_ref)
    up = RowScatter(wires, moves, dw_hbm.at[0], *scratch[26:30], oup_ref)
    out_sum = Scatter(wires, gr_s, 3, 1, True, *scratch[30:36], oo_ref)
    query_sum = Scatter(wires, gr_s, 0, 1, True, *scratch[36:42], oq_ref)
    later = [moves.start(h_hbm, h_s), moves.start(m_hbm, m_s)]
    get_maps = moves.start(w_hbm.at[0:3], w_s.at[0:3])
    wires.greet(
        flips(n)
        + [{"y": s} for s in range(1, ny)]
        + [{"x": s} for s in range(1, nx)]
        + [{"c": 1}]
    )
    chip_rows, width = dc_s.shape
    slot = m_s.shape[0]
    own = chip_rows // 2
    strip = min(STRIP, own)
    pairs = q_s.shape[1] // PAIR
    deep = om_s.shape[1]
    mine = pl.ds(pl.multiple_of(c * own, own), own)
    other = pl.ds(pl.multiple_of((1 - c) * own, own), own)
    bound = jnp.full((1, chip_rows), reaches[order[at["z"] * ny + at["y"]]], jnp.int32)
    held = {}
    steps = {}
    for name, group in ((DOWN, down), (UP, up), (OUT, out_sum), (QUERY, query_sum)):
        register(steps, name, group)

    def step(name):
        def keep(function):
            steps[name] = function
            return function

        return keep

    @step(LOAD)
    def _():
        for copy in loads:
            copy.wait()

    @step(HEADS)
    def _():
        mat_rows(g_s, dc_s, w_s.at[3], chip_rows, strip)

    for p in range(pairs):

        def pair(p=p):
            attend_pair_back(
                p, 256, bound, q_s, k_s, v_s, o_s, l_ref, g_s, dq_s, dk_s, dv_s, ds_s
            )

        steps[TWIN + p] = pair

    @step(INPUT + PART)
    def _():
        get_maps.wait()

        def body(rows):
            give_s[rows, :] = dot(dq_s[rows, :], w_s[0], 1, 1).astype(BF)

        loop_rows(chip_rows, strip, body)
        held["rows"] = wires.send(give_s.at[other], got_s, c=1)

    @step(MEMORY + PART)
    def _():
        piece = min(512, width)

        def body(rows):
            for col in range(0, width, piece):
                some = slice(col, col + piece)
                sums = dot(dk_s[rows, :], w_s[1, some, :], 1, 1)
                sums = (sums + dot(dv_s[rows, :], w_s[2, some, :], 1, 1)).astype(BF)
                for b in range(piece // deep):
                    index = col // deep + b
                    pm_s[index // 2, index % 2, rows, :] = sums[:, b * deep : (b + 1) * deep]

        loop_rows(slot, strip, body)
        held["memory"] = wires.send(pm_s.at[:, 1 - c], rm_s, c=1)

    @step(NORM)
    def _():
        held["rows"].wait_recv()
        upstream = give_s[mine, :].astype(F32) + got_s[...].astype(F32)
        grad, normed = norm_back_rows(x_ref[...], upstream, p_ref[1:2, :])
        total = dx_ref[...] + grad
        odx_ref[...] = total
        db_s[mine, :] = total.astype(BF)
        held["near"] = wires.send(db_s.at[mine], db_s.at[mine], c=1)
        line = lax.broadcasted_iota(jnp.int32, on_ref.shape, 0)
        on_ref[...] = jnp.where(line == 1, row_sum(upstream * normed), 0.0) + jnp.where(
            line == 5, row_sum(upstream), 0.0
        )

    @step(MEMORY + ON)
    def _():
        held["memory"].wait_recv()
        held["far"] = []
        for t in range(1, nx):
            index = (x + t) % nx
            sm_s[t - 1] = (pm_s[index, c].astype(F32) + rm_s[index].astype(F32)).astype(BF)
            held["far"].append(wires.send(sm_s.at[t - 1], cm_s.at[t - 1], x=t))

    @step(MEMORY + END)
    def _():
        total = pm_s[x, c].astype(F32) + rm_s[x].astype(F32)
        for t in range(1, nx):
            held["far"][t - 1].wait_recv()
            total = total + cm_s[t - 1].astype(F32)
        om_s[...] = total.astype(BF)
        moves.store(om_s, om)

    def weight_grad(i, left, right):
        size = min(256, width)
        for col in range(0, width, size):
            cols = slice(col, col + size)
            gr_s[i, cols, :] = dot(left[:, cols], right[...], 0, 0).astype(BF)

    @step(GRAD + OUTPUT)
    def _():
        weight_grad(3, dc_s, o_s)

    @step(GRAD + QUERIES)
    def _():
        later[0].wait()
        weight_grad(0, h_s, dq_s)

    @step(GRAD + TWIN)
    def _():
        later[1].wait()
        weight_grad(1, m_s, dk_s)
        weight_grad(2, m_s, dv_s)
        moves.store(gr_s.at[1:3], og)

    @step(ROWS + END)
    def _():
        held["near"].wait_recv()
        moves.store(db_s, odb)

    plan = backward_plan(
        CROSS_PLAN, nz, pairs,
        [LOAD, HEADS] + spelled(n, [(DOWN, (BEGIN,)), (UP, (BEGIN,))]),
        [INPUT + PART, MEMORY + PART, NORM, MEMORY + ON, GRAD + OUTPUT, GRAD + QUERIES, GRAD + TWIN],
        spelled(n, [(DOWN, (ALONG,)), (UP, (ALONG,)), (OUT, WHOLE), (QUERY, WHOLE)])
        + [MEMORY + END, ROWS + END],
    )
    for name in plan:
        steps[name]()
    osq_ref[...] = squares((oup_ref, odown_ref, oq_ref, oo_ref))
    moves.close()
    wires.close()


def cross_back(
    order, reaches, rows_grad, resid_grad, maps, saved, normed, frames, resid, params, ffn_grads
):
    n = grid_sizes()
    nz, ny, nx = n["z"], n["y"], n["x"]
    queries, keys, values, mixed, logsum = saved
    chip_rows, width = rows_grad.shape
    own = chip_rows // 2
    slot, local = keys.shape
    hidden = ffn_grads.shape[2]
    rows, wide = width // (nz * ny), local // nx
    deep = width // (2 * nx)
    copies = 2 * RowScatter.copies(n) + 2 * Scatter.copies(n) + 3 + (nx - 1)
    vmem = pl.BlockSpec(memory_space=pltpu.VMEM)
    smem = pl.BlockSpec(memory_space=pltpu.SMEM)
    hbm = pl.BlockSpec(memory_space=pl.ANY)
    half = lambda *shape: pltpu.VMEM(shape, BF)
    return pl.pallas_call(
        functools.partial(cross_back_kernel, n),
        out_shape=[
            jax.ShapeDtypeStruct((rows, hidden), F32),
            jax.ShapeDtypeStruct((rows, hidden), F32),
            jax.ShapeDtypeStruct((1, rows, wide), F32),
            jax.ShapeDtypeStruct((1, rows, wide), F32),
            jax.ShapeDtypeStruct((2, width, local), BF),
            jax.ShapeDtypeStruct((own, width), F32),
            jax.ShapeDtypeStruct((chip_rows, width), BF),
            jax.ShapeDtypeStruct((slot, deep), BF),
            jax.ShapeDtypeStruct(params.shape, F32),
            jax.ShapeDtypeStruct(ONE, F32),
        ],
        in_specs=[smem, smem, hbm, vmem] + [hbm] * 5 + [vmem, hbm, hbm, vmem, vmem, hbm],
        out_specs=[vmem] * 4 + [hbm, vmem, hbm, hbm, vmem, vmem],
        scratch_shapes=[
            half(chip_rows, width),
            half(4, width, local),
            half(chip_rows, local),
            half(slot, local),
            half(slot, local),
            half(chip_rows, local),
            half(chip_rows, width),
            half(slot, width),
            half(chip_rows, local),
            half(chip_rows, local),
            half(slot, local),
            half(slot, local),
            half(2, slot, chip_rows),
            half(4, width, local),
            half(chip_rows, width),
            half(own, width),
            half(chip_rows, width),
            half(nx, 2, slot, deep),
            half(nx, slot, deep),
            half(nx - 1, slot, deep),
            half(nx - 1, slot, deep),
            half(slot, deep),
        ]
        + RowScatter.scratch(n, rows, hidden) * 2
        + Scatter.scratch(n, 1, True, rows, wide) * 2
        + [
            pltpu.SemaphoreType.DMA((copies,)),
            pltpu.SemaphoreType.DMA((copies,)),
            pltpu.SemaphoreType.DMA((14 + 2 * nz,)),
        ],
        compiler_params=pltpu.CompilerParams(
            collective_id=5, has_side_effects=True, vmem_limit_bytes=56 * 2**20
        ),
        name="cross_back",
    )(
        order, reaches, rows_grad, resid_grad, maps, queries, keys, values, mixed, logsum, normed, frames,
        resid, params, ffn_grads,
    )


def self_back_kernel(
    n, order, lengths, db_hbm, dx_ref, w_hbm, q_hbm, k_hbm, v_hbm, o_hbm, l_ref, h_hbm, x_ref, p_ref,
    cg_hbm, m_hbm, np_ref, nq_ref, sq_ref, oc_ref, oo_ref, oq_ref, op_ref, os_ref, om_ref, on_ref,
    norm_ref, *scratch,
):
    (
        db_s, w_s, q_s, k_s, v_s, o_s, h_s, g_s, dq_s, dk_s, dv_s, ds_s, cg_s, gr_s, part_s, rc_s,
        sx_s, rx_s, out_s, np_s, nn_s, nf_s,
    ) = scratch[:22]
    one_s, near_s, sum_s, far_s = scratch[46:50]
    send_sem, recv_sem, go_sem, come_sem, move_sem = scratch[-5:]
    at = grid_place()
    z, y, x, c = at["z"], at["y"], at["x"], at["c"]
    nz, ny, nx = n["z"], n["y"], n["x"]
    data, model = z * ny + y, x * 2 + c
    wires = Wires(n, at, send_sem, recv_sem)
    moves = Moves(move_sem)
    get_cross = moves.start(cg_hbm, cg_s)
    loads = [
        moves.start(a, b)
        for a, b in (
            (db_hbm, db_s), (w_hbm.at[3], w_s.at[3]), (o_hbm, o_s), (q_hbm, q_s), (k_hbm, k_s),
            (v_hbm, v_s),
        )
    ]
    later = [moves.start(h_hbm, h_s), moves.start(w_hbm.at[0:3], w_s.at[0:3])]
    wires.greet(
        [
            dict(z=sz, y=sy, x=sx, c=sc)
            for sz in range(nz)
            for sy in range(ny)
            for sx in range(nx)
            for sc in range(2)
            if sz or sy or sx or sc
        ]
    )
    cross_sum = Scatter(wires, cg_s, 0, 2, False, *scratch[22:28], oc_ref)
    out_sum = Scatter(wires, gr_s, 3, 1, True, *scratch[28:34], oo_ref)
    query_sum = Scatter(wires, gr_s, 0, 1, True, *scratch[34:40], oq_ref)
    pair_sum = Scatter(wires, gr_s, 1, 2, False, *scratch[40:46], op_ref)
    chip_rows, width = db_s.shape
    slot = h_s.shape[0]
    own = chip_rows // 2
    strip = min(STRIP, own)
    pairs = q_s.shape[1] // PAIR
    chip_start = x * chip_rows
    bound = lax.broadcasted_iota(jnp.int32, (1, chip_rows), 1) + chip_start + 1
    bound = jnp.minimum(bound, lengths[order[data]])
    held = {}
    steps = {}
    for name, group in (
        (CROSS, cross_sum), (OUT, out_sum), (QUERY, query_sum), (KEYS, pair_sum)
    ):
        register(steps, name, group)

    def step(name):
        def keep(function):
            steps[name] = function
            return function

        return keep

    @step(LOAD + OTHER)
    def _():
        get_cross.wait()

    @step(LOAD)
    def _():
        for copy in loads:
            copy.wait()

    @step(MEMORY + GO)
    def _():
        held["memory"] = [
            wires.send(m_hbm.at[wires.peer(**shift)[0]], om_ref.at[data], **shift)
            for shift in dp_shifts(n)
        ]
        held["memory own"] = moves.start(m_hbm.at[data], om_ref.at[data])

    @step(MEMORY + END)
    def _():
        for copy in held["memory"]:
            copy.wait_recv()
        held["memory own"].wait()

    @step(HEADS)
    def _():
        mat_rows(g_s, db_s, w_s.at[3], chip_rows, strip)

    for p in range(pairs):

        def pair(p=p):
            attend_pair_back(
                p, 256, bound, q_s, k_s, v_s, o_s, l_ref, g_s, dq_s, dk_s, dv_s, ds_s
            )

        steps[TWIN + p] = pair

    def block(chip, core):
        return pl.ds(pl.multiple_of((chip * 2 + core) * own, own), own)

    def need(index):
        if later[index] is not None:
            later[index].wait()
            later[index] = None

    @step(INPUT + PART)
    def _():
        need(1)
        def keys_values(rows):
            sums = dot(dk_s[rows, :], w_s[1], 1, 1) + dot(dv_s[rows, :], w_s[2], 1, 1)
            part_s[rows, :] = sums.astype(BF)

        loop_rows(slot, strip, keys_values)

        def queries(rows):
            here = shifted(rows, chip_start)
            sums = part_s[here, :].astype(F32) + dot(dq_s[rows, :], w_s[0], 1, 1)
            part_s[here, :] = sums.astype(BF)

        loop_rows(chip_rows, strip, queries)
        held["core"] = [
            wires.send(part_s.at[block(b, 1 - c)], rc_s.at[b], c=1) for b in range(nx)
        ]

    @step(INPUT + ON)
    def _():
        for copy in held["core"]:
            copy.wait_recv()
        held["far"] = []
        for t in range(1, nx):
            index = (x + t) % nx
            sums = part_s[block(index, c), :].astype(F32) + rc_s[index].astype(F32)
            sx_s[t - 1] = sums.astype(BF)
            held["far"].append(wires.send(sx_s.at[t - 1], rx_s.at[t - 1], x=t))

    def weight_grad(i, left, right):
        size = min(256, width)
        for col in range(0, width, size):
            cols = slice(col, col + size)
            gr_s[i, cols, :] = dot(left[:, cols], right[...], 0, 0).astype(BF)

    @step(GRAD + OUTPUT)
    def _():
        weight_grad(3, db_s, o_s)

    @step(GRAD + QUERIES)
    def _():
        need(0)
        weight_grad(0, h_s.at[pl.ds(pl.multiple_of(chip_start, chip_rows), chip_rows)], dq_s)

    @step(GRAD + TWIN)
    def _():
        need(0)
        weight_grad(1, h_s, dk_s)
        weight_grad(2, h_s, dv_s)

    lines, deep = os_ref.shape[1], os_ref.shape[2]
    blocks = own // lines

    def homeward():
        for b in range(blocks):
            for m in range(2 * nx):
                target = (model * blocks + b, m)
                src = out_s.at[b * lines : (b + 1) * lines, m * deep : (m + 1) * deep]
                mine = jnp.logical_and(target[0] == data, model == m)
                remote = pltpu.make_async_remote_copy(
                    src_ref=src,
                    dst_ref=os_ref.at[data],
                    send_sem=go_sem.at[b * 2 * nx + m],
                    recv_sem=come_sem.at[data],
                    device_id=target,
                    device_id_type=pl.DeviceIdType.MESH,
                )
                yield mine, remote, pltpu.make_async_copy(src, os_ref.at[data], come_sem.at[data])

    @step(NORM)
    def _():
        upstream = part_s[block(x, c), :].astype(F32) + rc_s[x].astype(F32)
        for t in range(1, nx):
            held["far"][t - 1].wait_recv()
            upstream = upstream + rx_s[t - 1].astype(F32)
        grad, normed = norm_back_rows(x_ref[...].astype(F32), upstream, p_ref[0:1, :])
        out_s[...] = (dx_ref[...] + grad).astype(BF)
        for mine, remote, here in homeward():
            pl.when(mine)(lambda: here.start())
            pl.when(jnp.logical_not(mine))(lambda: remote.start())
        line = lax.broadcasted_iota(jnp.int32, np_ref.shape, 0)
        params = (
            np_ref[...]
            + nq_ref[...]
            + jnp.where(line == 0, row_sum(upstream * normed), 0.0)
            + jnp.where(line == 4, row_sum(upstream), 0.0)
        )
        columns = on_ref.shape[1]
        for k in range(nz * ny):
            np_s[0, k] = params[:, k * columns : (k + 1) * columns]
        held["norm near"] = [
            wires.send(np_s.at[0], nn_s.at[i], **s) for i, s in enumerate(mp_shifts(n))
        ]

    @step(HOME + END)
    def _():
        total = np_s[0]
        for i, copy in enumerate(held["norm near"]):
            copy.wait_recv()
            total = total + nn_s[i]
        np_s[1] = total
        held["norm far"] = [
            wires.send(np_s.at[1, wires.peer(**shift)[0]], nf_s.at[i], **shift)
            for i, shift in enumerate(dp_shifts(n))
        ]

    plan = backward_plan(
        SELF_PLAN, nz, pairs,
        [MEMORY + GO, LOAD + OTHER, LOAD, HEADS] + spelled(n, [(CROSS, (BEGIN,))]),
        [INPUT + PART, INPUT + ON, GRAD + OUTPUT, GRAD + QUERIES, GRAD + TWIN],
        spelled(n, [(CROSS, (MIDDLE, ALONG)), (OUT, WHOLE)])
        + [NORM, HOME + END]
        + spelled(n, [(QUERY, WHOLE), (KEYS, WHOLE)])
        + [MEMORY + END],
    )
    for name in plan:
        steps[name]()
    total = np_s[1, data]
    for i, copy in enumerate(held["norm far"]):
        copy.wait_recv()
        total = total + nf_s[i]
    on_ref[...] = total
    norm_squares = jnp.sum(total * total) / (2 * nx * ONE[0] * ONE[1])
    total = sq_ref[...] + squares((oc_ref, oo_ref, oq_ref, op_ref)) + norm_squares
    one_s[...] = total
    copies = [wires.send(one_s, near_s.at[i], **s) for i, s in enumerate(mp_shifts(n))]
    for i, copy in enumerate(copies):
        copy.wait_recv()
        total = total + near_s[i]
    sum_s[...] = total
    copies = [wires.send(sum_s, far_s.at[i], **s) for i, s in enumerate(dp_shifts(n))]
    for i, copy in enumerate(copies):
        copy.wait_recv()
        total = total + far_s[i]
    norm_ref[0] = jnp.sqrt(jnp.sum(total))
    for mine, remote, here in homeward():
        pl.when(jnp.logical_not(mine))(lambda: remote.wait_send())
    for r in range(nz * ny):
        pltpu.make_async_copy(os_ref.at[r], os_ref.at[r], come_sem.at[r]).wait()
    wires.close()


def self_back(
    order, lengths, rows_grad, resid_grad, maps, saved, normed, inputs, params, cross_grads, memory,
    norm_ffn, norm_cross, square_part,
):
    n = grid_sizes()
    nz, ny, nx = n["z"], n["y"], n["x"]
    data, model = nz * ny, 2 * nx
    queries, keys, values, mixed, logsum = saved
    chip_rows, width = rows_grad.shape
    own = chip_rows // 2
    slot, local = keys.shape
    rows, wide = width // data, local // nx
    utterances, lines, deep = memory.shape
    columns = width // data
    copies = 4 * Scatter.copies(n) + 3 * (data - 1) + nx + (nx - 1) + 2 * (model - 1)
    vmem = pl.BlockSpec(memory_space=pltpu.VMEM)
    smem = pl.BlockSpec(memory_space=pltpu.SMEM)
    hbm = pl.BlockSpec(memory_space=pl.ANY)
    half = lambda *shape: pltpu.VMEM(shape, BF)
    return pl.pallas_call(
        functools.partial(self_back_kernel, n),
        out_shape=[
            jax.ShapeDtypeStruct((2, rows, wide), F32),
            jax.ShapeDtypeStruct((1, rows, wide), F32),
            jax.ShapeDtypeStruct((1, rows, wide), F32),
            jax.ShapeDtypeStruct((2, rows, wide), F32),
            jax.ShapeDtypeStruct((data, lines, deep), BF),
            jax.ShapeDtypeStruct((data, lines, deep), BF),
            jax.ShapeDtypeStruct((params.shape[0], columns), F32),
            jax.ShapeDtypeStruct((1,), F32),
        ],
        in_specs=[smem, smem, hbm, vmem]
        + [hbm] * 5
        + [vmem, hbm, vmem, vmem, hbm, hbm, vmem, vmem, vmem],
        out_specs=[vmem] * 4 + [hbm, hbm, vmem, smem],
        scratch_shapes=[
            half(chip_rows, width),
            half(4, width, local),
            half(chip_rows, local),
            half(slot, local),
            half(slot, local),
            half(chip_rows, local),
            half(slot, width),
            half(chip_rows, local),
            half(chip_rows, local),
            half(slot, local),
            half(slot, local),
            half(2, slot, chip_rows),
            half(2, width, local),
            half(4, width, local),
            half(slot, width),
            half(nx, own, width),
            half(nx - 1, own, width),
            half(nx - 1, own, width),
            half(own, width),
            pltpu.VMEM((2, data, params.shape[0], columns), F32),
            pltpu.VMEM((model - 1, data, params.shape[0], columns), F32),
            pltpu.VMEM((data - 1, params.shape[0], columns), F32),
        ]
        + Scatter.scratch(n, 2, False, rows, wide)
        + Scatter.scratch(n, 1, True, rows, wide)
        + Scatter.scratch(n, 1, True, rows, wide)
        + Scatter.scratch(n, 2, False, rows, wide)
        + [
            pltpu.VMEM(ONE, F32),
            pltpu.VMEM((model - 1,) + ONE, F32),
            pltpu.VMEM(ONE, F32),
            pltpu.VMEM((data - 1,) + ONE, F32),
            pltpu.SemaphoreType.DMA((copies,)),
            pltpu.SemaphoreType.DMA((copies,)),
            pltpu.SemaphoreType.DMA((data,)),
            pltpu.SemaphoreType.DMA((data,)),
            pltpu.SemaphoreType.DMA((14,)),
        ],
        compiler_params=pltpu.CompilerParams(
            collective_id=1, has_side_effects=True, vmem_limit_bytes=56 * 2**20
        ),
        name="self_back",
    )(
        order, lengths, rows_grad, resid_grad, maps, queries, keys, values, mixed, logsum, normed,
        inputs, params, cross_grads, memory, norm_ffn, norm_cross, square_part,
    )


def adam_step(weight, moment, square, gradient, step_rate, weight_decay):
    moment_new = BETA_FIRST * moment + (1.0 - BETA_FIRST) * gradient
    square_new = BETA_SECOND * square + (1.0 - BETA_SECOND) * gradient * gradient
    moment_hat = moment_new / (1.0 - BETA_FIRST**STEP)
    square_hat = square_new / (1.0 - BETA_SECOND**STEP)
    updated = weight - step_rate * (
        moment_hat / (jnp.sqrt(square_hat) + ADAM_EPSILON) + weight_decay * weight
    )
    return (updated, moment_new, square_new)


def update_kernel(order, norm, *refs):
    grads, refs = refs[:9], refs[9:]
    back, refs = refs[:2], refs[2:]
    old, refs = refs[:12], refs[12:]
    home, refs = refs[:2], refs[2:]
    new, refs = refs[:12], refs[12:]
    vault, refs = refs[:12], refs[12:]
    back_s, home_s, move_sem = refs[:2], refs[2:4], refs[4]
    moves = Moves(move_sem)
    loads = {}
    for kind in (2, 1, 0):
        loads[kind] = [moves.start(old[3 * j + kind], vault[3 * j + kind]) for j in range(4)]
    back_loads = [moves.start(a, b) for a, b in zip(back, back_s)]
    clip_scale = jnp.minimum(1.0, THRESHOLD / (norm[0] + 1e-06))

    def apply(kind, part, gradient, rate, decay):
        weight, moment, square, average = (vault[3 * j + kind] for j in range(4))
        updated, moment_new, square_new = adam_step(
            weight[part], moment[part], square[part], clip_scale * gradient, rate, decay
        )
        mixed = AVERAGING * average[part] + (1.0 - AVERAGING) * updated
        for j, value in enumerate((updated, moment_new, square_new, mixed)):
            vault[3 * j + kind][part] = value
            moves.store(vault[3 * j + kind].at[part], new[3 * j + kind].at[part])

    sq, sp, so, cq, cp, co, up, down, line = grads
    for copy in loads[2]:
        copy.wait()
    apply(2, slice(None), line[...], NORM_RATE, 0.0)
    for copy in loads[1]:
        copy.wait()
    for part, ref in ((0, up), (1, down)):
        apply(1, slice(part, part + 1), ref[...][None], MATRIX_RATE, MATRIX_DECAY)
    for copy in loads[0]:
        copy.wait()
    for part, ref in (
        (slice(0, 1), sq), (slice(1, 3), sp), (slice(3, 4), so), (slice(4, 5), cq),
        (slice(5, 7), cp), (slice(7, 8), co),
    ):
        apply(0, part, ref[...], MATRIX_RATE, MATRIX_DECAY)

    utterances = home_s[0].shape[0]
    for copy in back_loads:
        copy.wait()
    for i in range(utterances):
        place = 0
        for r in range(utterances):
            place = place + jnp.where(order[r] == i, r, 0)
        for src, dst in zip(back_s, home_s):
            dst[i] = src[place].astype(F32)
    for src, dst in zip(home_s, home):
        moves.store(src, dst)
    moves.close()


def update(order, norm, grads, back, old):
    vmem = pl.BlockSpec(memory_space=pltpu.VMEM)
    smem = pl.BlockSpec(memory_space=pltpu.SMEM)
    hbm = pl.BlockSpec(memory_space=pl.ANY)
    full = lambda v: jax.ShapeDtypeStruct(v.shape, F32)
    return pl.pallas_call(
        update_kernel,
        out_shape=[full(v) for v in back] + [full(v) for v in old],
        in_specs=[smem, smem] + [vmem] * 9 + [hbm] * 14,
        out_specs=[hbm] * 14,
        scratch_shapes=[pltpu.VMEM(v.shape, F32) for v in old]
        + [pltpu.VMEM(v.shape, BF) for v in back]
        + [pltpu.VMEM(v.shape, F32) for v in back]
        + [pltpu.SemaphoreType.DMA((60,))],
        compiler_params=pltpu.CompilerParams(vmem_limit_bytes=56 * 2**20),
        name="update",
    )(order, norm, *grads, *back, *old)


def per_device(
    states,
    memory,
    cotangent,
    lengths,
    memory_lengths,
    regroup_order,
    attn_weights,
    ffn_weights,
    norm_params,
    attn_mean,
    ffn_mean,
    norm_mean,
    attn_square,
    ffn_square,
    norm_square,
    attn_average,
    ffn_average,
    norm_average,
):
    n = grid_sizes()
    at = grid_place()
    nz, ny, nx = n["z"], n["y"], n["x"]
    data_index = lax.axis_index("dp")
    model_index = lax.axis_index("mp")
    data_size = lax.axis_size("dp")
    width = states.shape[2] * lax.axis_size("mp")
    slot = states.shape[1] * data_size
    own_rows = cotangent.shape[1]
    chip_rows = 2 * own_rows
    chip_start = at["x"] * chip_rows

    (
        weights_self,
        weights_cross,
        ffn_maps,
        norm_values,
        frames,
        inputs,
        normed_first,
        query_self,
        key_self,
        value_self,
        mixed_self,
        logsum_self,
        resid_one_own,
        normed_second,
        query_cross,
        key_cross,
        value_cross,
        mixed_cross,
        logsum_cross,
        resid_two_own,
        normed_third,
    ) = forward(
        regroup_order,
        lengths,
        memory_lengths,
        states,
        memory,
        norm_params,
        attn_weights,
        ffn_weights,
        own_rows,
    )

    layer_output, grad_two, cross_rows, ffn_grads, norm_ffn = feed_forward(
        regroup_order, lengths, normed_third, resid_two_own, ffn_maps, cotangent[0], norm_values
    )
    (
        shard_up,
        shard_down,
        cross_q,
        cross_o,
        cross_grads,
        grad_one,
        self_rows,
        memory_part,
        norm_cross,
        square_part,
    ) = (
        cross_back(
            regroup_order,
            memory_lengths,
            cross_rows,
            grad_two,
            weights_cross,
            (query_cross, key_cross, value_cross, mixed_cross, logsum_cross),
            normed_second,
            frames,
            resid_one_own,
            norm_values,
            ffn_grads,
        )
    )
    cross_p, self_o, self_q, self_p, back_states, back_memory, norm_shard, grad_norm = self_back(
        regroup_order,
        lengths,
        self_rows,
        grad_one,
        weights_self,
        (query_self, key_self, value_self, mixed_self, logsum_self),
        normed_first,
        inputs,
        norm_values,
        cross_grads,
        memory_part.reshape(data_size, -1, memory_part.shape[1]),
        norm_ffn,
        norm_cross,
        square_part,
    )
    grads = (self_q, self_p, self_o, cross_q, cross_p, cross_o, shard_up, shard_down, norm_shard)
    results = update(
        regroup_order,
        grad_norm,
        grads,
        (back_states, back_memory),
        (
            attn_weights,
            ffn_weights,
            norm_params,
            attn_mean,
            ffn_mean,
            norm_mean,
            attn_square,
            ffn_square,
            norm_square,
            attn_average,
            ffn_average,
            norm_average,
        ),
    )
    return (layer_output[None],) + tuple(results) + (grad_norm[0],)


def solution(mesh):
    rows = P(None, "dp", "mp")
    line = P(None, "dp")
    return jax.shard_map(
        per_device,
        mesh=mesh,
        in_specs=(rows, rows, P("dp", "mp", None), P(), P(), P())
        + (rows, rows, line) * 4,
        out_specs=(P("dp", "mp", None), rows, rows) + (rows, rows, line) * 4 + (P(),),
        check_vma=False,
    )
```

```python
import functools

import jax
import jax.numpy as jnp
from jax import lax
from jax.experimental import pallas as pl
from jax.experimental.pallas import tpu as pltpu
from jax.sharding import PartitionSpec as P

HD = 64
STEP = 10


EPSILON = 1e-05
NEGATIVE = -1000000000.0
BETA_FIRST = 0.9
BETA_SECOND = 0.999
ADAM_EPSILON = 1e-08
MATRIX_RATE = 0.05
NORM_RATE = 1.0
MATRIX_DECAY = 0.1
AVERAGING = 0.7
THRESHOLD = 1.0
BF = jnp.bfloat16
F32 = jnp.float32


(
    CROSS, DOWN, FIRST, GRAD, HOME, INPUT, KEYS, LOAD, MEMORY, OUT, QUERY, ROWS, SECOND, SELF, STATES, THIRD, UP,
) = range(1000, 18000, 1000)
(
    ALONG, BEGIN, END, FAN, GO, HEADS, LINE, MIDDLE, NORM, ON, OTHER, OUTPUT, PART, PASS, QUERIES, TURN, TWIN,
) = range(10, 180, 10)


def grid_sizes():
    dp = lax.axis_size("dp")
    mp = lax.axis_size("mp")
    ny = 1 << ((dp.bit_length() - 1) // 2)
    return {"z": dp // ny, "y": ny, "x": mp // 2, "c": 2}


def grid_place():
    n = grid_sizes()
    dp = lax.axis_index("dp")
    mp = lax.axis_index("mp")
    return {"z": dp // n["y"], "y": dp % n["y"], "x": mp // 2, "c": mp % 2}


def dot(left, right, left_dim, right_dim):
    return lax.dot_general(
        left, right, (((left_dim,), (right_dim,)), ((), ())), preferred_element_type=F32
    )


PAIR = 2 * HD


def only_head(value, head):
    lane = lax.broadcasted_iota(jnp.int32, value.shape, 1)
    keep = (lane < HD) if head == 0 else (lane >= HD)
    return jnp.where(keep, value, jnp.zeros_like(value))


def attend_pair(p, chunk, bound, q_ref, k_ref, v_ref, o_ref, sum_ref, score_ref, weight_ref):
    lanes = pl.ds(pl.multiple_of(p * PAIR, PAIR), PAIR)
    keys = k_ref.shape[0]
    queries = q_ref[:, lanes] * BF(HD**-0.5)
    values = v_ref[:, lanes]
    mixed = []
    for head in range(2):
        masked = only_head(queries, head)
        top = None
        for start in range(0, keys, chunk):
            block = slice(start, start + chunk)
            scores = dot(k_ref[block, lanes], masked, 1, 1)
            position = lax.broadcasted_iota(jnp.int32, scores.shape, 0) + start
            scores = jnp.where(position < bound, scores, NEGATIVE)
            score_ref[head, block, :] = scores
            highest = jnp.max(scores, axis=0, keepdims=True)
            top = highest if top is None else jnp.maximum(top, highest)
        total = None
        for start in range(0, keys, chunk):
            block = slice(start, start + chunk)
            raised = jnp.exp(score_ref[head, block, :] - top)
            part = jnp.sum(raised, axis=0, keepdims=True)
            total = part if total is None else total + part
            weight_ref[head, block, :] = raised.astype(BF)
        out = dot(values, weight_ref[head], 0, 0)[head * HD : (head + 1) * HD]
        mixed.append(out * (1.0 / total))
        sum_ref[p, head : head + 1, :] = top + jnp.log(total)
    o_ref[:, lanes] = jnp.concatenate(mixed, axis=0).T.astype(BF)


def attend_pair_back(
    p, chunk, bound, q_ref, k_ref, v_ref, o_ref, sum_ref, g_ref, dq_ref, dk_ref, dv_ref, ds_ref
):
    lanes = pl.ds(pl.multiple_of(p * PAIR, PAIR), PAIR)
    keys = k_ref.shape[0]
    queries = q_ref[:, lanes] * BF(HD**-0.5)
    grads = g_ref[:, lanes]
    product = (grads.astype(F32) * o_ref[:, lanes].astype(F32)).T
    head_q = [only_head(queries, head) for head in range(2)]
    head_g = [only_head(grads, head) for head in range(2)]
    shift = [
        jnp.sum(product[head * HD : (head + 1) * HD], axis=0, keepdims=True) for head in range(2)
    ]
    for start in range(0, keys, chunk):
        block = slice(start, start + chunk)
        key_block, value_block = k_ref[block, lanes], v_ref[block, lanes]
        grad_value, grad_key = 0.0, 0.0
        for head in range(2):
            scores = dot(key_block, head_q[head], 1, 1)
            position = lax.broadcasted_iota(jnp.int32, scores.shape, 0) + start
            scores = jnp.where(position < bound, scores, NEGATIVE)
            weights = jnp.exp(scores - sum_ref[p, head : head + 1, :])
            grad_weights = dot(value_block, head_g[head], 1, 1)
            grad_scores = (weights * (grad_weights - shift[head])).astype(BF)
            ds_ref[head, block, :] = grad_scores
            grad_value = grad_value + dot(weights.astype(BF), head_g[head], 1, 0)
            grad_key = grad_key + dot(grad_scores, head_q[head], 1, 0)
        dv_ref[block, lanes] = grad_value.astype(BF)
        dk_ref[block, lanes] = grad_key.astype(BF)
    key_all = k_ref[:, lanes]
    parts = [dot(key_all, ds_ref[h], 0, 0)[h * HD : (h + 1) * HD] for h in range(2)]
    dq_ref[:, lanes] = (jnp.concatenate(parts, axis=0).T * HD**-0.5).astype(BF)


def flipped(index, mask):
    bit = 1
    result = index
    while bit <= mask:
        if mask & bit:
            result = result + bit * (1 - 2 * ((index // bit) % 2))
        bit *= 2
    return result


class Wires:
    def __init__(self, sizes, place, send_sem, recv_sem):
        self.sizes, self.place = sizes, place
        self.send_sem, self.recv_sem = send_sem, recv_sem
        self.count = 0
        self.started = []
        self.maybe = []

    def peer(self, z=0, y=0, x=0, c=0, flip=0):
        n, at = self.sizes, self.place
        pz, py = (at["z"] + z) % n["z"], (at["y"] + y) % n["y"]
        if flip:
            pz = flipped(at["z"], flip)
        px, pc = (at["x"] + x) % n["x"], (at["c"] + c) % 2
        return (pz * n["y"] + py, px * 2 + pc)

    def send(self, src, dst, **shift):
        copy = pltpu.make_async_remote_copy(
            src_ref=src,
            dst_ref=dst,
            send_sem=self.send_sem.at[self.count],
            recv_sem=self.recv_sem.at[self.count],
            device_id=self.peer(**shift),
            device_id_type=pl.DeviceIdType.MESH,
        )
        self.count += 1
        copy.start()
        self.started.append(copy)
        return copy

    def send_if(self, condition, src, dst, recv_sem, **shift):
        copy = pltpu.make_async_remote_copy(
            src_ref=src,
            dst_ref=dst,
            send_sem=self.send_sem.at[self.count],
            recv_sem=recv_sem,
            device_id=self.peer(**shift),
            device_id_type=pl.DeviceIdType.MESH,
        )
        self.count += 1
        pl.when(condition)(copy.start)
        self.maybe.append((condition, copy))

    def greet(self, shifts):
        barrier = pltpu.get_barrier_semaphore()
        for shift in shifts:
            pl.semaphore_signal(
                barrier, inc=1, device_id=self.peer(**shift), device_id_type=pl.DeviceIdType.MESH
            )
        pl.semaphore_wait(barrier, len(shifts))

    def close(self):
        for copy in self.started:
            copy.wait_send()
        for condition, copy in self.maybe:
            pl.when(condition)(copy.wait_send)


def dp_shifts(n):
    return [{"z": z, "y": y} for z in range(n["z"]) for y in range(n["y"]) if z or y]


def mp_shifts(n):
    return [{"x": x, "c": c} for x in range(n["x"]) for c in range(2) if x or c]


def loop_rows(total, step, body):
    def one(i, carry):
        body(pl.ds(pl.multiple_of(i * step, step), step))
        return carry

    lax.fori_loop(0, total // step, one, 0)


def shifted(rows, offset):
    return pl.ds(pl.multiple_of(rows.start + offset, rows.size), rows.size)


def mat_rows(out_ref, left_ref, right_ref, total, step, offset=0):
    def body(rows):
        left = left_ref[shifted(rows, offset), :]
        out_ref[rows, :] = dot(left, right_ref[...], 1, 0).astype(BF)

    loop_rows(total, step, body)


class Moves:
    def __init__(self, sem):
        self.sem = sem
        self.count = 0
        self.open = []

    def start(self, src, dst):
        copy = pltpu.make_async_copy(src, dst, self.sem.at[self.count])
        self.count += 1
        copy.start()
        return copy

    def store(self, src, dst):
        self.open.append(self.start(src, dst))

    def close(self):
        for copy in self.open:
            copy.wait()


class Line:
    def __init__(self, wires, spot, sem):
        self.wires, self.spot, self.sem = wires, spot, sem
        self.nz, self.z = wires.sizes["z"], wires.place["z"]

    def start(self, src):
        z, nz = self.z, self.nz
        if nz > 1:
            self.wires.send_if(z < nz - 1, src, self.spot(z), self.sem.at[1], z=1)
            self.wires.send_if(z > 0, src, self.spot(z), self.sem.at[nz - 1], z=nz - 1)

    def step_back(self, k):
        total = 0
        for i in range(self.nz):
            order = sorted(range(1, self.nz), key=lambda s: s if s <= i else self.nz - s)
            total = total + jnp.where(self.z == i, order[k - 1], 0)
        return total

    def arrive(self, k):
        z, nz = self.z, self.nz
        s = self.step_back(k)
        source = (z + nz - s) % nz
        spot = self.spot(source)
        pltpu.make_async_copy(spot, spot, self.sem.at[s]).wait()
        below = s <= z
        above = s > z
        self.wires.send_if(
            jnp.logical_and(below, z < nz - 1), spot, spot, self.sem.at[(s + 1) % nz], z=1
        )
        self.wires.send_if(
            jnp.logical_and(above, z > 0), spot, spot, self.sem.at[s - 1], z=nz - 1
        )
        return source

    @staticmethod
    def copies(nz):
        return 2 + 2 * (nz - 1)


class Gather:
    def __init__(self, wires, src, out, cut, sem):
        self.wires, self.src, self.out, self.cut = wires, src, out, cut
        self.n, self.at = wires.sizes, wires.place
        self.line = Line(wires, lambda i: self.spot(i, 0, 0), sem)
        self.source, self.to_y, self.to_x = {0: self.at["z"]}, {}, {}
        self.last = []

    def spot(self, chip_z, sy, sx, mats=slice(None)):
        rows, wide = self.src.shape[1], self.src.shape[2]
        n, at = self.n, self.at
        block = chip_z * n["y"] + (at["y"] + n["y"] - sy) % n["y"]
        column = (at["x"] + n["x"] - sx) % n["x"]
        return self.out.at[
            mats,
            pl.ds(pl.multiple_of(block * rows, rows), rows),
            pl.ds(pl.multiple_of(column * wide, wide), wide),
        ]

    def fan(self, k, src=None):
        spot = self.spot(self.source[k], 0, 0)
        src = spot if src is None else src
        for s in range(1, self.n["y"]):
            self.to_y[k, s] = self.wires.send(src, spot, y=s)
        for s in range(1, self.n["x"]):
            self.to_x[k, s] = self.wires.send(src, spot, x=s)

    def begin(self):
        self.line.start(self.src)
        self.fan(0, self.src)

    def arrive(self, k):
        self.source[k] = self.line.arrive(k)
        self.fan(k)

    def corner(self, k):
        count = self.src.shape[0]
        for sy in range(1, self.n["y"]):
            self.to_y[k, sy].wait_recv()
            part = self.spot(self.source[k], sy, 0, slice(0, self.cut))
            for s in range(1, self.n["x"]):
                self.last.append(self.wires.send(part, part, x=s))
        for sx in range(1, self.n["x"]):
            self.to_x[k, sx].wait_recv()
            if self.cut < count:
                part = self.spot(self.source[k], 0, sx, slice(self.cut, count))
                for s in range(1, self.n["y"]):
                    self.last.append(self.wires.send(part, part, y=s))

    def finish(self):
        for copy in self.last:
            copy.wait_recv()

    @staticmethod
    def copies(n):
        nz, ny, nx = n["z"], n["y"], n["x"]
        return Line.copies(nz) + nz * (ny - 1 + nx - 1) + 2 * nz * (ny - 1) * (nx - 1)


class RowGather:
    def __init__(self, wires, src, out, z_first, sem):
        self.wires, self.src, self.out, self.z_first = wires, src, out, z_first
        self.n, self.at = wires.sizes, wires.place
        spot = (lambda i: self.spot(i, 0)) if z_first else self.band
        self.line = Line(wires, spot, sem)
        self.to_y = []

    def spot(self, chip_z, sy):
        rows, ny = self.src.shape[0], self.n["y"]
        block = chip_z * ny + (self.at["y"] + ny - sy) % ny
        return self.out.at[pl.ds(pl.multiple_of(block * rows, rows), rows)]

    def band(self, chip_z):
        rows = self.src.shape[0] * self.n["y"]
        return self.out.at[pl.ds(pl.multiple_of(chip_z * rows, rows), rows)]

    def across(self, source, src=None):
        spot = self.spot(source, 0)
        src = spot if src is None else src
        for s in range(1, self.n["y"]):
            self.to_y.append(self.wires.send(src, spot, y=s))

    def begin(self):
        if self.z_first:
            self.line.start(self.src)
        self.across(self.at["z"], self.src)

    def turn(self):
        for copy in self.to_y:
            copy.wait_recv()
        self.line.start(self.band(self.at["z"]))

    def arrive(self, k):
        source = self.line.arrive(k)
        if self.z_first:
            self.across(source)

    def finish(self):
        if self.z_first:
            for copy in self.to_y:
                copy.wait_recv()

    @staticmethod
    def copies(n):
        return Line.copies(n["z"]) + n["z"] * (n["y"] - 1)


def norm_rows(values, p_ref, index):
    centered = values - jnp.mean(values, axis=-1, keepdims=True)
    variance = jnp.mean(centered * centered, axis=-1, keepdims=True)
    normed = centered * lax.rsqrt(variance + EPSILON)
    return (normed * p_ref[index : index + 1, :] + p_ref[index + 4 : index + 5, :]).astype(BF)


STRIP = 256


FORWARD_PLAN = (
    CROSS + FAN, SELF + FAN, SELF + LINE, SELF + PASS + 1, SELF + PASS + 2, CROSS + TURN + 0,
    STATES + GO, CROSS + LINE, SELF + PASS + 3, DOWN + BEGIN, MEMORY + GO, SELF + TURN + 0,
    CROSS + PASS + 1, SELF + TURN + 1, SELF + TURN + 3, STATES + ON, SELF + TURN + 2, UP + BEGIN,
    DOWN + LINE, STATES + TWIN, MEMORY + ON, STATES + END, CROSS + PASS + 2, DOWN + PASS + 1,
    FIRST + NORM, SELF + END, SELF + HEADS, CROSS + PASS + 3, SELF + TWIN + 0, CROSS + TURN + 1,
    SELF + TWIN + 1, MEMORY + TWIN, SELF + TWIN + 2, CROSS + TURN + 2, DOWN + PASS + 2,
    SELF + TWIN + 3, MEMORY + END, CROSS + TURN + 3, SELF + OUTPUT, UP + PASS + 1, UP + PASS + 2,
    SECOND + NORM, CROSS + END, MEMORY + HEADS, CROSS + QUERIES, CROSS + TWIN + 0,
    CROSS + TWIN + 1, UP + PASS + 3, CROSS + TWIN + 2, CROSS + TWIN + 3, CROSS + OUTPUT,
    DOWN + PASS + 3, UP + END, DOWN + END, THIRD + NORM,
)


def forward_plan(nz, pairs):
    if nz == 4 and pairs == 4:
        return FORWARD_PLAN
    passes = lambda group: [group + PASS + k for k in range(1, nz)]
    turns = lambda group: [group + TURN + k for k in range(nz)]
    plan = [STATES + GO, SELF + LINE, SELF + FAN, CROSS + LINE, CROSS + FAN, MEMORY + GO]
    plan += [STATES + ON, STATES + TWIN, STATES + END, FIRST + NORM]
    plan += passes(SELF) + turns(SELF) + [MEMORY + ON, MEMORY + TWIN, SELF + END]
    plan += [SELF + HEADS] + [SELF + TWIN + p for p in range(pairs)] + [SELF + OUTPUT]
    plan += [UP + BEGIN, DOWN + BEGIN] + passes(CROSS) + turns(CROSS) + passes(UP)
    plan += [SECOND + NORM, MEMORY + END, CROSS + END, DOWN + LINE, MEMORY + HEADS]
    plan += [CROSS + QUERIES] + [CROSS + TWIN + p for p in range(pairs)] + [CROSS + OUTPUT]
    return tuple(plan + passes(DOWN) + [THIRD + NORM, UP + END, DOWN + END])


def forward_kernel(
    n, own_rows, order, lengths, reaches, st_ref, me_ref, pr_ref, wa_ref, wf_ref,
    ows, owc, owf, op_ref, ofr, oin, oh1, oq, ok, ov, oo, ol, ox1, oh2, oq2, ok2, ov2, oo2, ol2,
    ox2, oh3,
    stage_s, pin_s, pall_s, p_s, wl_s, fl_s,
    x_s, m_s, w_s, c_s, h1_s, q_s, k_s, v_s, o_s, l_s, x1_s, h2_s, q2_s, k2_s, v2_s, o2_s, l2_s,
    x2_s, h3_s, give_s, got_s, score_s, weight_s,
    send_sem, recv_sem, self_sem, cross_sem, up_sem, down_sem, move_sem,
):
    at = grid_place()
    z, y, x, c = at["z"], at["y"], at["x"], at["c"]
    nz, ny, nx = n["z"], n["y"], n["x"]
    data, model = z * ny + y, x * 2 + c
    wires = Wires(n, at, send_sem, recv_sem)
    moves = Moves(move_sem)
    utterances, lines, deep = st_ref.shape
    mats = w_s.shape[0]
    for r in range(utterances):
        stage_s[0, r] = st_ref[order[r]]
        stage_s[1, r] = me_ref[order[r]]
    wl_s[...] = wa_ref[...].astype(BF)
    fl_s[...] = wf_ref[...].astype(BF)
    pin_s[...] = pr_ref[...].astype(BF).astype(F32)
    wires.greet(dp_shifts(n) + [{"x": s} for s in range(1, nx)] + [{"c": 1}])

    def patch(ref):
        return ref.at[
            pl.ds(pl.multiple_of(data * lines, lines), lines),
            pl.ds(pl.multiple_of(model * deep, deep), deep),
        ]

    def column(ref, sx, sc):
        index = ((x + nx - sx) % nx) * 2 + (c + 2 - sc) % 2
        return ref.at[:, pl.ds(pl.multiple_of(index * deep, deep), deep)]

    def spread(i, out):
        copies = []
        for shift in dp_shifts(n):
            target = wires.peer(**shift)[0]
            copies.append(wires.send(stage_s.at[i, target], patch(out), **shift))
        return copies, moves.start(stage_s.at[i, data], patch(out))

    def forward_columns(out, spreading):
        copies, own = spreading
        own.wait()
        for copy in copies:
            copy.wait_recv()
        near = [wires.send(column(out, 0, 0), column(out, 0, 0), x=s) for s in range(1, nx)]
        return near, [wires.send(column(out, 0, 0), column(out, 0, 0), c=1)]

    def pair_columns(out, near, pair):
        for s in range(1, nx):
            near[s - 1].wait_recv()
            pair.append(wires.send(column(out, s, 0), column(out, s, 0), c=1))

    own_self = wl_s.at[0:mats]
    own_cross = wl_s.at[mats : 2 * mats]
    near_self = Gather(wires, own_self, w_s, mats // 2, self_sem)
    near_cross = Gather(wires, own_cross, c_s, mats // 2, cross_sem)
    up_gather = RowGather(wires, fl_s.at[0], owf.at[0], True, up_sem)
    down_gather = RowGather(wires, fl_s.at[1], owf.at[1], False, down_sem)
    here = [
        moves.start(own_self, near_self.spot(z, 0, 0)),
        moves.start(own_cross, near_cross.spot(z, 0, 0)),
        moves.start(pin_s, pall_s.at[data]),
    ]
    down_here = moves.start(fl_s.at[1], down_gather.spot(z, 0))
    up_here = moves.start(fl_s.at[0], up_gather.spot(z, 0))
    params = [wires.send(pin_s, pall_s.at[data], **shift) for shift in dp_shifts(n)]
    slot, width = x_s.shape
    chip_rows = 2 * own_rows
    chip_start = x * chip_rows
    strip = min(STRIP, own_rows)
    pairs = q_s.shape[1] // PAIR
    own = pl.ds(pl.multiple_of(c * own_rows, own_rows), own_rows)
    held = {}
    steps = {}

    def step(name):
        def keep(function):
            steps[name] = function
            return function

        return keep

    for name, i, ref in ((STATES, 0, x_s), (MEMORY, 1, m_s)):

        def go(name=name, i=i, ref=ref):
            held[name] = spread(i, ref)

        def on(name=name, ref=ref):
            held[name] = forward_columns(ref, held[name])

        def pair(name=name, ref=ref):
            pair_columns(ref, *held[name])

        def end(name=name):
            for copy in held[name][1]:
                copy.wait_recv()

        steps.update(
            {name + GO: go, name + ON: on, name + TWIN: pair, name + END: end}
        )
    for name, gather in ((SELF, near_self), (CROSS, near_cross)):
        steps[name + LINE] = functools.partial(gather.line.start, gather.src)
        steps[name + FAN] = functools.partial(gather.fan, 0, gather.src)
        for k in range(nz):
            steps[name + PASS + k] = functools.partial(gather.arrive, k)
            steps[name + TURN + k] = functools.partial(gather.corner, k)
    for name, gather in ((UP, up_gather), (DOWN, down_gather)):
        steps[name + BEGIN] = gather.begin
        steps[name + END] = gather.finish
        for k in range(1, nz):
            steps[name + PASS + k] = functools.partial(gather.arrive, k)

    @step(DOWN + LINE)
    def _():
        down_here.wait()
        down_gather.turn()

    @step(SELF + END)
    def _():
        for copy in here[:1]:
            copy.wait()
        near_self.finish()
        moves.store(w_s, ows)

    @step(CROSS + END)
    def _():
        here[1].wait()
        near_cross.finish()
        moves.store(c_s, owc)

    @step(FIRST + NORM)
    def _():
        for copy in params:
            copy.wait_recv()
        here[2].wait()
        for i in range(nz * ny):
            columns = pall_s.shape[2]
            p_s[:, i * columns : (i + 1) * columns] = pall_s[i]
        op_ref[...] = p_s[...]

        def first_norm(rows):
            h1_s[rows, :] = norm_rows(x_s[rows, :].astype(F32), p_s, 0)

        loop_rows(slot, strip, first_norm)
        moves.store(h1_s, oh1)
        moves.store(x_s.at[pl.ds(pl.multiple_of(model * own_rows, own_rows), own_rows)], oin)

    @step(SELF + HEADS)
    def _():
        mat_rows(q_s, h1_s, w_s.at[0], chip_rows, strip, chip_start)
        mat_rows(k_s, h1_s, w_s.at[1], slot, strip)
        mat_rows(v_s, h1_s, w_s.at[2], slot, strip)
        for ref, out in ((q_s, oq), (k_s, ok), (v_s, ov)):
            moves.store(ref, out)

    @step(MEMORY + HEADS)
    def _():
        mat_rows(k2_s, m_s, c_s.at[1], slot, strip)
        mat_rows(v2_s, m_s, c_s.at[2], slot, strip)
        for ref, out in ((k2_s, ok2), (v2_s, ov2), (m_s, ofr)):
            moves.store(ref, out)

    @step(CROSS + QUERIES)
    def _():
        mat_rows(q2_s, h2_s, c_s.at[0], chip_rows, strip)
        moves.store(q2_s, oq2)

    reach_self = lax.broadcasted_iota(jnp.int32, (1, chip_rows), 1) + chip_start + 1
    reach_self = jnp.minimum(reach_self, lengths[order[data]])
    reach_cross = jnp.full((1, chip_rows), reaches[order[data]], jnp.int32)
    for p in range(pairs):

        def self_pair(p=p):
            attend_pair(p, 256, reach_self, q_s, k_s, v_s, o_s, l_s, score_s, weight_s)

        def cross_pair(p=p):
            attend_pair(p, 256, reach_cross, q2_s, k2_s, v2_s, o2_s, l2_s, score_s, weight_s)

        steps[SELF + TWIN + p] = self_pair
        steps[CROSS + TWIN + p] = cross_pair

    def give(index, mixed, out_map):
        def body(rows):
            give_s[index, rows, :] = dot(mixed[rows, :], out_map[...], 1, 1).astype(BF)

        loop_rows(chip_rows, strip, body)
        held[index] = wires.send(give_s.at[index], got_s.at[index], c=1)

    def total(index, rows):
        return give_s[index, rows, :].astype(F32) + got_s[index, rows, :].astype(F32)

    @step(SELF + OUTPUT)
    def _():
        moves.store(o_s, oo)
        moves.store(l_s, ol)
        give(0, o_s, w_s.at[3])

    @step(CROSS + OUTPUT)
    def _():
        moves.store(o2_s, oo2)
        moves.store(l2_s, ol2)
        give(1, o2_s, c_s.at[3])

    @step(SECOND + NORM)
    def _():
        held[0].wait_recv()

        def second_norm(rows):
            values = x_s[shifted(rows, chip_start), :].astype(F32) + total(0, rows)
            x1_s[rows, :] = values
            h2_s[rows, :] = norm_rows(values, p_s, 1)

        loop_rows(chip_rows, strip, second_norm)
        moves.store(x1_s.at[own], ox1)
        moves.store(h2_s, oh2)

    @step(THIRD + NORM)
    def _():
        held[1].wait_recv()

        def third_norm(rows):
            values = x1_s[rows, :] + total(1, rows)
            x2_s[rows, :] = values
            h3_s[rows, :] = norm_rows(values, p_s, 2)

        loop_rows(chip_rows, strip, third_norm)
        moves.store(x2_s.at[own], ox2)
        moves.store(h3_s, oh3)

    for name in forward_plan(nz, pairs):
        steps[name]()
    up_here.wait()
    moves.close()
    wires.close()


def forward(order, lengths, reaches, states, memory, params, attn, ffn, own_rows):
    n = grid_sizes()
    nz, ny, nx = n["z"], n["y"], n["x"]
    data = nz * ny
    utterances, lines, deep = states.shape
    slot, width = lines * data, deep * 2 * nx
    mats = attn.shape[0] // 2
    local = attn.shape[2] * nx
    hidden = ffn.shape[2]
    chip_rows = 2 * own_rows
    pairs = local // PAIR
    copies = (
        2 * Gather.copies(n) + 2 * RowGather.copies(n) + 3 * (data - 1) + 2 * (2 * (nx - 1) + 1) + 2
    )
    vmem = pl.BlockSpec(memory_space=pltpu.VMEM)
    smem = pl.BlockSpec(memory_space=pltpu.SMEM)
    hbm = pl.BlockSpec(memory_space=pl.ANY)
    half = lambda *shape: (shape, BF)
    full = lambda *shape: (shape, F32)
    saved = [
        half(slot, width),
        half(chip_rows, local),
        half(slot, local),
        half(slot, local),
        half(chip_rows, local),
        full(pairs, 2, chip_rows),
        full(own_rows, width),
        half(chip_rows, width),
        half(chip_rows, local),
        half(slot, local),
        half(slot, local),
        half(chip_rows, local),
        full(pairs, 2, chip_rows),
        full(own_rows, width),
        half(chip_rows, width),
    ]
    outs = [
        half(mats, width, local),
        half(mats, width, local),
        half(2, width, hidden),
        full(params.shape[0], width),
        half(slot, width),
        half(own_rows, width),
    ] + saved
    scratch = [
        half(2, utterances, lines, deep),
        full(*params.shape),
        full(data, *params.shape),
        full(params.shape[0], width),
        half(*attn.shape),
        half(*ffn.shape),
        half(slot, width),
        half(slot, width),
        half(mats, width, local),
        half(mats, width, local),
        half(slot, width),
        half(chip_rows, local),
        half(slot, local),
        half(slot, local),
        half(chip_rows, local),
        full(pairs, 2, chip_rows),
        full(chip_rows, width),
        half(chip_rows, width),
        half(chip_rows, local),
        half(slot, local),
        half(slot, local),
        half(chip_rows, local),
        full(pairs, 2, chip_rows),
        full(chip_rows, width),
        half(chip_rows, width),
        half(2, chip_rows, width),
        half(2, chip_rows, width),
        full(2, slot, chip_rows),
        half(2, slot, chip_rows),
    ]
    return pl.pallas_call(
        functools.partial(forward_kernel, n, own_rows),
        out_shape=[jax.ShapeDtypeStruct(s, t) for s, t in outs],
        in_specs=[smem, smem, smem, vmem, vmem, vmem, vmem, vmem],
        out_specs=[hbm] * 3 + [vmem] + [hbm] * (len(outs) - 4),
        scratch_shapes=[pltpu.VMEM(s, t) for s, t in scratch]
        + [
            pltpu.SemaphoreType.DMA((copies,)),
            pltpu.SemaphoreType.DMA((copies,)),
        ]
        + [pltpu.SemaphoreType.DMA((nz,))] * 4
        + [pltpu.SemaphoreType.DMA((32,))],
        compiler_params=pltpu.CompilerParams(
            collective_id=3, has_side_effects=True, vmem_limit_bytes=56 * 2**20
        ),
        name="forward",
    )(order, lengths, reaches, states, memory, params, attn, ffn)


def early_zones(n):
    return [n["z"] - 1, n["z"] - 3] if n["z"] >= 4 else []


def norm_back_rows(values, grad, gain):
    centered = values - jnp.mean(values, axis=-1, keepdims=True)
    scale = lax.rsqrt(jnp.mean(centered * centered, axis=-1, keepdims=True) + EPSILON)
    normed = centered * scale
    up = grad * gain
    back = scale * (
        up
        - jnp.mean(up, axis=-1, keepdims=True)
        - normed * jnp.mean(up * normed, axis=-1, keepdims=True)
    )
    return back, normed


def row_sum(values):
    return jnp.sum(values, axis=0, keepdims=True)


SPLIT = 2


def ffn_kernel(
    n, order, lengths, h_hbm, x_ref, w_hbm, ct_ref, p_ref,
    oy_ref, odx_ref, odc, odw, oe, on_ref,
    h_s, f_s, a_s, d_s, u_s, w_s, keep_s, far_s, give_s, got_s, cross_s, crossed_s, back_s, come_s,
    x3_s, dx3_s, dc_s, dw_s, early_s, send_sem, recv_sem, move_sem,
):
    at = grid_place()
    wires = Wires(n, at, send_sem, recv_sem)
    moves = Moves(move_sem)
    nx, c = n["x"], at["c"]
    length = lengths[order[at["z"] * n["y"] + at["y"]]]
    own, width = x_ref.shape
    part = own // SPLIT
    start_own = pl.multiple_of(c * own, own)
    start_other = pl.multiple_of((1 - c) * own, own)
    get_w = moves.start(w_hbm, w_s)
    get_own = moves.start(h_hbm.at[pl.ds(start_own, own)], h_s.at[pl.ds(0, own)])
    get_other = moves.start(h_hbm.at[pl.ds(start_other, own)], h_s.at[pl.ds(own, own)])
    ny = n["y"]
    wires.greet(
        [{"x": s} for s in range(1, nx)] + [{"y": s} for s in range(1, ny)] + [{"c": 1}]
    )

    def far_at(t, k, j):
        return 2 * own + (((t - 1) * SPLIT + k) * 2 + j) * part

    def spread(src, dst, k):
        return [
            wires.send(src.at[pl.ds(k * part, part)], dst.at[pl.ds(far_at(t, k, 0), part)], x=t)
            for t in range(1, nx)
        ]

    def onward(dst, t, k):
        return wires.send(
            dst.at[pl.ds(far_at(t, k, 0), part)], dst.at[pl.ds(far_at(t, k, 1), part)], c=1
        )

    def up(rows):
        hidden = dot(h_s[rows, :], w_s[0], 1, 0)
        inner = 0.7978845608028654 * (hidden + 0.044715 * (hidden * hidden * hidden))
        bend = jnp.tanh(inner)
        a_s[rows, :] = (0.5 * hidden * (1.0 + bend)).astype(BF)
        slope = 0.7978845608028654 * (1.0 + 0.134145 * (hidden * hidden))
        d_s[rows, :] = 0.5 * (1.0 + bend) + 0.5 * hidden * (1.0 - bend * bend) * slope
        return dot(a_s[rows, :], w_s[1], 1, 1)

    def down(rows):
        grad = dot(f_s[rows, :], w_s[1], 1, 0)
        u_s[rows, :] = (grad * d_s[rows, :]).astype(BF)
        return dot(u_s[rows, :], w_s[0], 1, 1)

    def other_core(phase, work):
        give_s[phase] = work(slice(own, 2 * own)).astype(BF)
        return wires.send(give_s.at[phase], got_s.at[phase], c=1)

    def far_part(phase, work, t, k):
        sums = work(slice(far_at(t, k, 0), far_at(t, k, 0) + 2 * part))
        far_s[t - 1, k] = sums[:part]
        cross_s[phase, t - 1, k] = sums[part:].astype(BF)
        return wires.send(cross_s.at[phase, t - 1, k], crossed_s.at[phase, t - 1, k], c=1)

    def return_part(phase, t, k, crossing):
        crossing.wait_recv()
        back_s[phase, t - 1, k] = (far_s[t - 1, k] + crossed_s[phase, t - 1, k].astype(F32)).astype(
            BF
        )
        return wires.send(back_s.at[phase, t - 1, k], come_s.at[phase, t - 1, k], x=nx - t)

    def far_phase(phase, work, buffer, arriving, arrived=None):
        homing = {}
        for k in range(SPLIT):
            crossed = []
            for t in range(1, nx):
                arriving[k][t - 1].wait_recv()
                crossed.append(onward(buffer, t, k))
            crossing = []
            for copy in crossed:
                copy.wait_recv()
            if arrived is not None and k == SPLIT - 1:
                arrived()
            for t in range(1, nx):
                crossing.append(far_part(phase, work, t, k))
            for t in range(1, nx):
                homing[k, t] = return_part(phase, t, k, crossing[t - 1])
        return homing

    def own_part(phase, k, homing):
        rows = slice(k * part, (k + 1) * part)
        total = keep_s[rows, :] + got_s[phase, rows, :].astype(F32)
        for t in range(1, nx):
            homing[k, t].wait_recv()
            total = total + come_s[phase, t - 1, k].astype(F32)
        return total

    get_own.wait()
    arriving = [spread(h_s, h_s, k) for k in range(SPLIT)]
    get_w.wait()
    get_other.wait()
    swap = other_core(0, up)
    keep_s[...] = up(slice(0, own))
    homing = far_phase(0, up, h_s, arriving)
    swap.wait_recv()
    gain_final, bias_final = 0.0, 0.0
    arriving, near = [], []
    first_row = (at["x"] * 2 + c) * own
    for k in range(SPLIT):
        rows = slice(k * part, (k + 1) * part)
        values = x_ref[rows, :] + own_part(0, k, homing)
        x3 = values
        centered = x3 - jnp.mean(x3, axis=-1, keepdims=True)
        variance = jnp.mean(centered * centered, axis=-1, keepdims=True)
        normed = centered * lax.rsqrt(variance + EPSILON)
        oy_ref[rows, :] = (normed * p_ref[3:4, :] + p_ref[7:8, :]).astype(BF)
        position = lax.broadcasted_iota(jnp.int32, (part, 1), 0) + (first_row + k * part)
        seed = jnp.where(position < length, ct_ref[rows, :].astype(F32), 0.0)
        grad, normed = norm_back_rows(x3, seed, p_ref[3:4, :])
        gain_final = gain_final + row_sum(seed * normed)
        bias_final = bias_final + row_sum(seed)
        dx3_s[rows, :] = grad
        f_s[rows, :] = grad.astype(BF)
        arriving.append(spread(f_s, f_s, k))
        near.append(
            wires.send(f_s.at[pl.ds(k * part, part)], f_s.at[pl.ds(own + k * part, part)], c=1)
        )
    keep_s[...] = down(slice(0, own))
    for copy in near:
        copy.wait_recv()
    swap = other_core(1, down)
    rows_each = width // (n["z"] * ny)
    zone_rows = ny * rows_each
    early = early_zones(n)
    ahead = []

    def strip_of(i, left, right, m):
        start = flipped(at["z"], m) * zone_rows
        cols = pl.ds(pl.multiple_of(start, zone_rows), zone_rows)
        dw_s[i, cols, :] = dot(left[:, cols], right[...], 0, 0).astype(BF)
        return start

    def start_early():
        for index, m in enumerate(early):
            start = strip_of(1, f_s, a_s, m)
            for t in range(1, ny):
                band = start + (at["y"] + t) % ny * rows_each
                band = pl.ds(pl.multiple_of(band, rows_each), rows_each)
                ahead.append(wires.send(dw_s.at[1, band], early_s.at[t - 1, index], y=t))

    homing = far_phase(1, down, f_s, arriving, start_early)
    for m in range(n["z"]):
        if m not in early:
            strip_of(1, f_s, a_s, m)
    moves.store(dw_s.at[1], odw.at[1])
    for m in range(n["z"]):
        strip_of(0, h_s, u_s, m)
    moves.store(dw_s.at[0], odw.at[0])
    swap.wait_recv()
    gain_third, bias_third = 0.0, 0.0
    near = []
    for k in range(SPLIT):
        rows = slice(k * part, (k + 1) * part)
        upstream = own_part(1, k, homing)
        grad, normed = norm_back_rows(x_ref[rows, :], upstream, p_ref[2:3, :])
        gain_third = gain_third + row_sum(upstream * normed)
        bias_third = bias_third + row_sum(upstream)
        total = dx3_s[rows, :] + grad
        odx_ref[rows, :] = total
        here = pl.ds(start_own + k * part, part)
        dc_s[here, :] = total.astype(BF)
        near.append(wires.send(dc_s.at[here], dc_s.at[here], c=1))
    line = lax.broadcasted_iota(jnp.int32, on_ref.shape, 0)
    sums = jnp.zeros(on_ref.shape, F32)
    for index, value in ((2, gain_third), (3, gain_final), (6, bias_third), (7, bias_final)):
        sums = sums + jnp.where(line == index, value, 0.0)
    on_ref[...] = sums
    for copy in near:
        copy.wait_recv()
    moves.store(dc_s, odc)
    for copy in ahead:
        copy.wait_recv()
    moves.store(early_s, oe)
    moves.close()
    wires.close()


def feed_forward(order, lengths, normed, resid, maps, cotangent, params):
    n = grid_sizes()
    chip_rows, width = normed.shape
    own = chip_rows // 2
    hidden = maps.shape[2]
    nx = n["x"]
    rows = chip_rows * nx
    part = own // SPLIT
    rows_each = width // (n["z"] * n["y"])
    ahead = (n["y"] - 1, len(early_zones(n)), rows_each, hidden)
    copies = 2 * (SPLIT * (nx - 1) * 4 + 1) + 2 * SPLIT + ahead[0] * ahead[1]
    vmem = pl.BlockSpec(memory_space=pltpu.VMEM)
    smem = pl.BlockSpec(memory_space=pltpu.SMEM)
    hbm = pl.BlockSpec(memory_space=pl.ANY)
    far = (2, nx - 1, SPLIT, part, width)
    return pl.pallas_call(
        functools.partial(ffn_kernel, n),
        out_shape=[
            jax.ShapeDtypeStruct((own, width), BF),
            jax.ShapeDtypeStruct((own, width), F32),
            jax.ShapeDtypeStruct((chip_rows, width), BF),
            jax.ShapeDtypeStruct((2, width, hidden), BF),
            jax.ShapeDtypeStruct(ahead, BF),
            jax.ShapeDtypeStruct(params.shape, F32),
        ],
        in_specs=[smem, smem, hbm, vmem, hbm, vmem, vmem],
        out_specs=[vmem, vmem, hbm, hbm, hbm, vmem],
        scratch_shapes=[
            pltpu.VMEM((rows, width), BF),
            pltpu.VMEM((rows, width), BF),
            pltpu.VMEM((rows, hidden), BF),
            pltpu.VMEM((rows, hidden), F32),
            pltpu.VMEM((rows, hidden), BF),
            pltpu.VMEM((2, width, hidden), BF),
            pltpu.VMEM((own, width), F32),
            pltpu.VMEM((nx - 1, SPLIT, part, width), F32),
            pltpu.VMEM((2, own, width), BF),
            pltpu.VMEM((2, own, width), BF),
            pltpu.VMEM(far, BF),
            pltpu.VMEM(far, BF),
            pltpu.VMEM(far, BF),
            pltpu.VMEM(far, BF),
            pltpu.VMEM((own, width), F32),
            pltpu.VMEM((own, width), F32),
            pltpu.VMEM((chip_rows, width), BF),
            pltpu.VMEM((2, width, hidden), BF),
            pltpu.VMEM(ahead, BF),
            pltpu.SemaphoreType.DMA((copies,)),
            pltpu.SemaphoreType.DMA((copies,)),
            pltpu.SemaphoreType.DMA((8,)),
        ],
        compiler_params=pltpu.CompilerParams(
            collective_id=4, has_side_effects=True, vmem_limit_bytes=56 * 2**20
        ),
        name="feed_forward",
    )(order, lengths, normed, resid, maps, cotangent, params)


CROSS_PLAN = (
    UP + BEGIN + 3, DOWN + ALONG + 1, LOAD, HEADS, DOWN + ALONG + 3, GRAD + OUTPUT,
    DOWN + BEGIN + 2, OUT + BEGIN + 3, TWIN + 0, OUT + BEGIN + 2, UP + ALONG + 3,
    OUT + BEGIN + 1, UP + BEGIN + 1, UP + BEGIN + 2, TWIN + 1, OUT + BEGIN + 0, TWIN + 2,
    DOWN + ALONG + 2, TWIN + 3, GRAD + QUERIES, QUERY + BEGIN + 1, QUERY + BEGIN + 3,
    QUERY + BEGIN + 2, MEMORY + PART, QUERY + BEGIN + 0, DOWN + BEGIN + 0, OUT + MIDDLE + 3,
    GRAD + TWIN, OUT + MIDDLE + 1, UP + ALONG + 1, INPUT + PART, QUERY + MIDDLE + 3,
    UP + ALONG + 2, OUT + MIDDLE + 2, OUT + ALONG + 3, MEMORY + ON, QUERY + MIDDLE + 1,
    OUT + ALONG + 1, OUT + MIDDLE + 0, QUERY + ALONG + 3, QUERY + MIDDLE + 2, UP + BEGIN + 0,
    OUT + ALONG + 2, DOWN + ALONG + 0, NORM, QUERY + MIDDLE + 0, QUERY + ALONG + 1,
    QUERY + ALONG + 2, OUT + ALONG + 0, ROWS + END, MEMORY + END, UP + ALONG + 0,
    QUERY + ALONG + 0,
)

SELF_PLAN = (
    MEMORY + GO, LOAD + OTHER, LOAD, CROSS + BEGIN + 3, CROSS + BEGIN + 2, GRAD + OUTPUT,
    OUT + BEGIN + 1, CROSS + BEGIN + 1, OUT + BEGIN + 0, HEADS, OUT + BEGIN + 3, OUT + BEGIN + 2,
    TWIN + 0, TWIN + 1, CROSS + MIDDLE + 3, TWIN + 2, TWIN + 3, GRAD + QUERIES, OUT + MIDDLE + 3,
    QUERY + BEGIN + 3, QUERY + BEGIN + 1, GRAD + TWIN, KEYS + BEGIN + 3, INPUT + PART,
    OUT + MIDDLE + 2, CROSS + ALONG + 3, OUT + ALONG + 3, CROSS + MIDDLE + 2, INPUT + ON,
    KEYS + BEGIN + 2, QUERY + MIDDLE + 3, OUT + MIDDLE + 1, KEYS + MIDDLE + 3, KEYS + MIDDLE + 2,
    OUT + ALONG + 2, CROSS + ALONG + 2, KEYS + BEGIN + 1, QUERY + BEGIN + 2, MEMORY + END,
    QUERY + MIDDLE + 1, OUT + ALONG + 1, QUERY + ALONG + 3, NORM, KEYS + ALONG + 3,
    QUERY + ALONG + 1, CROSS + BEGIN + 0, CROSS + MIDDLE + 1, QUERY + MIDDLE + 2,
    KEYS + ALONG + 2, QUERY + BEGIN + 0, HOME + END, KEYS + BEGIN + 0, KEYS + MIDDLE + 1,
    CROSS + MIDDLE + 0, OUT + MIDDLE + 0, CROSS + ALONG + 1, QUERY + ALONG + 2,
    KEYS + MIDDLE + 0, KEYS + ALONG + 1, QUERY + MIDDLE + 0, QUERY + ALONG + 0,
    CROSS + ALONG + 0, OUT + ALONG + 0, KEYS + ALONG + 0,
)

def backward_plan(tuned, nz, pairs, head, parts, tail):
    if nz == 4 and pairs == 4:
        return tuned
    plan = list(head) + [TWIN + p for p in range(pairs)] + list(parts)
    return tuple(plan) + tuple(tail)


class Halving:
    def zones(self):
        return range(self.n["z"] - 1, -1, -1)

    def zone(self, m):
        return flipped(self.at["z"], m)

    def sources(self, m):
        top = (m & -m) if m else self.n["z"]
        found, bit = [], 1
        while bit < top:
            found.append(m + bit)
            bit *= 2
        return found

    def settle(self, m, total, out):
        for k in self.sources(m):
            self.by_z[k].wait_recv()
            total = total + self.r3[k - 1].astype(F32)
        if m:
            self.s3[m - 1] = total.astype(BF)
            self.by_z[m] = self.wires.send(self.s3.at[m - 1], self.r3.at[m - 1], flip=m & -m)
        else:
            out[...] = total


def flips(n):
    found, bit = [], 1
    while bit < n["z"]:
        found.append({"flip": bit})
        bit *= 2
    return found


class RowScatter(Halving):
    def __init__(self, wires, moves, src, own, r1, s3, r3, out, ahead=None):
        self.wires, self.moves, self.src, self.own = wires, moves, src, own
        self.r1, self.s3, self.r3, self.out = r1, s3, r3, out
        self.n, self.at = wires.sizes, wires.place
        self.by_y, self.by_z = {}, {}
        self.loads = {m: moves.start(self.band(m, 0), own.at[m]) for m in self.zones()}
        self.early = []
        if ahead is not None:
            self.early = early_zones(self.n)
            for i, m in enumerate(self.early):
                for t in range(1, self.n["y"]):
                    self.by_y[m, t] = moves.start(ahead.at[t - 1, i], r1.at[t - 1, m])

    def band(self, m, t):
        rows = self.own.shape[1]
        index = self.zone(m) * self.n["y"] + (self.at["y"] + t) % self.n["y"]
        return self.src.at[pl.ds(pl.multiple_of(index * rows, rows), rows)]

    def begin(self, m):
        if m in self.early:
            return
        for t in range(1, self.n["y"]):
            self.by_y[m, t] = self.wires.send(self.band(m, t), self.r1.at[t - 1, m], y=t)

    def along(self, m):
        self.loads[m].wait()
        total = self.own[m].astype(F32)
        for t in range(1, self.n["y"]):
            if m in self.early:
                self.by_y[m, t].wait()
            else:
                self.by_y[m, t].wait_recv()
            total = total + self.r1[t - 1, m].astype(F32)
        self.settle(m, total, self.out)

    @staticmethod
    def copies(n):
        return n["z"] * (n["y"] - 1) + n["z"] - 1

    @staticmethod
    def scratch(n, rows, wide):
        nz, ny = n["z"], n["y"]
        return [
            pltpu.VMEM((nz, rows, wide), BF),
            pltpu.VMEM((ny - 1, nz, rows, wide), BF),
            pltpu.VMEM((nz - 1, rows, wide), BF),
            pltpu.VMEM((nz - 1, rows, wide), BF),
        ]


class Scatter(Halving):
    def __init__(self, wires, grads, first, count, x_first, r1, s2, r2, acc, s3, r3, out):
        self.wires, self.grads = wires, grads
        self.first, self.count, self.x_first = first, count, x_first
        self.r1, self.s2, self.r2, self.acc, self.s3, self.r3 = r1, s2, r2, acc, s3, r3
        self.out = out
        self.n, self.at = wires.sizes, wires.place
        self.rows, self.wide = acc.shape[2], acc.shape[3]
        self.stage1, self.stage2, self.by_z = {}, {}, {}

    def part(self, m, band, bands, column, columns):
        rows, wide = self.rows, self.wide
        start = self.zone(m) * self.n["y"] + band
        return self.grads.at[
            pl.ds(self.first, self.count),
            pl.ds(pl.multiple_of(start * rows, rows), bands * rows),
            pl.ds(pl.multiple_of(column * wide, wide), columns * wide),
        ]

    def begin(self, m):
        nx, ny = self.n["x"], self.n["y"]
        if self.x_first:
            for t in range(1, nx):
                src = self.part(m, 0, ny, (self.at["x"] + t) % nx, 1)
                self.stage1[m, t] = self.wires.send(src, self.r1.at[t - 1, m], x=t)
        else:
            for t in range(1, ny):
                src = self.part(m, (self.at["y"] + t) % ny, 1, 0, nx)
                self.stage1[m, t] = self.wires.send(src, self.r1.at[t - 1, m], y=t)

    def middle(self, m):
        nx, ny, rows, wide = self.n["x"], self.n["y"], self.rows, self.wide
        x, y = self.at["x"], self.at["y"]
        inner, outer = (ny, nx) if self.x_first else (nx, ny)
        for t in range(1, outer):
            self.stage1[m, t].wait_recv()
        for b in range(inner):
            if self.x_first:
                band = (y + b) % ny
                total = self.part(m, band, 1, x, 1)[...].astype(F32)
                here = (slice(None), pl.ds(pl.multiple_of(band * rows, rows), rows), slice(None))
            else:
                column = (x + b) % nx
                total = self.part(m, y, 1, column, 1)[...].astype(F32)
                here = (slice(None), slice(None), pl.ds(pl.multiple_of(column * wide, wide), wide))
            for t in range(1, outer):
                total = total + self.r1.at[t - 1, m][here].astype(F32)
            if b == 0:
                self.acc[m] = total
            else:
                self.s2[b - 1, m] = total.astype(BF)
        for t in range(1, inner):
            way = {"y": t} if self.x_first else {"x": t}
            self.stage2[m, t] = self.wires.send(self.s2.at[t - 1, m], self.r2.at[t - 1, m], **way)

    def along(self, m):
        inner = self.n["y"] if self.x_first else self.n["x"]
        total = self.acc[m]
        for t in range(1, inner):
            self.stage2[m, t].wait_recv()
            total = total + self.r2[t - 1, m].astype(F32)
        self.settle(m, total, self.out)

    @staticmethod
    def copies(n):
        nz, ny, nx = n["z"], n["y"], n["x"]
        return nz * (nx - 1 + ny - 1) + nz - 1

    @staticmethod
    def scratch(n, count, x_first, rows, wide):
        nz, ny, nx = n["z"], n["y"], n["x"]
        inner = ny if x_first else nx
        if x_first:
            first = (nx - 1, nz, count, ny * rows, wide)
        else:
            first = (ny - 1, nz, count, rows, nx * wide)
        return [
            pltpu.VMEM(first, BF),
            pltpu.VMEM((inner - 1, nz, count, rows, wide), BF),
            pltpu.VMEM((inner - 1, nz, count, rows, wide), BF),
            pltpu.VMEM((nz, count, rows, wide), F32),
            pltpu.VMEM((nz - 1, count, rows, wide), BF),
            pltpu.VMEM((nz - 1, count, rows, wide), BF),
        ]


ONE = (8, 128)


def squares(refs):
    total = jnp.zeros(ONE, F32)
    for ref in refs:
        value = ref[...]
        total = total + jnp.sum((value * value).reshape((-1,) + ONE), axis=0)
    return total


def register(steps, name, group):
    for m in group.zones():
        steps[name + BEGIN + m] = functools.partial(group.begin, m)
        steps[name + ALONG + m] = functools.partial(group.along, m)
        if hasattr(group, "middle"):
            steps[name + MIDDLE + m] = functools.partial(group.middle, m)


def spelled(n, names):
    plan = []
    for name, kinds in names:
        for kind in kinds:
            plan += [name + kind + m for m in range(n["z"] - 1, -1, -1)]
    return plan


WHOLE = (BEGIN, MIDDLE, ALONG)


def cross_back_kernel(
    n, order, reaches, dc_hbm, dx_ref, w_hbm, q_hbm, k_hbm, v_hbm, o_hbm, l_ref, h_hbm, m_hbm, x_ref, p_ref,
    dw_hbm, early_hbm, oup_ref, odown_ref, oq_ref, oo_ref, og, odx_ref, odb, om, on_ref, osq_ref, *scratch,
):
    (
        dc_s, w_s, q_s, k_s, v_s, o_s, h_s, m_s, g_s, dq_s, dk_s, dv_s, ds_s, gr_s, give_s, got_s,
        db_s, pm_s, rm_s, sm_s, cm_s, om_s,
    ) = scratch[:22]
    send_sem, recv_sem, move_sem = scratch[-3:]
    at = grid_place()
    x, c = at["x"], at["c"]
    nz, ny, nx = n["z"], n["y"], n["x"]
    wires = Wires(n, at, send_sem, recv_sem)
    moves = Moves(move_sem)
    loads = [
        moves.start(a, b)
        for a, b in (
            (dc_hbm, dc_s), (w_hbm.at[3], w_s.at[3]), (o_hbm, o_s), (q_hbm, q_s), (k_hbm, k_s),
            (v_hbm, v_s),
        )
    ]
    down = RowScatter(wires, moves, dw_hbm.at[1], *scratch[22:26], odown_ref, early_hbm)
    up = RowScatter(wires, moves, dw_hbm.at[0], *scratch[26:30], oup_ref)
    out_sum = Scatter(wires, gr_s, 3, 1, True, *scratch[30:36], oo_ref)
    query_sum = Scatter(wires, gr_s, 0, 1, True, *scratch[36:42], oq_ref)
    later = [moves.start(h_hbm, h_s), moves.start(m_hbm, m_s)]
    get_maps = moves.start(w_hbm.at[0:3], w_s.at[0:3])
    wires.greet(
        flips(n)
        + [{"y": s} for s in range(1, ny)]
        + [{"x": s} for s in range(1, nx)]
        + [{"c": 1}]
    )
    chip_rows, width = dc_s.shape
    slot = m_s.shape[0]
    own = chip_rows // 2
    strip = min(STRIP, own)
    pairs = q_s.shape[1] // PAIR
    deep = om_s.shape[1]
    mine = pl.ds(pl.multiple_of(c * own, own), own)
    other = pl.ds(pl.multiple_of((1 - c) * own, own), own)
    bound = jnp.full((1, chip_rows), reaches[order[at["z"] * ny + at["y"]]], jnp.int32)
    held = {}
    steps = {}
    for name, group in ((DOWN, down), (UP, up), (OUT, out_sum), (QUERY, query_sum)):
        register(steps, name, group)

    def step(name):
        def keep(function):
            steps[name] = function
            return function

        return keep

    @step(LOAD)
    def _():
        for copy in loads:
            copy.wait()

    @step(HEADS)
    def _():
        mat_rows(g_s, dc_s, w_s.at[3], chip_rows, strip)

    for p in range(pairs):

        def pair(p=p):
            attend_pair_back(
                p, 256, bound, q_s, k_s, v_s, o_s, l_ref, g_s, dq_s, dk_s, dv_s, ds_s
            )

        steps[TWIN + p] = pair

    maps = [get_maps]

    def need_maps():
        while maps:
            maps.pop().wait()

    @step(INPUT + PART)
    def _():
        need_maps()

        def body(rows):
            give_s[rows, :] = dot(dq_s[rows, :], w_s[0], 1, 1).astype(BF)

        loop_rows(chip_rows, strip, body)
        held["rows"] = wires.send(give_s.at[other], got_s, c=1)

    @step(MEMORY + PART)
    def _():
        need_maps()
        piece = min(512, width)

        def body(rows):
            for col in range(0, width, piece):
                some = slice(col, col + piece)
                sums = dot(dk_s[rows, :], w_s[1, some, :], 1, 1)
                sums = (sums + dot(dv_s[rows, :], w_s[2, some, :], 1, 1)).astype(BF)
                for b in range(piece // deep):
                    index = col // deep + b
                    pm_s[index // 2, index % 2, rows, :] = sums[:, b * deep : (b + 1) * deep]

        loop_rows(slot, strip, body)
        held["memory"] = wires.send(pm_s.at[:, 1 - c], rm_s, c=1)

    @step(NORM)
    def _():
        held["rows"].wait_recv()
        upstream = give_s[mine, :].astype(F32) + got_s[...].astype(F32)
        grad, normed = norm_back_rows(x_ref[...], upstream, p_ref[1:2, :])
        total = dx_ref[...] + grad
        odx_ref[...] = total
        db_s[mine, :] = total.astype(BF)
        held["near"] = wires.send(db_s.at[mine], db_s.at[mine], c=1)
        line = lax.broadcasted_iota(jnp.int32, on_ref.shape, 0)
        on_ref[...] = jnp.where(line == 1, row_sum(upstream * normed), 0.0) + jnp.where(
            line == 5, row_sum(upstream), 0.0
        )

    @step(MEMORY + ON)
    def _():
        held["memory"].wait_recv()
        held["far"] = []
        for t in range(1, nx):
            index = (x + t) % nx
            sm_s[t - 1] = (pm_s[index, c].astype(F32) + rm_s[index].astype(F32)).astype(BF)
            held["far"].append(wires.send(sm_s.at[t - 1], cm_s.at[t - 1], x=t))

    @step(MEMORY + END)
    def _():
        total = pm_s[x, c].astype(F32) + rm_s[x].astype(F32)
        for t in range(1, nx):
            held["far"][t - 1].wait_recv()
            total = total + cm_s[t - 1].astype(F32)
        om_s[...] = total.astype(BF)
        moves.store(om_s, om)

    def weight_grad(i, left, right):
        size = min(256, width)
        for col in range(0, width, size):
            cols = slice(col, col + size)
            gr_s[i, cols, :] = dot(left[:, cols], right[...], 0, 0).astype(BF)

    @step(GRAD + OUTPUT)
    def _():
        weight_grad(3, dc_s, o_s)

    @step(GRAD + QUERIES)
    def _():
        later[0].wait()
        weight_grad(0, h_s, dq_s)

    @step(GRAD + TWIN)
    def _():
        later[1].wait()
        weight_grad(1, m_s, dk_s)
        weight_grad(2, m_s, dv_s)
        moves.store(gr_s.at[1:3], og)

    @step(ROWS + END)
    def _():
        held["near"].wait_recv()
        moves.store(db_s, odb)

    plan = backward_plan(
        CROSS_PLAN, nz, pairs,
        [LOAD, HEADS] + spelled(n, [(DOWN, (BEGIN,)), (UP, (BEGIN,))]),
        [INPUT + PART, MEMORY + PART, NORM, MEMORY + ON, GRAD + OUTPUT, GRAD + QUERIES, GRAD + TWIN],
        spelled(n, [(DOWN, (ALONG,)), (UP, (ALONG,)), (OUT, WHOLE), (QUERY, WHOLE)])
        + [MEMORY + END, ROWS + END],
    )
    for name in plan:
        steps[name]()
    osq_ref[...] = squares((oup_ref, odown_ref, oq_ref, oo_ref))
    moves.close()
    wires.close()


def cross_back(
    order, reaches, rows_grad, resid_grad, maps, saved, normed, frames, resid, params, ffn_grads,
    early,
):
    n = grid_sizes()
    nz, ny, nx = n["z"], n["y"], n["x"]
    queries, keys, values, mixed, logsum = saved
    chip_rows, width = rows_grad.shape
    own = chip_rows // 2
    slot, local = keys.shape
    hidden = ffn_grads.shape[2]
    rows, wide = width // (nz * ny), local // nx
    deep = width // (2 * nx)
    copies = 2 * RowScatter.copies(n) + 2 * Scatter.copies(n) + 3 + (nx - 1)
    vmem = pl.BlockSpec(memory_space=pltpu.VMEM)
    smem = pl.BlockSpec(memory_space=pltpu.SMEM)
    hbm = pl.BlockSpec(memory_space=pl.ANY)
    half = lambda *shape: pltpu.VMEM(shape, BF)
    return pl.pallas_call(
        functools.partial(cross_back_kernel, n),
        out_shape=[
            jax.ShapeDtypeStruct((rows, hidden), F32),
            jax.ShapeDtypeStruct((rows, hidden), F32),
            jax.ShapeDtypeStruct((1, rows, wide), F32),
            jax.ShapeDtypeStruct((1, rows, wide), F32),
            jax.ShapeDtypeStruct((2, width, local), BF),
            jax.ShapeDtypeStruct((own, width), F32),
            jax.ShapeDtypeStruct((chip_rows, width), BF),
            jax.ShapeDtypeStruct((slot, deep), BF),
            jax.ShapeDtypeStruct(params.shape, F32),
            jax.ShapeDtypeStruct(ONE, F32),
        ],
        in_specs=[smem, smem, hbm, vmem] + [hbm] * 5 + [vmem, hbm, hbm, vmem, vmem, hbm, hbm],
        out_specs=[vmem] * 4 + [hbm, vmem, hbm, hbm, vmem, vmem],
        scratch_shapes=[
            half(chip_rows, width),
            half(4, width, local),
            half(chip_rows, local),
            half(slot, local),
            half(slot, local),
            half(chip_rows, local),
            half(chip_rows, width),
            half(slot, width),
            half(chip_rows, local),
            half(chip_rows, local),
            half(slot, local),
            half(slot, local),
            half(2, slot, chip_rows),
            half(4, width, local),
            half(chip_rows, width),
            half(own, width),
            half(chip_rows, width),
            half(nx, 2, slot, deep),
            half(nx, slot, deep),
            half(nx - 1, slot, deep),
            half(nx - 1, slot, deep),
            half(slot, deep),
        ]
        + RowScatter.scratch(n, rows, hidden) * 2
        + Scatter.scratch(n, 1, True, rows, wide) * 2
        + [
            pltpu.SemaphoreType.DMA((copies,)),
            pltpu.SemaphoreType.DMA((copies,)),
            pltpu.SemaphoreType.DMA((14 + 2 * nz + 2 * (ny - 1),)),
        ],
        compiler_params=pltpu.CompilerParams(
            collective_id=5, has_side_effects=True, vmem_limit_bytes=56 * 2**20
        ),
        name="cross_back",
    )(
        order, reaches, rows_grad, resid_grad, maps, queries, keys, values, mixed, logsum, normed, frames,
        resid, params, ffn_grads, early,
    )


def self_back_kernel(
    n, order, lengths, db_hbm, dx_ref, w_hbm, q_hbm, k_hbm, v_hbm, o_hbm, l_ref, h_hbm, x_ref, p_ref,
    cg_hbm, m_hbm, np_ref, nq_ref, sq_ref, oc_ref, oo_ref, oq_ref, op_ref, os_ref, om_ref, on_ref,
    norm_ref, *scratch,
):
    (
        db_s, w_s, q_s, k_s, v_s, o_s, h_s, g_s, dq_s, dk_s, dv_s, ds_s, cg_s, gr_s, part_s, rc_s,
        sx_s, rx_s, out_s, np_s, nn_s, nf_s,
    ) = scratch[:22]
    one_s, near_s, sum_s, far_s = scratch[46:50]
    send_sem, recv_sem, go_sem, come_sem, move_sem = scratch[-5:]
    at = grid_place()
    z, y, x, c = at["z"], at["y"], at["x"], at["c"]
    nz, ny, nx = n["z"], n["y"], n["x"]
    data, model = z * ny + y, x * 2 + c
    wires = Wires(n, at, send_sem, recv_sem)
    moves = Moves(move_sem)
    get_cross = moves.start(cg_hbm, cg_s)
    loads = [
        moves.start(a, b)
        for a, b in (
            (db_hbm, db_s), (w_hbm.at[3], w_s.at[3]), (o_hbm, o_s), (q_hbm, q_s), (k_hbm, k_s),
            (v_hbm, v_s),
        )
    ]
    later = [moves.start(h_hbm, h_s), moves.start(w_hbm.at[0:3], w_s.at[0:3])]
    wires.greet(
        [
            dict(z=sz, y=sy, x=sx, c=sc)
            for sz in range(nz)
            for sy in range(ny)
            for sx in range(nx)
            for sc in range(2)
            if sz or sy or sx or sc
        ]
    )
    cross_sum = Scatter(wires, cg_s, 0, 2, False, *scratch[22:28], oc_ref)
    out_sum = Scatter(wires, gr_s, 3, 1, True, *scratch[28:34], oo_ref)
    query_sum = Scatter(wires, gr_s, 0, 1, True, *scratch[34:40], oq_ref)
    pair_sum = Scatter(wires, gr_s, 1, 2, False, *scratch[40:46], op_ref)
    chip_rows, width = db_s.shape
    slot = h_s.shape[0]
    own = chip_rows // 2
    strip = min(STRIP, own)
    pairs = q_s.shape[1] // PAIR
    chip_start = x * chip_rows
    bound = lax.broadcasted_iota(jnp.int32, (1, chip_rows), 1) + chip_start + 1
    bound = jnp.minimum(bound, lengths[order[data]])
    held = {}
    steps = {}
    for name, group in (
        (CROSS, cross_sum), (OUT, out_sum), (QUERY, query_sum), (KEYS, pair_sum)
    ):
        register(steps, name, group)

    def step(name):
        def keep(function):
            steps[name] = function
            return function

        return keep

    @step(LOAD + OTHER)
    def _():
        get_cross.wait()

    @step(LOAD)
    def _():
        for copy in loads:
            copy.wait()

    @step(MEMORY + GO)
    def _():
        held["memory"] = [
            wires.send(m_hbm.at[wires.peer(**shift)[0]], om_ref.at[data], **shift)
            for shift in dp_shifts(n)
        ]
        held["memory own"] = moves.start(m_hbm.at[data], om_ref.at[data])

    @step(MEMORY + END)
    def _():
        for copy in held["memory"]:
            copy.wait_recv()
        held["memory own"].wait()

    @step(HEADS)
    def _():
        mat_rows(g_s, db_s, w_s.at[3], chip_rows, strip)

    for p in range(pairs):

        def pair(p=p):
            attend_pair_back(
                p, 256, bound, q_s, k_s, v_s, o_s, l_ref, g_s, dq_s, dk_s, dv_s, ds_s
            )

        steps[TWIN + p] = pair

    def block(chip, core):
        return pl.ds(pl.multiple_of((chip * 2 + core) * own, own), own)

    def need(index):
        if later[index] is not None:
            later[index].wait()
            later[index] = None

    @step(INPUT + PART)
    def _():
        need(1)
        def keys_values(rows):
            sums = dot(dk_s[rows, :], w_s[1], 1, 1) + dot(dv_s[rows, :], w_s[2], 1, 1)
            part_s[rows, :] = sums.astype(BF)

        loop_rows(slot, strip, keys_values)

        def queries(rows):
            here = shifted(rows, chip_start)
            sums = part_s[here, :].astype(F32) + dot(dq_s[rows, :], w_s[0], 1, 1)
            part_s[here, :] = sums.astype(BF)

        loop_rows(chip_rows, strip, queries)
        held["core"] = [
            wires.send(part_s.at[block(b, 1 - c)], rc_s.at[b], c=1) for b in range(nx)
        ]

    @step(INPUT + ON)
    def _():
        for copy in held["core"]:
            copy.wait_recv()
        held["far"] = []
        for t in range(1, nx):
            index = (x + t) % nx
            sums = part_s[block(index, c), :].astype(F32) + rc_s[index].astype(F32)
            sx_s[t - 1] = sums.astype(BF)
            held["far"].append(wires.send(sx_s.at[t - 1], rx_s.at[t - 1], x=t))

    def weight_grad(i, left, right):
        size = min(256, width)
        for col in range(0, width, size):
            cols = slice(col, col + size)
            gr_s[i, cols, :] = dot(left[:, cols], right[...], 0, 0).astype(BF)

    @step(GRAD + OUTPUT)
    def _():
        weight_grad(3, db_s, o_s)

    @step(GRAD + QUERIES)
    def _():
        need(0)
        weight_grad(0, h_s.at[pl.ds(pl.multiple_of(chip_start, chip_rows), chip_rows)], dq_s)

    @step(GRAD + TWIN)
    def _():
        need(0)
        weight_grad(1, h_s, dk_s)
        weight_grad(2, h_s, dv_s)

    lines, deep = os_ref.shape[1], os_ref.shape[2]
    blocks = own // lines

    def homeward():
        for b in range(blocks):
            for m in range(2 * nx):
                target = (model * blocks + b, m)
                src = out_s.at[b * lines : (b + 1) * lines, m * deep : (m + 1) * deep]
                mine = jnp.logical_and(target[0] == data, model == m)
                remote = pltpu.make_async_remote_copy(
                    src_ref=src,
                    dst_ref=os_ref.at[data],
                    send_sem=go_sem.at[b * 2 * nx + m],
                    recv_sem=come_sem.at[data],
                    device_id=target,
                    device_id_type=pl.DeviceIdType.MESH,
                )
                yield mine, remote, pltpu.make_async_copy(src, os_ref.at[data], come_sem.at[data])

    @step(NORM)
    def _():
        upstream = part_s[block(x, c), :].astype(F32) + rc_s[x].astype(F32)
        for t in range(1, nx):
            held["far"][t - 1].wait_recv()
            upstream = upstream + rx_s[t - 1].astype(F32)
        grad, normed = norm_back_rows(x_ref[...].astype(F32), upstream, p_ref[0:1, :])
        out_s[...] = (dx_ref[...] + grad).astype(BF)
        for mine, remote, here in homeward():
            pl.when(mine)(lambda: here.start())
            pl.when(jnp.logical_not(mine))(lambda: remote.start())
        line = lax.broadcasted_iota(jnp.int32, np_ref.shape, 0)
        params = (
            np_ref[...]
            + nq_ref[...]
            + jnp.where(line == 0, row_sum(upstream * normed), 0.0)
            + jnp.where(line == 4, row_sum(upstream), 0.0)
        )
        columns = on_ref.shape[1]
        for k in range(nz * ny):
            np_s[0, k] = params[:, k * columns : (k + 1) * columns]
        held["norm near"] = [
            wires.send(np_s.at[0], nn_s.at[i], **s) for i, s in enumerate(mp_shifts(n))
        ]

    @step(HOME + END)
    def _():
        total = np_s[0]
        for i, copy in enumerate(held["norm near"]):
            copy.wait_recv()
            total = total + nn_s[i]
        np_s[1] = total
        held["norm far"] = [
            wires.send(np_s.at[1, wires.peer(**shift)[0]], nf_s.at[i], **shift)
            for i, shift in enumerate(dp_shifts(n))
        ]

    plan = backward_plan(
        SELF_PLAN, nz, pairs,
        [MEMORY + GO, LOAD + OTHER, LOAD, HEADS] + spelled(n, [(CROSS, (BEGIN,))]),
        [INPUT + PART, INPUT + ON, GRAD + OUTPUT, GRAD + QUERIES, GRAD + TWIN],
        spelled(n, [(CROSS, (MIDDLE, ALONG)), (OUT, WHOLE)])
        + [NORM, HOME + END]
        + spelled(n, [(QUERY, WHOLE), (KEYS, WHOLE)])
        + [MEMORY + END],
    )
    for name in plan:
        steps[name]()
    total = np_s[1, data]
    for i, copy in enumerate(held["norm far"]):
        copy.wait_recv()
        total = total + nf_s[i]
    on_ref[...] = total
    norm_squares = jnp.sum(total * total) / (2 * nx * ONE[0] * ONE[1])
    total = sq_ref[...] + squares((oc_ref, oo_ref, oq_ref, op_ref)) + norm_squares
    one_s[...] = total
    copies = [wires.send(one_s, near_s.at[i], **s) for i, s in enumerate(mp_shifts(n))]
    for i, copy in enumerate(copies):
        copy.wait_recv()
        total = total + near_s[i]
    sum_s[...] = total
    copies = [wires.send(sum_s, far_s.at[i], **s) for i, s in enumerate(dp_shifts(n))]
    for i, copy in enumerate(copies):
        copy.wait_recv()
        total = total + far_s[i]
    norm_ref[0] = jnp.sqrt(jnp.sum(total))
    for mine, remote, here in homeward():
        pl.when(jnp.logical_not(mine))(lambda: remote.wait_send())
    for r in range(nz * ny):
        pltpu.make_async_copy(os_ref.at[r], os_ref.at[r], come_sem.at[r]).wait()
    wires.close()


def self_back(
    order, lengths, rows_grad, resid_grad, maps, saved, normed, inputs, params, cross_grads, memory,
    norm_ffn, norm_cross, square_part,
):
    n = grid_sizes()
    nz, ny, nx = n["z"], n["y"], n["x"]
    data, model = nz * ny, 2 * nx
    queries, keys, values, mixed, logsum = saved
    chip_rows, width = rows_grad.shape
    own = chip_rows // 2
    slot, local = keys.shape
    rows, wide = width // data, local // nx
    utterances, lines, deep = memory.shape
    columns = width // data
    copies = 4 * Scatter.copies(n) + 3 * (data - 1) + nx + (nx - 1) + 2 * (model - 1)
    vmem = pl.BlockSpec(memory_space=pltpu.VMEM)
    smem = pl.BlockSpec(memory_space=pltpu.SMEM)
    hbm = pl.BlockSpec(memory_space=pl.ANY)
    half = lambda *shape: pltpu.VMEM(shape, BF)
    return pl.pallas_call(
        functools.partial(self_back_kernel, n),
        out_shape=[
            jax.ShapeDtypeStruct((2, rows, wide), F32),
            jax.ShapeDtypeStruct((1, rows, wide), F32),
            jax.ShapeDtypeStruct((1, rows, wide), F32),
            jax.ShapeDtypeStruct((2, rows, wide), F32),
            jax.ShapeDtypeStruct((data, lines, deep), BF),
            jax.ShapeDtypeStruct((data, lines, deep), BF),
            jax.ShapeDtypeStruct((params.shape[0], columns), F32),
            jax.ShapeDtypeStruct((1,), F32),
        ],
        in_specs=[smem, smem, hbm, vmem]
        + [hbm] * 5
        + [vmem, hbm, vmem, vmem, hbm, hbm, vmem, vmem, vmem],
        out_specs=[vmem] * 4 + [hbm, hbm, vmem, smem],
        scratch_shapes=[
            half(chip_rows, width),
            half(4, width, local),
            half(chip_rows, local),
            half(slot, local),
            half(slot, local),
            half(chip_rows, local),
            half(slot, width),
            half(chip_rows, local),
            half(chip_rows, local),
            half(slot, local),
            half(slot, local),
            half(2, slot, chip_rows),
            half(2, width, local),
            half(4, width, local),
            half(slot, width),
            half(nx, own, width),
            half(nx - 1, own, width),
            half(nx - 1, own, width),
            half(own, width),
            pltpu.VMEM((2, data, params.shape[0], columns), F32),
            pltpu.VMEM((model - 1, data, params.shape[0], columns), F32),
            pltpu.VMEM((data - 1, params.shape[0], columns), F32),
        ]
        + Scatter.scratch(n, 2, False, rows, wide)
        + Scatter.scratch(n, 1, True, rows, wide)
        + Scatter.scratch(n, 1, True, rows, wide)
        + Scatter.scratch(n, 2, False, rows, wide)
        + [
            pltpu.VMEM(ONE, F32),
            pltpu.VMEM((model - 1,) + ONE, F32),
            pltpu.VMEM(ONE, F32),
            pltpu.VMEM((data - 1,) + ONE, F32),
            pltpu.SemaphoreType.DMA((copies,)),
            pltpu.SemaphoreType.DMA((copies,)),
            pltpu.SemaphoreType.DMA((data,)),
            pltpu.SemaphoreType.DMA((data,)),
            pltpu.SemaphoreType.DMA((14,)),
        ],
        compiler_params=pltpu.CompilerParams(
            collective_id=1, has_side_effects=True, vmem_limit_bytes=56 * 2**20
        ),
        name="self_back",
    )(
        order, lengths, rows_grad, resid_grad, maps, queries, keys, values, mixed, logsum, normed,
        inputs, params, cross_grads, memory, norm_ffn, norm_cross, square_part,
    )


def adam_step(weight, moment, square, gradient, step_rate, weight_decay):
    moment_new = BETA_FIRST * moment + (1.0 - BETA_FIRST) * gradient
    square_new = BETA_SECOND * square + (1.0 - BETA_SECOND) * gradient * gradient
    moment_hat = moment_new / (1.0 - BETA_FIRST**STEP)
    square_hat = square_new / (1.0 - BETA_SECOND**STEP)
    updated = weight - step_rate * (
        moment_hat / (jnp.sqrt(square_hat) + ADAM_EPSILON) + weight_decay * weight
    )
    return (updated, moment_new, square_new)


def update_kernel(order, norm, *refs):
    grads, refs = refs[:9], refs[9:]
    back, refs = refs[:2], refs[2:]
    old, refs = refs[:12], refs[12:]
    home, refs = refs[:2], refs[2:]
    new, refs = refs[:12], refs[12:]
    vault, refs = refs[:12], refs[12:]
    back_s, home_s, move_sem = refs[:2], refs[2:4], refs[4]
    moves = Moves(move_sem)
    loads = {}
    for kind in (2, 1, 0):
        loads[kind] = [moves.start(old[3 * j + kind], vault[3 * j + kind]) for j in range(4)]
    back_loads = [moves.start(a, b) for a, b in zip(back, back_s)]
    clip_scale = jnp.minimum(1.0, THRESHOLD / (norm[0] + 1e-06))

    def apply(kind, part, gradient, rate, decay):
        weight, moment, square, average = (vault[3 * j + kind] for j in range(4))
        updated, moment_new, square_new = adam_step(
            weight[part], moment[part], square[part], clip_scale * gradient, rate, decay
        )
        mixed = AVERAGING * average[part] + (1.0 - AVERAGING) * updated
        for j, value in enumerate((updated, moment_new, square_new, mixed)):
            vault[3 * j + kind][part] = value
            moves.store(vault[3 * j + kind].at[part], new[3 * j + kind].at[part])

    sq, sp, so, cq, cp, co, up, down, line = grads
    for copy in loads[2]:
        copy.wait()
    apply(2, slice(None), line[...], NORM_RATE, 0.0)
    for copy in loads[1]:
        copy.wait()
    for part, ref in ((0, up), (1, down)):
        apply(1, slice(part, part + 1), ref[...][None], MATRIX_RATE, MATRIX_DECAY)
    for copy in loads[0]:
        copy.wait()
    for part, ref in (
        (slice(0, 1), sq), (slice(1, 3), sp), (slice(3, 4), so), (slice(4, 5), cq),
        (slice(5, 7), cp), (slice(7, 8), co),
    ):
        apply(0, part, ref[...], MATRIX_RATE, MATRIX_DECAY)

    utterances = home_s[0].shape[0]
    for copy in back_loads:
        copy.wait()
    for i in range(utterances):
        place = 0
        for r in range(utterances):
            place = place + jnp.where(order[r] == i, r, 0)
        for src, dst in zip(back_s, home_s):
            dst[i] = src[place].astype(F32)
    for src, dst in zip(home_s, home):
        moves.store(src, dst)
    moves.close()


def update(order, norm, grads, back, old):
    vmem = pl.BlockSpec(memory_space=pltpu.VMEM)
    smem = pl.BlockSpec(memory_space=pltpu.SMEM)
    hbm = pl.BlockSpec(memory_space=pl.ANY)
    full = lambda v: jax.ShapeDtypeStruct(v.shape, F32)
    return pl.pallas_call(
        update_kernel,
        out_shape=[full(v) for v in back] + [full(v) for v in old],
        in_specs=[smem, smem] + [vmem] * 9 + [hbm] * 14,
        out_specs=[hbm] * 14,
        scratch_shapes=[pltpu.VMEM(v.shape, F32) for v in old]
        + [pltpu.VMEM(v.shape, BF) for v in back]
        + [pltpu.VMEM(v.shape, F32) for v in back]
        + [pltpu.SemaphoreType.DMA((60,))],
        compiler_params=pltpu.CompilerParams(vmem_limit_bytes=56 * 2**20),
        name="update",
    )(order, norm, *grads, *back, *old)


def per_device(
    states,
    memory,
    cotangent,
    lengths,
    memory_lengths,
    regroup_order,
    attn_weights,
    ffn_weights,
    norm_params,
    attn_mean,
    ffn_mean,
    norm_mean,
    attn_square,
    ffn_square,
    norm_square,
    attn_average,
    ffn_average,
    norm_average,
):
    n = grid_sizes()
    at = grid_place()
    nz, ny, nx = n["z"], n["y"], n["x"]
    data_index = lax.axis_index("dp")
    model_index = lax.axis_index("mp")
    data_size = lax.axis_size("dp")
    width = states.shape[2] * lax.axis_size("mp")
    slot = states.shape[1] * data_size
    own_rows = cotangent.shape[1]
    chip_rows = 2 * own_rows
    chip_start = at["x"] * chip_rows

    (
        weights_self,
        weights_cross,
        ffn_maps,
        norm_values,
        frames,
        inputs,
        normed_first,
        query_self,
        key_self,
        value_self,
        mixed_self,
        logsum_self,
        resid_one_own,
        normed_second,
        query_cross,
        key_cross,
        value_cross,
        mixed_cross,
        logsum_cross,
        resid_two_own,
        normed_third,
    ) = forward(
        regroup_order,
        lengths,
        memory_lengths,
        states,
        memory,
        norm_params,
        attn_weights,
        ffn_weights,
        own_rows,
    )

    layer_output, grad_two, cross_rows, ffn_grads, early, norm_ffn = feed_forward(
        regroup_order, lengths, normed_third, resid_two_own, ffn_maps, cotangent[0], norm_values
    )
    (
        shard_up,
        shard_down,
        cross_q,
        cross_o,
        cross_grads,
        grad_one,
        self_rows,
        memory_part,
        norm_cross,
        square_part,
    ) = (
        cross_back(
            regroup_order,
            memory_lengths,
            cross_rows,
            grad_two,
            weights_cross,
            (query_cross, key_cross, value_cross, mixed_cross, logsum_cross),
            normed_second,
            frames,
            resid_one_own,
            norm_values,
            ffn_grads,
            early,
        )
    )
    cross_p, self_o, self_q, self_p, back_states, back_memory, norm_shard, grad_norm = self_back(
        regroup_order,
        lengths,
        self_rows,
        grad_one,
        weights_self,
        (query_self, key_self, value_self, mixed_self, logsum_self),
        normed_first,
        inputs,
        norm_values,
        cross_grads,
        memory_part.reshape(data_size, -1, memory_part.shape[1]),
        norm_ffn,
        norm_cross,
        square_part,
    )
    grads = (self_q, self_p, self_o, cross_q, cross_p, cross_o, shard_up, shard_down, norm_shard)
    results = update(
        regroup_order,
        grad_norm,
        grads,
        (back_states, back_memory),
        (
            attn_weights,
            ffn_weights,
            norm_params,
            attn_mean,
            ffn_mean,
            norm_mean,
            attn_square,
            ffn_square,
            norm_square,
            attn_average,
            ffn_average,
            norm_average,
        ),
    )
    return (layer_output[None],) + tuple(results) + (grad_norm[0],)


def solution(mesh):
    rows = P(None, "dp", "mp")
    line = P(None, "dp")
    return jax.shard_map(
        per_device,
        mesh=mesh,
        in_specs=(rows, rows, P("dp", "mp", None), P(), P(), P())
        + (rows, rows, line) * 4,
        out_specs=(P("dp", "mp", None), rows, rows) + (rows, rows, line) * 4 + (P(),),
        check_vma=False,
    )
```

```python
import functools

import jax
import jax.numpy as jnp
from jax import lax
from jax.experimental import pallas as pl
from jax.experimental.pallas import tpu as pltpu
from jax.sharding import PartitionSpec as P

HD = 64
STEP = 10


EPSILON = 1e-05
NEGATIVE = -1000000000.0
BETA_FIRST = 0.9
BETA_SECOND = 0.999
ADAM_EPSILON = 1e-08
MATRIX_RATE = 0.05
NORM_RATE = 1.0
MATRIX_DECAY = 0.1
AVERAGING = 0.7
THRESHOLD = 1.0
BF = jnp.bfloat16
F32 = jnp.float32


(
    CROSS, DOWN, FIRST, GRAD, HOME, INPUT, KEYS, LOAD, MEMORY, OUT, QUERY, ROWS, SECOND, SELF, STATES, THIRD, UP,
) = range(1000, 18000, 1000)
(
    ALONG, BEGIN, END, FAN, GO, HEADS, LINE, MIDDLE, NORM, ON, OTHER, OUTPUT, PART, PASS, QUERIES, TURN, TWIN,
) = range(10, 180, 10)


def grid_sizes():
    dp = lax.axis_size("dp")
    mp = lax.axis_size("mp")
    ny = 1 << ((dp.bit_length() - 1) // 2)
    return {"z": dp // ny, "y": ny, "x": mp // 2, "c": 2}


def grid_place():
    n = grid_sizes()
    dp = lax.axis_index("dp")
    mp = lax.axis_index("mp")
    return {"z": dp // n["y"], "y": dp % n["y"], "x": mp // 2, "c": mp % 2}


def dot(left, right, left_dim, right_dim):
    return lax.dot_general(
        left, right, (((left_dim,), (right_dim,)), ((), ())), preferred_element_type=F32
    )


PAIR = 2 * HD


def only_head(value, head):
    lane = lax.broadcasted_iota(jnp.int32, value.shape, 1)
    keep = (lane < HD) if head == 0 else (lane >= HD)
    return jnp.where(keep, value, jnp.zeros_like(value))


def attend_pair(p, chunk, bound, q_ref, k_ref, v_ref, o_ref, sum_ref, score_ref, weight_ref):
    lanes = pl.ds(pl.multiple_of(p * PAIR, PAIR), PAIR)
    keys = k_ref.shape[0]
    queries = q_ref[:, lanes] * BF(HD**-0.5)
    values = v_ref[:, lanes]
    mixed = []
    for head in range(2):
        masked = only_head(queries, head)
        top = None
        for start in range(0, keys, chunk):
            block = slice(start, start + chunk)
            scores = dot(k_ref[block, lanes], masked, 1, 1)
            position = lax.broadcasted_iota(jnp.int32, scores.shape, 0) + start
            scores = jnp.where(position < bound, scores, NEGATIVE)
            score_ref[head, block, :] = scores
            highest = jnp.max(scores, axis=0, keepdims=True)
            top = highest if top is None else jnp.maximum(top, highest)
        total = None
        for start in range(0, keys, chunk):
            block = slice(start, start + chunk)
            raised = jnp.exp(score_ref[head, block, :] - top)
            part = jnp.sum(raised, axis=0, keepdims=True)
            total = part if total is None else total + part
            weight_ref[head, block, :] = raised.astype(BF)
        out = dot(values, weight_ref[head], 0, 0)[head * HD : (head + 1) * HD]
        mixed.append(out * (1.0 / total))
        sum_ref[p, head : head + 1, :] = top + jnp.log(total)
    o_ref[:, lanes] = jnp.concatenate(mixed, axis=0).T.astype(BF)


def attend_pair_back(
    p, chunk, bound, q_ref, k_ref, v_ref, o_ref, sum_ref, g_ref, dq_ref, dk_ref, dv_ref, ds_ref
):
    lanes = pl.ds(pl.multiple_of(p * PAIR, PAIR), PAIR)
    keys = k_ref.shape[0]
    queries = q_ref[:, lanes] * BF(HD**-0.5)
    grads = g_ref[:, lanes]
    product = (grads.astype(F32) * o_ref[:, lanes].astype(F32)).T
    head_q = [only_head(queries, head) for head in range(2)]
    head_g = [only_head(grads, head) for head in range(2)]
    shift = [
        jnp.sum(product[head * HD : (head + 1) * HD], axis=0, keepdims=True) for head in range(2)
    ]
    for start in range(0, keys, chunk):
        block = slice(start, start + chunk)
        key_block, value_block = k_ref[block, lanes], v_ref[block, lanes]
        grad_value, grad_key = 0.0, 0.0
        for head in range(2):
            scores = dot(key_block, head_q[head], 1, 1)
            position = lax.broadcasted_iota(jnp.int32, scores.shape, 0) + start
            scores = jnp.where(position < bound, scores, NEGATIVE)
            weights = jnp.exp(scores - sum_ref[p, head : head + 1, :])
            grad_weights = dot(value_block, head_g[head], 1, 1)
            grad_scores = (weights * (grad_weights - shift[head])).astype(BF)
            ds_ref[head, block, :] = grad_scores
            grad_value = grad_value + dot(weights.astype(BF), head_g[head], 1, 0)
            grad_key = grad_key + dot(grad_scores, head_q[head], 1, 0)
        dv_ref[block, lanes] = grad_value.astype(BF)
        dk_ref[block, lanes] = grad_key.astype(BF)
    key_all = k_ref[:, lanes]
    parts = [dot(key_all, ds_ref[h], 0, 0)[h * HD : (h + 1) * HD] for h in range(2)]
    dq_ref[:, lanes] = (jnp.concatenate(parts, axis=0).T * HD**-0.5).astype(BF)


def flipped(index, mask):
    bit = 1
    result = index
    while bit <= mask:
        if mask & bit:
            result = result + bit * (1 - 2 * ((index // bit) % 2))
        bit *= 2
    return result


class Wires:
    def __init__(self, sizes, place, send_sem, recv_sem):
        self.sizes, self.place = sizes, place
        self.send_sem, self.recv_sem = send_sem, recv_sem
        self.count = 0
        self.started = []
        self.maybe = []

    def peer(self, z=0, y=0, x=0, c=0, flip=0):
        n, at = self.sizes, self.place
        pz, py = (at["z"] + z) % n["z"], (at["y"] + y) % n["y"]
        if flip:
            pz = flipped(at["z"], flip)
        px, pc = (at["x"] + x) % n["x"], (at["c"] + c) % 2
        return (pz * n["y"] + py, px * 2 + pc)

    def send(self, src, dst, **shift):
        copy = pltpu.make_async_remote_copy(
            src_ref=src,
            dst_ref=dst,
            send_sem=self.send_sem.at[self.count],
            recv_sem=self.recv_sem.at[self.count],
            device_id=self.peer(**shift),
            device_id_type=pl.DeviceIdType.MESH,
        )
        self.count += 1
        copy.start()
        self.started.append(copy)
        return copy

    def send_if(self, condition, src, dst, recv_sem, **shift):
        copy = pltpu.make_async_remote_copy(
            src_ref=src,
            dst_ref=dst,
            send_sem=self.send_sem.at[self.count],
            recv_sem=recv_sem,
            device_id=self.peer(**shift),
            device_id_type=pl.DeviceIdType.MESH,
        )
        self.count += 1
        pl.when(condition)(copy.start)
        self.maybe.append((condition, copy))

    def greet(self, shifts):
        barrier = pltpu.get_barrier_semaphore()
        for shift in shifts:
            pl.semaphore_signal(
                barrier, inc=1, device_id=self.peer(**shift), device_id_type=pl.DeviceIdType.MESH
            )
        pl.semaphore_wait(barrier, len(shifts))

    def close(self):
        for copy in self.started:
            copy.wait_send()
        for condition, copy in self.maybe:
            pl.when(condition)(copy.wait_send)


def dp_shifts(n):
    return [{"z": z, "y": y} for z in range(n["z"]) for y in range(n["y"]) if z or y]


def mp_shifts(n):
    return [{"x": x, "c": c} for x in range(n["x"]) for c in range(2) if x or c]


def loop_rows(total, step, body):
    def one(i, carry):
        body(pl.ds(pl.multiple_of(i * step, step), step))
        return carry

    lax.fori_loop(0, total // step, one, 0)


def shifted(rows, offset):
    return pl.ds(pl.multiple_of(rows.start + offset, rows.size), rows.size)


def mat_rows(out_ref, left_ref, right_ref, total, step, offset=0):
    def body(rows):
        left = left_ref[shifted(rows, offset), :]
        out_ref[rows, :] = dot(left, right_ref[...], 1, 0).astype(BF)

    loop_rows(total, step, body)


class Moves:
    def __init__(self, sem):
        self.sem = sem
        self.count = 0
        self.open = []

    def start(self, src, dst):
        copy = pltpu.make_async_copy(src, dst, self.sem.at[self.count])
        self.count += 1
        copy.start()
        return copy

    def store(self, src, dst):
        self.open.append(self.start(src, dst))

    def close(self):
        for copy in self.open:
            copy.wait()


class Line:
    def __init__(self, wires, spot, sem):
        self.wires, self.spot, self.sem = wires, spot, sem
        self.nz, self.z = wires.sizes["z"], wires.place["z"]

    def start(self, src):
        z, nz = self.z, self.nz
        if nz > 1:
            self.wires.send_if(z < nz - 1, src, self.spot(z), self.sem.at[1], z=1)
            self.wires.send_if(z > 0, src, self.spot(z), self.sem.at[nz - 1], z=nz - 1)

    def step_back(self, k):
        total = 0
        for i in range(self.nz):
            order = sorted(range(1, self.nz), key=lambda s: s if s <= i else self.nz - s)
            total = total + jnp.where(self.z == i, order[k - 1], 0)
        return total

    def arrive(self, k):
        z, nz = self.z, self.nz
        s = self.step_back(k)
        source = (z + nz - s) % nz
        spot = self.spot(source)
        pltpu.make_async_copy(spot, spot, self.sem.at[s]).wait()
        below = s <= z
        above = s > z
        self.wires.send_if(
            jnp.logical_and(below, z < nz - 1), spot, spot, self.sem.at[(s + 1) % nz], z=1
        )
        self.wires.send_if(
            jnp.logical_and(above, z > 0), spot, spot, self.sem.at[s - 1], z=nz - 1
        )
        return source

    @staticmethod
    def copies(nz):
        return 2 + 2 * (nz - 1)


class Gather:
    def __init__(self, wires, src, out, cut, sem):
        self.wires, self.src, self.out, self.cut = wires, src, out, cut
        self.n, self.at = wires.sizes, wires.place
        self.line = Line(wires, lambda i: self.spot(i, 0, 0), sem)
        self.source, self.to_y, self.to_x = {0: self.at["z"]}, {}, {}
        self.last = []

    def spot(self, chip_z, sy, sx, mats=slice(None)):
        rows, wide = self.src.shape[1], self.src.shape[2]
        n, at = self.n, self.at
        block = chip_z * n["y"] + (at["y"] + n["y"] - sy) % n["y"]
        column = (at["x"] + n["x"] - sx) % n["x"]
        return self.out.at[
            mats,
            pl.ds(pl.multiple_of(block * rows, rows), rows),
            pl.ds(pl.multiple_of(column * wide, wide), wide),
        ]

    def fan(self, k, src=None):
        spot = self.spot(self.source[k], 0, 0)
        src = spot if src is None else src
        for s in range(1, self.n["y"]):
            self.to_y[k, s] = self.wires.send(src, spot, y=s)
        for s in range(1, self.n["x"]):
            self.to_x[k, s] = self.wires.send(src, spot, x=s)

    def begin(self):
        self.line.start(self.src)
        self.fan(0, self.src)

    def arrive(self, k):
        self.source[k] = self.line.arrive(k)
        self.fan(k)

    def corner(self, k):
        count = self.src.shape[0]
        for sy in range(1, self.n["y"]):
            self.to_y[k, sy].wait_recv()
            part = self.spot(self.source[k], sy, 0, slice(0, self.cut))
            for s in range(1, self.n["x"]):
                self.last.append(self.wires.send(part, part, x=s))
        for sx in range(1, self.n["x"]):
            self.to_x[k, sx].wait_recv()
            if self.cut < count:
                part = self.spot(self.source[k], 0, sx, slice(self.cut, count))
                for s in range(1, self.n["y"]):
                    self.last.append(self.wires.send(part, part, y=s))

    def finish(self):
        for copy in self.last:
            copy.wait_recv()

    @staticmethod
    def copies(n):
        nz, ny, nx = n["z"], n["y"], n["x"]
        return Line.copies(nz) + nz * (ny - 1 + nx - 1) + 2 * nz * (ny - 1) * (nx - 1)


class RowGather:
    def __init__(self, wires, src, out, z_first, sem):
        self.wires, self.src, self.out, self.z_first = wires, src, out, z_first
        self.n, self.at = wires.sizes, wires.place
        spot = (lambda i: self.spot(i, 0)) if z_first else self.band
        self.line = Line(wires, spot, sem)
        self.to_y = []

    def spot(self, chip_z, sy):
        rows, ny = self.src.shape[0], self.n["y"]
        block = chip_z * ny + (self.at["y"] + ny - sy) % ny
        return self.out.at[pl.ds(pl.multiple_of(block * rows, rows), rows)]

    def band(self, chip_z):
        rows = self.src.shape[0] * self.n["y"]
        return self.out.at[pl.ds(pl.multiple_of(chip_z * rows, rows), rows)]

    def across(self, source, src=None):
        spot = self.spot(source, 0)
        src = spot if src is None else src
        for s in range(1, self.n["y"]):
            self.to_y.append(self.wires.send(src, spot, y=s))

    def begin(self):
        if self.z_first:
            self.line.start(self.src)
        self.across(self.at["z"], self.src)

    def turn(self):
        for copy in self.to_y:
            copy.wait_recv()
        self.line.start(self.band(self.at["z"]))

    def arrive(self, k):
        source = self.line.arrive(k)
        if self.z_first:
            self.across(source)

    def finish(self):
        if self.z_first:
            for copy in self.to_y:
                copy.wait_recv()

    @staticmethod
    def copies(n):
        return Line.copies(n["z"]) + n["z"] * (n["y"] - 1)


def norm_rows(values, p_ref, index):
    centered = values - jnp.mean(values, axis=-1, keepdims=True)
    variance = jnp.mean(centered * centered, axis=-1, keepdims=True)
    normed = centered * lax.rsqrt(variance + EPSILON)
    return (normed * p_ref[index : index + 1, :] + p_ref[index + 4 : index + 5, :]).astype(BF)


STRIP = 256


FORWARD_PLAN = (
    CROSS + FAN, SELF + FAN, SELF + LINE, SELF + PASS + 1, SELF + PASS + 2, CROSS + TURN + 0,
    STATES + GO, CROSS + LINE, SELF + PASS + 3, DOWN + BEGIN, MEMORY + GO, SELF + TURN + 0,
    CROSS + PASS + 1, SELF + TURN + 1, SELF + TURN + 3, STATES + ON, SELF + TURN + 2, UP + BEGIN,
    DOWN + LINE, STATES + TWIN, MEMORY + ON, STATES + END, CROSS + PASS + 2, DOWN + PASS + 1,
    FIRST + NORM, SELF + END, SELF + HEADS, CROSS + PASS + 3, SELF + TWIN + 0, CROSS + TURN + 1,
    SELF + TWIN + 1, MEMORY + TWIN, SELF + TWIN + 2, CROSS + TURN + 2, DOWN + PASS + 2,
    SELF + TWIN + 3, MEMORY + END, CROSS + TURN + 3, SELF + OUTPUT, UP + PASS + 1, UP + PASS + 2,
    SECOND + NORM, CROSS + END, MEMORY + HEADS, CROSS + QUERIES, CROSS + TWIN + 0,
    CROSS + TWIN + 1, UP + PASS + 3, CROSS + TWIN + 2, CROSS + TWIN + 3, CROSS + OUTPUT,
    DOWN + PASS + 3, UP + END, DOWN + END, THIRD + NORM,
)


def forward_plan(nz, pairs):
    if nz == 4 and pairs == 4:
        return FORWARD_PLAN
    passes = lambda group: [group + PASS + k for k in range(1, nz)]
    turns = lambda group: [group + TURN + k for k in range(nz)]
    plan = [STATES + GO, SELF + LINE, SELF + FAN, CROSS + LINE, CROSS + FAN, MEMORY + GO]
    plan += [STATES + ON, STATES + TWIN, STATES + END, FIRST + NORM]
    plan += passes(SELF) + turns(SELF) + [MEMORY + ON, MEMORY + TWIN, SELF + END]
    plan += [SELF + HEADS] + [SELF + TWIN + p for p in range(pairs)] + [SELF + OUTPUT]
    plan += [UP + BEGIN, DOWN + BEGIN] + passes(CROSS) + turns(CROSS) + passes(UP)
    plan += [SECOND + NORM, MEMORY + END, CROSS + END, DOWN + LINE, MEMORY + HEADS]
    plan += [CROSS + QUERIES] + [CROSS + TWIN + p for p in range(pairs)] + [CROSS + OUTPUT]
    return tuple(plan + passes(DOWN) + [THIRD + NORM, UP + END, DOWN + END])


def forward_kernel(
    n, own_rows, order, lengths, reaches, st_ref, me_ref, pr_ref, wa_ref, wf_ref,
    ows, owc, owf, op_ref, ofr, oin, oh1, oq, ok, ov, oo, ol, ox1, oh2, oq2, ok2, ov2, oo2, ol2,
    ox2, oh3,
    stage_s, pin_s, pall_s, p_s, wl_s, fl_s,
    x_s, m_s, w_s, c_s, h1_s, q_s, k_s, v_s, o_s, l_s, x1_s, h2_s, q2_s, k2_s, v2_s, o2_s, l2_s,
    x2_s, h3_s, give_s, got_s, score_s, weight_s,
    send_sem, recv_sem, self_sem, cross_sem, up_sem, down_sem, move_sem,
):
    at = grid_place()
    z, y, x, c = at["z"], at["y"], at["x"], at["c"]
    nz, ny, nx = n["z"], n["y"], n["x"]
    data, model = z * ny + y, x * 2 + c
    wires = Wires(n, at, send_sem, recv_sem)
    moves = Moves(move_sem)
    utterances, lines, deep = st_ref.shape
    mats = w_s.shape[0]
    for r in range(utterances):
        stage_s[0, r] = st_ref[order[r]]
        stage_s[1, r] = me_ref[order[r]]
    wl_s[...] = wa_ref[...].astype(BF)
    fl_s[...] = wf_ref[...].astype(BF)
    pin_s[...] = pr_ref[...].astype(BF).astype(F32)
    wires.greet(dp_shifts(n) + [{"x": s} for s in range(1, nx)] + [{"c": 1}])

    def patch(ref):
        return ref.at[
            pl.ds(pl.multiple_of(data * lines, lines), lines),
            pl.ds(pl.multiple_of(model * deep, deep), deep),
        ]

    def column(ref, sx, sc):
        index = ((x + nx - sx) % nx) * 2 + (c + 2 - sc) % 2
        return ref.at[:, pl.ds(pl.multiple_of(index * deep, deep), deep)]

    def spread(i, out):
        copies = []
        for shift in dp_shifts(n):
            target = wires.peer(**shift)[0]
            copies.append(wires.send(stage_s.at[i, target], patch(out), **shift))
        return copies, moves.start(stage_s.at[i, data], patch(out))

    def forward_columns(out, spreading):
        copies, own = spreading
        own.wait()
        for copy in copies:
            copy.wait_recv()
        near = [wires.send(column(out, 0, 0), column(out, 0, 0), x=s) for s in range(1, nx)]
        return near, [wires.send(column(out, 0, 0), column(out, 0, 0), c=1)]

    def pair_columns(out, near, pair):
        for s in range(1, nx):
            near[s - 1].wait_recv()
            pair.append(wires.send(column(out, s, 0), column(out, s, 0), c=1))

    own_self = wl_s.at[0:mats]
    own_cross = wl_s.at[mats : 2 * mats]
    near_self = Gather(wires, own_self, w_s, mats // 2, self_sem)
    near_cross = Gather(wires, own_cross, c_s, mats // 2, cross_sem)
    up_gather = RowGather(wires, fl_s.at[0], owf.at[0], True, up_sem)
    down_gather = RowGather(wires, fl_s.at[1], owf.at[1], False, down_sem)
    here = [
        moves.start(own_self, near_self.spot(z, 0, 0)),
        moves.start(own_cross, near_cross.spot(z, 0, 0)),
        moves.start(pin_s, pall_s.at[data]),
    ]
    down_here = moves.start(fl_s.at[1], down_gather.spot(z, 0))
    up_here = moves.start(fl_s.at[0], up_gather.spot(z, 0))
    params = [wires.send(pin_s, pall_s.at[data], **shift) for shift in dp_shifts(n)]
    slot, width = x_s.shape
    chip_rows = 2 * own_rows
    chip_start = x * chip_rows
    strip = min(STRIP, own_rows)
    pairs = q_s.shape[1] // PAIR
    own = pl.ds(pl.multiple_of(c * own_rows, own_rows), own_rows)
    held = {}
    steps = {}

    def step(name):
        def keep(function):
            steps[name] = function
            return function

        return keep

    for name, i, ref in ((STATES, 0, x_s), (MEMORY, 1, m_s)):

        def go(name=name, i=i, ref=ref):
            held[name] = spread(i, ref)

        def on(name=name, ref=ref):
            held[name] = forward_columns(ref, held[name])

        def pair(name=name, ref=ref):
            pair_columns(ref, *held[name])

        def end(name=name):
            for copy in held[name][1]:
                copy.wait_recv()

        steps.update(
            {name + GO: go, name + ON: on, name + TWIN: pair, name + END: end}
        )
    for name, gather in ((SELF, near_self), (CROSS, near_cross)):
        steps[name + LINE] = functools.partial(gather.line.start, gather.src)
        steps[name + FAN] = functools.partial(gather.fan, 0, gather.src)
        for k in range(nz):
            steps[name + PASS + k] = functools.partial(gather.arrive, k)
            steps[name + TURN + k] = functools.partial(gather.corner, k)
    for name, gather in ((UP, up_gather), (DOWN, down_gather)):
        steps[name + BEGIN] = gather.begin
        steps[name + END] = gather.finish
        for k in range(1, nz):
            steps[name + PASS + k] = functools.partial(gather.arrive, k)

    @step(DOWN + LINE)
    def _():
        down_here.wait()
        down_gather.turn()

    @step(SELF + END)
    def _():
        for copy in here[:1]:
            copy.wait()
        near_self.finish()
        moves.store(w_s, ows)

    @step(CROSS + END)
    def _():
        here[1].wait()
        near_cross.finish()
        moves.store(c_s, owc)

    @step(FIRST + NORM)
    def _():
        for copy in params:
            copy.wait_recv()
        here[2].wait()
        for i in range(nz * ny):
            columns = pall_s.shape[2]
            p_s[:, i * columns : (i + 1) * columns] = pall_s[i]
        op_ref[...] = p_s[...]

        def first_norm(rows):
            h1_s[rows, :] = norm_rows(x_s[rows, :].astype(F32), p_s, 0)

        loop_rows(slot, strip, first_norm)
        moves.store(h1_s, oh1)
        moves.store(x_s.at[pl.ds(pl.multiple_of(model * own_rows, own_rows), own_rows)], oin)

    @step(SELF + HEADS)
    def _():
        mat_rows(q_s, h1_s, w_s.at[0], chip_rows, strip, chip_start)
        mat_rows(k_s, h1_s, w_s.at[1], slot, strip)
        mat_rows(v_s, h1_s, w_s.at[2], slot, strip)
        for ref, out in ((q_s, oq), (k_s, ok), (v_s, ov)):
            moves.store(ref, out)

    @step(MEMORY + HEADS)
    def _():
        mat_rows(k2_s, m_s, c_s.at[1], slot, strip)
        mat_rows(v2_s, m_s, c_s.at[2], slot, strip)
        for ref, out in ((k2_s, ok2), (v2_s, ov2), (m_s, ofr)):
            moves.store(ref, out)

    @step(CROSS + QUERIES)
    def _():
        mat_rows(q2_s, h2_s, c_s.at[0], chip_rows, strip)
        moves.store(q2_s, oq2)

    reach_self = lax.broadcasted_iota(jnp.int32, (1, chip_rows), 1) + chip_start + 1
    reach_self = jnp.minimum(reach_self, lengths[order[data]])
    reach_cross = jnp.full((1, chip_rows), reaches[order[data]], jnp.int32)
    for p in range(pairs):

        def self_pair(p=p):
            attend_pair(p, 256, reach_self, q_s, k_s, v_s, o_s, l_s, score_s, weight_s)

        def cross_pair(p=p):
            attend_pair(p, 256, reach_cross, q2_s, k2_s, v2_s, o2_s, l2_s, score_s, weight_s)

        steps[SELF + TWIN + p] = self_pair
        steps[CROSS + TWIN + p] = cross_pair

    def give(index, mixed, out_map):
        def body(rows):
            give_s[index, rows, :] = dot(mixed[rows, :], out_map[...], 1, 1).astype(BF)

        loop_rows(chip_rows, strip, body)
        held[index] = wires.send(give_s.at[index], got_s.at[index], c=1)

    def total(index, rows):
        return give_s[index, rows, :].astype(F32) + got_s[index, rows, :].astype(F32)

    @step(SELF + OUTPUT)
    def _():
        moves.store(o_s, oo)
        moves.store(l_s, ol)
        give(0, o_s, w_s.at[3])

    @step(CROSS + OUTPUT)
    def _():
        moves.store(o2_s, oo2)
        moves.store(l2_s, ol2)
        give(1, o2_s, c_s.at[3])

    @step(SECOND + NORM)
    def _():
        held[0].wait_recv()

        def second_norm(rows):
            values = x_s[shifted(rows, chip_start), :].astype(F32) + total(0, rows)
            x1_s[rows, :] = values
            h2_s[rows, :] = norm_rows(values, p_s, 1)

        loop_rows(chip_rows, strip, second_norm)
        moves.store(x1_s.at[own], ox1)
        moves.store(h2_s, oh2)

    @step(THIRD + NORM)
    def _():
        held[1].wait_recv()

        def third_norm(rows):
            values = x1_s[rows, :] + total(1, rows)
            x2_s[rows, :] = values
            h3_s[rows, :] = norm_rows(values, p_s, 2)

        loop_rows(chip_rows, strip, third_norm)
        moves.store(x2_s.at[own], ox2)
        moves.store(h3_s, oh3)

    for name in forward_plan(nz, pairs):
        steps[name]()
    up_here.wait()
    moves.close()
    wires.close()


def forward(order, lengths, reaches, states, memory, params, attn, ffn, own_rows):
    n = grid_sizes()
    nz, ny, nx = n["z"], n["y"], n["x"]
    data = nz * ny
    utterances, lines, deep = states.shape
    slot, width = lines * data, deep * 2 * nx
    mats = attn.shape[0] // 2
    local = attn.shape[2] * nx
    hidden = ffn.shape[2]
    chip_rows = 2 * own_rows
    pairs = local // PAIR
    copies = (
        2 * Gather.copies(n) + 2 * RowGather.copies(n) + 3 * (data - 1) + 2 * (2 * (nx - 1) + 1) + 2
    )
    vmem = pl.BlockSpec(memory_space=pltpu.VMEM)
    smem = pl.BlockSpec(memory_space=pltpu.SMEM)
    hbm = pl.BlockSpec(memory_space=pl.ANY)
    half = lambda *shape: (shape, BF)
    full = lambda *shape: (shape, F32)
    saved = [
        half(slot, width),
        half(chip_rows, local),
        half(slot, local),
        half(slot, local),
        half(chip_rows, local),
        full(pairs, 2, chip_rows),
        full(own_rows, width),
        half(chip_rows, width),
        half(chip_rows, local),
        half(slot, local),
        half(slot, local),
        half(chip_rows, local),
        full(pairs, 2, chip_rows),
        full(own_rows, width),
        half(chip_rows, width),
    ]
    outs = [
        half(mats, width, local),
        half(mats, width, local),
        half(2, width, hidden),
        full(params.shape[0], width),
        half(slot, width),
        half(own_rows, width),
    ] + saved
    scratch = [
        half(2, utterances, lines, deep),
        full(*params.shape),
        full(data, *params.shape),
        full(params.shape[0], width),
        half(*attn.shape),
        half(*ffn.shape),
        half(slot, width),
        half(slot, width),
        half(mats, width, local),
        half(mats, width, local),
        half(slot, width),
        half(chip_rows, local),
        half(slot, local),
        half(slot, local),
        half(chip_rows, local),
        full(pairs, 2, chip_rows),
        full(chip_rows, width),
        half(chip_rows, width),
        half(chip_rows, local),
        half(slot, local),
        half(slot, local),
        half(chip_rows, local),
        full(pairs, 2, chip_rows),
        full(chip_rows, width),
        half(chip_rows, width),
        half(2, chip_rows, width),
        half(2, chip_rows, width),
        full(2, slot, chip_rows),
        half(2, slot, chip_rows),
    ]
    return pl.pallas_call(
        functools.partial(forward_kernel, n, own_rows),
        out_shape=[jax.ShapeDtypeStruct(s, t) for s, t in outs],
        in_specs=[smem, smem, smem, vmem, vmem, vmem, vmem, vmem],
        out_specs=[hbm] * 3 + [vmem] + [hbm] * (len(outs) - 4),
        scratch_shapes=[pltpu.VMEM(s, t) for s, t in scratch]
        + [
            pltpu.SemaphoreType.DMA((copies,)),
            pltpu.SemaphoreType.DMA((copies,)),
        ]
        + [pltpu.SemaphoreType.DMA((nz,))] * 4
        + [pltpu.SemaphoreType.DMA((32,))],
        compiler_params=pltpu.CompilerParams(
            collective_id=3, has_side_effects=True, vmem_limit_bytes=56 * 2**20
        ),
        name="forward",
    )(order, lengths, reaches, states, memory, params, attn, ffn)


def early_zones(n):
    return [n["z"] - 1, n["z"] - 3] if n["z"] >= 4 else []


def norm_back_rows(values, grad, gain):
    centered = values - jnp.mean(values, axis=-1, keepdims=True)
    scale = lax.rsqrt(jnp.mean(centered * centered, axis=-1, keepdims=True) + EPSILON)
    normed = centered * scale
    up = grad * gain
    back = scale * (
        up
        - jnp.mean(up, axis=-1, keepdims=True)
        - normed * jnp.mean(up * normed, axis=-1, keepdims=True)
    )
    return back, normed


def row_sum(values):
    return jnp.sum(values, axis=0, keepdims=True)


SPLIT = 2


def ffn_kernel(
    n, order, lengths, h_hbm, x_ref, w_hbm, ct_ref, p_ref,
    oy_ref, odx_ref, odc, odw, oe, on_ref,
    h_s, f_s, a_s, d_s, u_s, w_s, keep_s, far_s, give_s, got_s, cross_s, crossed_s, back_s, come_s,
    x3_s, dx3_s, dc_s, dw_s, early_s, send_sem, recv_sem, move_sem,
):
    at = grid_place()
    wires = Wires(n, at, send_sem, recv_sem)
    moves = Moves(move_sem)
    nx, c = n["x"], at["c"]
    length = lengths[order[at["z"] * n["y"] + at["y"]]]
    own, width = x_ref.shape
    part = own // SPLIT
    start_own = pl.multiple_of(c * own, own)
    start_other = pl.multiple_of((1 - c) * own, own)
    get_w = moves.start(w_hbm, w_s)
    get_own = moves.start(h_hbm.at[pl.ds(start_own, own)], h_s.at[pl.ds(0, own)])
    get_other = moves.start(h_hbm.at[pl.ds(start_other, own)], h_s.at[pl.ds(own, own)])
    ny = n["y"]
    wires.greet(
        [{"x": s} for s in range(1, nx)] + [{"y": s} for s in range(1, ny)] + [{"c": 1}]
    )

    def far_at(t, k, j):
        return 2 * own + (((t - 1) * SPLIT + k) * 2 + j) * part

    def spread(src, dst, k):
        return [
            wires.send(src.at[pl.ds(k * part, part)], dst.at[pl.ds(far_at(t, k, 0), part)], x=t)
            for t in range(1, nx)
        ]

    def onward(dst, t, k):
        return wires.send(
            dst.at[pl.ds(far_at(t, k, 0), part)], dst.at[pl.ds(far_at(t, k, 1), part)], c=1
        )

    def up(rows):
        hidden = dot(h_s[rows, :], w_s[0], 1, 0)
        inner = 0.7978845608028654 * (hidden + 0.044715 * (hidden * hidden * hidden))
        bend = jnp.tanh(inner)
        a_s[rows, :] = (0.5 * hidden * (1.0 + bend)).astype(BF)
        slope = 0.7978845608028654 * (1.0 + 0.134145 * (hidden * hidden))
        d_s[rows, :] = 0.5 * (1.0 + bend) + 0.5 * hidden * (1.0 - bend * bend) * slope
        return dot(a_s[rows, :], w_s[1], 1, 1)

    def down(rows):
        grad = dot(f_s[rows, :], w_s[1], 1, 0)
        u_s[rows, :] = (grad * d_s[rows, :]).astype(BF)
        return dot(u_s[rows, :], w_s[0], 1, 1)

    def other_core(phase, work):
        give_s[phase] = work(slice(own, 2 * own)).astype(BF)
        return wires.send(give_s.at[phase], got_s.at[phase], c=1)

    def far_part(phase, work, t, k):
        sums = work(slice(far_at(t, k, 0), far_at(t, k, 0) + 2 * part))
        far_s[t - 1, k] = sums[:part]
        cross_s[phase, t - 1, k] = sums[part:].astype(BF)
        return wires.send(cross_s.at[phase, t - 1, k], crossed_s.at[phase, t - 1, k], c=1)

    def return_part(phase, t, k, crossing):
        crossing.wait_recv()
        back_s[phase, t - 1, k] = (far_s[t - 1, k] + crossed_s[phase, t - 1, k].astype(F32)).astype(
            BF
        )
        return wires.send(back_s.at[phase, t - 1, k], come_s.at[phase, t - 1, k], x=nx - t)

    def far_phase(phase, work, buffer, arriving, arrived=None):
        homing = {}
        for k in range(SPLIT):
            crossed = []
            for t in range(1, nx):
                arriving[k][t - 1].wait_recv()
                crossed.append(onward(buffer, t, k))
            crossing = []
            for copy in crossed:
                copy.wait_recv()
            if arrived is not None and k == SPLIT - 1:
                arrived()
            for t in range(1, nx):
                crossing.append(far_part(phase, work, t, k))
            for t in range(1, nx):
                homing[k, t] = return_part(phase, t, k, crossing[t - 1])
        return homing

    def own_part(phase, k, homing):
        rows = slice(k * part, (k + 1) * part)
        total = keep_s[rows, :] + got_s[phase, rows, :].astype(F32)
        for t in range(1, nx):
            homing[k, t].wait_recv()
            total = total + come_s[phase, t - 1, k].astype(F32)
        return total

    own_rows = h_hbm.at[pl.ds(start_own, own)]
    arriving = [spread(own_rows, h_s, k) for k in range(SPLIT)]
    get_own.wait()
    get_w.wait()
    get_other.wait()
    swap = other_core(0, up)
    keep_s[...] = up(slice(0, own))
    homing = far_phase(0, up, h_s, arriving)
    swap.wait_recv()
    gain_final, bias_final = 0.0, 0.0
    arriving, near = [], []
    first_row = (at["x"] * 2 + c) * own
    for k in range(SPLIT):
        rows = slice(k * part, (k + 1) * part)
        values = x_ref[rows, :] + own_part(0, k, homing)
        x3 = values
        centered = x3 - jnp.mean(x3, axis=-1, keepdims=True)
        variance = jnp.mean(centered * centered, axis=-1, keepdims=True)
        normed = centered * lax.rsqrt(variance + EPSILON)
        oy_ref[rows, :] = (normed * p_ref[3:4, :] + p_ref[7:8, :]).astype(BF)
        position = lax.broadcasted_iota(jnp.int32, (part, 1), 0) + (first_row + k * part)
        seed = jnp.where(position < length, ct_ref[rows, :].astype(F32), 0.0)
        grad, normed = norm_back_rows(x3, seed, p_ref[3:4, :])
        gain_final = gain_final + row_sum(seed * normed)
        bias_final = bias_final + row_sum(seed)
        dx3_s[rows, :] = grad
        f_s[rows, :] = grad.astype(BF)
        arriving.append(spread(f_s, f_s, k))
        near.append(
            wires.send(f_s.at[pl.ds(k * part, part)], f_s.at[pl.ds(own + k * part, part)], c=1)
        )
    keep_s[...] = down(slice(0, own))
    for copy in near:
        copy.wait_recv()
    swap = other_core(1, down)
    rows_each = width // (n["z"] * ny)
    zone_rows = ny * rows_each
    early = early_zones(n)
    ahead = []

    def strip_of(i, left, right, m):
        start = flipped(at["z"], m) * zone_rows
        cols = pl.ds(pl.multiple_of(start, zone_rows), zone_rows)
        dw_s[i, cols, :] = dot(left[:, cols], right[...], 0, 0).astype(BF)
        return start

    def start_early():
        for index, m in enumerate(early):
            start = strip_of(1, f_s, a_s, m)
            for t in range(1, ny):
                band = start + (at["y"] + t) % ny * rows_each
                band = pl.ds(pl.multiple_of(band, rows_each), rows_each)
                ahead.append(wires.send(dw_s.at[1, band], early_s.at[t - 1, index], y=t))

    homing = far_phase(1, down, f_s, arriving, start_early)
    for m in range(n["z"]):
        if m not in early:
            strip_of(1, f_s, a_s, m)
    moves.store(dw_s.at[1], odw.at[1])
    for m in range(n["z"]):
        strip_of(0, h_s, u_s, m)
    moves.store(dw_s.at[0], odw.at[0])
    swap.wait_recv()
    gain_third, bias_third = 0.0, 0.0
    near = []
    for k in range(SPLIT):
        rows = slice(k * part, (k + 1) * part)
        upstream = own_part(1, k, homing)
        grad, normed = norm_back_rows(x_ref[rows, :], upstream, p_ref[2:3, :])
        gain_third = gain_third + row_sum(upstream * normed)
        bias_third = bias_third + row_sum(upstream)
        total = dx3_s[rows, :] + grad
        odx_ref[rows, :] = total
        here = pl.ds(start_own + k * part, part)
        dc_s[here, :] = total.astype(BF)
        near.append(wires.send(dc_s.at[here], dc_s.at[here], c=1))
    line = lax.broadcasted_iota(jnp.int32, on_ref.shape, 0)
    sums = jnp.zeros(on_ref.shape, F32)
    for index, value in ((2, gain_third), (3, gain_final), (6, bias_third), (7, bias_final)):
        sums = sums + jnp.where(line == index, value, 0.0)
    on_ref[...] = sums
    for copy in near:
        copy.wait_recv()
    moves.store(dc_s, odc)
    for copy in ahead:
        copy.wait_recv()
    moves.store(early_s, oe)
    moves.close()
    wires.close()


def feed_forward(order, lengths, normed, resid, maps, cotangent, params):
    n = grid_sizes()
    chip_rows, width = normed.shape
    own = chip_rows // 2
    hidden = maps.shape[2]
    nx = n["x"]
    rows = chip_rows * nx
    part = own // SPLIT
    rows_each = width // (n["z"] * n["y"])
    ahead = (n["y"] - 1, len(early_zones(n)), rows_each, hidden)
    copies = 2 * (SPLIT * (nx - 1) * 4 + 1) + 2 * SPLIT + ahead[0] * ahead[1]
    vmem = pl.BlockSpec(memory_space=pltpu.VMEM)
    smem = pl.BlockSpec(memory_space=pltpu.SMEM)
    hbm = pl.BlockSpec(memory_space=pl.ANY)
    far = (2, nx - 1, SPLIT, part, width)
    return pl.pallas_call(
        functools.partial(ffn_kernel, n),
        out_shape=[
            jax.ShapeDtypeStruct((own, width), BF),
            jax.ShapeDtypeStruct((own, width), F32),
            jax.ShapeDtypeStruct((chip_rows, width), BF),
            jax.ShapeDtypeStruct((2, width, hidden), BF),
            jax.ShapeDtypeStruct(ahead, BF),
            jax.ShapeDtypeStruct(params.shape, F32),
        ],
        in_specs=[smem, smem, hbm, vmem, hbm, vmem, vmem],
        out_specs=[vmem, vmem, hbm, hbm, hbm, vmem],
        scratch_shapes=[
            pltpu.VMEM((rows, width), BF),
            pltpu.VMEM((rows, width), BF),
            pltpu.VMEM((rows, hidden), BF),
            pltpu.VMEM((rows, hidden), F32),
            pltpu.VMEM((rows, hidden), BF),
            pltpu.VMEM((2, width, hidden), BF),
            pltpu.VMEM((own, width), F32),
            pltpu.VMEM((nx - 1, SPLIT, part, width), F32),
            pltpu.VMEM((2, own, width), BF),
            pltpu.VMEM((2, own, width), BF),
            pltpu.VMEM(far, BF),
            pltpu.VMEM(far, BF),
            pltpu.VMEM(far, BF),
            pltpu.VMEM(far, BF),
            pltpu.VMEM((own, width), F32),
            pltpu.VMEM((own, width), F32),
            pltpu.VMEM((chip_rows, width), BF),
            pltpu.VMEM((2, width, hidden), BF),
            pltpu.VMEM(ahead, BF),
            pltpu.SemaphoreType.DMA((copies,)),
            pltpu.SemaphoreType.DMA((copies,)),
            pltpu.SemaphoreType.DMA((8,)),
        ],
        compiler_params=pltpu.CompilerParams(
            collective_id=4, has_side_effects=True, vmem_limit_bytes=56 * 2**20
        ),
        name="feed_forward",
    )(order, lengths, normed, resid, maps, cotangent, params)


CROSS_PLAN = (
    UP + BEGIN + 3, DOWN + ALONG + 1, LOAD, HEADS, DOWN + ALONG + 3, GRAD + OUTPUT,
    DOWN + BEGIN + 2, OUT + BEGIN + 3, TWIN + 0, OUT + BEGIN + 2, UP + ALONG + 3,
    OUT + BEGIN + 1, UP + BEGIN + 1, UP + BEGIN + 2, TWIN + 1, OUT + BEGIN + 0, TWIN + 2,
    DOWN + ALONG + 2, TWIN + 3, GRAD + QUERIES, QUERY + BEGIN + 1, QUERY + BEGIN + 3,
    QUERY + BEGIN + 2, MEMORY + PART, QUERY + BEGIN + 0, DOWN + BEGIN + 0, OUT + MIDDLE + 3,
    GRAD + TWIN, OUT + MIDDLE + 1, UP + ALONG + 1, INPUT + PART, QUERY + MIDDLE + 3,
    UP + ALONG + 2, OUT + MIDDLE + 2, OUT + ALONG + 3, MEMORY + ON, QUERY + MIDDLE + 1,
    OUT + ALONG + 1, OUT + MIDDLE + 0, QUERY + ALONG + 3, QUERY + MIDDLE + 2, UP + BEGIN + 0,
    OUT + ALONG + 2, DOWN + ALONG + 0, NORM, QUERY + MIDDLE + 0, QUERY + ALONG + 1,
    QUERY + ALONG + 2, OUT + ALONG + 0, ROWS + END, MEMORY + END, UP + ALONG + 0,
    QUERY + ALONG + 0,
)

SELF_PLAN = (
    MEMORY + GO, LOAD + OTHER, LOAD, CROSS + BEGIN + 3, CROSS + BEGIN + 2, GRAD + OUTPUT,
    OUT + BEGIN + 1, CROSS + BEGIN + 1, OUT + BEGIN + 0, HEADS, OUT + BEGIN + 3, OUT + BEGIN + 2,
    TWIN + 0, TWIN + 1, CROSS + MIDDLE + 3, TWIN + 2, TWIN + 3, GRAD + QUERIES, OUT + MIDDLE + 3,
    QUERY + BEGIN + 3, QUERY + BEGIN + 1, GRAD + TWIN, KEYS + BEGIN + 3, INPUT + PART,
    OUT + MIDDLE + 2, CROSS + ALONG + 3, OUT + ALONG + 3, CROSS + MIDDLE + 2, INPUT + ON,
    KEYS + BEGIN + 2, QUERY + MIDDLE + 3, OUT + MIDDLE + 1, KEYS + MIDDLE + 3, KEYS + MIDDLE + 2,
    OUT + ALONG + 2, CROSS + ALONG + 2, KEYS + BEGIN + 1, QUERY + BEGIN + 2, MEMORY + END,
    QUERY + MIDDLE + 1, OUT + ALONG + 1, QUERY + ALONG + 3, NORM, KEYS + ALONG + 3,
    QUERY + ALONG + 1, CROSS + BEGIN + 0, CROSS + MIDDLE + 1, QUERY + MIDDLE + 2,
    KEYS + ALONG + 2, QUERY + BEGIN + 0, HOME + END, KEYS + BEGIN + 0, KEYS + MIDDLE + 1,
    CROSS + MIDDLE + 0, OUT + MIDDLE + 0, CROSS + ALONG + 1, QUERY + ALONG + 2,
    KEYS + MIDDLE + 0, KEYS + ALONG + 1, QUERY + MIDDLE + 0, QUERY + ALONG + 0,
    CROSS + ALONG + 0, OUT + ALONG + 0, KEYS + ALONG + 0,
)

def backward_plan(tuned, nz, pairs, head, parts, tail):
    if nz == 4 and pairs == 4:
        return tuned
    plan = list(head) + [TWIN + p for p in range(pairs)] + list(parts)
    return tuple(plan) + tuple(tail)


class Halving:
    def zones(self):
        return range(self.n["z"] - 1, -1, -1)

    def zone(self, m):
        return flipped(self.at["z"], m)

    def sources(self, m):
        top = (m & -m) if m else self.n["z"]
        found, bit = [], 1
        while bit < top:
            found.append(m + bit)
            bit *= 2
        return found

    def settle(self, m, total, out):
        for k in self.sources(m):
            self.by_z[k].wait_recv()
            total = total + self.r3[k - 1].astype(F32)
        if m:
            self.s3[m - 1] = total.astype(BF)
            self.by_z[m] = self.wires.send(self.s3.at[m - 1], self.r3.at[m - 1], flip=m & -m)
        else:
            out[...] = total


def flips(n):
    found, bit = [], 1
    while bit < n["z"]:
        found.append({"flip": bit})
        bit *= 2
    return found


class RowScatter(Halving):
    def __init__(self, wires, moves, src, own, r1, s3, r3, out, ahead=None):
        self.wires, self.moves, self.src, self.own = wires, moves, src, own
        self.r1, self.s3, self.r3, self.out = r1, s3, r3, out
        self.n, self.at = wires.sizes, wires.place
        self.by_y, self.by_z = {}, {}
        self.loads = {m: moves.start(self.band(m, 0), own.at[m]) for m in self.zones()}
        self.early = []
        if ahead is not None:
            self.early = early_zones(self.n)
            for i, m in enumerate(self.early):
                for t in range(1, self.n["y"]):
                    self.by_y[m, t] = moves.start(ahead.at[t - 1, i], r1.at[t - 1, m])

    def band(self, m, t):
        rows = self.own.shape[1]
        index = self.zone(m) * self.n["y"] + (self.at["y"] + t) % self.n["y"]
        return self.src.at[pl.ds(pl.multiple_of(index * rows, rows), rows)]

    def begin(self, m):
        if m in self.early:
            return
        for t in range(1, self.n["y"]):
            self.by_y[m, t] = self.wires.send(self.band(m, t), self.r1.at[t - 1, m], y=t)

    def along(self, m):
        self.loads[m].wait()
        total = self.own[m].astype(F32)
        for t in range(1, self.n["y"]):
            if m in self.early:
                self.by_y[m, t].wait()
            else:
                self.by_y[m, t].wait_recv()
            total = total + self.r1[t - 1, m].astype(F32)
        self.settle(m, total, self.out)

    @staticmethod
    def copies(n):
        return n["z"] * (n["y"] - 1) + n["z"] - 1

    @staticmethod
    def scratch(n, rows, wide):
        nz, ny = n["z"], n["y"]
        return [
            pltpu.VMEM((nz, rows, wide), BF),
            pltpu.VMEM((ny - 1, nz, rows, wide), BF),
            pltpu.VMEM((nz - 1, rows, wide), BF),
            pltpu.VMEM((nz - 1, rows, wide), BF),
        ]


class Scatter(Halving):
    def __init__(self, wires, grads, first, count, x_first, r1, s2, r2, acc, s3, r3, out):
        self.wires, self.grads = wires, grads
        self.first, self.count, self.x_first = first, count, x_first
        self.r1, self.s2, self.r2, self.acc, self.s3, self.r3 = r1, s2, r2, acc, s3, r3
        self.out = out
        self.n, self.at = wires.sizes, wires.place
        self.rows, self.wide = acc.shape[2], acc.shape[3]
        self.stage1, self.stage2, self.by_z = {}, {}, {}

    def part(self, m, band, bands, column, columns):
        rows, wide = self.rows, self.wide
        start = self.zone(m) * self.n["y"] + band
        return self.grads.at[
            pl.ds(self.first, self.count),
            pl.ds(pl.multiple_of(start * rows, rows), bands * rows),
            pl.ds(pl.multiple_of(column * wide, wide), columns * wide),
        ]

    def begin(self, m):
        nx, ny = self.n["x"], self.n["y"]
        if self.x_first:
            for t in range(1, nx):
                src = self.part(m, 0, ny, (self.at["x"] + t) % nx, 1)
                self.stage1[m, t] = self.wires.send(src, self.r1.at[t - 1, m], x=t)
        else:
            for t in range(1, ny):
                src = self.part(m, (self.at["y"] + t) % ny, 1, 0, nx)
                self.stage1[m, t] = self.wires.send(src, self.r1.at[t - 1, m], y=t)

    def middle(self, m):
        nx, ny, rows, wide = self.n["x"], self.n["y"], self.rows, self.wide
        x, y = self.at["x"], self.at["y"]
        inner, outer = (ny, nx) if self.x_first else (nx, ny)
        for t in range(1, outer):
            self.stage1[m, t].wait_recv()
        for b in range(inner):
            if self.x_first:
                band = (y + b) % ny
                total = self.part(m, band, 1, x, 1)[...].astype(F32)
                here = (slice(None), pl.ds(pl.multiple_of(band * rows, rows), rows), slice(None))
            else:
                column = (x + b) % nx
                total = self.part(m, y, 1, column, 1)[...].astype(F32)
                here = (slice(None), slice(None), pl.ds(pl.multiple_of(column * wide, wide), wide))
            for t in range(1, outer):
                total = total + self.r1.at[t - 1, m][here].astype(F32)
            if b == 0:
                self.acc[m] = total
            else:
                self.s2[b - 1, m] = total.astype(BF)
        for t in range(1, inner):
            way = {"y": t} if self.x_first else {"x": t}
            self.stage2[m, t] = self.wires.send(self.s2.at[t - 1, m], self.r2.at[t - 1, m], **way)

    def along(self, m):
        inner = self.n["y"] if self.x_first else self.n["x"]
        total = self.acc[m]
        for t in range(1, inner):
            self.stage2[m, t].wait_recv()
            total = total + self.r2[t - 1, m].astype(F32)
        self.settle(m, total, self.out)

    @staticmethod
    def copies(n):
        nz, ny, nx = n["z"], n["y"], n["x"]
        return nz * (nx - 1 + ny - 1) + nz - 1

    @staticmethod
    def scratch(n, count, x_first, rows, wide):
        nz, ny, nx = n["z"], n["y"], n["x"]
        inner = ny if x_first else nx
        if x_first:
            first = (nx - 1, nz, count, ny * rows, wide)
        else:
            first = (ny - 1, nz, count, rows, nx * wide)
        return [
            pltpu.VMEM(first, BF),
            pltpu.VMEM((inner - 1, nz, count, rows, wide), BF),
            pltpu.VMEM((inner - 1, nz, count, rows, wide), BF),
            pltpu.VMEM((nz, count, rows, wide), F32),
            pltpu.VMEM((nz - 1, count, rows, wide), BF),
            pltpu.VMEM((nz - 1, count, rows, wide), BF),
        ]


ONE = (8, 128)


def squares(refs):
    total = jnp.zeros(ONE, F32)
    for ref in refs:
        value = ref[...]
        total = total + jnp.sum((value * value).reshape((-1,) + ONE), axis=0)
    return total


def register(steps, name, group):
    for m in group.zones():
        steps[name + BEGIN + m] = functools.partial(group.begin, m)
        steps[name + ALONG + m] = functools.partial(group.along, m)
        if hasattr(group, "middle"):
            steps[name + MIDDLE + m] = functools.partial(group.middle, m)


def spelled(n, names):
    plan = []
    for name, kinds in names:
        for kind in kinds:
            plan += [name + kind + m for m in range(n["z"] - 1, -1, -1)]
    return plan


WHOLE = (BEGIN, MIDDLE, ALONG)


def cross_back_kernel(
    n, order, reaches, dc_hbm, dx_ref, w_hbm, q_hbm, k_hbm, v_hbm, o_hbm, l_ref, h_hbm, m_hbm, x_ref, p_ref,
    dw_hbm, early_hbm, oup_ref, odown_ref, oq_ref, oo_ref, og, odx_ref, odb, om, on_ref, osq_ref, *scratch,
):
    (
        dc_s, w_s, q_s, k_s, v_s, o_s, h_s, m_s, g_s, dq_s, dk_s, dv_s, ds_s, gr_s, give_s, got_s,
        db_s, pm_s, rm_s, sm_s, cm_s, om_s,
    ) = scratch[:22]
    send_sem, recv_sem, move_sem = scratch[-3:]
    at = grid_place()
    x, c = at["x"], at["c"]
    nz, ny, nx = n["z"], n["y"], n["x"]
    wires = Wires(n, at, send_sem, recv_sem)
    moves = Moves(move_sem)
    loads = [
        moves.start(a, b)
        for a, b in (
            (dc_hbm, dc_s), (w_hbm.at[3], w_s.at[3]), (o_hbm, o_s), (q_hbm, q_s), (k_hbm, k_s),
            (v_hbm, v_s),
        )
    ]
    down = RowScatter(wires, moves, dw_hbm.at[1], *scratch[22:26], odown_ref, early_hbm)
    up = RowScatter(wires, moves, dw_hbm.at[0], *scratch[26:30], oup_ref)
    out_sum = Scatter(wires, gr_s, 3, 1, True, *scratch[30:36], oo_ref)
    query_sum = Scatter(wires, gr_s, 0, 1, True, *scratch[36:42], oq_ref)
    later = [moves.start(h_hbm, h_s), moves.start(m_hbm, m_s)]
    get_maps = moves.start(w_hbm.at[0:3], w_s.at[0:3])
    wires.greet(
        flips(n)
        + [{"y": s} for s in range(1, ny)]
        + [{"x": s} for s in range(1, nx)]
        + [{"c": 1}]
    )
    chip_rows, width = dc_s.shape
    slot = m_s.shape[0]
    own = chip_rows // 2
    strip = min(STRIP, own)
    pairs = q_s.shape[1] // PAIR
    deep = om_s.shape[1]
    mine = pl.ds(pl.multiple_of(c * own, own), own)
    other = pl.ds(pl.multiple_of((1 - c) * own, own), own)
    bound = jnp.full((1, chip_rows), reaches[order[at["z"] * ny + at["y"]]], jnp.int32)
    held = {}
    steps = {}
    for name, group in ((DOWN, down), (UP, up), (OUT, out_sum), (QUERY, query_sum)):
        register(steps, name, group)

    def step(name):
        def keep(function):
            steps[name] = function
            return function

        return keep

    @step(LOAD)
    def _():
        for copy in loads:
            copy.wait()

    @step(HEADS)
    def _():
        mat_rows(g_s, dc_s, w_s.at[3], chip_rows, strip)

    for p in range(pairs):

        def pair(p=p):
            attend_pair_back(
                p, 256, bound, q_s, k_s, v_s, o_s, l_ref, g_s, dq_s, dk_s, dv_s, ds_s
            )

        steps[TWIN + p] = pair

    maps = [get_maps]

    def need_maps():
        while maps:
            maps.pop().wait()

    @step(INPUT + PART)
    def _():
        need_maps()

        def body(rows):
            give_s[rows, :] = dot(dq_s[rows, :], w_s[0], 1, 1).astype(BF)

        loop_rows(chip_rows, strip, body)
        held["rows"] = wires.send(give_s.at[other], got_s, c=1)

    @step(MEMORY + PART)
    def _():
        need_maps()
        piece = min(512, width)

        def body(rows):
            for col in range(0, width, piece):
                some = slice(col, col + piece)
                sums = dot(dk_s[rows, :], w_s[1, some, :], 1, 1)
                sums = (sums + dot(dv_s[rows, :], w_s[2, some, :], 1, 1)).astype(BF)
                for b in range(piece // deep):
                    index = col // deep + b
                    pm_s[index // 2, index % 2, rows, :] = sums[:, b * deep : (b + 1) * deep]

        loop_rows(slot, strip, body)
        held["memory"] = wires.send(pm_s.at[:, 1 - c], rm_s, c=1)

    @step(NORM)
    def _():
        held["rows"].wait_recv()
        upstream = give_s[mine, :].astype(F32) + got_s[...].astype(F32)
        grad, normed = norm_back_rows(x_ref[...], upstream, p_ref[1:2, :])
        total = dx_ref[...] + grad
        odx_ref[...] = total
        db_s[mine, :] = total.astype(BF)
        held["near"] = wires.send(db_s.at[mine], db_s.at[mine], c=1)
        line = lax.broadcasted_iota(jnp.int32, on_ref.shape, 0)
        on_ref[...] = jnp.where(line == 1, row_sum(upstream * normed), 0.0) + jnp.where(
            line == 5, row_sum(upstream), 0.0
        )

    @step(MEMORY + ON)
    def _():
        held["memory"].wait_recv()
        held["far"] = []
        for t in range(1, nx):
            index = (x + t) % nx
            sm_s[t - 1] = (pm_s[index, c].astype(F32) + rm_s[index].astype(F32)).astype(BF)
            held["far"].append(wires.send(sm_s.at[t - 1], cm_s.at[t - 1], x=t))

    @step(MEMORY + END)
    def _():
        total = pm_s[x, c].astype(F32) + rm_s[x].astype(F32)
        for t in range(1, nx):
            held["far"][t - 1].wait_recv()
            total = total + cm_s[t - 1].astype(F32)
        om_s[...] = total.astype(BF)
        moves.store(om_s, om)

    def weight_grad(i, left, right):
        size = min(256, width)
        for col in range(0, width, size):
            cols = slice(col, col + size)
            gr_s[i, cols, :] = dot(left[:, cols], right[...], 0, 0).astype(BF)

    @step(GRAD + OUTPUT)
    def _():
        weight_grad(3, dc_s, o_s)

    @step(GRAD + QUERIES)
    def _():
        later[0].wait()
        weight_grad(0, h_s, dq_s)

    @step(GRAD + TWIN)
    def _():
        later[1].wait()
        weight_grad(1, m_s, dk_s)
        weight_grad(2, m_s, dv_s)
        moves.store(gr_s.at[1:3], og)

    @step(ROWS + END)
    def _():
        held["near"].wait_recv()
        moves.store(db_s, odb)

    plan = backward_plan(
        CROSS_PLAN, nz, pairs,
        [LOAD, HEADS] + spelled(n, [(DOWN, (BEGIN,)), (UP, (BEGIN,))]),
        [INPUT + PART, MEMORY + PART, NORM, MEMORY + ON, GRAD + OUTPUT, GRAD + QUERIES, GRAD + TWIN],
        spelled(n, [(DOWN, (ALONG,)), (UP, (ALONG,)), (OUT, WHOLE), (QUERY, WHOLE)])
        + [MEMORY + END, ROWS + END],
    )
    for name in plan:
        steps[name]()
    osq_ref[...] = squares((oup_ref, odown_ref, oq_ref, oo_ref))
    moves.close()
    wires.close()


def cross_back(
    order, reaches, rows_grad, resid_grad, maps, saved, normed, frames, resid, params, ffn_grads,
    early,
):
    n = grid_sizes()
    nz, ny, nx = n["z"], n["y"], n["x"]
    queries, keys, values, mixed, logsum = saved
    chip_rows, width = rows_grad.shape
    own = chip_rows // 2
    slot, local = keys.shape
    hidden = ffn_grads.shape[2]
    rows, wide = width // (nz * ny), local // nx
    deep = width // (2 * nx)
    copies = 2 * RowScatter.copies(n) + 2 * Scatter.copies(n) + 3 + (nx - 1)
    vmem = pl.BlockSpec(memory_space=pltpu.VMEM)
    smem = pl.BlockSpec(memory_space=pltpu.SMEM)
    hbm = pl.BlockSpec(memory_space=pl.ANY)
    half = lambda *shape: pltpu.VMEM(shape, BF)
    return pl.pallas_call(
        functools.partial(cross_back_kernel, n),
        out_shape=[
            jax.ShapeDtypeStruct((rows, hidden), F32),
            jax.ShapeDtypeStruct((rows, hidden), F32),
            jax.ShapeDtypeStruct((1, rows, wide), F32),
            jax.ShapeDtypeStruct((1, rows, wide), F32),
            jax.ShapeDtypeStruct((2, width, local), BF),
            jax.ShapeDtypeStruct((own, width), F32),
            jax.ShapeDtypeStruct((chip_rows, width), BF),
            jax.ShapeDtypeStruct((slot, deep), BF),
            jax.ShapeDtypeStruct(params.shape, F32),
            jax.ShapeDtypeStruct(ONE, F32),
        ],
        in_specs=[smem, smem, hbm, vmem] + [hbm] * 5 + [vmem, hbm, hbm, vmem, vmem, hbm, hbm],
        out_specs=[vmem] * 4 + [hbm, vmem, hbm, hbm, vmem, vmem],
        scratch_shapes=[
            half(chip_rows, width),
            half(4, width, local),
            half(chip_rows, local),
            half(slot, local),
            half(slot, local),
            half(chip_rows, local),
            half(chip_rows, width),
            half(slot, width),
            half(chip_rows, local),
            half(chip_rows, local),
            half(slot, local),
            half(slot, local),
            half(2, slot, chip_rows),
            half(4, width, local),
            half(chip_rows, width),
            half(own, width),
            half(chip_rows, width),
            half(nx, 2, slot, deep),
            half(nx, slot, deep),
            half(nx - 1, slot, deep),
            half(nx - 1, slot, deep),
            half(slot, deep),
        ]
        + RowScatter.scratch(n, rows, hidden) * 2
        + Scatter.scratch(n, 1, True, rows, wide) * 2
        + [
            pltpu.SemaphoreType.DMA((copies,)),
            pltpu.SemaphoreType.DMA((copies,)),
            pltpu.SemaphoreType.DMA((14 + 2 * nz + 2 * (ny - 1),)),
        ],
        compiler_params=pltpu.CompilerParams(
            collective_id=5, has_side_effects=True, vmem_limit_bytes=56 * 2**20
        ),
        name="cross_back",
    )(
        order, reaches, rows_grad, resid_grad, maps, queries, keys, values, mixed, logsum, normed, frames,
        resid, params, ffn_grads, early,
    )


def self_back_kernel(
    n, order, lengths, db_hbm, dx_ref, w_hbm, q_hbm, k_hbm, v_hbm, o_hbm, l_ref, h_hbm, x_ref, p_ref,
    cg_hbm, m_hbm, np_ref, nq_ref, sq_ref, oc_ref, oo_ref, oq_ref, op_ref, os_ref, om_ref, on_ref,
    norm_ref, *scratch,
):
    (
        db_s, w_s, q_s, k_s, v_s, o_s, h_s, g_s, dq_s, dk_s, dv_s, ds_s, cg_s, gr_s, part_s, rc_s,
        sx_s, rx_s, out_s, np_s, nn_s, nf_s,
    ) = scratch[:22]
    one_s, near_s, sum_s, far_s = scratch[46:50]
    send_sem, recv_sem, go_sem, come_sem, move_sem = scratch[-5:]
    at = grid_place()
    z, y, x, c = at["z"], at["y"], at["x"], at["c"]
    nz, ny, nx = n["z"], n["y"], n["x"]
    data, model = z * ny + y, x * 2 + c
    wires = Wires(n, at, send_sem, recv_sem)
    moves = Moves(move_sem)
    get_cross = moves.start(cg_hbm, cg_s)
    loads = [
        moves.start(a, b)
        for a, b in (
            (db_hbm, db_s), (w_hbm.at[3], w_s.at[3]), (o_hbm, o_s), (q_hbm, q_s), (k_hbm, k_s),
            (v_hbm, v_s),
        )
    ]
    later = [moves.start(h_hbm, h_s), moves.start(w_hbm.at[0:3], w_s.at[0:3])]
    wires.greet(
        [
            dict(z=sz, y=sy, x=sx, c=sc)
            for sz in range(nz)
            for sy in range(ny)
            for sx in range(nx)
            for sc in range(2)
            if sz or sy or sx or sc
        ]
    )
    cross_sum = Scatter(wires, cg_s, 0, 2, False, *scratch[22:28], oc_ref)
    out_sum = Scatter(wires, gr_s, 3, 1, True, *scratch[28:34], oo_ref)
    query_sum = Scatter(wires, gr_s, 0, 1, True, *scratch[34:40], oq_ref)
    pair_sum = Scatter(wires, gr_s, 1, 2, False, *scratch[40:46], op_ref)
    chip_rows, width = db_s.shape
    slot = h_s.shape[0]
    own = chip_rows // 2
    strip = min(STRIP, own)
    pairs = q_s.shape[1] // PAIR
    chip_start = x * chip_rows
    bound = lax.broadcasted_iota(jnp.int32, (1, chip_rows), 1) + chip_start + 1
    bound = jnp.minimum(bound, lengths[order[data]])
    held = {}
    steps = {}
    for name, group in (
        (CROSS, cross_sum), (OUT, out_sum), (QUERY, query_sum), (KEYS, pair_sum)
    ):
        register(steps, name, group)

    def step(name):
        def keep(function):
            steps[name] = function
            return function

        return keep

    @step(LOAD + OTHER)
    def _():
        get_cross.wait()

    @step(LOAD)
    def _():
        for copy in loads:
            copy.wait()

    @step(MEMORY + GO)
    def _():
        held["memory"] = [
            wires.send(m_hbm.at[wires.peer(**shift)[0]], om_ref.at[data], **shift)
            for shift in dp_shifts(n)
        ]
        held["memory own"] = moves.start(m_hbm.at[data], om_ref.at[data])

    @step(MEMORY + END)
    def _():
        for copy in held["memory"]:
            copy.wait_recv()
        held["memory own"].wait()

    @step(HEADS)
    def _():
        mat_rows(g_s, db_s, w_s.at[3], chip_rows, strip)

    for p in range(pairs):

        def pair(p=p):
            attend_pair_back(
                p, 256, bound, q_s, k_s, v_s, o_s, l_ref, g_s, dq_s, dk_s, dv_s, ds_s
            )

        steps[TWIN + p] = pair

    def block(chip, core):
        return pl.ds(pl.multiple_of((chip * 2 + core) * own, own), own)

    def need(index):
        if later[index] is not None:
            later[index].wait()
            later[index] = None

    @step(INPUT + PART)
    def _():
        need(1)
        def keys_values(rows):
            sums = dot(dk_s[rows, :], w_s[1], 1, 1) + dot(dv_s[rows, :], w_s[2], 1, 1)
            part_s[rows, :] = sums.astype(BF)

        loop_rows(slot, strip, keys_values)

        def queries(rows):
            here = shifted(rows, chip_start)
            sums = part_s[here, :].astype(F32) + dot(dq_s[rows, :], w_s[0], 1, 1)
            part_s[here, :] = sums.astype(BF)

        loop_rows(chip_rows, strip, queries)
        held["core"] = [
            wires.send(part_s.at[block(b, 1 - c)], rc_s.at[b], c=1) for b in range(nx)
        ]

    @step(INPUT + ON)
    def _():
        for copy in held["core"]:
            copy.wait_recv()
        held["far"] = []
        for t in range(1, nx):
            index = (x + t) % nx
            sums = part_s[block(index, c), :].astype(F32) + rc_s[index].astype(F32)
            sx_s[t - 1] = sums.astype(BF)
            held["far"].append(wires.send(sx_s.at[t - 1], rx_s.at[t - 1], x=t))

    def weight_grad(i, left, right):
        size = min(256, width)
        for col in range(0, width, size):
            cols = slice(col, col + size)
            gr_s[i, cols, :] = dot(left[:, cols], right[...], 0, 0).astype(BF)

    @step(GRAD + OUTPUT)
    def _():
        weight_grad(3, db_s, o_s)

    @step(GRAD + QUERIES)
    def _():
        need(0)
        weight_grad(0, h_s.at[pl.ds(pl.multiple_of(chip_start, chip_rows), chip_rows)], dq_s)

    @step(GRAD + TWIN)
    def _():
        need(0)
        weight_grad(1, h_s, dk_s)
        weight_grad(2, h_s, dv_s)

    lines, deep = os_ref.shape[1], os_ref.shape[2]
    blocks = own // lines

    def homeward():
        for b in range(blocks):
            for m in range(2 * nx):
                target = (model * blocks + b, m)
                src = out_s.at[b * lines : (b + 1) * lines, m * deep : (m + 1) * deep]
                mine = jnp.logical_and(target[0] == data, model == m)
                remote = pltpu.make_async_remote_copy(
                    src_ref=src,
                    dst_ref=os_ref.at[data],
                    send_sem=go_sem.at[b * 2 * nx + m],
                    recv_sem=come_sem.at[data],
                    device_id=target,
                    device_id_type=pl.DeviceIdType.MESH,
                )
                yield mine, remote, pltpu.make_async_copy(src, os_ref.at[data], come_sem.at[data])

    @step(NORM)
    def _():
        upstream = part_s[block(x, c), :].astype(F32) + rc_s[x].astype(F32)
        for t in range(1, nx):
            held["far"][t - 1].wait_recv()
            upstream = upstream + rx_s[t - 1].astype(F32)
        grad, normed = norm_back_rows(x_ref[...].astype(F32), upstream, p_ref[0:1, :])
        out_s[...] = (dx_ref[...] + grad).astype(BF)
        for mine, remote, here in homeward():
            pl.when(mine)(lambda: here.start())
            pl.when(jnp.logical_not(mine))(lambda: remote.start())
        line = lax.broadcasted_iota(jnp.int32, np_ref.shape, 0)
        params = (
            np_ref[...]
            + nq_ref[...]
            + jnp.where(line == 0, row_sum(upstream * normed), 0.0)
            + jnp.where(line == 4, row_sum(upstream), 0.0)
        )
        columns = on_ref.shape[1]
        for k in range(nz * ny):
            np_s[0, k] = params[:, k * columns : (k + 1) * columns]
        held["norm near"] = [
            wires.send(np_s.at[0], nn_s.at[i], **s) for i, s in enumerate(mp_shifts(n))
        ]

    @step(HOME + END)
    def _():
        total = np_s[0]
        for i, copy in enumerate(held["norm near"]):
            copy.wait_recv()
            total = total + nn_s[i]
        np_s[1] = total
        held["norm far"] = [
            wires.send(np_s.at[1, wires.peer(**shift)[0]], nf_s.at[i], **shift)
            for i, shift in enumerate(dp_shifts(n))
        ]

    plan = backward_plan(
        SELF_PLAN, nz, pairs,
        [MEMORY + GO, LOAD + OTHER, LOAD, HEADS] + spelled(n, [(CROSS, (BEGIN,))]),
        [INPUT + PART, INPUT + ON, GRAD + OUTPUT, GRAD + QUERIES, GRAD + TWIN],
        spelled(n, [(CROSS, (MIDDLE, ALONG)), (OUT, WHOLE)])
        + [NORM, HOME + END]
        + spelled(n, [(QUERY, WHOLE), (KEYS, WHOLE)])
        + [MEMORY + END],
    )
    for name in plan:
        steps[name]()
    total = np_s[1, data]
    for i, copy in enumerate(held["norm far"]):
        copy.wait_recv()
        total = total + nf_s[i]
    on_ref[...] = total
    norm_squares = jnp.sum(total * total) / (2 * nx * ONE[0] * ONE[1])
    total = sq_ref[...] + squares((oc_ref, oo_ref, oq_ref, op_ref)) + norm_squares
    one_s[...] = total
    copies = [wires.send(one_s, near_s.at[i], **s) for i, s in enumerate(mp_shifts(n))]
    for i, copy in enumerate(copies):
        copy.wait_recv()
        total = total + near_s[i]
    sum_s[...] = total
    copies = [wires.send(sum_s, far_s.at[i], **s) for i, s in enumerate(dp_shifts(n))]
    for i, copy in enumerate(copies):
        copy.wait_recv()
        total = total + far_s[i]
    norm_ref[0] = jnp.sqrt(jnp.sum(total))
    for mine, remote, here in homeward():
        pl.when(jnp.logical_not(mine))(lambda: remote.wait_send())
    for r in range(nz * ny):
        pltpu.make_async_copy(os_ref.at[r], os_ref.at[r], come_sem.at[r]).wait()
    wires.close()


def self_back(
    order, lengths, rows_grad, resid_grad, maps, saved, normed, inputs, params, cross_grads, memory,
    norm_ffn, norm_cross, square_part,
):
    n = grid_sizes()
    nz, ny, nx = n["z"], n["y"], n["x"]
    data, model = nz * ny, 2 * nx
    queries, keys, values, mixed, logsum = saved
    chip_rows, width = rows_grad.shape
    own = chip_rows // 2
    slot, local = keys.shape
    rows, wide = width // data, local // nx
    utterances, lines, deep = memory.shape
    columns = width // data
    copies = 4 * Scatter.copies(n) + 3 * (data - 1) + nx + (nx - 1) + 2 * (model - 1)
    vmem = pl.BlockSpec(memory_space=pltpu.VMEM)
    smem = pl.BlockSpec(memory_space=pltpu.SMEM)
    hbm = pl.BlockSpec(memory_space=pl.ANY)
    half = lambda *shape: pltpu.VMEM(shape, BF)
    return pl.pallas_call(
        functools.partial(self_back_kernel, n),
        out_shape=[
            jax.ShapeDtypeStruct((2, rows, wide), F32),
            jax.ShapeDtypeStruct((1, rows, wide), F32),
            jax.ShapeDtypeStruct((1, rows, wide), F32),
            jax.ShapeDtypeStruct((2, rows, wide), F32),
            jax.ShapeDtypeStruct((data, lines, deep), BF),
            jax.ShapeDtypeStruct((data, lines, deep), BF),
            jax.ShapeDtypeStruct((params.shape[0], columns), F32),
            jax.ShapeDtypeStruct((1,), F32),
        ],
        in_specs=[smem, smem, hbm, vmem]
        + [hbm] * 5
        + [vmem, hbm, vmem, vmem, hbm, hbm, vmem, vmem, vmem],
        out_specs=[vmem] * 4 + [hbm, hbm, vmem, smem],
        scratch_shapes=[
            half(chip_rows, width),
            half(4, width, local),
            half(chip_rows, local),
            half(slot, local),
            half(slot, local),
            half(chip_rows, local),
            half(slot, width),
            half(chip_rows, local),
            half(chip_rows, local),
            half(slot, local),
            half(slot, local),
            half(2, slot, chip_rows),
            half(2, width, local),
            half(4, width, local),
            half(slot, width),
            half(nx, own, width),
            half(nx - 1, own, width),
            half(nx - 1, own, width),
            half(own, width),
            pltpu.VMEM((2, data, params.shape[0], columns), F32),
            pltpu.VMEM((model - 1, data, params.shape[0], columns), F32),
            pltpu.VMEM((data - 1, params.shape[0], columns), F32),
        ]
        + Scatter.scratch(n, 2, False, rows, wide)
        + Scatter.scratch(n, 1, True, rows, wide)
        + Scatter.scratch(n, 1, True, rows, wide)
        + Scatter.scratch(n, 2, False, rows, wide)
        + [
            pltpu.VMEM(ONE, F32),
            pltpu.VMEM((model - 1,) + ONE, F32),
            pltpu.VMEM(ONE, F32),
            pltpu.VMEM((data - 1,) + ONE, F32),
            pltpu.SemaphoreType.DMA((copies,)),
            pltpu.SemaphoreType.DMA((copies,)),
            pltpu.SemaphoreType.DMA((data,)),
            pltpu.SemaphoreType.DMA((data,)),
            pltpu.SemaphoreType.DMA((14,)),
        ],
        compiler_params=pltpu.CompilerParams(
            collective_id=1, has_side_effects=True, vmem_limit_bytes=56 * 2**20
        ),
        name="self_back",
    )(
        order, lengths, rows_grad, resid_grad, maps, queries, keys, values, mixed, logsum, normed,
        inputs, params, cross_grads, memory, norm_ffn, norm_cross, square_part,
    )


def adam_step(weight, moment, square, gradient, step_rate, weight_decay):
    moment_new = BETA_FIRST * moment + (1.0 - BETA_FIRST) * gradient
    square_new = BETA_SECOND * square + (1.0 - BETA_SECOND) * gradient * gradient
    moment_hat = moment_new * (1.0 / (1.0 - BETA_FIRST**STEP))
    square_hat = square_new * (1.0 / (1.0 - BETA_SECOND**STEP))
    updated = weight - step_rate * (
        moment_hat / (jnp.sqrt(square_hat) + ADAM_EPSILON) + weight_decay * weight
    )
    return (updated, moment_new, square_new)


def update_kernel(order, norm, *refs):
    grads, refs = refs[:9], refs[9:]
    y_hbm, refs = refs[0], refs[1:]
    back, refs = refs[:2], refs[2:]
    old, refs = refs[:12], refs[12:]
    oy, refs = refs[0], refs[1:]
    home, refs = refs[:2], refs[2:]
    new, refs = refs[:12], refs[12:]
    vault, refs = refs[:12], refs[12:]
    back_s, home_s, y_s, move_sem = refs[:2], refs[2:4], refs[4], refs[5]
    moves = Moves(move_sem)
    back_loads = [moves.start(a, b) for a, b in zip(back, back_s)]
    loads = {}
    for kind in (2, 1, 0):
        loads[kind] = [moves.start(old[3 * j + kind], vault[3 * j + kind]) for j in range(4)]
    get_y = moves.start(y_hbm, y_s)
    clip_scale = jnp.minimum(1.0, THRESHOLD / (norm[0] + 1e-06))

    def apply(kind, part, gradient, rate, decay):
        weight, moment, square, average = (vault[3 * j + kind] for j in range(4))
        updated, moment_new, square_new = adam_step(
            weight[part], moment[part], square[part], clip_scale * gradient, rate, decay
        )
        mixed = AVERAGING * average[part] + (1.0 - AVERAGING) * updated
        for j, value in enumerate((updated, moment_new, square_new, mixed)):
            vault[3 * j + kind][part] = value
            moves.store(vault[3 * j + kind].at[part], new[3 * j + kind].at[part])

    utterances = home_s[0].shape[0]
    for copy in back_loads:
        copy.wait()
    for i in range(utterances):
        place = 0
        for r in range(utterances):
            place = place + jnp.where(order[r] == i, r, 0)
        for src, dst in zip(back_s, home_s):
            dst[i] = src[place].astype(F32)
    for src, dst in zip(home_s, home):
        moves.store(src, dst)

    sq, sp, so, cq, cp, co, up, down, line = grads
    for copy in loads[2]:
        copy.wait()
    apply(2, slice(None), line[...], NORM_RATE, 0.0)
    for copy in loads[1]:
        copy.wait()
    for part, ref in ((0, up), (1, down)):
        apply(1, slice(part, part + 1), ref[...][None], MATRIX_RATE, MATRIX_DECAY)
    for copy in loads[0]:
        copy.wait()
    for part, ref in (
        (slice(0, 1), sq), (slice(1, 3), sp), (slice(3, 4), so), (slice(4, 5), cq),
        (slice(5, 7), cp), (slice(7, 8), co),
    ):
        apply(0, part, ref[...], MATRIX_RATE, MATRIX_DECAY)

    get_y.wait()
    moves.store(y_s, oy)
    moves.close()


def update(order, norm, grads, output, back, old):
    vmem = pl.BlockSpec(memory_space=pltpu.VMEM)
    smem = pl.BlockSpec(memory_space=pltpu.SMEM)
    hbm = pl.BlockSpec(memory_space=pl.ANY)
    full = lambda v: jax.ShapeDtypeStruct(v.shape, F32)
    return pl.pallas_call(
        update_kernel,
        out_shape=[jax.ShapeDtypeStruct(output.shape, BF)]
        + [full(v) for v in back]
        + [full(v) for v in old],
        in_specs=[smem, smem] + [vmem] * 9 + [hbm] * 15,
        out_specs=[hbm] * 15,
        scratch_shapes=[pltpu.VMEM(v.shape, F32) for v in old]
        + [pltpu.VMEM(v.shape, BF) for v in back]
        + [pltpu.VMEM(v.shape, F32) for v in back]
        + [pltpu.VMEM(output.shape, BF)]
        + [pltpu.SemaphoreType.DMA((64,))],
        compiler_params=pltpu.CompilerParams(vmem_limit_bytes=56 * 2**20),
        name="update",
    )(order, norm, *grads, output, *back, *old)


def per_device(
    states,
    memory,
    cotangent,
    lengths,
    memory_lengths,
    regroup_order,
    attn_weights,
    ffn_weights,
    norm_params,
    attn_mean,
    ffn_mean,
    norm_mean,
    attn_square,
    ffn_square,
    norm_square,
    attn_average,
    ffn_average,
    norm_average,
):
    n = grid_sizes()
    at = grid_place()
    nz, ny, nx = n["z"], n["y"], n["x"]
    data_index = lax.axis_index("dp")
    model_index = lax.axis_index("mp")
    data_size = lax.axis_size("dp")
    width = states.shape[2] * lax.axis_size("mp")
    slot = states.shape[1] * data_size
    own_rows = cotangent.shape[1]
    chip_rows = 2 * own_rows
    chip_start = at["x"] * chip_rows

    (
        weights_self,
        weights_cross,
        ffn_maps,
        norm_values,
        frames,
        inputs,
        normed_first,
        query_self,
        key_self,
        value_self,
        mixed_self,
        logsum_self,
        resid_one_own,
        normed_second,
        query_cross,
        key_cross,
        value_cross,
        mixed_cross,
        logsum_cross,
        resid_two_own,
        normed_third,
    ) = forward(
        regroup_order,
        lengths,
        memory_lengths,
        states,
        memory,
        norm_params,
        attn_weights,
        ffn_weights,
        own_rows,
    )

    layer_output, grad_two, cross_rows, ffn_grads, early, norm_ffn = feed_forward(
        regroup_order, lengths, normed_third, resid_two_own, ffn_maps, cotangent[0], norm_values
    )
    (
        shard_up,
        shard_down,
        cross_q,
        cross_o,
        cross_grads,
        grad_one,
        self_rows,
        memory_part,
        norm_cross,
        square_part,
    ) = (
        cross_back(
            regroup_order,
            memory_lengths,
            cross_rows,
            grad_two,
            weights_cross,
            (query_cross, key_cross, value_cross, mixed_cross, logsum_cross),
            normed_second,
            frames,
            resid_one_own,
            norm_values,
            ffn_grads,
            early,
        )
    )
    cross_p, self_o, self_q, self_p, back_states, back_memory, norm_shard, grad_norm = self_back(
        regroup_order,
        lengths,
        self_rows,
        grad_one,
        weights_self,
        (query_self, key_self, value_self, mixed_self, logsum_self),
        normed_first,
        inputs,
        norm_values,
        cross_grads,
        memory_part.reshape(data_size, -1, memory_part.shape[1]),
        norm_ffn,
        norm_cross,
        square_part,
    )
    grads = (self_q, self_p, self_o, cross_q, cross_p, cross_o, shard_up, shard_down, norm_shard)
    results = update(
        regroup_order,
        grad_norm,
        grads,
        layer_output,
        (back_states, back_memory),
        (
            attn_weights,
            ffn_weights,
            norm_params,
            attn_mean,
            ffn_mean,
            norm_mean,
            attn_square,
            ffn_square,
            norm_square,
            attn_average,
            ffn_average,
            norm_average,
        ),
    )
    return (results[0][None],) + tuple(results[1:]) + (grad_norm[0],)


def solution(mesh):
    rows = P(None, "dp", "mp")
    line = P(None, "dp")
    return jax.shard_map(
        per_device,
        mesh=mesh,
        in_specs=(rows, rows, P("dp", "mp", None), P(), P(), P())
        + (rows, rows, line) * 4,
        out_specs=(P("dp", "mp", None), rows, rows) + (rows, rows, line) * 4 + (P(),),
        check_vma=False,
    )
```

```python
import functools

import jax
import jax.numpy as jnp
from jax import lax
from jax.experimental import pallas as pl
from jax.experimental.pallas import tpu as pltpu
from jax.sharding import PartitionSpec as P

HD = 64
STEP = 10


EPSILON = 1e-05
NEGATIVE = -1000000000.0
BETA_FIRST = 0.9
BETA_SECOND = 0.999
ADAM_EPSILON = 1e-08
MATRIX_RATE = 0.05
NORM_RATE = 1.0
MATRIX_DECAY = 0.1
AVERAGING = 0.7
THRESHOLD = 1.0
BF = jnp.bfloat16
F32 = jnp.float32


(
    CROSS, DOWN, FIRST, GRAD, HOME, INPUT, KEYS, LOAD, MEMORY, OUT, QUERY, ROWS, SECOND, SELF, STATES, THIRD, UP,
) = range(1000, 18000, 1000)
(
    ALONG, BEGIN, END, FAN, GO, HEADS, LINE, MIDDLE, NORM, ON, OTHER, OUTPUT, PART, PASS, QUERIES, TURN, TWIN,
) = range(10, 180, 10)


def grid_sizes():
    dp = lax.axis_size("dp")
    mp = lax.axis_size("mp")
    ny = 1 << ((dp.bit_length() - 1) // 2)
    return {"z": dp // ny, "y": ny, "x": mp // 2, "c": 2}


def grid_place():
    n = grid_sizes()
    dp = lax.axis_index("dp")
    mp = lax.axis_index("mp")
    return {"z": dp // n["y"], "y": dp % n["y"], "x": mp // 2, "c": mp % 2}


def dot(left, right, left_dim, right_dim):
    return lax.dot_general(
        left, right, (((left_dim,), (right_dim,)), ((), ())), preferred_element_type=F32
    )


PAIR = 2 * HD


def only_head(value, head):
    lane = lax.broadcasted_iota(jnp.int32, value.shape, 1)
    keep = (lane < HD) if head == 0 else (lane >= HD)
    return jnp.where(keep, value, jnp.zeros_like(value))


def attend_pair(p, chunk, bound, q_ref, k_ref, v_ref, o_ref, sum_ref, score_ref, weight_ref):
    lanes = pl.ds(pl.multiple_of(p * PAIR, PAIR), PAIR)
    keys = k_ref.shape[0]
    queries = q_ref[:, lanes] * BF(HD**-0.5)
    values = v_ref[:, lanes]
    mixed = []
    for head in range(2):
        masked = only_head(queries, head)
        top = None
        for start in range(0, keys, chunk):
            block = slice(start, start + chunk)
            scores = dot(k_ref[block, lanes], masked, 1, 1)
            position = lax.broadcasted_iota(jnp.int32, scores.shape, 0) + start
            scores = jnp.where(position < bound, scores, NEGATIVE)
            score_ref[head, block, :] = scores
            highest = jnp.max(scores, axis=0, keepdims=True)
            top = highest if top is None else jnp.maximum(top, highest)
        total = None
        for start in range(0, keys, chunk):
            block = slice(start, start + chunk)
            raised = jnp.exp(score_ref[head, block, :] - top)
            part = jnp.sum(raised, axis=0, keepdims=True)
            total = part if total is None else total + part
            weight_ref[head, block, :] = raised.astype(BF)
        out = dot(values, weight_ref[head], 0, 0)[head * HD : (head + 1) * HD]
        mixed.append(out * (1.0 / total))
        sum_ref[p, head : head + 1, :] = top + jnp.log(total)
    o_ref[:, lanes] = jnp.concatenate(mixed, axis=0).T.astype(BF)


def attend_pair_back(
    p, chunk, bound, q_ref, k_ref, v_ref, o_ref, sum_ref, g_ref, dq_ref, dk_ref, dv_ref, ds_ref
):
    lanes = pl.ds(pl.multiple_of(p * PAIR, PAIR), PAIR)
    keys = k_ref.shape[0]
    queries = q_ref[:, lanes] * BF(HD**-0.5)
    grads = g_ref[:, lanes]
    product = (grads.astype(F32) * o_ref[:, lanes].astype(F32)).T
    head_q = [only_head(queries, head) for head in range(2)]
    head_g = [only_head(grads, head) for head in range(2)]
    shift = [
        jnp.sum(product[head * HD : (head + 1) * HD], axis=0, keepdims=True) for head in range(2)
    ]
    for start in range(0, keys, chunk):
        block = slice(start, start + chunk)
        key_block, value_block = k_ref[block, lanes], v_ref[block, lanes]
        grad_value, grad_key = 0.0, 0.0
        for head in range(2):
            scores = dot(key_block, head_q[head], 1, 1)
            position = lax.broadcasted_iota(jnp.int32, scores.shape, 0) + start
            scores = jnp.where(position < bound, scores, NEGATIVE)
            weights = jnp.exp(scores - sum_ref[p, head : head + 1, :])
            grad_weights = dot(value_block, head_g[head], 1, 1)
            grad_scores = (weights * (grad_weights - shift[head])).astype(BF)
            ds_ref[head, block, :] = grad_scores
            grad_value = grad_value + dot(weights.astype(BF), head_g[head], 1, 0)
            grad_key = grad_key + dot(grad_scores, head_q[head], 1, 0)
        dv_ref[block, lanes] = grad_value.astype(BF)
        dk_ref[block, lanes] = grad_key.astype(BF)
    key_all = k_ref[:, lanes]
    parts = [dot(key_all, ds_ref[h], 0, 0)[h * HD : (h + 1) * HD] for h in range(2)]
    dq_ref[:, lanes] = (jnp.concatenate(parts, axis=0).T * HD**-0.5).astype(BF)


def flipped(index, mask):
    bit = 1
    result = index
    while bit <= mask:
        if mask & bit:
            result = result + bit * (1 - 2 * ((index // bit) % 2))
        bit *= 2
    return result


class Wires:
    def __init__(self, sizes, place, send_sem, recv_sem):
        self.sizes, self.place = sizes, place
        self.send_sem, self.recv_sem = send_sem, recv_sem
        self.count = 0
        self.started = []
        self.maybe = []

    def peer(self, z=0, y=0, x=0, c=0, flip=0):
        n, at = self.sizes, self.place
        pz, py = (at["z"] + z) % n["z"], (at["y"] + y) % n["y"]
        if flip:
            pz = flipped(at["z"], flip)
        px, pc = (at["x"] + x) % n["x"], (at["c"] + c) % 2
        return (pz * n["y"] + py, px * 2 + pc)

    def send(self, src, dst, **shift):
        copy = pltpu.make_async_remote_copy(
            src_ref=src,
            dst_ref=dst,
            send_sem=self.send_sem.at[self.count],
            recv_sem=self.recv_sem.at[self.count],
            device_id=self.peer(**shift),
            device_id_type=pl.DeviceIdType.MESH,
        )
        self.count += 1
        copy.start()
        self.started.append(copy)
        return copy

    def send_if(self, condition, src, dst, recv_sem, **shift):
        copy = pltpu.make_async_remote_copy(
            src_ref=src,
            dst_ref=dst,
            send_sem=self.send_sem.at[self.count],
            recv_sem=recv_sem,
            device_id=self.peer(**shift),
            device_id_type=pl.DeviceIdType.MESH,
        )
        self.count += 1
        pl.when(condition)(copy.start)
        self.maybe.append((condition, copy))

    def greet(self, shifts):
        barrier = pltpu.get_barrier_semaphore()
        for shift in shifts:
            pl.semaphore_signal(
                barrier, inc=1, device_id=self.peer(**shift), device_id_type=pl.DeviceIdType.MESH
            )
        pl.semaphore_wait(barrier, len(shifts))

    def close(self):
        for copy in self.started:
            copy.wait_send()
        for condition, copy in self.maybe:
            pl.when(condition)(copy.wait_send)


def dp_shifts(n):
    return [{"z": z, "y": y} for z in range(n["z"]) for y in range(n["y"]) if z or y]


def mp_shifts(n):
    return [{"x": x, "c": c} for x in range(n["x"]) for c in range(2) if x or c]


def loop_rows(total, step, body):
    def one(i, carry):
        body(pl.ds(pl.multiple_of(i * step, step), step))
        return carry

    lax.fori_loop(0, total // step, one, 0)


def shifted(rows, offset):
    return pl.ds(pl.multiple_of(rows.start + offset, rows.size), rows.size)


def mat_rows(out_ref, left_ref, right_ref, total, step, offset=0):
    def body(rows):
        left = left_ref[shifted(rows, offset), :]
        out_ref[rows, :] = dot(left, right_ref[...], 1, 0).astype(BF)

    loop_rows(total, step, body)


class Moves:
    def __init__(self, sem):
        self.sem = sem
        self.count = 0
        self.open = []

    def start(self, src, dst):
        copy = pltpu.make_async_copy(src, dst, self.sem.at[self.count])
        self.count += 1
        copy.start()
        return copy

    def store(self, src, dst):
        self.open.append(self.start(src, dst))

    def close(self):
        for copy in self.open:
            copy.wait()


class Line:
    def __init__(self, wires, spot, sem):
        self.wires, self.spot, self.sem = wires, spot, sem
        self.nz, self.z = wires.sizes["z"], wires.place["z"]

    def start(self, src):
        z, nz = self.z, self.nz
        if nz > 1:
            self.wires.send_if(z < nz - 1, src, self.spot(z), self.sem.at[1], z=1)
            self.wires.send_if(z > 0, src, self.spot(z), self.sem.at[nz - 1], z=nz - 1)

    def step_back(self, k):
        total = 0
        for i in range(self.nz):
            order = sorted(range(1, self.nz), key=lambda s: s if s <= i else self.nz - s)
            total = total + jnp.where(self.z == i, order[k - 1], 0)
        return total

    def arrive(self, k):
        z, nz = self.z, self.nz
        s = self.step_back(k)
        source = (z + nz - s) % nz
        spot = self.spot(source)
        pltpu.make_async_copy(spot, spot, self.sem.at[s]).wait()
        below = s <= z
        above = s > z
        self.wires.send_if(
            jnp.logical_and(below, z < nz - 1), spot, spot, self.sem.at[(s + 1) % nz], z=1
        )
        self.wires.send_if(
            jnp.logical_and(above, z > 0), spot, spot, self.sem.at[s - 1], z=nz - 1
        )
        return source

    @staticmethod
    def copies(nz):
        return 2 + 2 * (nz - 1)


class Gather:
    def __init__(self, wires, src, out, cut, sem):
        self.wires, self.src, self.out, self.cut = wires, src, out, cut
        self.n, self.at = wires.sizes, wires.place
        self.line = Line(wires, lambda i: self.spot(i, 0, 0), sem)
        self.source, self.to_y, self.to_x = {0: self.at["z"]}, {}, {}
        self.last = []

    def spot(self, chip_z, sy, sx, mats=slice(None)):
        rows, wide = self.src.shape[1], self.src.shape[2]
        n, at = self.n, self.at
        block = chip_z * n["y"] + (at["y"] + n["y"] - sy) % n["y"]
        column = (at["x"] + n["x"] - sx) % n["x"]
        return self.out.at[
            mats,
            pl.ds(pl.multiple_of(block * rows, rows), rows),
            pl.ds(pl.multiple_of(column * wide, wide), wide),
        ]

    def fan(self, k, src=None):
        spot = self.spot(self.source[k], 0, 0)
        src = spot if src is None else src
        for s in range(1, self.n["y"]):
            self.to_y[k, s] = self.wires.send(src, spot, y=s)
        for s in range(1, self.n["x"]):
            self.to_x[k, s] = self.wires.send(src, spot, x=s)

    def begin(self):
        self.line.start(self.src)
        self.fan(0, self.src)

    def arrive(self, k):
        self.source[k] = self.line.arrive(k)
        self.fan(k)

    def corner(self, k):
        count = self.src.shape[0]
        for sy in range(1, self.n["y"]):
            self.to_y[k, sy].wait_recv()
            part = self.spot(self.source[k], sy, 0, slice(0, self.cut))
            for s in range(1, self.n["x"]):
                self.last.append(self.wires.send(part, part, x=s))
        for sx in range(1, self.n["x"]):
            self.to_x[k, sx].wait_recv()
            if self.cut < count:
                part = self.spot(self.source[k], 0, sx, slice(self.cut, count))
                for s in range(1, self.n["y"]):
                    self.last.append(self.wires.send(part, part, y=s))

    def finish(self):
        for copy in self.last:
            copy.wait_recv()

    @staticmethod
    def copies(n):
        nz, ny, nx = n["z"], n["y"], n["x"]
        return Line.copies(nz) + nz * (ny - 1 + nx - 1) + 2 * nz * (ny - 1) * (nx - 1)


class RowGather:
    def __init__(self, wires, src, out, z_first, sem):
        self.wires, self.src, self.out, self.z_first = wires, src, out, z_first
        self.n, self.at = wires.sizes, wires.place
        spot = (lambda i: self.spot(i, 0)) if z_first else self.band
        self.line = Line(wires, spot, sem)
        self.to_y = []

    def spot(self, chip_z, sy):
        rows, ny = self.src.shape[0], self.n["y"]
        block = chip_z * ny + (self.at["y"] + ny - sy) % ny
        return self.out.at[pl.ds(pl.multiple_of(block * rows, rows), rows)]

    def band(self, chip_z):
        rows = self.src.shape[0] * self.n["y"]
        return self.out.at[pl.ds(pl.multiple_of(chip_z * rows, rows), rows)]

    def across(self, source, src=None):
        spot = self.spot(source, 0)
        src = spot if src is None else src
        for s in range(1, self.n["y"]):
            self.to_y.append(self.wires.send(src, spot, y=s))

    def begin(self):
        if self.z_first:
            self.line.start(self.src)
        self.across(self.at["z"], self.src)

    def turn(self):
        for copy in self.to_y:
            copy.wait_recv()
        self.line.start(self.band(self.at["z"]))

    def arrive(self, k):
        source = self.line.arrive(k)
        if self.z_first:
            self.across(source)

    def finish(self):
        if self.z_first:
            for copy in self.to_y:
                copy.wait_recv()

    @staticmethod
    def copies(n):
        return Line.copies(n["z"]) + n["z"] * (n["y"] - 1)


def norm_rows(values, p_ref, index):
    centered = values - jnp.mean(values, axis=-1, keepdims=True)
    variance = jnp.mean(centered * centered, axis=-1, keepdims=True)
    normed = centered * lax.rsqrt(variance + EPSILON)
    return (normed * p_ref[index : index + 1, :] + p_ref[index + 4 : index + 5, :]).astype(BF)


STRIP = 256


FORWARD_PLAN = (
    SELF + LINE, SELF + FAN, CROSS + LINE, CROSS + FAN, SELF + TURN + 0, STATES + GO,
    SELF + PASS + 1, DOWN + BEGIN, SELF + PASS + 2, MEMORY + GO, CROSS + PASS + 1, STATES + ON,
    SELF + PASS + 3, SELF + TURN + 2, CROSS + PASS + 2, SELF + TURN + 1, STATES + TWIN,
    DOWN + LINE, STATES + END, SELF + TURN + 3, MEMORY + ON, FIRST + NORM, CROSS + TURN + 0,
    CROSS + PASS + 3, DOWN + PASS + 1, CROSS + TURN + 2, DOWN + PASS + 2, SELF + END, UP + BEGIN,
    SELF + HEADS, SELF + TWIN + 0, CROSS + TURN + 1, SELF + TWIN + 1, MEMORY + TWIN,
    SELF + TWIN + 2, MEMORY + END, SELF + TWIN + 3, SELF + OUTPUT, CROSS + TURN + 3,
    DOWN + PASS + 3, SECOND + NORM, UP + PASS + 1, CROSS + END, MEMORY + HEADS, CROSS + QUERIES,
    UP + PASS + 2, CROSS + TWIN + 0, CROSS + TWIN + 1, CROSS + TWIN + 2, UP + PASS + 3,
    CROSS + TWIN + 3, CROSS + OUTPUT, UP + END, DOWN + END, THIRD + NORM,
)


def forward_plan(nz, pairs):
    if nz == 4 and pairs == 4:
        return FORWARD_PLAN
    passes = lambda group: [group + PASS + k for k in range(1, nz)]
    turns = lambda group: [group + TURN + k for k in range(nz)]
    plan = [STATES + GO, SELF + LINE, SELF + FAN, CROSS + LINE, CROSS + FAN, MEMORY + GO]
    plan += [STATES + ON, STATES + TWIN, STATES + END, FIRST + NORM]
    plan += passes(SELF) + turns(SELF) + [MEMORY + ON, MEMORY + TWIN, SELF + END]
    plan += [SELF + HEADS] + [SELF + TWIN + p for p in range(pairs)] + [SELF + OUTPUT]
    plan += [UP + BEGIN, DOWN + BEGIN] + passes(CROSS) + turns(CROSS) + passes(UP)
    plan += [SECOND + NORM, MEMORY + END, CROSS + END, DOWN + LINE, MEMORY + HEADS]
    plan += [CROSS + QUERIES] + [CROSS + TWIN + p for p in range(pairs)] + [CROSS + OUTPUT]
    return tuple(plan + passes(DOWN) + [THIRD + NORM, UP + END, DOWN + END])


def forward_kernel(
    n, own_rows, order, lengths, reaches, st_ref, me_ref, pr_ref, wa_ref, wf_ref,
    ows, owc, owf, op_ref, ofr, oin, oh1, oq, ok, ov, oo, ol, ox1, oh2, oq2, ok2, ov2, oo2, ol2,
    ox2, oh3,
    stage_s, pin_s, pall_s, p_s, wl_s, fl_s,
    x_s, m_s, w_s, c_s, h1_s, q_s, k_s, v_s, o_s, l_s, x1_s, h2_s, q2_s, k2_s, v2_s, o2_s, l2_s,
    x2_s, h3_s, give_s, got_s, score_s, weight_s,
    send_sem, recv_sem, self_sem, cross_sem, up_sem, down_sem, move_sem,
):
    at = grid_place()
    z, y, x, c = at["z"], at["y"], at["x"], at["c"]
    nz, ny, nx = n["z"], n["y"], n["x"]
    data, model = z * ny + y, x * 2 + c
    wires = Wires(n, at, send_sem, recv_sem)
    moves = Moves(move_sem)
    utterances, lines, deep = st_ref.shape
    mats = w_s.shape[0]
    for r in range(utterances):
        stage_s[0, r] = st_ref[order[r]]
        stage_s[1, r] = me_ref[order[r]]
    wl_s[...] = wa_ref[...].astype(BF)
    fl_s[...] = wf_ref[...].astype(BF)
    pin_s[...] = pr_ref[...].astype(BF).astype(F32)
    wires.greet(dp_shifts(n) + [{"x": s} for s in range(1, nx)] + [{"c": 1}])

    def patch(ref):
        return ref.at[
            pl.ds(pl.multiple_of(data * lines, lines), lines),
            pl.ds(pl.multiple_of(model * deep, deep), deep),
        ]

    def column(ref, sx, sc):
        index = ((x + nx - sx) % nx) * 2 + (c + 2 - sc) % 2
        return ref.at[:, pl.ds(pl.multiple_of(index * deep, deep), deep)]

    def spread(i, out):
        copies = []
        for shift in dp_shifts(n):
            target = wires.peer(**shift)[0]
            copies.append(wires.send(stage_s.at[i, target], patch(out), **shift))
        return copies, moves.start(stage_s.at[i, data], patch(out))

    def forward_columns(out, spreading):
        copies, own = spreading
        own.wait()
        for copy in copies:
            copy.wait_recv()
        near = [wires.send(column(out, 0, 0), column(out, 0, 0), x=s) for s in range(1, nx)]
        return near, [wires.send(column(out, 0, 0), column(out, 0, 0), c=1)]

    def pair_columns(out, near, pair):
        for s in range(1, nx):
            near[s - 1].wait_recv()
            pair.append(wires.send(column(out, s, 0), column(out, s, 0), c=1))

    own_self = wl_s.at[0:mats]
    own_cross = wl_s.at[mats : 2 * mats]
    near_self = Gather(wires, own_self, w_s, mats // 2, self_sem)
    near_cross = Gather(wires, own_cross, c_s, mats // 2, cross_sem)
    up_gather = RowGather(wires, fl_s.at[0], owf.at[0], True, up_sem)
    down_gather = RowGather(wires, fl_s.at[1], owf.at[1], False, down_sem)
    here = [
        moves.start(own_self, near_self.spot(z, 0, 0)),
        moves.start(own_cross, near_cross.spot(z, 0, 0)),
        moves.start(pin_s, pall_s.at[data]),
    ]
    down_here = moves.start(fl_s.at[1], down_gather.spot(z, 0))
    up_here = moves.start(fl_s.at[0], up_gather.spot(z, 0))
    params = [wires.send(pin_s, pall_s.at[data], **shift) for shift in dp_shifts(n)]
    slot, width = x_s.shape
    chip_rows = 2 * own_rows
    chip_start = x * chip_rows
    strip = min(STRIP, own_rows)
    pairs = q_s.shape[1] // PAIR
    own = pl.ds(pl.multiple_of(c * own_rows, own_rows), own_rows)
    held = {}
    steps = {}

    def step(name):
        def keep(function):
            steps[name] = function
            return function

        return keep

    for name, i, ref in ((STATES, 0, x_s), (MEMORY, 1, m_s)):

        def go(name=name, i=i, ref=ref):
            held[name] = spread(i, ref)

        def on(name=name, ref=ref):
            held[name] = forward_columns(ref, held[name])

        def pair(name=name, ref=ref):
            pair_columns(ref, *held[name])

        def end(name=name):
            for copy in held[name][1]:
                copy.wait_recv()

        steps.update(
            {name + GO: go, name + ON: on, name + TWIN: pair, name + END: end}
        )
    for name, gather in ((SELF, near_self), (CROSS, near_cross)):
        steps[name + LINE] = functools.partial(gather.line.start, gather.src)
        steps[name + FAN] = functools.partial(gather.fan, 0, gather.src)
        for k in range(nz):
            steps[name + PASS + k] = functools.partial(gather.arrive, k)
            steps[name + TURN + k] = functools.partial(gather.corner, k)
    for name, gather in ((UP, up_gather), (DOWN, down_gather)):
        steps[name + BEGIN] = gather.begin
        steps[name + END] = gather.finish
        for k in range(1, nz):
            steps[name + PASS + k] = functools.partial(gather.arrive, k)

    @step(DOWN + LINE)
    def _():
        down_here.wait()
        down_gather.turn()

    @step(SELF + END)
    def _():
        for copy in here[:1]:
            copy.wait()
        near_self.finish()
        moves.store(w_s, ows)

    @step(CROSS + END)
    def _():
        here[1].wait()
        near_cross.finish()
        moves.store(c_s, owc)

    @step(FIRST + NORM)
    def _():
        for copy in params:
            copy.wait_recv()
        here[2].wait()
        for i in range(nz * ny):
            columns = pall_s.shape[2]
            p_s[:, i * columns : (i + 1) * columns] = pall_s[i]
        op_ref[...] = p_s[...]

        def first_norm(rows):
            h1_s[rows, :] = norm_rows(x_s[rows, :].astype(F32), p_s, 0)

        loop_rows(slot, strip, first_norm)
        moves.store(h1_s, oh1)
        moves.store(x_s.at[pl.ds(pl.multiple_of(model * own_rows, own_rows), own_rows)], oin)

    @step(SELF + HEADS)
    def _():
        mat_rows(q_s, h1_s, w_s.at[0], chip_rows, strip, chip_start)
        mat_rows(k_s, h1_s, w_s.at[1], slot, strip)
        mat_rows(v_s, h1_s, w_s.at[2], slot, strip)
        for ref, out in ((q_s, oq), (k_s, ok), (v_s, ov)):
            moves.store(ref, out)

    @step(MEMORY + HEADS)
    def _():
        mat_rows(k2_s, m_s, c_s.at[1], slot, strip)
        mat_rows(v2_s, m_s, c_s.at[2], slot, strip)
        for ref, out in ((k2_s, ok2), (v2_s, ov2), (m_s, ofr)):
            moves.store(ref, out)

    @step(CROSS + QUERIES)
    def _():
        mat_rows(q2_s, h2_s, c_s.at[0], chip_rows, strip)
        moves.store(q2_s, oq2)

    reach_self = lax.broadcasted_iota(jnp.int32, (1, chip_rows), 1) + chip_start + 1
    reach_self = jnp.minimum(reach_self, lengths[order[data]])
    reach_cross = jnp.full((1, chip_rows), reaches[order[data]], jnp.int32)
    for p in range(pairs):

        def self_pair(p=p):
            attend_pair(p, 256, reach_self, q_s, k_s, v_s, o_s, l_s, score_s, weight_s)

        def cross_pair(p=p):
            attend_pair(p, 256, reach_cross, q2_s, k2_s, v2_s, o2_s, l2_s, score_s, weight_s)

        steps[SELF + TWIN + p] = self_pair
        steps[CROSS + TWIN + p] = cross_pair

    def give(index, mixed, out_map):
        def body(rows):
            give_s[index, rows, :] = dot(mixed[rows, :], out_map[...], 1, 1).astype(BF)

        loop_rows(chip_rows, strip, body)
        held[index] = wires.send(give_s.at[index], got_s.at[index], c=1)

    def total(index, rows):
        return give_s[index, rows, :].astype(F32) + got_s[index, rows, :].astype(F32)

    @step(SELF + OUTPUT)
    def _():
        moves.store(o_s, oo)
        moves.store(l_s, ol)
        give(0, o_s, w_s.at[3])

    @step(CROSS + OUTPUT)
    def _():
        moves.store(o2_s, oo2)
        moves.store(l2_s, ol2)
        give(1, o2_s, c_s.at[3])

    @step(SECOND + NORM)
    def _():
        held[0].wait_recv()

        def second_norm(rows):
            values = x_s[shifted(rows, chip_start), :].astype(F32) + total(0, rows)
            x1_s[rows, :] = values
            h2_s[rows, :] = norm_rows(values, p_s, 1)

        loop_rows(chip_rows, strip, second_norm)
        moves.store(x1_s.at[own], ox1)
        moves.store(h2_s, oh2)

    @step(THIRD + NORM)
    def _():
        held[1].wait_recv()

        def third_norm(rows):
            values = x1_s[rows, :] + total(1, rows)
            x2_s[rows, :] = values
            h3_s[rows, :] = norm_rows(values, p_s, 2)

        loop_rows(chip_rows, strip, third_norm)
        moves.store(x2_s.at[own], ox2)
        moves.store(h3_s, oh3)

    for name in forward_plan(nz, pairs):
        steps[name]()
    up_here.wait()
    moves.close()
    wires.close()


def forward(order, lengths, reaches, states, memory, params, attn, ffn, own_rows):
    n = grid_sizes()
    nz, ny, nx = n["z"], n["y"], n["x"]
    data = nz * ny
    utterances, lines, deep = states.shape
    slot, width = lines * data, deep * 2 * nx
    mats = attn.shape[0] // 2
    local = attn.shape[2] * nx
    hidden = ffn.shape[2]
    chip_rows = 2 * own_rows
    pairs = local // PAIR
    copies = (
        2 * Gather.copies(n) + 2 * RowGather.copies(n) + 3 * (data - 1) + 2 * (2 * (nx - 1) + 1) + 2
    )
    vmem = pl.BlockSpec(memory_space=pltpu.VMEM)
    smem = pl.BlockSpec(memory_space=pltpu.SMEM)
    hbm = pl.BlockSpec(memory_space=pl.ANY)
    half = lambda *shape: (shape, BF)
    full = lambda *shape: (shape, F32)
    saved = [
        half(slot, width),
        half(chip_rows, local),
        half(slot, local),
        half(slot, local),
        half(chip_rows, local),
        full(pairs, 2, chip_rows),
        full(own_rows, width),
        half(chip_rows, width),
        half(chip_rows, local),
        half(slot, local),
        half(slot, local),
        half(chip_rows, local),
        full(pairs, 2, chip_rows),
        full(own_rows, width),
        half(chip_rows, width),
    ]
    outs = [
        half(mats, width, local),
        half(mats, width, local),
        half(2, width, hidden),
        full(params.shape[0], width),
        half(slot, width),
        half(own_rows, width),
    ] + saved
    scratch = [
        half(2, utterances, lines, deep),
        full(*params.shape),
        full(data, *params.shape),
        full(params.shape[0], width),
        half(*attn.shape),
        half(*ffn.shape),
        half(slot, width),
        half(slot, width),
        half(mats, width, local),
        half(mats, width, local),
        half(slot, width),
        half(chip_rows, local),
        half(slot, local),
        half(slot, local),
        half(chip_rows, local),
        full(pairs, 2, chip_rows),
        full(chip_rows, width),
        half(chip_rows, width),
        half(chip_rows, local),
        half(slot, local),
        half(slot, local),
        half(chip_rows, local),
        full(pairs, 2, chip_rows),
        full(chip_rows, width),
        half(chip_rows, width),
        half(2, chip_rows, width),
        half(2, chip_rows, width),
        full(2, slot, chip_rows),
        half(2, slot, chip_rows),
    ]
    return pl.pallas_call(
        functools.partial(forward_kernel, n, own_rows),
        out_shape=[jax.ShapeDtypeStruct(s, t) for s, t in outs],
        in_specs=[smem, smem, smem, vmem, vmem, vmem, vmem, vmem],
        out_specs=[hbm] * 3 + [vmem] + [hbm] * (len(outs) - 4),
        scratch_shapes=[pltpu.VMEM(s, t) for s, t in scratch]
        + [
            pltpu.SemaphoreType.DMA((copies,)),
            pltpu.SemaphoreType.DMA((copies,)),
        ]
        + [pltpu.SemaphoreType.DMA((nz,))] * 4
        + [pltpu.SemaphoreType.DMA((32,))],
        compiler_params=pltpu.CompilerParams(
            collective_id=3, has_side_effects=True, vmem_limit_bytes=56 * 2**20
        ),
        name="forward",
    )(order, lengths, reaches, states, memory, params, attn, ffn)


def early_zones(n):
    return [n["z"] - 1, n["z"] - 3] if n["z"] >= 4 else []


def norm_back_rows(values, grad, gain):
    centered = values - jnp.mean(values, axis=-1, keepdims=True)
    scale = lax.rsqrt(jnp.mean(centered * centered, axis=-1, keepdims=True) + EPSILON)
    normed = centered * scale
    up = grad * gain
    back = scale * (
        up
        - jnp.mean(up, axis=-1, keepdims=True)
        - normed * jnp.mean(up * normed, axis=-1, keepdims=True)
    )
    return back, normed


def row_sum(values):
    return jnp.sum(values, axis=0, keepdims=True)


SPLIT = 2


def ffn_kernel(
    n, order, lengths, h_hbm, x_ref, w_hbm, ct_ref, p_ref,
    oy_ref, odx_ref, odc, odw, oe, on_ref,
    h_s, f_s, a_s, d_s, u_s, w_s, keep_s, far_s, give_s, got_s, cross_s, crossed_s, back_s, come_s,
    x3_s, dx3_s, dc_s, dw_s, early_s, send_sem, recv_sem, move_sem,
):
    at = grid_place()
    wires = Wires(n, at, send_sem, recv_sem)
    moves = Moves(move_sem)
    nx, c = n["x"], at["c"]
    length = lengths[order[at["z"] * n["y"] + at["y"]]]
    own, width = x_ref.shape
    part = own // SPLIT
    start_own = pl.multiple_of(c * own, own)
    start_other = pl.multiple_of((1 - c) * own, own)
    get_w = moves.start(w_hbm, w_s)
    get_own = moves.start(h_hbm.at[pl.ds(start_own, own)], h_s.at[pl.ds(0, own)])
    get_other = moves.start(h_hbm.at[pl.ds(start_other, own)], h_s.at[pl.ds(own, own)])
    ny = n["y"]
    wires.greet(
        [{"x": s} for s in range(1, nx)] + [{"y": s} for s in range(1, ny)] + [{"c": 1}]
    )

    def far_at(t, k, j):
        return 2 * own + (((t - 1) * SPLIT + k) * 2 + j) * part

    def spread(src, dst, k):
        return [
            wires.send(src.at[pl.ds(k * part, part)], dst.at[pl.ds(far_at(t, k, 0), part)], x=t)
            for t in range(1, nx)
        ]

    def onward(dst, t, k):
        return wires.send(
            dst.at[pl.ds(far_at(t, k, 0), part)], dst.at[pl.ds(far_at(t, k, 1), part)], c=1
        )

    def up(rows):
        hidden = dot(h_s[rows, :], w_s[0], 1, 0)
        inner = 0.7978845608028654 * (hidden + 0.044715 * (hidden * hidden * hidden))
        bend = jnp.tanh(inner)
        a_s[rows, :] = (0.5 * hidden * (1.0 + bend)).astype(BF)
        slope = 0.7978845608028654 * (1.0 + 0.134145 * (hidden * hidden))
        d_s[rows, :] = 0.5 * (1.0 + bend) + 0.5 * hidden * (1.0 - bend * bend) * slope
        return dot(a_s[rows, :], w_s[1], 1, 1)

    def down(rows):
        grad = dot(f_s[rows, :], w_s[1], 1, 0)
        u_s[rows, :] = (grad * d_s[rows, :]).astype(BF)
        return dot(u_s[rows, :], w_s[0], 1, 1)

    def other_core(phase, work):
        give_s[phase] = work(slice(own, 2 * own)).astype(BF)
        return wires.send(give_s.at[phase], got_s.at[phase], c=1)

    def far_part(phase, work, t, k):
        sums = work(slice(far_at(t, k, 0), far_at(t, k, 0) + 2 * part))
        far_s[t - 1, k] = sums[:part]
        cross_s[phase, t - 1, k] = sums[part:].astype(BF)
        return wires.send(cross_s.at[phase, t - 1, k], crossed_s.at[phase, t - 1, k], c=1)

    def return_part(phase, t, k, crossing):
        crossing.wait_recv()
        back_s[phase, t - 1, k] = (far_s[t - 1, k] + crossed_s[phase, t - 1, k].astype(F32)).astype(
            BF
        )
        return wires.send(back_s.at[phase, t - 1, k], come_s.at[phase, t - 1, k], x=nx - t)

    def far_phase(phase, work, buffer, arriving, arrived=None):
        homing = {}
        for k in range(SPLIT):
            crossed = []
            for t in range(1, nx):
                arriving[k][t - 1].wait_recv()
                crossed.append(onward(buffer, t, k))
            crossing = []
            for copy in crossed:
                copy.wait_recv()
            if arrived is not None and k == SPLIT - 1:
                arrived()
            for t in range(1, nx):
                crossing.append(far_part(phase, work, t, k))
            for t in range(1, nx):
                homing[k, t] = return_part(phase, t, k, crossing[t - 1])
        return homing

    def own_part(phase, k, homing):
        rows = slice(k * part, (k + 1) * part)
        total = keep_s[rows, :] + got_s[phase, rows, :].astype(F32)
        for t in range(1, nx):
            homing[k, t].wait_recv()
            total = total + come_s[phase, t - 1, k].astype(F32)
        return total

    own_rows = h_hbm.at[pl.ds(start_own, own)]
    arriving = [spread(own_rows, h_s, k) for k in range(SPLIT)]
    get_own.wait()
    get_w.wait()
    get_other.wait()
    swap = other_core(0, up)
    keep_s[...] = up(slice(0, own))
    homing = far_phase(0, up, h_s, arriving)
    swap.wait_recv()
    gain_final, bias_final = 0.0, 0.0
    arriving, near = [], []
    first_row = (at["x"] * 2 + c) * own
    for k in range(SPLIT):
        rows = slice(k * part, (k + 1) * part)
        values = x_ref[rows, :] + own_part(0, k, homing)
        x3 = values
        centered = x3 - jnp.mean(x3, axis=-1, keepdims=True)
        variance = jnp.mean(centered * centered, axis=-1, keepdims=True)
        normed = centered * lax.rsqrt(variance + EPSILON)
        oy_ref[rows, :] = (normed * p_ref[3:4, :] + p_ref[7:8, :]).astype(BF)
        position = lax.broadcasted_iota(jnp.int32, (part, 1), 0) + (first_row + k * part)
        seed = jnp.where(position < length, ct_ref[rows, :].astype(F32), 0.0)
        grad, normed = norm_back_rows(x3, seed, p_ref[3:4, :])
        gain_final = gain_final + row_sum(seed * normed)
        bias_final = bias_final + row_sum(seed)
        dx3_s[rows, :] = grad
        f_s[rows, :] = grad.astype(BF)
        arriving.append(spread(f_s, f_s, k))
        near.append(
            wires.send(f_s.at[pl.ds(k * part, part)], f_s.at[pl.ds(own + k * part, part)], c=1)
        )
    keep_s[...] = down(slice(0, own))
    for copy in near:
        copy.wait_recv()
    swap = other_core(1, down)
    rows_each = width // (n["z"] * ny)
    zone_rows = ny * rows_each
    early = early_zones(n)
    ahead = []

    def strip_of(i, left, right, m):
        start = flipped(at["z"], m) * zone_rows
        cols = pl.ds(pl.multiple_of(start, zone_rows), zone_rows)
        dw_s[i, cols, :] = dot(left[:, cols], right[...], 0, 0).astype(BF)
        return start

    def start_early():
        for index, m in enumerate(early):
            start = strip_of(1, f_s, a_s, m)
            for t in range(1, ny):
                band = start + (at["y"] + t) % ny * rows_each
                band = pl.ds(pl.multiple_of(band, rows_each), rows_each)
                ahead.append(wires.send(dw_s.at[1, band], early_s.at[t - 1, index], y=t))

    homing = far_phase(1, down, f_s, arriving, start_early)
    for m in range(n["z"]):
        if m not in early:
            strip_of(1, f_s, a_s, m)
    moves.store(dw_s.at[1], odw.at[1])
    for m in range(n["z"]):
        strip_of(0, h_s, u_s, m)
    moves.store(dw_s.at[0], odw.at[0])
    swap.wait_recv()
    gain_third, bias_third = 0.0, 0.0
    near = []
    for k in range(SPLIT):
        rows = slice(k * part, (k + 1) * part)
        upstream = own_part(1, k, homing)
        grad, normed = norm_back_rows(x_ref[rows, :], upstream, p_ref[2:3, :])
        gain_third = gain_third + row_sum(upstream * normed)
        bias_third = bias_third + row_sum(upstream)
        total = dx3_s[rows, :] + grad
        odx_ref[rows, :] = total
        here = pl.ds(start_own + k * part, part)
        dc_s[here, :] = total.astype(BF)
        near.append(wires.send(dc_s.at[here], dc_s.at[here], c=1))
    line = lax.broadcasted_iota(jnp.int32, on_ref.shape, 0)
    sums = jnp.zeros(on_ref.shape, F32)
    for index, value in ((2, gain_third), (3, gain_final), (6, bias_third), (7, bias_final)):
        sums = sums + jnp.where(line == index, value, 0.0)
    on_ref[...] = sums
    for copy in near:
        copy.wait_recv()
    moves.store(dc_s, odc)
    for copy in ahead:
        copy.wait_recv()
    moves.store(early_s, oe)
    moves.close()
    wires.close()


def feed_forward(order, lengths, normed, resid, maps, cotangent, params):
    n = grid_sizes()
    chip_rows, width = normed.shape
    own = chip_rows // 2
    hidden = maps.shape[2]
    nx = n["x"]
    rows = chip_rows * nx
    part = own // SPLIT
    rows_each = width // (n["z"] * n["y"])
    ahead = (n["y"] - 1, len(early_zones(n)), rows_each, hidden)
    copies = 2 * (SPLIT * (nx - 1) * 4 + 1) + 2 * SPLIT + ahead[0] * ahead[1]
    vmem = pl.BlockSpec(memory_space=pltpu.VMEM)
    smem = pl.BlockSpec(memory_space=pltpu.SMEM)
    hbm = pl.BlockSpec(memory_space=pl.ANY)
    far = (2, nx - 1, SPLIT, part, width)
    return pl.pallas_call(
        functools.partial(ffn_kernel, n),
        out_shape=[
            jax.ShapeDtypeStruct((own, width), BF),
            jax.ShapeDtypeStruct((own, width), F32),
            jax.ShapeDtypeStruct((chip_rows, width), BF),
            jax.ShapeDtypeStruct((2, width, hidden), BF),
            jax.ShapeDtypeStruct(ahead, BF),
            jax.ShapeDtypeStruct(params.shape, F32),
        ],
        in_specs=[smem, smem, hbm, vmem, hbm, vmem, vmem],
        out_specs=[vmem, vmem, hbm, hbm, hbm, vmem],
        scratch_shapes=[
            pltpu.VMEM((rows, width), BF),
            pltpu.VMEM((rows, width), BF),
            pltpu.VMEM((rows, hidden), BF),
            pltpu.VMEM((rows, hidden), F32),
            pltpu.VMEM((rows, hidden), BF),
            pltpu.VMEM((2, width, hidden), BF),
            pltpu.VMEM((own, width), F32),
            pltpu.VMEM((nx - 1, SPLIT, part, width), F32),
            pltpu.VMEM((2, own, width), BF),
            pltpu.VMEM((2, own, width), BF),
            pltpu.VMEM(far, BF),
            pltpu.VMEM(far, BF),
            pltpu.VMEM(far, BF),
            pltpu.VMEM(far, BF),
            pltpu.VMEM((own, width), F32),
            pltpu.VMEM((own, width), F32),
            pltpu.VMEM((chip_rows, width), BF),
            pltpu.VMEM((2, width, hidden), BF),
            pltpu.VMEM(ahead, BF),
            pltpu.SemaphoreType.DMA((copies,)),
            pltpu.SemaphoreType.DMA((copies,)),
            pltpu.SemaphoreType.DMA((8,)),
        ],
        compiler_params=pltpu.CompilerParams(
            collective_id=4, has_side_effects=True, vmem_limit_bytes=56 * 2**20
        ),
        name="feed_forward",
    )(order, lengths, normed, resid, maps, cotangent, params)


CROSS_PLAN = (
    UP + BEGIN + 3, DOWN + ALONG + 1, LOAD, HEADS, DOWN + ALONG + 3, GRAD + OUTPUT,
    DOWN + BEGIN + 2, OUT + BEGIN + 3, TWIN + 0, OUT + BEGIN + 2, UP + ALONG + 3,
    OUT + BEGIN + 1, UP + BEGIN + 1, UP + BEGIN + 2, TWIN + 1, OUT + BEGIN + 0, TWIN + 2,
    DOWN + ALONG + 2, TWIN + 3, GRAD + QUERIES, QUERY + BEGIN + 1, QUERY + BEGIN + 3,
    QUERY + BEGIN + 2, MEMORY + PART, QUERY + BEGIN + 0, DOWN + BEGIN + 0, OUT + MIDDLE + 3,
    GRAD + TWIN, OUT + MIDDLE + 1, UP + ALONG + 1, INPUT + PART, QUERY + MIDDLE + 3,
    UP + ALONG + 2, OUT + MIDDLE + 2, OUT + ALONG + 3, MEMORY + ON, QUERY + MIDDLE + 1,
    OUT + ALONG + 1, OUT + MIDDLE + 0, QUERY + ALONG + 3, QUERY + MIDDLE + 2, UP + BEGIN + 0,
    OUT + ALONG + 2, DOWN + ALONG + 0, NORM, QUERY + MIDDLE + 0, QUERY + ALONG + 1,
    QUERY + ALONG + 2, OUT + ALONG + 0, ROWS + END, MEMORY + END, UP + ALONG + 0,
    QUERY + ALONG + 0,
)

SELF_PLAN = (
    MEMORY + GO, LOAD + OTHER, LOAD, CROSS + BEGIN + 3, CROSS + BEGIN + 2, GRAD + OUTPUT,
    OUT + BEGIN + 1, CROSS + BEGIN + 1, OUT + BEGIN + 0, HEADS, OUT + BEGIN + 3, OUT + BEGIN + 2,
    TWIN + 0, TWIN + 1, CROSS + MIDDLE + 3, TWIN + 2, TWIN + 3, GRAD + QUERIES, OUT + MIDDLE + 3,
    QUERY + BEGIN + 3, QUERY + BEGIN + 1, GRAD + TWIN, KEYS + BEGIN + 3, INPUT + PART,
    OUT + MIDDLE + 2, CROSS + ALONG + 3, OUT + ALONG + 3, CROSS + MIDDLE + 2, INPUT + ON,
    KEYS + BEGIN + 2, QUERY + MIDDLE + 3, OUT + MIDDLE + 1, KEYS + MIDDLE + 3, KEYS + MIDDLE + 2,
    OUT + ALONG + 2, CROSS + ALONG + 2, KEYS + BEGIN + 1, QUERY + BEGIN + 2, MEMORY + END,
    QUERY + MIDDLE + 1, OUT + ALONG + 1, QUERY + ALONG + 3, NORM, KEYS + ALONG + 3,
    QUERY + ALONG + 1, CROSS + BEGIN + 0, CROSS + MIDDLE + 1, QUERY + MIDDLE + 2,
    KEYS + ALONG + 2, QUERY + BEGIN + 0, HOME + END, KEYS + BEGIN + 0, KEYS + MIDDLE + 1,
    CROSS + MIDDLE + 0, OUT + MIDDLE + 0, CROSS + ALONG + 1, QUERY + ALONG + 2,
    KEYS + MIDDLE + 0, KEYS + ALONG + 1, QUERY + MIDDLE + 0, QUERY + ALONG + 0,
    CROSS + ALONG + 0, OUT + ALONG + 0, KEYS + ALONG + 0,
)

def backward_plan(tuned, nz, pairs, head, parts, tail):
    if nz == 4 and pairs == 4:
        return tuned
    plan = list(head) + [TWIN + p for p in range(pairs)] + list(parts)
    return tuple(plan) + tuple(tail)


class Halving:
    def zones(self):
        return range(self.n["z"] - 1, -1, -1)

    def zone(self, m):
        return flipped(self.at["z"], m)

    def sources(self, m):
        top = (m & -m) if m else self.n["z"]
        found, bit = [], 1
        while bit < top:
            found.append(m + bit)
            bit *= 2
        return found

    def settle(self, m, total, out):
        for k in self.sources(m):
            self.by_z[k].wait_recv()
            total = total + self.r3[k - 1].astype(F32)
        if m:
            self.s3[m - 1] = total.astype(BF)
            self.by_z[m] = self.wires.send(self.s3.at[m - 1], self.r3.at[m - 1], flip=m & -m)
        else:
            out[...] = total


def flips(n):
    found, bit = [], 1
    while bit < n["z"]:
        found.append({"flip": bit})
        bit *= 2
    return found


class RowScatter(Halving):
    def __init__(self, wires, moves, src, own, r1, s3, r3, out, ahead=None):
        self.wires, self.moves, self.src, self.own = wires, moves, src, own
        self.r1, self.s3, self.r3, self.out = r1, s3, r3, out
        self.n, self.at = wires.sizes, wires.place
        self.by_y, self.by_z = {}, {}
        self.loads = {m: moves.start(self.band(m, 0), own.at[m]) for m in self.zones()}
        self.early = []
        if ahead is not None:
            self.early = early_zones(self.n)
            for i, m in enumerate(self.early):
                for t in range(1, self.n["y"]):
                    self.by_y[m, t] = moves.start(ahead.at[t - 1, i], r1.at[t - 1, m])

    def band(self, m, t):
        rows = self.own.shape[1]
        index = self.zone(m) * self.n["y"] + (self.at["y"] + t) % self.n["y"]
        return self.src.at[pl.ds(pl.multiple_of(index * rows, rows), rows)]

    def begin(self, m):
        if m in self.early:
            return
        for t in range(1, self.n["y"]):
            self.by_y[m, t] = self.wires.send(self.band(m, t), self.r1.at[t - 1, m], y=t)

    def along(self, m):
        self.loads[m].wait()
        total = self.own[m].astype(F32)
        for t in range(1, self.n["y"]):
            if m in self.early:
                self.by_y[m, t].wait()
            else:
                self.by_y[m, t].wait_recv()
            total = total + self.r1[t - 1, m].astype(F32)
        self.settle(m, total, self.out)

    @staticmethod
    def copies(n):
        return n["z"] * (n["y"] - 1) + n["z"] - 1

    @staticmethod
    def scratch(n, rows, wide):
        nz, ny = n["z"], n["y"]
        return [
            pltpu.VMEM((nz, rows, wide), BF),
            pltpu.VMEM((ny - 1, nz, rows, wide), BF),
            pltpu.VMEM((nz - 1, rows, wide), BF),
            pltpu.VMEM((nz - 1, rows, wide), BF),
        ]


class Scatter(Halving):
    def __init__(self, wires, grads, first, count, x_first, r1, s2, r2, acc, s3, r3, out):
        self.wires, self.grads = wires, grads
        self.first, self.count, self.x_first = first, count, x_first
        self.r1, self.s2, self.r2, self.acc, self.s3, self.r3 = r1, s2, r2, acc, s3, r3
        self.out = out
        self.n, self.at = wires.sizes, wires.place
        self.rows, self.wide = acc.shape[2], acc.shape[3]
        self.stage1, self.stage2, self.by_z = {}, {}, {}

    def part(self, m, band, bands, column, columns):
        rows, wide = self.rows, self.wide
        start = self.zone(m) * self.n["y"] + band
        return self.grads.at[
            pl.ds(self.first, self.count),
            pl.ds(pl.multiple_of(start * rows, rows), bands * rows),
            pl.ds(pl.multiple_of(column * wide, wide), columns * wide),
        ]

    def begin(self, m):
        nx, ny = self.n["x"], self.n["y"]
        if self.x_first:
            for t in range(1, nx):
                src = self.part(m, 0, ny, (self.at["x"] + t) % nx, 1)
                self.stage1[m, t] = self.wires.send(src, self.r1.at[t - 1, m], x=t)
        else:
            for t in range(1, ny):
                src = self.part(m, (self.at["y"] + t) % ny, 1, 0, nx)
                self.stage1[m, t] = self.wires.send(src, self.r1.at[t - 1, m], y=t)

    def middle(self, m):
        nx, ny, rows, wide = self.n["x"], self.n["y"], self.rows, self.wide
        x, y = self.at["x"], self.at["y"]
        inner, outer = (ny, nx) if self.x_first else (nx, ny)
        for t in range(1, outer):
            self.stage1[m, t].wait_recv()
        for b in range(inner):
            if self.x_first:
                band = (y + b) % ny
                total = self.part(m, band, 1, x, 1)[...].astype(F32)
                here = (slice(None), pl.ds(pl.multiple_of(band * rows, rows), rows), slice(None))
            else:
                column = (x + b) % nx
                total = self.part(m, y, 1, column, 1)[...].astype(F32)
                here = (slice(None), slice(None), pl.ds(pl.multiple_of(column * wide, wide), wide))
            for t in range(1, outer):
                total = total + self.r1.at[t - 1, m][here].astype(F32)
            if b == 0:
                self.acc[m] = total
            else:
                self.s2[b - 1, m] = total.astype(BF)
        for t in range(1, inner):
            way = {"y": t} if self.x_first else {"x": t}
            self.stage2[m, t] = self.wires.send(self.s2.at[t - 1, m], self.r2.at[t - 1, m], **way)

    def along(self, m):
        inner = self.n["y"] if self.x_first else self.n["x"]
        total = self.acc[m]
        for t in range(1, inner):
            self.stage2[m, t].wait_recv()
            total = total + self.r2[t - 1, m].astype(F32)
        self.settle(m, total, self.out)

    @staticmethod
    def copies(n):
        nz, ny, nx = n["z"], n["y"], n["x"]
        return nz * (nx - 1 + ny - 1) + nz - 1

    @staticmethod
    def scratch(n, count, x_first, rows, wide):
        nz, ny, nx = n["z"], n["y"], n["x"]
        inner = ny if x_first else nx
        if x_first:
            first = (nx - 1, nz, count, ny * rows, wide)
        else:
            first = (ny - 1, nz, count, rows, nx * wide)
        return [
            pltpu.VMEM(first, BF),
            pltpu.VMEM((inner - 1, nz, count, rows, wide), BF),
            pltpu.VMEM((inner - 1, nz, count, rows, wide), BF),
            pltpu.VMEM((nz, count, rows, wide), F32),
            pltpu.VMEM((nz - 1, count, rows, wide), BF),
            pltpu.VMEM((nz - 1, count, rows, wide), BF),
        ]


ONE = (8, 128)


def squares(refs):
    total = jnp.zeros(ONE, F32)
    for ref in refs:
        value = ref[...]
        total = total + jnp.sum((value * value).reshape((-1,) + ONE), axis=0)
    return total


def register(steps, name, group):
    for m in group.zones():
        steps[name + BEGIN + m] = functools.partial(group.begin, m)
        steps[name + ALONG + m] = functools.partial(group.along, m)
        if hasattr(group, "middle"):
            steps[name + MIDDLE + m] = functools.partial(group.middle, m)


def spelled(n, names):
    plan = []
    for name, kinds in names:
        for kind in kinds:
            plan += [name + kind + m for m in range(n["z"] - 1, -1, -1)]
    return plan


WHOLE = (BEGIN, MIDDLE, ALONG)


def cross_back_kernel(
    n, order, reaches, dc_hbm, dx_ref, w_hbm, q_hbm, k_hbm, v_hbm, o_hbm, l_ref, h_hbm, m_hbm, x_ref, p_ref,
    dw_hbm, early_hbm, oup_ref, odown_ref, oq_ref, oo_ref, og, odx_ref, odb, om, on_ref, osq_ref, *scratch,
):
    (
        dc_s, w_s, q_s, k_s, v_s, o_s, h_s, m_s, g_s, dq_s, dk_s, dv_s, ds_s, gr_s, give_s, got_s,
        db_s, pm_s, rm_s, sm_s, cm_s, om_s,
    ) = scratch[:22]
    send_sem, recv_sem, move_sem = scratch[-3:]
    at = grid_place()
    x, c = at["x"], at["c"]
    nz, ny, nx = n["z"], n["y"], n["x"]
    wires = Wires(n, at, send_sem, recv_sem)
    moves = Moves(move_sem)
    loads = [
        moves.start(a, b)
        for a, b in (
            (dc_hbm, dc_s), (w_hbm.at[3], w_s.at[3]), (o_hbm, o_s), (q_hbm, q_s), (k_hbm, k_s),
            (v_hbm, v_s),
        )
    ]
    down = RowScatter(wires, moves, dw_hbm.at[1], *scratch[22:26], odown_ref, early_hbm)
    up = RowScatter(wires, moves, dw_hbm.at[0], *scratch[26:30], oup_ref)
    out_sum = Scatter(wires, gr_s, 3, 1, True, *scratch[30:36], oo_ref)
    query_sum = Scatter(wires, gr_s, 0, 1, True, *scratch[36:42], oq_ref)
    later = [moves.start(h_hbm, h_s), moves.start(m_hbm, m_s)]
    get_maps = moves.start(w_hbm.at[0:3], w_s.at[0:3])
    wires.greet(
        flips(n)
        + [{"y": s} for s in range(1, ny)]
        + [{"x": s} for s in range(1, nx)]
        + [{"c": 1}]
    )
    chip_rows, width = dc_s.shape
    slot = m_s.shape[0]
    own = chip_rows // 2
    strip = min(STRIP, own)
    pairs = q_s.shape[1] // PAIR
    deep = om_s.shape[1]
    mine = pl.ds(pl.multiple_of(c * own, own), own)
    other = pl.ds(pl.multiple_of((1 - c) * own, own), own)
    bound = jnp.full((1, chip_rows), reaches[order[at["z"] * ny + at["y"]]], jnp.int32)
    held = {}
    steps = {}
    for name, group in ((DOWN, down), (UP, up), (OUT, out_sum), (QUERY, query_sum)):
        register(steps, name, group)

    def step(name):
        def keep(function):
            steps[name] = function
            return function

        return keep

    @step(LOAD)
    def _():
        for copy in loads:
            copy.wait()

    @step(HEADS)
    def _():
        mat_rows(g_s, dc_s, w_s.at[3], chip_rows, strip)

    for p in range(pairs):

        def pair(p=p):
            attend_pair_back(
                p, 256, bound, q_s, k_s, v_s, o_s, l_ref, g_s, dq_s, dk_s, dv_s, ds_s
            )

        steps[TWIN + p] = pair

    maps = [get_maps]

    def need_maps():
        while maps:
            maps.pop().wait()

    @step(INPUT + PART)
    def _():
        need_maps()

        def body(rows):
            give_s[rows, :] = dot(dq_s[rows, :], w_s[0], 1, 1).astype(BF)

        loop_rows(chip_rows, strip, body)
        held["rows"] = wires.send(give_s.at[other], got_s, c=1)

    @step(MEMORY + PART)
    def _():
        need_maps()
        piece = min(512, width)

        def body(rows):
            for col in range(0, width, piece):
                some = slice(col, col + piece)
                sums = dot(dk_s[rows, :], w_s[1, some, :], 1, 1)
                sums = (sums + dot(dv_s[rows, :], w_s[2, some, :], 1, 1)).astype(BF)
                for b in range(piece // deep):
                    index = col // deep + b
                    pm_s[index // 2, index % 2, rows, :] = sums[:, b * deep : (b + 1) * deep]

        loop_rows(slot, strip, body)
        held["memory"] = wires.send(pm_s.at[:, 1 - c], rm_s, c=1)

    @step(NORM)
    def _():
        held["rows"].wait_recv()
        upstream = give_s[mine, :].astype(F32) + got_s[...].astype(F32)
        grad, normed = norm_back_rows(x_ref[...], upstream, p_ref[1:2, :])
        total = dx_ref[...] + grad
        odx_ref[...] = total
        db_s[mine, :] = total.astype(BF)
        held["near"] = wires.send(db_s.at[mine], db_s.at[mine], c=1)
        line = lax.broadcasted_iota(jnp.int32, on_ref.shape, 0)
        on_ref[...] = jnp.where(line == 1, row_sum(upstream * normed), 0.0) + jnp.where(
            line == 5, row_sum(upstream), 0.0
        )

    @step(MEMORY + ON)
    def _():
        held["memory"].wait_recv()
        held["far"] = []
        for t in range(1, nx):
            index = (x + t) % nx
            sm_s[t - 1] = (pm_s[index, c].astype(F32) + rm_s[index].astype(F32)).astype(BF)
            held["far"].append(wires.send(sm_s.at[t - 1], cm_s.at[t - 1], x=t))

    @step(MEMORY + END)
    def _():
        total = pm_s[x, c].astype(F32) + rm_s[x].astype(F32)
        for t in range(1, nx):
            held["far"][t - 1].wait_recv()
            total = total + cm_s[t - 1].astype(F32)
        om_s[...] = total.astype(BF)
        moves.store(om_s, om)

    def weight_grad(i, left, right):
        size = min(256, width)
        for col in range(0, width, size):
            cols = slice(col, col + size)
            gr_s[i, cols, :] = dot(left[:, cols], right[...], 0, 0).astype(BF)

    @step(GRAD + OUTPUT)
    def _():
        weight_grad(3, dc_s, o_s)

    @step(GRAD + QUERIES)
    def _():
        later[0].wait()
        weight_grad(0, h_s, dq_s)

    @step(GRAD + TWIN)
    def _():
        later[1].wait()
        weight_grad(1, m_s, dk_s)
        weight_grad(2, m_s, dv_s)
        moves.store(gr_s.at[1:3], og)

    @step(ROWS + END)
    def _():
        held["near"].wait_recv()
        moves.store(db_s, odb)

    plan = backward_plan(
        CROSS_PLAN, nz, pairs,
        [LOAD, HEADS] + spelled(n, [(DOWN, (BEGIN,)), (UP, (BEGIN,))]),
        [INPUT + PART, MEMORY + PART, NORM, MEMORY + ON, GRAD + OUTPUT, GRAD + QUERIES, GRAD + TWIN],
        spelled(n, [(DOWN, (ALONG,)), (UP, (ALONG,)), (OUT, WHOLE), (QUERY, WHOLE)])
        + [MEMORY + END, ROWS + END],
    )
    for name in plan:
        steps[name]()
    osq_ref[...] = squares((oup_ref, odown_ref, oq_ref, oo_ref))
    moves.close()
    wires.close()


def cross_back(
    order, reaches, rows_grad, resid_grad, maps, saved, normed, frames, resid, params, ffn_grads,
    early,
):
    n = grid_sizes()
    nz, ny, nx = n["z"], n["y"], n["x"]
    queries, keys, values, mixed, logsum = saved
    chip_rows, width = rows_grad.shape
    own = chip_rows // 2
    slot, local = keys.shape
    hidden = ffn_grads.shape[2]
    rows, wide = width // (nz * ny), local // nx
    deep = width // (2 * nx)
    copies = 2 * RowScatter.copies(n) + 2 * Scatter.copies(n) + 3 + (nx - 1)
    vmem = pl.BlockSpec(memory_space=pltpu.VMEM)
    smem = pl.BlockSpec(memory_space=pltpu.SMEM)
    hbm = pl.BlockSpec(memory_space=pl.ANY)
    half = lambda *shape: pltpu.VMEM(shape, BF)
    return pl.pallas_call(
        functools.partial(cross_back_kernel, n),
        out_shape=[
            jax.ShapeDtypeStruct((rows, hidden), F32),
            jax.ShapeDtypeStruct((rows, hidden), F32),
            jax.ShapeDtypeStruct((1, rows, wide), F32),
            jax.ShapeDtypeStruct((1, rows, wide), F32),
            jax.ShapeDtypeStruct((2, width, local), BF),
            jax.ShapeDtypeStruct((own, width), F32),
            jax.ShapeDtypeStruct((chip_rows, width), BF),
            jax.ShapeDtypeStruct((slot, deep), BF),
            jax.ShapeDtypeStruct(params.shape, F32),
            jax.ShapeDtypeStruct(ONE, F32),
        ],
        in_specs=[smem, smem, hbm, vmem] + [hbm] * 5 + [vmem, hbm, hbm, vmem, vmem, hbm, hbm],
        out_specs=[vmem] * 4 + [hbm, vmem, hbm, hbm, vmem, vmem],
        scratch_shapes=[
            half(chip_rows, width),
            half(4, width, local),
            half(chip_rows, local),
            half(slot, local),
            half(slot, local),
            half(chip_rows, local),
            half(chip_rows, width),
            half(slot, width),
            half(chip_rows, local),
            half(chip_rows, local),
            half(slot, local),
            half(slot, local),
            half(2, slot, chip_rows),
            half(4, width, local),
            half(chip_rows, width),
            half(own, width),
            half(chip_rows, width),
            half(nx, 2, slot, deep),
            half(nx, slot, deep),
            half(nx - 1, slot, deep),
            half(nx - 1, slot, deep),
            half(slot, deep),
        ]
        + RowScatter.scratch(n, rows, hidden) * 2
        + Scatter.scratch(n, 1, True, rows, wide) * 2
        + [
            pltpu.SemaphoreType.DMA((copies,)),
            pltpu.SemaphoreType.DMA((copies,)),
            pltpu.SemaphoreType.DMA((14 + 2 * nz + 2 * (ny - 1),)),
        ],
        compiler_params=pltpu.CompilerParams(
            collective_id=5, has_side_effects=True, vmem_limit_bytes=56 * 2**20
        ),
        name="cross_back",
    )(
        order, reaches, rows_grad, resid_grad, maps, queries, keys, values, mixed, logsum, normed, frames,
        resid, params, ffn_grads, early,
    )


def self_back_kernel(
    n, order, lengths, db_hbm, dx_ref, w_hbm, q_hbm, k_hbm, v_hbm, o_hbm, l_ref, h_hbm, x_ref, p_ref,
    cg_hbm, m_hbm, np_ref, nq_ref, sq_ref, oc_ref, oo_ref, oq_ref, op_ref, os_ref, om_ref, on_ref,
    norm_ref, *scratch,
):
    (
        db_s, w_s, q_s, k_s, v_s, o_s, h_s, g_s, dq_s, dk_s, dv_s, ds_s, cg_s, gr_s, part_s, rc_s,
        sx_s, rx_s, out_s, np_s, nn_s, nf_s,
    ) = scratch[:22]
    one_s, near_s, sum_s, far_s = scratch[46:50]
    send_sem, recv_sem, go_sem, come_sem, move_sem = scratch[-5:]
    at = grid_place()
    z, y, x, c = at["z"], at["y"], at["x"], at["c"]
    nz, ny, nx = n["z"], n["y"], n["x"]
    data, model = z * ny + y, x * 2 + c
    wires = Wires(n, at, send_sem, recv_sem)
    moves = Moves(move_sem)
    get_cross = moves.start(cg_hbm, cg_s)
    loads = [
        moves.start(a, b)
        for a, b in (
            (db_hbm, db_s), (w_hbm.at[3], w_s.at[3]), (o_hbm, o_s), (q_hbm, q_s), (k_hbm, k_s),
            (v_hbm, v_s),
        )
    ]
    later = [moves.start(h_hbm, h_s), moves.start(w_hbm.at[0:3], w_s.at[0:3])]
    wires.greet(
        [
            dict(z=sz, y=sy, x=sx, c=sc)
            for sz in range(nz)
            for sy in range(ny)
            for sx in range(nx)
            for sc in range(2)
            if sz or sy or sx or sc
        ]
    )
    cross_sum = Scatter(wires, cg_s, 0, 2, False, *scratch[22:28], oc_ref)
    out_sum = Scatter(wires, gr_s, 3, 1, True, *scratch[28:34], oo_ref)
    query_sum = Scatter(wires, gr_s, 0, 1, True, *scratch[34:40], oq_ref)
    pair_sum = Scatter(wires, gr_s, 1, 2, False, *scratch[40:46], op_ref)
    chip_rows, width = db_s.shape
    slot = h_s.shape[0]
    own = chip_rows // 2
    strip = min(STRIP, own)
    pairs = q_s.shape[1] // PAIR
    chip_start = x * chip_rows
    bound = lax.broadcasted_iota(jnp.int32, (1, chip_rows), 1) + chip_start + 1
    bound = jnp.minimum(bound, lengths[order[data]])
    held = {}
    steps = {}
    for name, group in (
        (CROSS, cross_sum), (OUT, out_sum), (QUERY, query_sum), (KEYS, pair_sum)
    ):
        register(steps, name, group)

    def step(name):
        def keep(function):
            steps[name] = function
            return function

        return keep

    @step(LOAD + OTHER)
    def _():
        get_cross.wait()

    @step(LOAD)
    def _():
        for copy in loads:
            copy.wait()

    @step(MEMORY + GO)
    def _():
        held["memory"] = [
            wires.send(m_hbm.at[wires.peer(**shift)[0]], om_ref.at[data], **shift)
            for shift in dp_shifts(n)
        ]
        held["memory own"] = moves.start(m_hbm.at[data], om_ref.at[data])

    @step(MEMORY + END)
    def _():
        for copy in held["memory"]:
            copy.wait_recv()
        held["memory own"].wait()

    @step(HEADS)
    def _():
        mat_rows(g_s, db_s, w_s.at[3], chip_rows, strip)

    for p in range(pairs):

        def pair(p=p):
            attend_pair_back(
                p, 256, bound, q_s, k_s, v_s, o_s, l_ref, g_s, dq_s, dk_s, dv_s, ds_s
            )

        steps[TWIN + p] = pair

    def block(chip, core):
        return pl.ds(pl.multiple_of((chip * 2 + core) * own, own), own)

    def need(index):
        if later[index] is not None:
            later[index].wait()
            later[index] = None

    @step(INPUT + PART)
    def _():
        need(1)
        def keys_values(rows):
            sums = dot(dk_s[rows, :], w_s[1], 1, 1) + dot(dv_s[rows, :], w_s[2], 1, 1)
            part_s[rows, :] = sums.astype(BF)

        loop_rows(slot, strip, keys_values)

        def queries(rows):
            here = shifted(rows, chip_start)
            sums = part_s[here, :].astype(F32) + dot(dq_s[rows, :], w_s[0], 1, 1)
            part_s[here, :] = sums.astype(BF)

        loop_rows(chip_rows, strip, queries)
        held["core"] = [
            wires.send(part_s.at[block(b, 1 - c)], rc_s.at[b], c=1) for b in range(nx)
        ]

    @step(INPUT + ON)
    def _():
        for copy in held["core"]:
            copy.wait_recv()
        held["far"] = []
        for t in range(1, nx):
            index = (x + t) % nx
            sums = part_s[block(index, c), :].astype(F32) + rc_s[index].astype(F32)
            sx_s[t - 1] = sums.astype(BF)
            held["far"].append(wires.send(sx_s.at[t - 1], rx_s.at[t - 1], x=t))

    def weight_grad(i, left, right):
        size = min(256, width)
        for col in range(0, width, size):
            cols = slice(col, col + size)
            gr_s[i, cols, :] = dot(left[:, cols], right[...], 0, 0).astype(BF)

    @step(GRAD + OUTPUT)
    def _():
        weight_grad(3, db_s, o_s)

    @step(GRAD + QUERIES)
    def _():
        need(0)
        weight_grad(0, h_s.at[pl.ds(pl.multiple_of(chip_start, chip_rows), chip_rows)], dq_s)

    @step(GRAD + TWIN)
    def _():
        need(0)
        weight_grad(1, h_s, dk_s)
        weight_grad(2, h_s, dv_s)

    lines, deep = os_ref.shape[1], os_ref.shape[2]
    blocks = own // lines

    def homeward():
        for b in range(blocks):
            for m in range(2 * nx):
                target = (model * blocks + b, m)
                src = out_s.at[b * lines : (b + 1) * lines, m * deep : (m + 1) * deep]
                mine = jnp.logical_and(target[0] == data, model == m)
                remote = pltpu.make_async_remote_copy(
                    src_ref=src,
                    dst_ref=os_ref.at[data],
                    send_sem=go_sem.at[b * 2 * nx + m],
                    recv_sem=come_sem.at[data],
                    device_id=target,
                    device_id_type=pl.DeviceIdType.MESH,
                )
                yield mine, remote, pltpu.make_async_copy(src, os_ref.at[data], come_sem.at[data])

    @step(NORM)
    def _():
        upstream = part_s[block(x, c), :].astype(F32) + rc_s[x].astype(F32)
        for t in range(1, nx):
            held["far"][t - 1].wait_recv()
            upstream = upstream + rx_s[t - 1].astype(F32)
        grad, normed = norm_back_rows(x_ref[...].astype(F32), upstream, p_ref[0:1, :])
        out_s[...] = (dx_ref[...] + grad).astype(BF)
        for mine, remote, here in homeward():
            pl.when(mine)(lambda: here.start())
            pl.when(jnp.logical_not(mine))(lambda: remote.start())
        line = lax.broadcasted_iota(jnp.int32, np_ref.shape, 0)
        params = (
            np_ref[...]
            + nq_ref[...]
            + jnp.where(line == 0, row_sum(upstream * normed), 0.0)
            + jnp.where(line == 4, row_sum(upstream), 0.0)
        )
        columns = on_ref.shape[1]
        for k in range(nz * ny):
            np_s[0, k] = params[:, k * columns : (k + 1) * columns]
        held["norm near"] = [
            wires.send(np_s.at[0], nn_s.at[i], **s) for i, s in enumerate(mp_shifts(n))
        ]

    @step(HOME + END)
    def _():
        total = np_s[0]
        for i, copy in enumerate(held["norm near"]):
            copy.wait_recv()
            total = total + nn_s[i]
        np_s[1] = total
        held["norm far"] = [
            wires.send(np_s.at[1, wires.peer(**shift)[0]], nf_s.at[i], **shift)
            for i, shift in enumerate(dp_shifts(n))
        ]

    plan = backward_plan(
        SELF_PLAN, nz, pairs,
        [MEMORY + GO, LOAD + OTHER, LOAD, HEADS] + spelled(n, [(CROSS, (BEGIN,))]),
        [INPUT + PART, INPUT + ON, GRAD + OUTPUT, GRAD + QUERIES, GRAD + TWIN],
        spelled(n, [(CROSS, (MIDDLE, ALONG)), (OUT, WHOLE)])
        + [NORM, HOME + END]
        + spelled(n, [(QUERY, WHOLE), (KEYS, WHOLE)])
        + [MEMORY + END],
    )
    for name in plan:
        steps[name]()
    total = np_s[1, data]
    for i, copy in enumerate(held["norm far"]):
        copy.wait_recv()
        total = total + nf_s[i]
    on_ref[...] = total
    norm_squares = jnp.sum(total * total) / (2 * nx * ONE[0] * ONE[1])
    total = sq_ref[...] + squares((oc_ref, oo_ref, oq_ref, op_ref)) + norm_squares
    one_s[...] = total
    copies = [wires.send(one_s, near_s.at[i], **s) for i, s in enumerate(mp_shifts(n))]
    for i, copy in enumerate(copies):
        copy.wait_recv()
        total = total + near_s[i]
    sum_s[...] = total
    copies = [wires.send(sum_s, far_s.at[i], **s) for i, s in enumerate(dp_shifts(n))]
    for i, copy in enumerate(copies):
        copy.wait_recv()
        total = total + far_s[i]
    norm_ref[0] = jnp.sqrt(jnp.sum(total))
    for mine, remote, here in homeward():
        pl.when(jnp.logical_not(mine))(lambda: remote.wait_send())
    for r in range(nz * ny):
        pltpu.make_async_copy(os_ref.at[r], os_ref.at[r], come_sem.at[r]).wait()
    wires.close()


def self_back(
    order, lengths, rows_grad, resid_grad, maps, saved, normed, inputs, params, cross_grads, memory,
    norm_ffn, norm_cross, square_part,
):
    n = grid_sizes()
    nz, ny, nx = n["z"], n["y"], n["x"]
    data, model = nz * ny, 2 * nx
    queries, keys, values, mixed, logsum = saved
    chip_rows, width = rows_grad.shape
    own = chip_rows // 2
    slot, local = keys.shape
    rows, wide = width // data, local // nx
    utterances, lines, deep = memory.shape
    columns = width // data
    copies = 4 * Scatter.copies(n) + 3 * (data - 1) + nx + (nx - 1) + 2 * (model - 1)
    vmem = pl.BlockSpec(memory_space=pltpu.VMEM)
    smem = pl.BlockSpec(memory_space=pltpu.SMEM)
    hbm = pl.BlockSpec(memory_space=pl.ANY)
    half = lambda *shape: pltpu.VMEM(shape, BF)
    return pl.pallas_call(
        functools.partial(self_back_kernel, n),
        out_shape=[
            jax.ShapeDtypeStruct((2, rows, wide), F32),
            jax.ShapeDtypeStruct((1, rows, wide), F32),
            jax.ShapeDtypeStruct((1, rows, wide), F32),
            jax.ShapeDtypeStruct((2, rows, wide), F32),
            jax.ShapeDtypeStruct((data, lines, deep), BF),
            jax.ShapeDtypeStruct((data, lines, deep), BF),
            jax.ShapeDtypeStruct((params.shape[0], columns), F32),
            jax.ShapeDtypeStruct((1,), F32),
        ],
        in_specs=[smem, smem, hbm, vmem]
        + [hbm] * 5
        + [vmem, hbm, vmem, vmem, hbm, hbm, vmem, vmem, vmem],
        out_specs=[vmem] * 4 + [hbm, hbm, vmem, smem],
        scratch_shapes=[
            half(chip_rows, width),
            half(4, width, local),
            half(chip_rows, local),
            half(slot, local),
            half(slot, local),
            half(chip_rows, local),
            half(slot, width),
            half(chip_rows, local),
            half(chip_rows, local),
            half(slot, local),
            half(slot, local),
            half(2, slot, chip_rows),
            half(2, width, local),
            half(4, width, local),
            half(slot, width),
            half(nx, own, width),
            half(nx - 1, own, width),
            half(nx - 1, own, width),
            half(own, width),
            pltpu.VMEM((2, data, params.shape[0], columns), F32),
            pltpu.VMEM((model - 1, data, params.shape[0], columns), F32),
            pltpu.VMEM((data - 1, params.shape[0], columns), F32),
        ]
        + Scatter.scratch(n, 2, False, rows, wide)
        + Scatter.scratch(n, 1, True, rows, wide)
        + Scatter.scratch(n, 1, True, rows, wide)
        + Scatter.scratch(n, 2, False, rows, wide)
        + [
            pltpu.VMEM(ONE, F32),
            pltpu.VMEM((model - 1,) + ONE, F32),
            pltpu.VMEM(ONE, F32),
            pltpu.VMEM((data - 1,) + ONE, F32),
            pltpu.SemaphoreType.DMA((copies,)),
            pltpu.SemaphoreType.DMA((copies,)),
            pltpu.SemaphoreType.DMA((data,)),
            pltpu.SemaphoreType.DMA((data,)),
            pltpu.SemaphoreType.DMA((14,)),
        ],
        compiler_params=pltpu.CompilerParams(
            collective_id=1, has_side_effects=True, vmem_limit_bytes=56 * 2**20
        ),
        name="self_back",
    )(
        order, lengths, rows_grad, resid_grad, maps, queries, keys, values, mixed, logsum, normed,
        inputs, params, cross_grads, memory, norm_ffn, norm_cross, square_part,
    )


def adam_step(weight, moment, square, gradient, step_rate, weight_decay):
    moment_new = BETA_FIRST * moment + (1.0 - BETA_FIRST) * gradient
    square_new = BETA_SECOND * square + (1.0 - BETA_SECOND) * gradient * gradient
    moment_hat = moment_new * (1.0 / (1.0 - BETA_FIRST**STEP))
    square_hat = square_new * (1.0 / (1.0 - BETA_SECOND**STEP))
    updated = weight - step_rate * (
        moment_hat / (jnp.sqrt(square_hat) + ADAM_EPSILON) + weight_decay * weight
    )
    return (updated, moment_new, square_new)


def update_kernel(order, norm, *refs):
    grads, refs = refs[:9], refs[9:]
    y_hbm, refs = refs[0], refs[1:]
    back, refs = refs[:2], refs[2:]
    old, refs = refs[:12], refs[12:]
    oy, refs = refs[0], refs[1:]
    home, refs = refs[:2], refs[2:]
    new, refs = refs[:12], refs[12:]
    vault, refs = refs[:12], refs[12:]
    back_s, home_s, y_s, move_sem = refs[:2], refs[2:4], refs[4], refs[5]
    moves = Moves(move_sem)
    back_loads = [moves.start(a, b) for a, b in zip(back, back_s)]
    loads = {}
    for kind in (2, 1, 0):
        loads[kind] = [moves.start(old[3 * j + kind], vault[3 * j + kind]) for j in range(4)]
    get_y = moves.start(y_hbm, y_s)
    clip_scale = jnp.minimum(1.0, THRESHOLD / (norm[0] + 1e-06))

    def apply(kind, part, gradient, rate, decay):
        weight, moment, square, average = (vault[3 * j + kind] for j in range(4))
        updated, moment_new, square_new = adam_step(
            weight[part], moment[part], square[part], clip_scale * gradient, rate, decay
        )
        mixed = AVERAGING * average[part] + (1.0 - AVERAGING) * updated
        for j, value in enumerate((updated, moment_new, square_new, mixed)):
            vault[3 * j + kind][part] = value
            moves.store(vault[3 * j + kind].at[part], new[3 * j + kind].at[part])

    utterances = home_s[0].shape[0]
    for copy in back_loads:
        copy.wait()
    for i in range(utterances):
        place = 0
        for r in range(utterances):
            place = place + jnp.where(order[r] == i, r, 0)
        for src, dst in zip(back_s, home_s):
            dst[i] = src[place].astype(F32)
    for src, dst in zip(home_s, home):
        moves.store(src, dst)

    sq, sp, so, cq, cp, co, up, down, line = grads
    for copy in loads[2]:
        copy.wait()
    apply(2, slice(None), line[...], NORM_RATE, 0.0)
    for copy in loads[1]:
        copy.wait()
    for part, ref in ((0, up), (1, down)):
        apply(1, slice(part, part + 1), ref[...][None], MATRIX_RATE, MATRIX_DECAY)
    for copy in loads[0]:
        copy.wait()
    for part, ref in (
        (slice(0, 1), sq), (slice(1, 3), sp), (slice(3, 4), so), (slice(4, 5), cq),
        (slice(5, 7), cp), (slice(7, 8), co),
    ):
        apply(0, part, ref[...], MATRIX_RATE, MATRIX_DECAY)

    get_y.wait()
    moves.store(y_s, oy)
    moves.close()


def update(order, norm, grads, output, back, old):
    vmem = pl.BlockSpec(memory_space=pltpu.VMEM)
    smem = pl.BlockSpec(memory_space=pltpu.SMEM)
    hbm = pl.BlockSpec(memory_space=pl.ANY)
    full = lambda v: jax.ShapeDtypeStruct(v.shape, F32)
    return pl.pallas_call(
        update_kernel,
        out_shape=[jax.ShapeDtypeStruct(output.shape, BF)]
        + [full(v) for v in back]
        + [full(v) for v in old],
        in_specs=[smem, smem] + [vmem] * 9 + [hbm] * 15,
        out_specs=[hbm] * 15,
        scratch_shapes=[pltpu.VMEM(v.shape, F32) for v in old]
        + [pltpu.VMEM(v.shape, BF) for v in back]
        + [pltpu.VMEM(v.shape, F32) for v in back]
        + [pltpu.VMEM(output.shape, BF)]
        + [pltpu.SemaphoreType.DMA((64,))],
        compiler_params=pltpu.CompilerParams(vmem_limit_bytes=56 * 2**20),
        name="update",
    )(order, norm, *grads, output, *back, *old)


def per_device(
    states,
    memory,
    cotangent,
    lengths,
    memory_lengths,
    regroup_order,
    attn_weights,
    ffn_weights,
    norm_params,
    attn_mean,
    ffn_mean,
    norm_mean,
    attn_square,
    ffn_square,
    norm_square,
    attn_average,
    ffn_average,
    norm_average,
):
    n = grid_sizes()
    at = grid_place()
    nz, ny, nx = n["z"], n["y"], n["x"]
    data_index = lax.axis_index("dp")
    model_index = lax.axis_index("mp")
    data_size = lax.axis_size("dp")
    width = states.shape[2] * lax.axis_size("mp")
    slot = states.shape[1] * data_size
    own_rows = cotangent.shape[1]
    chip_rows = 2 * own_rows
    chip_start = at["x"] * chip_rows

    (
        weights_self,
        weights_cross,
        ffn_maps,
        norm_values,
        frames,
        inputs,
        normed_first,
        query_self,
        key_self,
        value_self,
        mixed_self,
        logsum_self,
        resid_one_own,
        normed_second,
        query_cross,
        key_cross,
        value_cross,
        mixed_cross,
        logsum_cross,
        resid_two_own,
        normed_third,
    ) = forward(
        regroup_order,
        lengths,
        memory_lengths,
        states,
        memory,
        norm_params,
        attn_weights,
        ffn_weights,
        own_rows,
    )

    layer_output, grad_two, cross_rows, ffn_grads, early, norm_ffn = feed_forward(
        regroup_order, lengths, normed_third, resid_two_own, ffn_maps, cotangent[0], norm_values
    )
    (
        shard_up,
        shard_down,
        cross_q,
        cross_o,
        cross_grads,
        grad_one,
        self_rows,
        memory_part,
        norm_cross,
        square_part,
    ) = (
        cross_back(
            regroup_order,
            memory_lengths,
            cross_rows,
            grad_two,
            weights_cross,
            (query_cross, key_cross, value_cross, mixed_cross, logsum_cross),
            normed_second,
            frames,
            resid_one_own,
            norm_values,
            ffn_grads,
            early,
        )
    )
    cross_p, self_o, self_q, self_p, back_states, back_memory, norm_shard, grad_norm = self_back(
        regroup_order,
        lengths,
        self_rows,
        grad_one,
        weights_self,
        (query_self, key_self, value_self, mixed_self, logsum_self),
        normed_first,
        inputs,
        norm_values,
        cross_grads,
        memory_part.reshape(data_size, -1, memory_part.shape[1]),
        norm_ffn,
        norm_cross,
        square_part,
    )
    grads = (self_q, self_p, self_o, cross_q, cross_p, cross_o, shard_up, shard_down, norm_shard)
    results = update(
        regroup_order,
        grad_norm,
        grads,
        layer_output,
        (back_states, back_memory),
        (
            attn_weights,
            ffn_weights,
            norm_params,
            attn_mean,
            ffn_mean,
            norm_mean,
            attn_square,
            ffn_square,
            norm_square,
            attn_average,
            ffn_average,
            norm_average,
        ),
    )
    return (results[0][None],) + tuple(results[1:]) + (grad_norm[0],)


def solution(mesh):
    rows = P(None, "dp", "mp")
    line = P(None, "dp")
    return jax.shard_map(
        per_device,
        mesh=mesh,
        in_specs=(rows, rows, P("dp", "mp", None), P(), P(), P())
        + (rows, rows, line) * 4,
        out_specs=(P("dp", "mp", None), rows, rows) + (rows, rows, line) * 4 + (P(),),
        check_vma=False,
    )
```
